128 devices in a mesh: section: 2 (over y_lo), row: 4 (over y_hi, core), col: 16 (over x, z).
Axes of the slice: x: 4, y: 4 (y_hi: 2, y_lo: 2; y = y_hi * 2 + y_lo), z: 4, core: 2. Of those that a mesh axis runs over, the one named last changes fastest.
Arguments:
- inputs: bfloat16 [2, 16, 384, 1536], P(None, 'col', 'row'), may hold values from -6 to 6
- cotangent: bfloat16 [2, 16, 384, 1536], P(None, 'col', 'row'), may hold values from -6 to 6
- segment_ids: int32 [2, 16, 384], P(None, 'col'), may hold values from 0 to 1, as said below
- routes: int32 [2, 2, 16, 384, 4], P('section', None, 'col', 'row'), may hold values from 0 to 31, all different within a row; in each aligned block of 96 rows (0 to 95, 96 to 191, ..., all dimensions but the last counted through in order) at most 15 rows name the same one
- attn_gain: bfloat16 [2, 1536], P('section', ('row', 'col')), may hold values from 0.5 to 1.5
- w_query: bfloat16 [2, 1536, 1536], P('section', ('row', 'col')), may hold values from -0.15625 to 0.15625
- w_key: bfloat16 [2, 1536, 256], P('section', ('row', 'col')), may hold values from -0.15625 to 0.15625
- w_value: bfloat16 [2, 1536, 256], P('section', ('row', 'col')), may hold values from -0.15625 to 0.15625
- w_out: bfloat16 [2, 1536, 1536], P('section', ('row', 'col')), may hold values from -0.625 to 0.625
- ffn_gain: bfloat16 [2, 1536], P('section', ('row', 'col')), may hold values from 0.5 to 1.5
- w_router: bfloat16 [2, 1536, 32], P('section', ('row', 'col')), may hold values from -0.078125 to 0.078125
- w_gate: bfloat16 [2, 32, 768, 1536], P('section', 'col', 'row'), may hold values from -0.15625 to 0.15625
- w_up: bfloat16 [2, 32, 768, 1536], P('section', 'col', 'row'), may hold values from -0.15625 to 0.15625
- w_down: bfloat16 [2, 32, 768, 1536], P('section', 'col', 'row'), may hold values from -0.21875 to 0.21875
Outputs:
- layer_outputs: float32 [2, 2, 16, 384, 1536], P('section', None, 'col', 'row')
- input_grads: float32 [2, 2, 16, 384, 1536], P('section', None, 'col', 'row')
- attn_gain_grad: float32 [2, 1536], P('section', ('row', 'col'))
- query_grad: float32 [2, 1536, 1536], P('section', ('row', 'col'))
- key_grad: float32 [2, 1536, 256], P('section', ('row', 'col'))
- value_grad: float32 [2, 1536, 256], P('section', ('row', 'col'))
- out_grad: float32 [2, 1536, 1536], P('section', ('row', 'col'))
- ffn_gain_grad: float32 [2, 1536], P('section', ('row', 'col'))
- router_grad: float32 [2, 1536, 32], P('section', ('row', 'col'))
- gate_grad: float32 [2, 32, 768, 1536], P('section', 'col', 'row')
- up_grad: float32 [2, 32, 768, 1536], P('section', 'col', 'row')
- down_grad: float32 [2, 32, 768, 1536], P('section', 'col', 'row')
The draws below stay inside these ranges and needn't reach their ends.
Inputs may be any that keep to these rules, and one draw needn't show every extreme that they name: `segment_ids`: segment ids never fall along a sequence; a sequence holds one document or two, and each document has 144 positions or more; in each micro-batch one sequence is a single document from its first position to its last. In the rows of one device (aligned blocks of 96 tokens of one sequence) no expert is named by more than 15 routes, a bound that some block reaches.
All inputs are finite; a program needn't handle non-finite values.
Results may differ from the reference program's by a relative error of at most 0.025.
Values may be sent and summed in bfloat16 or wider, within the bound.
No kernel may reach another device: no remote copies, remote signals or barrier semaphores. Data moves between devices by JAX's collectives and lax.ppermute only.
A program may use at most 448 MiB of HBM per device.

```python
import math
import jax
import jax.numpy as jnp
import numpy as np
from jax import lax

D = 1536
HEADS = 12
KV_HEADS = 2
HEAD_DIM = 128
EFF = 768
EXPERTS = 32
TOP = 4
TOK_DEV = 96
MICRO = 2
LAYERS = 2
SEQS = 16
SEQ = 384
KVD = 256
CAP = 15


def draw_segment_ids(key, part):
    key = jax.random.fold_in(key, 7)
    cut_key, whole_key = jax.random.split(key)
    cuts = jax.random.randint(cut_key, (MICRO, SEQS, 1), 3 * SEQ // 8, SEQ - 3 * SEQ // 8 + 1)
    whole = jax.random.randint(whole_key, (MICRO, 1), 0, SEQS)
    keep_cuts = (jnp.arange(SEQS)[None, :] != whole).astype(jnp.int32)
    positions = jnp.arange(SEQ)
    segment = jnp.sum((positions[None, None, :, None] >= cuts[:, :, None, :]).astype(jnp.int32), -1)
    return (segment * keep_cuts[:, :, None]).astype(jnp.int32)


def block_scale(key, dims, shards, smallest, largest):
    def one(dim, blocks):
        steps = jax.random.uniform(jax.random.fold_in(jax.random.fold_in(key, 6), dim), (blocks,), jnp.float32, smallest / len(shards), largest / len(shards))
        return jnp.repeat(jnp.exp(steps), dims[dim] // blocks).reshape((-1,) + (1,) * (len(dims) - dim - 1))

    level = one(*shards[0])
    for cut in shards[1:]:
        level = level * one(*cut)
    return level


def deal_out(rng, own, number, rows, number_of, top, bound, skew):
    order = jax.random.permutation(rng, number_of)
    heavy_load, usual = portions_of(number_of, rows * top, bound, skew, True), portions_of(number_of, rows * top, bound, skew, False)
    places = jnp.arange(number_of)

    def named(tallies, rotation):
        used = int((tallies > 0).sum())
        fixed = max(1, used // 4)
        shifted = fixed + (places - fixed + rotation * (used - fixed)) % max(1, number_of - fixed)
        return jnp.zeros((number_of,), jnp.int32).at[order[jnp.where(places < fixed, places, shifted)]].set(jnp.asarray(tallies, jnp.int32))

    tallies = jnp.where(number % 4 == 0, named(heavy_load, number // 4), named(usual, number - number // 4 - 1))
    mixed = jax.random.permutation(jax.random.fold_in(own, 3), number_of)
    donor, receiver = mixed[0:number_of // 2 * 2:2], mixed[1:number_of // 2 * 2:2]
    room = jnp.minimum(tallies[donor] - 1, bound - tallies[receiver]) // 2
    room = jnp.where((donor == order[0]) | (receiver == order[0]) | (tallies[receiver] == 0), 0, jnp.maximum(room, 0))
    shifted = jax.random.randint(jax.random.fold_in(own, 4), (number_of // 2,), 0, 1 << 20) % (room + 1)
    tallies = tallies.at[donor].add(-shifted).at[receiver].add(shifted)
    members = jnp.searchsorted(jnp.cumsum(tallies), jnp.arange(rows * top), side="right").astype(jnp.int32)
    listing = members.reshape(top, rows).T
    listing = listing[jax.random.permutation(jax.random.fold_in(own, 1), rows)]
    rotation = jax.random.randint(jax.random.fold_in(own, 2), (rows, 1), 0, top)
    return jnp.take_along_axis(listing, (jnp.arange(top)[None, :] + rotation) % top, axis=1)


def portions_of(amount, total, bound, slope, full):
    weights = [(1 << 20) // math.isqrt(standing ** slope) + 1 for standing in range(1, amount + 1)]
    largest = bound if full else min(bound, max(-(-total // amount), total * weights[0] // sum(weights)))
    least = 1 if total - largest >= amount - 1 else 0
    given, surplus = [largest] + [least] * (amount - 1), total - largest - least * (amount - 1)
    while surplus > 0:
        movable = [i for i in range(1, amount) if given[i] < largest] or [i for i in range(1, amount) if given[i] < bound]
        mass, left = sum([weights[i] for i in movable]), surplus
        for i in movable:
            more = min(bound - given[i], max(1, left * weights[i] // mass), surplus)
            given[i] = given[i] + more
            surplus = surplus - more
    return np.array(given)


def bell_draw(own_key, shape, scale, reach, pieces=(), held_as=jnp.bfloat16):
    drawn = jax.random.normal(own_key, shape, jnp.float32) * scale
    if len(pieces) > 0:
        drawn = block_scale(own_key, shape, pieces, -0.22, 0.18) * drawn
    return jnp.clip(drawn, min=-reach, max=reach).astype(held_as)


def setup_inputs(seed: int = 0) -> dict:
    key_list = jax.random.split(jax.random.key(seed), 15)
    inputs = bell_draw(key_list[0], (MICRO, SEQS, SEQ, D), 1.0, 6.0, ((1, 16), (2, 4)))
    cotangent = bell_draw(key_list[1], (MICRO, SEQS, SEQ, D), 1.0, 6.0, ((1, 16), (2, 4)))
    segment_ids = draw_segment_ids(jax.random.fold_in(key_list[14], 71), 0)
    routes_keys = jax.random.split(jax.random.fold_in(key_list[3], 1), LAYERS * MICRO * SEQS * SEQ // TOK_DEV)
    routes_turns = jax.random.permutation(jax.random.fold_in(key_list[3], 3), LAYERS * MICRO * SEQS * SEQ // TOK_DEV)
    routes = jax.vmap(lambda own, number: deal_out(jax.random.fold_in(key_list[3], 2), own, number, TOK_DEV, EXPERTS, TOP, CAP, 1))(routes_keys, routes_turns).reshape((LAYERS, MICRO, SEQS, SEQ, TOP))
    attn_gain = jnp.clip(1.0 + 0.1 * jax.random.normal(key_list[4], (LAYERS, D), jnp.float32), 0.5, 1.5).astype(jnp.bfloat16)
    w_query = bell_draw(key_list[5], (LAYERS, D, D), D ** -0.5, 0.15625, ((0, 2), (1, 64)))
    w_key = bell_draw(key_list[6], (LAYERS, D, KVD), D ** -0.5, 0.15625, ((0, 2), (1, 64)))
    w_value = bell_draw(key_list[7], (LAYERS, D, KVD), D ** -0.5, 0.15625, ((0, 2), (1, 64)))
    w_out = bell_draw(key_list[8], (LAYERS, D, D), (D // 16) ** -0.5, 0.625, ((0, 2), (1, 64)))
    ffn_gain = jnp.clip(1.0 + 0.1 * jax.random.normal(key_list[9], (LAYERS, D), jnp.float32), 0.5, 1.5).astype(jnp.bfloat16)
    w_router = bell_draw(key_list[10], (LAYERS, D, EXPERTS), (4 * D) ** -0.5, 0.078125, ((0, 2), (1, 64)))
    w_gate = bell_draw(key_list[11], (LAYERS, EXPERTS, EFF, D), D ** -0.5, 0.15625, ((0, 2), (1, 16), (2, 4)))
    w_up = bell_draw(key_list[12], (LAYERS, EXPERTS, EFF, D), D ** -0.5, 0.15625, ((0, 2), (1, 16), (2, 4)))
    w_down = bell_draw(key_list[13], (LAYERS, EXPERTS, EFF, D), EFF ** -0.5, 0.21875, ((0, 2), (1, 16), (2, 4)))
    return dict(inputs=inputs, cotangent=cotangent, segment_ids=segment_ids, routes=routes, attn_gain=attn_gain, w_query=w_query, w_key=w_key, w_value=w_value, w_out=w_out, ffn_gain=ffn_gain, w_router=w_router, w_gate=w_gate, w_up=w_up, w_down=w_down)


@jax.custom_vjp
def low(v):
    return lax.optimization_barrier(v.astype(jnp.bfloat16)).astype(jnp.float32)

@jax.custom_vjp
def low_back(v):
    return v

def low_keep(v):
    return (low(v), None)

def low_pass(kept, grad):
    return (grad,)

def back_keep(v):
    return (v, None)

def back_low(kept, grad):
    return (low(grad),)
low.defvjp(low_keep, low_pass)
low_back.defvjp(back_keep, back_low)

def product(left, right):
    return jnp.matmul(left, right, precision=lax.Precision.HIGHEST)

def norm_apply(stream, gain):
    return stream * lax.rsqrt(lax.optimization_barrier(jnp.mean(stream * stream, -1, keepdims=True)) + 1e-06) * gain

def rotate(vectors, positions):
    half = vectors.shape[-1] // 2
    freqs = 10000.0 ** (-2.0 * jnp.arange(half).astype(jnp.float32) / vectors.shape[-1])
    angles = positions.astype(jnp.float32)[:, None] * freqs[None, :]
    cosine = jnp.cos(angles)[:, None, :]
    sine = jnp.sin(angles)[:, None, :]
    first = vectors[..., :half]
    second = vectors[..., half:]
    return jnp.concatenate([first * cosine - second * sine, second * cosine + first * sine], -1)

def gelu_tanh(values):
    return 0.5 * values * (1.0 + jnp.tanh(0.7978845608028654 * (values + 0.044715 * values * values * values)))

def attend(block):
    query_row, key_row, value_row, segment_row = block
    positions = jnp.arange(SEQ, dtype=jnp.int32)
    grouped = query_row.reshape(SEQ, KV_HEADS, HEADS // KV_HEADS, HEAD_DIM)
    scores = low_back(jnp.einsum('qhgd,khd->hgqk', grouped, key_row, precision=lax.Precision.HIGHEST) * HEAD_DIM ** (-0.5))
    mask = (positions[None, :] <= positions[:, None]) & (segment_row[None, :] == segment_row[:, None])
    weights = low(jax.nn.softmax(jnp.where(mask[None, None], scores, -1e+30), -1))
    return jnp.einsum('hgqk,khd->qhgd', weights, value_row, precision=lax.Precision.HIGHEST).reshape(SEQ, D)

def expert_apply(block):
    expert_rows, gate_weight, up_weight, down_weight = block
    gate = low_back(product(expert_rows, gate_weight.T))
    lifted = low_back(product(expert_rows, up_weight.T))
    hidden = low(gelu_tanh(gate) * lifted)
    return low_back(low(product(hidden, down_weight)))

def mixture(normed, chosen_routes, w_router, w_gate, w_up, w_down):
    tokens = SEQS * SEQ
    blocks = tokens // TOK_DEV
    logits = low_back(product(normed, w_router))
    probs = jax.nn.softmax(logits, -1)
    expert_ids = jnp.arange(EXPERTS, dtype=jnp.int32)
    chosen = (chosen_routes[:, :, None] == expert_ids[None, None, :]).astype(jnp.float32)
    picked = lax.optimization_barrier(jnp.sum(probs[:, None, :] * chosen, -1))
    gates = picked / lax.optimization_barrier(jnp.sum(picked, -1, keepdims=True))
    flat_routes = chosen_routes.reshape(tokens * TOP)
    hot_table = (flat_routes[:, None] == expert_ids[None, :]).astype(jnp.int32)
    blocked = hot_table.reshape(blocks, TOK_DEV * TOP, EXPERTS)
    before = (jnp.cumsum(blocked, 1) - blocked).reshape(tokens * TOP, EXPERTS)
    slot_rank = lax.optimization_barrier(jnp.sum(before * hot_table, -1))
    owner_block = jnp.arange(tokens * TOP, dtype=jnp.int32) // (TOK_DEV * TOP)
    rows_at = flat_routes * (blocks * CAP) + owner_block * CAP + slot_rank
    buffers = jnp.zeros((EXPERTS * blocks * CAP, D), jnp.float32).at[rows_at].add(jnp.repeat(normed, TOP, axis=0))
    produced = lax.map(jax.checkpoint(expert_apply), (buffers.reshape(EXPERTS, blocks * CAP, D), w_gate, w_up, w_down))
    picked_rows = produced.reshape(EXPERTS * blocks * CAP, D)[rows_at].reshape(tokens, TOP, D)
    return lax.optimization_barrier(jnp.sum(gates[:, :, None] * picked_rows, 1))

def layer(stream, segments, chosen_routes, layer_params):
    gain_attn, w_query, w_key, w_value, w_out, gain_ffn, w_router, w_gate, w_up, w_down = layer_params
    positions = jnp.arange(SEQ, dtype=jnp.int32)
    normed = low(norm_apply(stream, gain_attn))
    query = low(rotate(low_back(product(normed, w_query)).reshape(SEQS, SEQ, HEADS, HEAD_DIM), positions))
    key_proj = low(rotate(low_back(product(normed, w_key)).reshape(SEQS, SEQ, KV_HEADS, HEAD_DIM), positions))
    value_proj = low(low_back(product(normed, w_value))).reshape(SEQS, SEQ, KV_HEADS, HEAD_DIM)
    mixed = lax.map(jax.checkpoint(attend), (query, key_proj, value_proj, segments))
    mixed = low(low_back(mixed))
    middle = stream + low_back(product(mixed, w_out))
    normed_ffn = low(norm_apply(middle, gain_ffn))
    moe_out = mixture(normed_ffn.reshape(SEQS * SEQ, D), chosen_routes.reshape(SEQS * SEQ, TOP), w_router, w_gate, w_up, w_down)
    return middle + moe_out.reshape(SEQS, SEQ, D)

def reference(inputs, cotangent, segment_ids, routes, attn_gain, w_query, w_key, w_value, w_out, ffn_gain, w_router, w_gate, w_up, w_down):
    floats = tuple((item.astype(jnp.float32) for item in (attn_gain, w_query, w_key, w_value, w_out, ffn_gain, w_router, w_gate, w_up, w_down)))
    start = inputs.astype(jnp.float32)

    def forward(weights, start, shift_in):
        layer_outs = [[] for index in range(LAYERS)]
        for micro_index in range(MICRO):
            stream = start[micro_index]
            for layer_index in range(LAYERS):
                layer_params = tuple((item[layer_index] for item in weights))
                stream = layer(stream, segment_ids[micro_index], routes[layer_index, micro_index], layer_params)
                layer_outs[layer_index].append(stream)
                if layer_index == 0:
                    stream = stream + shift_in[micro_index]
        return jnp.stack([jnp.stack(outs) for outs in layer_outs])
    outputs, pullback = jax.vjp(forward, floats, start, jnp.zeros_like(start))
    target = cotangent.astype(jnp.float32)
    seeds = jnp.stack([jnp.zeros_like(target), target])
    weight_grads, start_grads, shift_grads = pullback(seeds)
    return (outputs, jnp.stack([start_grads, shift_grads]), weight_grads[0], weight_grads[1], weight_grads[2], weight_grads[3], weight_grads[4], weight_grads[5], weight_grads[6], weight_grads[7], weight_grads[8], weight_grads[9])
```

```python
import jax
import jax.numpy as jnp
from jax import lax
from jax.sharding import PartitionSpec as P

HEAD_DIM = 128
ROOMS = 16
EPSILON = 1e-06
LANES = 128
BF = jnp.bfloat16
F32 = jnp.float32


def dot(left, right, contract=(1, 0)):
    return lax.dot_general(
        left, right, (((contract[0],), (contract[1],)), ((), ())), preferred_element_type=F32
    )


def swapped(value, step):
    rows = lax.axis_size("row")
    return lax.ppermute(value, "row", [(r, r ^ step) for r in range(rows)])


def norm_parts(stream):
    return lax.rsqrt(jnp.mean(stream * stream, -1, keepdims=True) + EPSILON)


def norm_back(grad, stream, gain):
    inverse = norm_parts(stream)
    unit = stream * inverse
    scaled = grad * gain
    back = inverse * (scaled - unit * jnp.mean(scaled * unit, -1, keepdims=True))
    return back, jnp.sum(grad * unit, 0, keepdims=True)


def turned(vectors, cosine, sine):
    done = []
    for at in range(0, vectors.shape[1], HEAD_DIM):
        one = vectors[:, at : at + HEAD_DIM]
        half = HEAD_DIM // 2
        other = jnp.concatenate([one[:, half:], one[:, :half]], -1)
        done.append(one * cosine + other * sine)
    return jnp.concatenate(done, -1) if len(done) > 1 else done[0]


def stacked_heads(value, first, count):
    return jnp.concatenate(
        [value[:, (first + j) * HEAD_DIM : (first + j + 1) * HEAD_DIM] for j in range(count)], 0
    )


def unstacked_heads(value, count):
    tokens = value.shape[0] // count
    return jnp.concatenate([value[j * tokens : (j + 1) * tokens] for j in range(count)], 1)


def project(stream, gain, w_qkv, cosine, sine, width):
    normed = (stream * norm_parts(stream) * gain).astype(BF)
    qkv = dot(normed, w_qkv)
    kv_width = (qkv.shape[1] - width) // 2
    turned_part = turned(qkv[:, : width + kv_width], cosine, sine)
    query = turned_part[:, :width].astype(BF)
    pair = jnp.concatenate([turned_part[:, width:], qkv[:, width + kv_width :]], -1).astype(BF)
    return normed, query, pair


def attend(stream, query, pairs, bias, w_out, gain, w_router, chosen, dispatch):
    kv_heads = pairs.shape[1] // (2 * HEAD_DIM)
    group = query.shape[1] // HEAD_DIM // kv_heads
    biases = jnp.concatenate([bias] * group, 0)
    mixed, kept = [], []
    for h in range(kv_heads):
        keys = pairs[:, h * HEAD_DIM : (h + 1) * HEAD_DIM]
        values = pairs[:, (kv_heads + h) * HEAD_DIM : (kv_heads + h + 1) * HEAD_DIM]
        queries = stacked_heads(query, h * group, group)
        scores = dot(queries, keys, (1, 1)) * HEAD_DIM ** (-0.5) + biases
        expo = jnp.exp(scores - jnp.max(scores, -1, keepdims=True))
        probs = (expo / jnp.sum(expo, -1, keepdims=True)).astype(BF)
        kept.append(probs)
        mixed.append(unstacked_heads(dot(probs, values).astype(BF), group))
    mixed = jnp.concatenate(mixed, 1)
    middle = stream + dot(mixed, w_out)
    normed_ffn = (middle * norm_parts(middle) * gain).astype(BF)
    logits = jnp.where(chosen > 0, dot(normed_ffn, w_router), -1e30)
    expo = jnp.where(chosen > 0, jnp.exp(logits - jnp.max(logits, -1, keepdims=True)), 0.0)
    gates = expo / jnp.sum(expo, -1, keepdims=True)
    outgoing = dot(dispatch, normed_ffn).astype(BF)
    return mixed, middle, normed_ffn, gates, outgoing, jnp.stack(kept)


def rows_of(arrived, j):
    columns, slots, width = arrived.shape
    return arrived[:, j * ROOMS : (j + 1) * ROOMS].reshape(columns * ROOMS, width)


def rows_back(parts, columns):
    return jnp.concatenate([p.reshape(columns, ROOMS, p.shape[1]) for p in parts], 1)


def expert_forward(arrived, w_gate, w_up, w_down):
    produced, kept = [], []
    for j in range(w_gate.shape[0]):
        rows = rows_of(arrived, j)
        gate = dot(rows, w_gate[j], (1, 1))
        lifted = dot(rows, w_up[j], (1, 1))
        square = gate * gate
        bend = jnp.tanh(0.7978845608028654 * gate * (1.0 + 0.044715 * square))
        slope = 0.5 * (1.0 + bend) + 0.5 * gate * (1.0 - bend * bend) * (
            0.7978845608028654 * (1.0 + 3 * 0.044715 * square)
        )
        active = 0.5 * gate * (1.0 + bend)
        hidden = (active * lifted).astype(BF)
        produced.append(dot(hidden, w_down[j]).astype(BF))
        kept.append((hidden, active.astype(BF), (slope * lifted).astype(BF)))
    return rows_back(produced, arrived.shape[0]), tuple(kept)


def gates_of_slots(gates, spread, places):
    return dot(gates.astype(BF), spread) * places.astype(F32)


def combine(returned, middle, gates, spread, places):
    weights = gates_of_slots(gates, spread, places).astype(BF)
    return middle + dot(weights, returned)


def split_grads(grad, returned, gates, spread, places, dispatch):
    low = grad.astype(BF)
    inner = dot(low, returned, (1, 1)) * places.astype(F32)
    gate_grads = dot(inner.astype(BF), spread, (1, 1))
    logit_grads = gates * (gate_grads - jnp.sum(gates * gate_grads, -1, keepdims=True))
    slots = dispatch.shape[0]
    own = lax.broadcasted_iota(jnp.int32, (slots, LANES), 0) // ROOMS
    here = own == lax.broadcasted_iota(jnp.int32, (slots, LANES), 1)
    scale = jnp.sum(
        jnp.where(here, dot(dispatch, gates.astype(BF)), 0.0), -1, keepdims=True
    )
    return logit_grads.astype(BF), (dot(dispatch, low) * scale).astype(BF)


def expert_backward(arrived_grads, kept, w_gate, w_up, w_down):
    sent, backs = [], []
    for j in range(w_gate.shape[0]):
        hidden, active, bent = kept[j]
        hidden_grads = dot(rows_of(arrived_grads, j), w_down[j], (1, 1))
        gate_back = (hidden_grads * bent.astype(F32)).astype(BF)
        lifted_back = (hidden_grads * active.astype(F32)).astype(BF)
        sent.append((dot(gate_back, w_gate[j]) + dot(lifted_back, w_up[j])).astype(BF))
        backs.append((gate_back, lifted_back))
    return rows_back(sent, arrived_grads.shape[0]), tuple(backs)


def attend_back(
    token_grads, places, logit_grads, w_router, middle, gain, grad, w_out, query, pairs, probs,
    cosine, sine,
):
    ffn_grads = dot(places, token_grads) + dot(logit_grads, w_router, (1, 1))
    part, gain_grad = norm_back(ffn_grads, middle, gain)
    middle_grads = grad + part
    branch = middle_grads.astype(BF)
    mixed_grads = dot(branch, w_out, (1, 1)).astype(BF)
    kv_heads = pairs.shape[1] // (2 * HEAD_DIM)
    group = query.shape[1] // HEAD_DIM // kv_heads
    scale = HEAD_DIM ** (-0.5)
    query_grads, key_grads, value_grads = [], [], []
    for h in range(kv_heads):
        keys = pairs[:, h * HEAD_DIM : (h + 1) * HEAD_DIM]
        values = pairs[:, (kv_heads + h) * HEAD_DIM : (kv_heads + h + 1) * HEAD_DIM]
        queries = stacked_heads(query, h * group, group)
        above = stacked_heads(mixed_grads, h * group, group)
        weights = probs[h]
        wide = weights.astype(F32)
        weight_grads = dot(above, values, (1, 1))
        value_grads.append(dot(weights, above, (0, 0)))
        score_grads = (
            wide * (weight_grads - jnp.sum(wide * weight_grads, -1, keepdims=True))
        ).astype(BF)
        query_grads.append(unstacked_heads(dot(score_grads, keys) * scale, group))
        key_grads.append(dot(score_grads, queries, (0, 0)) * scale)
    query_back = turned(jnp.concatenate(query_grads, 1), cosine, -sine).astype(BF)
    pair_grads = jnp.concatenate(key_grads + value_grads, 1).astype(BF)
    return middle_grads, branch, query_back, pair_grads, gain_grad


def project_back(pair_parts, query_back, w_qkv, stream, gain, middle_grads, cosine, sine):
    total = sum(part.astype(F32) for part in pair_parts)
    kv_width = total.shape[1] // 2
    key_back = turned(total[:, :kv_width], cosine, -sine)
    backs = jnp.concatenate(
        [query_back, key_back.astype(BF), total[:, kv_width:].astype(BF)], 1
    )
    part, gain_grad = norm_back(dot(backs, w_qkv, (1, 1)), stream, gain)
    return middle_grads + part, backs, gain_grad


def over_columns(value):
    return lax.all_to_all(value, "col", split_axis=0, concat_axis=0, tiled=True)


def on_device(
    inputs, cotangent, segment_ids, routes, attn_gain, w_query, w_key, w_value, w_out, ffn_gain,
    w_router, w_gate, w_up, w_down,
):
    section = lax.axis_index("section")
    row = lax.axis_index("row")
    rows = lax.axis_size("row")
    columns = lax.axis_size("col")
    micro, tokens, width = inputs.shape[0], inputs.shape[2], inputs.shape[3]
    experts = w_router.shape[2]
    kv_width = w_key.shape[2]
    slots = experts * ROOMS
    share = width // rows
    shard = width // (rows * columns)
    pieces = range(micro)
    steps = range(rows)

    small = jnp.concatenate(
        [w_router[0], attn_gain[0][:, None], ffn_gain[0][:, None],
         jnp.zeros((shard, LANES - experts - 2), BF)], 1
    )
    first = jnp.concatenate([w_query[0], w_key[0], w_value[0], small], 1)
    first = lax.all_gather(first, ("row", "col"), axis=0, tiled=True)
    w_qkv = first[:, : width + 2 * kv_width]
    small = first[:, width + 2 * kv_width :]
    w_o = lax.all_gather(w_out[0], ("row", "col"), axis=0, tiled=True)
    gain_a = small[:, experts].astype(F32)[None, :]
    gain_f = small[:, experts + 1].astype(F32)[None, :]
    lane = jnp.arange(LANES, dtype=jnp.int32)
    w_r = jnp.where(lane[None, :] < experts, small, jnp.zeros_like(small))

    order = (0, 2, 1, 3)

    def whole(own):
        two = swapped(own, 2)
        one = swapped(own, 1)
        three = swapped(two, 1)
        return jnp.concatenate([own, two, one, three], 1)

    w_g, w_u, w_d = whole(w_gate[0]), whole(w_up[0]), whole(w_down[0])

    half = HEAD_DIM // 2
    freqs = 10000.0 ** (-2.0 * jnp.arange(half).astype(F32) / HEAD_DIM)
    positions = row * tokens + jnp.arange(tokens, dtype=jnp.int32)
    angles = positions.astype(F32)[:, None] * freqs[None, :]
    cosine = jnp.concatenate([jnp.cos(angles)] * 2, 1)
    sine = jnp.concatenate([-jnp.sin(angles), jnp.sin(angles)], 1)
    key_positions = jnp.concatenate(
        [(row ^ step) * tokens + jnp.arange(tokens, dtype=jnp.int32) for step in steps]
    )
    spread = (lane[:, None] == jnp.arange(slots, dtype=jnp.int32)[None, :] // ROOMS).astype(BF)
    below = (
        jnp.arange(tokens)[:, None] > jnp.arange(tokens)[None, :]
    ).astype(BF)
    biases, chosens, places, dispatches = [], [], [], []
    for m in pieces:
        segments = segment_ids[m, 0]
        own_segments = lax.dynamic_slice_in_dim(segments, row * tokens, tokens)
        key_segments = jnp.concatenate(
            [lax.dynamic_slice_in_dim(segments, (row ^ s) * tokens, tokens) for s in steps]
        )
        counted = (key_positions[None, :] <= positions[:, None]) & (
            key_segments[None, :] == own_segments[:, None]
        )
        biases.append(jnp.where(counted, 0.0, -1e30).astype(F32))
        chosen = jnp.any(routes[0, m, 0][:, :, None] == lane[None, None, :], 1)
        chosens.append(chosen.astype(F32))
        rank = dot(below, chosen.astype(BF))
        rank = jnp.where(chosen, rank, -1.0)[:, :experts]
        place = (
            rank[:, :, None] == jnp.arange(ROOMS, dtype=F32)[None, None, :]
        ).reshape(tokens, slots)
        places.append(place.astype(BF))
        dispatches.append(place.T.astype(BF))

    def forward(streams):
        done = []
        projected = [project(x, gain_a, w_qkv, cosine, sine, width) for x in streams]
        pairs = [
            jnp.concatenate([pair] + [swapped(pair, s) for s in steps[1:]], 0)
            for normed, query, pair in projected
        ]
        attended = [
            attend(
                streams[m], projected[m][1], pairs[m], biases[m], w_o, gain_f, w_r, chosens[m],
                dispatches[m],
            )
            for m in pieces
        ]
        arrived = [
            over_columns(a[4].reshape(columns, slots // columns, width)) for a in attended
        ]
        applied = [expert_forward(x, w_g, w_u, w_d) for x in arrived]
        returned = [over_columns(a[0]).reshape(slots, width) for a in applied]
        results = [
            combine(returned[m], attended[m][1], attended[m][3], spread, places[m])
            for m in pieces
        ]
        kept = [
            dict(
                stream=streams[m], normed=projected[m][0], query=projected[m][1], pairs=pairs[m],
                mixed=attended[m][0], middle=attended[m][1], normed_ffn=attended[m][2],
                gates=attended[m][3], probs=attended[m][5], arrived=arrived[m],
                applied=applied[m][1], returned=returned[m],
            )
            for m in pieces
        ]
        return results, kept

    def backward(grads, kept):
        split = [
            split_grads(
                grads[m], kept[m]["returned"], kept[m]["gates"], spread, places[m], dispatches[m]
            )
            for m in pieces
        ]
        arrived = [
            over_columns(s[1].reshape(columns, slots // columns, width)) for s in split
        ]
        applied = [
            expert_backward(arrived[m], kept[m]["applied"], w_g, w_u, w_d) for m in pieces
        ]
        returned = [over_columns(a[0]).reshape(slots, width) for a in applied]
        attended = [
            attend_back(
                returned[m], places[m], split[m][0], w_r, kept[m]["middle"], gain_f, grads[m],
                w_o, kept[m]["query"], kept[m]["pairs"], kept[m]["probs"], cosine, sine,
            )
            for m in pieces
        ]
        parts = [
            [a[3][:tokens]]
            + [swapped(a[3][s * tokens : (s + 1) * tokens], s) for s in steps[1:]]
            for a in attended
        ]
        projected = [
            project_back(
                parts[m], attended[m][2], w_qkv, kept[m]["stream"], gain_a, attended[m][0],
                cosine, sine,
            )
            for m in pieces
        ]
        return split, arrived, applied, attended, projected

    entering = [inputs[m, 0].astype(F32) for m in pieces]
    results, unused = forward(entering)
    handed = [lax.ppermute(r.astype(BF), "section", [(0, 1)]) for r in results]
    streams = [
        jnp.where(section == 1, handed[m].astype(F32), entering[m]) for m in pieces
    ]
    outputs, kept = forward(streams)

    targets = [cotangent[m, 0].astype(F32) for m in pieces]
    projected = backward(targets, kept)[4]
    handed = [lax.ppermute(p[0].astype(BF), "section", [(1, 0)]) for p in projected]
    grads = [
        jnp.where(section == 0, handed[m].astype(F32), targets[m]) for m in pieces
    ]
    split, arrived, applied, attended, projected = backward(grads, kept)
    input_grads = [p[0] for p in projected]

    def both(make):
        return jnp.stack(
            [jnp.concatenate([make(m, j) for m in pieces], 0) for j in range(w_g.shape[0])]
        )

    def summed_rows(left, right):
        def part(lo, hi):
            return lax.dot_general(
                left[:, :, lo:hi], right, (((1,), (1,)), ((0,), (0,))), preferred_element_type=F32
            ).astype(BF)

        half, quarter = left.shape[2] // 2, left.shape[2] // 4
        came = swapped(part(half, 2 * half), 1)
        mine = part(0, half).astype(F32) + came.astype(F32)
        far = swapped(mine[:, quarter:].astype(BF), 2)
        return mine[:, :quarter] + far.astype(F32)

    x_rows = both(lambda m, j: rows_of(kept[m]["arrived"], j))
    y_rows = both(lambda m, j: rows_of(arrived[m], j))
    hidden = both(lambda m, j: kept[m]["applied"][j][0])
    gate_back = both(lambda m, j: applied[m][1][j][0])
    lifted_back = both(lambda m, j: applied[m][1][j][1])
    grad_down = summed_rows(hidden, y_rows)
    grad_gate = summed_rows(gate_back, x_rows)
    grad_up = summed_rows(lifted_back, x_rows)

    def slices(values):
        value = jnp.concatenate(values, 0)
        cuts = [lax.dynamic_slice_in_dim(value, (row ^ s) * share, share, 1) for s in steps]
        return jnp.concatenate([cuts[0]] + [swapped(cuts[s], s) for s in steps[1:]], 0)

    def everyone(values):
        value = jnp.concatenate(values, 0)
        return jnp.concatenate([value] + [swapped(value, s) for s in steps[1:]], 0)

    def summed_columns(value):
        blocks = value.astype(BF).reshape(columns, shard, value.shape[1])
        return over_columns(blocks).astype(F32).sum(0)

    x_normed = slices([kept[m]["normed"] for m in pieces])
    x_mixed = slices([kept[m]["mixed"] for m in pieces])
    x_ffn = slices([kept[m]["normed_ffn"] for m in pieces])
    y_branch = everyone(
        [jnp.concatenate([attended[m][1], split[m][0]], 1) for m in pieces]
    )
    y_qkv = everyone([projected[m][1] for m in pieces])
    grad_first = summed_columns(
        jnp.concatenate(
            [dot(x_mixed, y_branch[:, :width], (0, 0)), dot(x_ffn, y_branch[:, width:], (0, 0))], 1
        )
    )
    gains = jnp.concatenate(
        [sum(projected[m][2] for m in pieces), sum(attended[m][4] for m in pieces)], 0
    )
    gain_cuts = [lax.dynamic_slice_in_dim(gains, (row ^ s) * share, share, 1) for s in steps]
    gains = gain_cuts[0] + sum(swapped(gain_cuts[s], s) for s in steps[1:])
    gains = jnp.concatenate([gains, jnp.zeros((LANES - 2, share), F32)], 0).T
    grad_second = summed_columns(
        jnp.concatenate([dot(x_normed, y_qkv, (0, 0)), gains], 1)
    )
    qkv_width = width + 2 * kv_width

    return (
        jnp.stack(outputs)[None, :, None],
        jnp.stack(input_grads)[None, :, None],
        grad_second[:, qkv_width][None],
        grad_second[:, :width][None],
        grad_second[:, width : width + kv_width][None],
        grad_second[:, width + kv_width : qkv_width][None],
        grad_first[:, :width][None],
        grad_second[:, qkv_width + 1][None],
        grad_first[:, width : width + experts][None],
        grad_gate[None],
        grad_up[None],
        grad_down[None],
    )


def solution(mesh):
    dense = P("section", ("row", "col"), None)
    gain = P("section", ("row", "col"))
    expert = P("section", "col", "row", None)
    token = P(None, "col", "row", None)
    layered = P("section", None, "col", "row", None)
    return jax.shard_map(
        on_device,
        mesh=mesh,
        in_specs=(
            token, token, P(None, "col", None), layered, gain, dense, dense, dense, dense, gain,
            dense, expert, expert, expert,
        ),
        out_specs=(
            layered, layered, gain, dense, dense, dense, dense, gain, dense, expert, expert, expert,
        ),
        check_vma=False,
    )
```

```python
import functools

import jax
import jax.numpy as jnp
from jax import lax
from jax.experimental import pallas as pl
from jax.experimental.pallas import tpu as pltpu
from jax.sharding import PartitionSpec as P

HEAD_DIM = 128
ROOMS = 16
EPSILON = 1e-06
LANES = 128
BF = jnp.bfloat16
F32 = jnp.float32
MIB = 1 << 20


def dot(left, right, contract=(1, 0)):
    return lax.dot_general(
        left, right, (((contract[0],), (contract[1],)), ((), ())), preferred_element_type=F32
    )


def like(shape, dtype):
    return jax.ShapeDtypeStruct(shape, dtype)


def call(body, outs, args, flops, far=(), scratch=(), vmem=48, scalars=(), waits=()):
    moved = sum(a.size * a.dtype.itemsize for a in (*args, *far, *outs))
    used = len(scalars) + len(args) + len(far)

    def run(*refs):
        body(*refs[:used], *refs[used + len(waits) :])

    return pl.pallas_call(
        run,
        out_shape=tuple(outs),
        in_specs=[pl.BlockSpec(memory_space=pltpu.SMEM)] * len(scalars)
        + [pl.BlockSpec(memory_space=pltpu.VMEM)] * len(args)
        + [pl.BlockSpec(memory_space=pl.ANY)] * (len(far) + len(waits)),
        out_specs=tuple(pl.BlockSpec(memory_space=pltpu.VMEM) for unused in outs),
        scratch_shapes=list(scratch),
        compiler_params=pltpu.CompilerParams(vmem_limit_bytes=vmem * MIB),
        cost_estimate=pl.CostEstimate(
            flops=int(flops), bytes_accessed=int(moved), transcendentals=0
        ),
        name=body.func.__name__ if isinstance(body, functools.partial) else body.__name__,
    )(*scalars, *args, *far, *waits)


def swapped(value, step):
    rows = lax.axis_size("row")
    return lax.ppermute(value, "row", [(r, r ^ step) for r in range(rows)])


def norm_parts(stream):
    return lax.rsqrt(jnp.mean(stream * stream, -1, keepdims=True) + EPSILON)


def norm_back(grad, stream, gain):
    inverse = norm_parts(stream)
    unit = stream * inverse
    scaled = grad * gain
    back = inverse * (scaled - unit * jnp.mean(scaled * unit, -1, keepdims=True))
    return back, jnp.sum(grad * unit, 0, keepdims=True)


def turned(vectors, cosine, sine):
    done = []
    for at in range(0, vectors.shape[1], HEAD_DIM):
        one = vectors[:, at : at + HEAD_DIM]
        done.append(one * cosine + pltpu.roll(one, HEAD_DIM // 2, 1) * sine)
    return jnp.concatenate(done, -1) if len(done) > 1 else done[0]


def stacked_heads(value, first, count):
    return jnp.concatenate(
        [value[:, (first + j) * HEAD_DIM : (first + j + 1) * HEAD_DIM] for j in range(count)], 0
    )


def unstacked_heads(value, count):
    tokens = value.shape[0] // count
    return jnp.concatenate([value[j * tokens : (j + 1) * tokens] for j in range(count)], 1)


def cuts_of(total, most=512):
    return [(at, min(most, total - at)) for at in range(0, total, most)]


def project(
    flag, came, entering, gain, cosine, sine, dense, stream, normed, query, pair, weights, sems
):
    width = stream.shape[1]
    cuts = cuts_of(weights.shape[1])
    copies = [
        pltpu.make_async_copy(
            dense.at[:, pl.ds(at, size)], weights.at[:, pl.ds(at, size)], sems.at[k]
        )
        for k, (at, size) in enumerate(cuts)
    ]
    for copy in copies:
        copy.start()
    x = jnp.where(flag[0] > 0, came[...].astype(F32), entering[...].astype(F32))
    stream[...] = x
    low = (x * norm_parts(x) * gain[...]).astype(BF)
    normed[...] = low
    keys = pair.shape[1] // 2
    for copy, (at, size) in zip(copies, cuts):
        copy.wait()
        part = dot(low, weights[:, at : at + size])
        for begin in range(at, at + size, HEAD_DIM):
            head = part[:, begin - at : begin - at + HEAD_DIM]
            if begin < width + keys:
                head = turned(head, cosine[...], sine[...])
            if begin < width:
                query[:, begin : begin + HEAD_DIM] = head.astype(BF)
            else:
                pair[:, begin - width : begin - width + HEAD_DIM] = head.astype(BF)


def attend(
    stream, query, pair0, pair1, pair2, pair3, bias, gain, chosen, dispatch, dense, mixed, middle,
    normed_ffn, gates, outgoing, probs, weights, router, sems,
):
    width = stream.shape[1]
    at = dense.shape[1] - width - LANES
    copies = [
        pltpu.make_async_copy(dense.at[:, pl.ds(at + LANES, width)], weights, sems.at[0]),
        pltpu.make_async_copy(dense.at[:, pl.ds(at, LANES)], router, sems.at[1]),
    ]
    for copy in copies:
        copy.start()
    pairs = jnp.concatenate([pair0[...], pair1[...], pair2[...], pair3[...]], 0)
    kv_heads = pairs.shape[1] // (2 * HEAD_DIM)
    group = width // HEAD_DIM // kv_heads
    biases = jnp.concatenate([bias[...]] * group, 0)
    tokens = stream.shape[0]
    for h in range(kv_heads):
        keys = pairs[:, h * HEAD_DIM : (h + 1) * HEAD_DIM]
        values = pairs[:, (kv_heads + h) * HEAD_DIM : (kv_heads + h + 1) * HEAD_DIM]
        queries = stacked_heads(query, h * group, group)
        scores = dot(queries, keys, (1, 1)) * HEAD_DIM ** (-0.5) + biases
        expo = jnp.exp(scores - jnp.max(scores, -1, keepdims=True))
        weight = (expo * (1.0 / jnp.sum(expo, -1, keepdims=True))).astype(BF)
        probs[h] = weight
        done = dot(weight, values).astype(BF)
        for j in range(group):
            begin = (h * group + j) * HEAD_DIM
            mixed[:, begin : begin + HEAD_DIM] = done[j * tokens : (j + 1) * tokens]
    copies[0].wait()
    x = stream[...] + dot(mixed[...], weights[...])
    middle[...] = x
    low = (x * norm_parts(x) * gain[...]).astype(BF)
    normed_ffn[...] = low
    copies[1].wait()
    taken = chosen[...] > 0
    logits = jnp.where(taken, dot(low, router[...]), -1e30)
    expo = jnp.where(taken, jnp.exp(logits - jnp.max(logits, -1, keepdims=True)), 0.0)
    gates[...] = expo / jnp.sum(expo, -1, keepdims=True)
    outgoing[...] = dot(dispatch[...], low).astype(BF).reshape(outgoing.shape)


def fetch(shards, weights, sems):
    copies = []
    for j in range(weights.shape[1]):
        line = []
        for k in range(weights.shape[0]):
            some = []
            for p in range(4):
                size = shards[k][p].shape[1]
                some.append(
                    pltpu.make_async_copy(
                        shards[k][p].at[j],
                        weights.at[k, j, pl.ds(p * size, size)],
                        sems.at[k, j, p],
                    )
                )
            line.append(some)
        copies.append(line)
    for line in copies:
        for some in line:
            for copy in some:
                copy.start()
    return copies


def done_with(copies):
    for copy in copies:
        copy.wait()


def rows_of(value, j):
    columns, unused, width = value.shape
    return value[:, j * ROOMS : (j + 1) * ROOMS, :].reshape(columns * ROOMS, width)


def expert_forward(keep, arrived, *refs):
    shards = [refs[4 * k : 4 * k + 4] for k in range(3)]
    outs, weights, sems = refs[12:-2], refs[-2], refs[-1]
    copies = fetch(shards, weights, sems)
    for j in range(weights.shape[1]):
        rows = rows_of(arrived, j)
        done_with(copies[j][0])
        gate = dot(rows, weights[0, j], (1, 1))
        done_with(copies[j][1])
        lifted = dot(rows, weights[1, j], (1, 1))
        square = gate * gate
        bend = jnp.tanh(0.7978845608028654 * gate * (1.0 + 0.044715 * square))
        active = 0.5 * gate * (1.0 + bend)
        hidden = (active * lifted).astype(BF)
        if keep:
            slope = 0.5 * (1.0 + bend) + 0.5 * gate * (1.0 - bend * bend) * (
                0.7978845608028654 * (1.0 + 3 * 0.044715 * square)
            )
            outs[1][j] = hidden
            outs[2][j] = active.astype(BF)
            outs[3][j] = (slope * lifted).astype(BF)
        done_with(copies[j][2])
        made = dot(hidden, weights[2, j]).astype(BF)
        outs[0][:, j * ROOMS : (j + 1) * ROOMS, :] = made.reshape(-1, ROOMS, made.shape[1])


def combine(returned, middle, gates, spread, places, result, low):
    weights = dot(gates[...].astype(BF), spread[...]) * places[...].astype(F32)
    rows = returned[...].reshape(-1, returned.shape[2])
    done = middle[...] + dot(weights.astype(BF), rows)
    result[...] = done
    low[...] = done.astype(BF)


def send_grads(flag, came, target, gates, dispatch, grad, outgoing):
    low = jnp.where(flag[0] > 0, came[...], target[...])
    grad[...] = low
    slots = dispatch.shape[0]
    own = lax.broadcasted_iota(jnp.int32, (slots, LANES), 0) // ROOMS
    here = own == lax.broadcasted_iota(jnp.int32, (slots, LANES), 1)
    scale = jnp.sum(
        jnp.where(here, dot(dispatch[...], gates[...].astype(BF)), 0.0), -1, keepdims=True
    )
    outgoing[...] = (dot(dispatch[...], low) * scale).astype(BF).reshape(outgoing.shape)


def expert_backward(arrived, active, bent, *refs):
    shards = [refs[4 * k : 4 * k + 4] for k in range(3)]
    sent, gate_back, lifted_back, weights, sems = refs[12:]
    copies = fetch(shards, weights, sems)
    for j in range(weights.shape[1]):
        done_with(copies[j][0])
        hidden_grads = dot(rows_of(arrived, j), weights[0, j], (1, 1))
        gate_part = (hidden_grads * bent[j].astype(F32)).astype(BF)
        lifted_part = (hidden_grads * active[j].astype(F32)).astype(BF)
        gate_back[j] = gate_part
        lifted_back[j] = lifted_part
        done_with(copies[j][1])
        done = dot(gate_part, weights[1, j])
        done_with(copies[j][2])
        done = (done + dot(lifted_part, weights[2, j])).astype(BF)
        sent[:, j * ROOMS : (j + 1) * ROOMS, :] = done.reshape(-1, ROOMS, done.shape[1])


def attend_back(
    keep, row, token_grads, returned, gates, spread, places, middle, gain, grad, query, pair0, pair1,
    pair2, pair3, probs, cosine, sine, dense, middle_grads, query_back, part0, part1, part2, part3,
    *rest,
):
    tokens, width = middle.shape
    kept, (branch, weights, router, sems) = rest[:-4], rest[-4:]
    at = dense.shape[1] - width - LANES
    copies = [
        pltpu.make_async_copy(dense.at[:, pl.ds(at, LANES)], router, sems.at[1]),
        pltpu.make_async_copy(dense.at[:, pl.ds(at + LANES, width)], weights, sems.at[0]),
    ]
    for copy in copies:
        copy.start()
    inner = dot(grad[...], returned[...].reshape(-1, width), (1, 1)) * places[...].astype(F32)
    gate_grads = dot(inner.astype(BF), spread[...], (1, 1))
    chances = gates[...]
    logit_grads = (
        chances * (gate_grads - jnp.sum(chances * gate_grads, -1, keepdims=True))
    ).astype(BF)
    ffn_grads = dot(places[...], token_grads[...].reshape(-1, width))
    copies[0].wait()
    ffn_grads = ffn_grads + dot(logit_grads, router[...], (1, 1))
    part, total = norm_back(ffn_grads, middle[...], gain[...])
    above = grad[...].astype(F32) + part
    middle_grads[...] = above
    low = above.astype(BF)
    if keep:
        kept[0][...] = logit_grads
        kept[1][...] = jnp.broadcast_to(total, kept[1].shape)
        branch[...] = low
        share = width // 4
        for s, out in enumerate(kept[2:]):
            out[...] = branch[:, pl.ds(pl.multiple_of((row[0] ^ s) * share, LANES), share)]
    copies[1].wait()
    mixed_grads = dot(low, weights[...], (1, 1)).astype(BF)
    pairs = jnp.concatenate([pair0[...], pair1[...], pair2[...], pair3[...]], 0)
    kv_heads = pairs.shape[1] // (2 * HEAD_DIM)
    group = width // HEAD_DIM // kv_heads
    scale = HEAD_DIM ** (-0.5)
    parts = (part0, part1, part2, part3)
    for h in range(kv_heads):
        keys = pairs[:, h * HEAD_DIM : (h + 1) * HEAD_DIM]
        values = pairs[:, (kv_heads + h) * HEAD_DIM : (kv_heads + h + 1) * HEAD_DIM]
        queries = stacked_heads(query, h * group, group)
        top = stacked_heads(mixed_grads, h * group, group)
        weight = probs[h]
        wide = weight.astype(F32)
        weight_grads = dot(top, values, (1, 1))
        value_grads = dot(weight, top, (0, 0)).astype(BF)
        inner = wide * weight_grads
        score_grads = (inner - wide * jnp.sum(inner, -1, keepdims=True)).astype(BF)
        query_grads = dot(score_grads, keys) * scale
        key_grads = (dot(score_grads, queries, (0, 0)) * scale).astype(BF)
        for j in range(group):
            begin = (h * group + j) * HEAD_DIM
            one = query_grads[j * tokens : (j + 1) * tokens]
            query_back[:, begin : begin + HEAD_DIM] = turned(one, cosine[...], -sine[...]).astype(BF)
        for p, part in enumerate(parts):
            part[:, h * HEAD_DIM : (h + 1) * HEAD_DIM] = key_grads[p * tokens : (p + 1) * tokens]
            begin = (kv_heads + h) * HEAD_DIM
            part[:, begin : begin + HEAD_DIM] = value_grads[p * tokens : (p + 1) * tokens]


def project_back(
    keep, row, part0, part1, part2, part3, query_back, stream, gain, middle_grads, cosine, sine,
    dense, grad, low, *rest,
):
    width = stream.shape[1]
    kept, (backs, weights, sems) = rest[:-3], rest[-3:]
    cuts = cuts_of(weights.shape[1])
    copies = [
        pltpu.make_async_copy(
            dense.at[:, pl.ds(at, size)], weights.at[:, pl.ds(at, size)], sems.at[k]
        )
        for k, (at, size) in enumerate(cuts)
    ]
    for copy in copies:
        copy.start()
    total = sum(part[...].astype(F32) for part in (part0, part1, part2, part3))
    keys = total.shape[1] // 2
    backs[:, :width] = query_back[...]
    backs[:, width : width + keys] = turned(total[:, :keys], cosine[...], -sine[...]).astype(BF)
    backs[:, width + keys :] = total[:, keys:].astype(BF)
    above = jnp.zeros(stream.shape, F32)
    for copy, (at, size) in zip(copies, cuts):
        copy.wait()
        above = above + dot(backs[:, at : at + size], weights[:, at : at + size], (1, 1))
    part, sums = norm_back(above, stream[...], gain[...])
    if keep:
        kept[0][...] = jnp.broadcast_to(sums, kept[0].shape)
        share = backs.shape[1] // 4
        for s, out in enumerate(kept[1:]):
            out[...] = backs[:, pl.ds(pl.multiple_of((row[0] ^ s) * share, LANES), share)]
    done = middle_grads[...] + part
    grad[...] = done
    low[...] = done.astype(BF)


def expert_weight_grads(half, left0, left1, right0, right1, first, second):
    size = first.shape[1]
    wide = 2 * size
    for j in range(first.shape[0]):
        total = dot(left0[j, :, half * wide : (half + 1) * wide], rows_of(right0, j), (0, 0))
        total = total + dot(
            left1[j, :, half * wide : (half + 1) * wide], rows_of(right1, j), (0, 0)
        )
        first[j] = total[:size].astype(BF)
        second[j] = total[size:].astype(BF)


def pack(*refs):
    for k, value in enumerate(refs[:-1]):
        refs[-1][k] = value[...]


def stacked(refs):
    return jnp.concatenate([r[...] for r in refs], 0)


def out_grads(*refs):
    lefts, rights, out = refs[:4], refs[4:12], refs[12]
    left = jnp.concatenate([one[k] for one in lefts for k in (2, 3)], 0)
    out[...] = dot(left, stacked(rights), (0, 0)).astype(BF)


def qkv_grads(*refs):
    lefts, rights, normed, logits, gains, out = (
        refs[:4], refs[4:12], refs[12:14], refs[14:16], refs[16:20], refs[20],
    )
    width, wide = out.shape
    left = jnp.concatenate([one[k] for one in lefts for k in (0, 1)], 0)
    out[:, : wide - LANES] = dot(left, stacked(rights), (0, 0)).astype(BF)
    first = gains[0][:1] + gains[1][:1]
    second = gains[2][:1] + gains[3][:1]
    line = lax.broadcasted_iota(jnp.int32, (LANES, width), 0)
    sums = jnp.where(
        line == LANES - 2, first, jnp.where(line == LANES - 1, second, jnp.zeros((1, 1), F32))
    )
    out[:, wide - LANES :] = (dot(stacked(normed), stacked(logits), (0, 0)) + sums.T).astype(BF)


def fold(row, first, second, out0, out1, out2, out3, total):
    share = first.shape[2]
    total[:, :share] = jnp.sum(first[...].astype(F32), 0)
    total[:, share:] = jnp.sum(second[...].astype(F32), 0)
    for s, out in enumerate((out0, out1, out2, out3)):
        size = out.shape[0]
        out[...] = total[pl.ds(pl.multiple_of((row[0] ^ s) * size, 8), size), :]


def finish(row, in0, in1, in2, in3, o_grad, q_grad, k_grad, v_grad, rest, total):
    share = o_grad.shape[1] // 4
    piece = total.shape[1] // 4
    ins = (in0, in1, in2, in3)
    for s, one in enumerate(ins):
        where = row[0] ^ s
        o_grad[:, pl.ds(pl.multiple_of(where * share, LANES), share)] = one[:, :share]
        total[:, pl.ds(pl.multiple_of(where * piece, LANES), piece)] = one[:, share : share + piece]
    rest[...] = sum(one[:, share + piece :] for one in ins)
    begin = 0
    for out in (q_grad, k_grad, v_grad):
        out[...] = total[:, begin : begin + out.shape[1]]
        begin += out.shape[1]


def over_columns(value):
    return lax.all_to_all(value, "col", split_axis=0, concat_axis=0, tiled=True)


def on_device(
    inputs, cotangent, segment_ids, routes, attn_gain, w_query, w_key, w_value, w_out, ffn_gain,
    w_router, w_gate, w_up, w_down,
):
    section = lax.axis_index("section")
    row = lax.axis_index("row")
    rows = lax.axis_size("row")
    columns = lax.axis_size("col")
    micro, tokens, width = inputs.shape[0], inputs.shape[2], inputs.shape[3]
    experts = w_router.shape[2]
    per_column = w_gate.shape[1]
    hidden_width = w_gate.shape[2] * rows
    kv_width = w_key.shape[2]
    qkv_width = width + 2 * kv_width
    slots = experts * ROOMS
    share = width // rows
    shard = width // (rows * columns)
    heads = width // HEAD_DIM
    kv_heads = kv_width // HEAD_DIM
    length = rows * tokens
    pieces = range(micro)
    steps = range(rows)
    here = row.astype(jnp.int32)[None]
    second = (section == 1).astype(jnp.int32)[None]
    block = (columns, slots // columns, width)

    dense = jnp.concatenate(
        [w_query[0], w_key[0], w_value[0], w_router[0], attn_gain[0][:, None], ffn_gain[0][:, None],
         jnp.zeros((shard, LANES - experts - 2), BF), w_out[0]], 1
    )
    dense = lax.all_gather(dense, ("row", "col"), axis=0, tiled=True)
    small = dense[:, qkv_width : qkv_width + LANES]
    gain_a = small[:, experts].astype(F32)[None, :]
    gain_f = small[:, experts + 1].astype(F32)[None, :]

    def shards_of(own):
        two = swapped(own, 2)
        return own, swapped(own, 1), two, swapped(two, 1)

    gate_shards, up_shards, down_shards = (
        shards_of(w_gate[0]), shards_of(w_up[0]), shards_of(w_down[0])
    )

    lane = jnp.arange(LANES, dtype=jnp.int32)
    half = HEAD_DIM // 2
    freqs = 10000.0 ** (-2.0 * jnp.arange(half).astype(F32) / HEAD_DIM)
    positions = row * tokens + jnp.arange(tokens, dtype=jnp.int32)
    angles = positions.astype(F32)[:, None] * freqs[None, :]
    cosine = jnp.concatenate([jnp.cos(angles)] * 2, 1)
    sine = jnp.concatenate([-jnp.sin(angles), jnp.sin(angles)], 1)
    key_positions = jnp.concatenate(
        [(row ^ step) * tokens + jnp.arange(tokens, dtype=jnp.int32) for step in steps]
    )
    spread = (lane[:, None] == jnp.arange(slots, dtype=jnp.int32)[None, :] // ROOMS).astype(BF)
    below = (jnp.arange(tokens)[:, None] > jnp.arange(tokens)[None, :]).astype(BF)
    biases, chosens, places, dispatches = [], [], [], []
    for m in pieces:
        segments = segment_ids[m, 0]
        own_segments = lax.dynamic_slice_in_dim(segments, row * tokens, tokens)
        key_segments = jnp.concatenate(
            [lax.dynamic_slice_in_dim(segments, (row ^ s) * tokens, tokens) for s in steps]
        )
        counted = (key_positions[None, :] <= positions[:, None]) & (
            key_segments[None, :] == own_segments[:, None]
        )
        biases.append(jnp.where(counted, 0.0, -1e30).astype(F32))
        chosen = jnp.any(routes[0, m, 0][:, :, None] == lane[None, None, :], 1)
        chosens.append(chosen.astype(F32))
        rank = dot(below, chosen.astype(BF))
        rank = jnp.where(chosen, rank, -1.0)[:, :experts]
        place = (
            rank[:, :, None] == jnp.arange(ROOMS, dtype=F32)[None, None, :]
        ).reshape(tokens, slots)
        places.append(place.astype(BF))
        dispatches.append(place.T.astype(BF))

    token_low, token_wide = like((tokens, width), BF), like((tokens, width), F32)
    pair_like = like((tokens, 2 * kv_width), BF)
    block_like = like(block, BF)
    sums_like = like((8, width), F32)
    kept_like = like((per_column, columns * ROOMS, hidden_width), BF)
    probs_like = like((kv_heads, heads // kv_heads * tokens, length), BF)
    qkv_scratch = [pltpu.VMEM((width, qkv_width), BF), pltpu.SemaphoreType.DMA((8,))]
    out_scratch = [
        pltpu.VMEM((width, width), BF), pltpu.VMEM((width, LANES), BF),
        pltpu.SemaphoreType.DMA((2,)),
    ]
    expert_scratch = [
        pltpu.VMEM((3, per_column, hidden_width, width), BF),
        pltpu.SemaphoreType.DMA((3, per_column, 4)),
    ]
    qkv_flops = 2 * tokens * width * qkv_width
    out_flops = 2 * tokens * width * width + 2 * slots * tokens * width
    score_flops = 2 * heads * tokens * length * HEAD_DIM
    expert_flops = 2 * slots * hidden_width * width

    def forward(came, entering, keep, waits=()):
        projected = [
            call(
                project, (token_wide, token_low, token_low, pair_like),
                (came[m], entering[m], gain_a, cosine, sine), qkv_flops, (dense,), qkv_scratch,
                scalars=(second,), waits=() if m else waits,
            )
            for m in pieces
        ]
        pairs = [[p[3]] + [swapped(p[3], s) for s in steps[1:]] for p in projected]
        attended = [
            call(
                attend,
                (token_low, token_wide, token_low, like((tokens, LANES), F32), block_like, probs_like),
                (projected[m][0], projected[m][2], *pairs[m], biases[m], gain_f, chosens[m],
                 dispatches[m]),
                out_flops + 2 * score_flops, (dense,), out_scratch,
            )
            for m in pieces
        ]
        arrived = [over_columns(a[4]) for a in attended]
        applied = [
            call(
                functools.partial(expert_forward, keep),
                (block_like,) + (kept_like,) * (3 if keep else 0), (arrived[m],), 3 * expert_flops,
                (*gate_shards, *up_shards, *down_shards), expert_scratch,
                waits=() if m else (attended[1][4],),
            )
            for m in pieces
        ]
        returned = [over_columns(a[0]) for a in applied]
        results = [
            call(
                combine, (token_wide, token_low),
                (returned[m], attended[m][1], attended[m][3], spread, places[m]),
                2 * slots * tokens * width, waits=() if m else (applied[1][0],),
            )
            for m in pieces
        ]
        return projected, pairs, attended, arrived, applied, returned, results

    def backward(came, targets, kept, lefts, keep, waits):
        projected, pairs, attended, entered, applied, returned, results = kept
        sent = [
            call(
                send_grads, (token_low, block_like),
                (came[m], targets[m], attended[m][3], dispatches[m]),
                2 * slots * tokens * width, scalars=(1 - second,),
            )
            for m in pieces
        ]
        arrived = [over_columns(s[1]) for s in sent]
        moved = [
            call(
                expert_backward, (block_like, kept_like, kept_like),
                (arrived[m], applied[m][2], applied[m][3]), 3 * expert_flops,
                (*down_shards, *gate_shards, *up_shards), expert_scratch,
                waits=() if m else (sent[1][1],),
            )
            for m in pieces
        ]
        back = [over_columns(a[0]) for a in moved]

        def halves(side):
            lefts = ([a[1] for a in applied], [a[1] for a in moved], [a[2] for a in moved])
            rights = (arrived, entered, entered)
            return [
                call(
                    functools.partial(expert_weight_grads, side),
                    (like((per_column, hidden_width // 4, width), BF),) * 2, (*left, *right),
                    expert_flops,
                )
                for left, right in zip(lefts, rights)
            ]

        far = halves(1)
        near = halves(0) if keep else []
        between = [p[0].astype(F32) + swapped(p[1], 1).astype(F32) for p in far]
        between = [b.astype(BF) for b in between]
        first_waits = [moved[1][0], *(p[0] for p in far), *(p[0] for p in near)]
        inner, parts, outer, branches = [], [], [], []
        for m in pieces:
            inner.append(
                call(
                    functools.partial(attend_back, keep),
                    (token_wide, token_low) + (pair_like,) * 4
                    + ((like((tokens, LANES), BF), sums_like)
                       + (like((tokens, share), BF),) * rows if keep else ()),
                    (back[m], returned[m], attended[m][3], spread, places[m], attended[m][1], gain_f,
                     sent[m][0], projected[m][2], *pairs[m], attended[m][5], cosine, sine),
                    out_flops + 4 * score_flops, (dense,),
                    [pltpu.VMEM((tokens, width), BF)] + out_scratch,
                    scalars=(here,),
                    waits=(*between, *waits[1]) if m else (*first_waits, *waits[0]),
                )
            )
        parts = [[a[2]] + [swapped(a[2 + s], s) for s in steps[1:]] for a in inner]
        if keep:
            branches = [[a[8]] + [swapped(a[8 + s], s) for s in steps[1:]] for a in inner]
            o_grads = call(
                out_grads, (like((width, share), BF),),
                (*lefts, *[b[s] for s in steps for b in branches]),
                2 * width * length * micro * share,
            )[0]
        outer = [
            call(
                functools.partial(project_back, keep),
                (token_wide, token_low)
                + ((sums_like,) + (like((tokens, qkv_width // rows), BF),) * rows if keep else ()),
                (*parts[m], inner[m][1], projected[m][0], gain_a, inner[m][0], cosine, sine),
                qkv_flops, (dense,), [pltpu.VMEM((tokens, qkv_width), BF)] + qkv_scratch,
                scalars=(here,), waits=(o_grads,) if m and keep else (),
            )
            for m in pieces
        ]
        if not keep:
            return outer, between
        backs = [[o[3]] + [swapped(o[3 + s], s) for s in steps[1:]] for o in outer]
        w_grads = call(
            qkv_grads, (like((width, qkv_width // rows + LANES), BF),),
            (*lefts, *[b[s] for s in steps for b in backs], *[a[2] for a in attended],
             *[a[6] for a in inner], *[o[2] for o in outer], *[a[7] for a in inner]),
            2 * width * length * micro * qkv_width // rows,
        )[0]
        return outer, between, near, o_grads, w_grads

    def by_columns(value):
        cut = value.reshape(rows, columns, shard, value.shape[1]).transpose(1, 0, 2, 3)
        return over_columns(cut.reshape(columns, rows * shard, value.shape[1]))

    def across(value, only):
        lines = [(only * rows + r, only * rows + (r ^ 2)) for r in range(rows)]
        return lax.ppermute(value, ("section", "row"), lines)

    entering = [inputs[m, 0] for m in pieces]
    moving = [g[k] for g in (gate_shards, up_shards, down_shards) for k in (1, 2)]
    results = forward(entering, entering, False, moving)[6]
    came = [lax.ppermute(r[1], "section", [(0, 1)]) for r in results]
    kept = forward(came, entering, True)
    projected, pairs, attended, arrived, applied, returned, results = kept
    left = call(
        pack, (like((2 * micro, tokens, width), BF),),
        [p[1] for p in projected] + [a[0] for a in attended], 0,
    )[0]
    two = swapped(left, 2)
    lefts = [left, swapped(left, 1), two, swapped(two, 1)]

    targets = [cotangent[m, 0] for m in pieces]
    outer, between = backward(targets, targets, kept, lefts, False, ((), lefts[1:]))
    came = [lax.ppermute(o[1], "section", [(1, 0)]) for o in outer]
    early = [across(b, 1) for b in between]
    done = [r[0] for r in results]
    outer, between, near, o_grads, w_grads = backward(
        came, targets, kept, lefts, True, ((*early, *done), ())
    )
    late = [across(b, 0) for b in between]
    expert_grads = [
        n[0].astype(F32) + swapped(n[1], 1).astype(F32) + e.astype(F32) + l.astype(F32)
        for n, e, l in zip(near, early, late)
    ]

    pieces_out = call(
        fold, (like((shard, share + qkv_width // rows + LANES), F32),) * rows,
        (by_columns(o_grads), by_columns(w_grads)), 0,
        scratch=[pltpu.VMEM((rows * shard, share + qkv_width // rows + LANES), F32)],
        scalars=(here,),
    )
    pieces_out = [pieces_out[0]] + [swapped(pieces_out[s], s) for s in steps[1:]]
    o_grad, q_grad, k_grad, v_grad, rest = call(
        finish,
        (like((shard, width), F32), like((shard, width), F32), like((shard, kv_width), F32),
         like((shard, kv_width), F32), like((shard, LANES), F32)),
        pieces_out, 0, scratch=[pltpu.VMEM((shard, qkv_width), F32)], scalars=(here,),
    )

    return (
        jnp.stack(done)[None, :, None],
        jnp.stack([o[0] for o in outer])[None, :, None],
        rest[:, LANES - 2][None],
        q_grad[None],
        k_grad[None],
        v_grad[None],
        o_grad[None],
        rest[:, LANES - 1][None],
        rest[:, :experts][None],
        expert_grads[1][None],
        expert_grads[2][None],
        expert_grads[0][None],
    )


def solution(mesh):
    dense = P("section", ("row", "col"), None)
    gain = P("section", ("row", "col"))
    expert = P("section", "col", "row", None)
    token = P(None, "col", "row", None)
    layered = P("section", None, "col", "row", None)
    return jax.shard_map(
        on_device,
        mesh=mesh,
        in_specs=(
            token, token, P(None, "col", None), layered, gain, dense, dense, dense, dense, gain,
            dense, expert, expert, expert,
        ),
        out_specs=(
            layered, layered, gain, dense, dense, dense, dense, gain, dense, expert, expert, expert,
        ),
        check_vma=False,
    )
```

```python
import functools

import jax
import jax.numpy as jnp
from jax import lax
from jax.experimental import pallas as pl
from jax.experimental.pallas import tpu as pltpu
from jax.sharding import PartitionSpec as P

HEAD_DIM = 128
ROOMS = 16
EPSILON = 1e-06
LANES = 128
BF = jnp.bfloat16
F32 = jnp.float32
MIB = 1 << 20


def dot(left, right, contract=(1, 0)):
    return lax.dot_general(
        left, right, (((contract[0],), (contract[1],)), ((), ())), preferred_element_type=F32
    )


def like(shape, dtype):
    return jax.ShapeDtypeStruct(shape, dtype)


def call(body, outs, args, flops, far=(), scratch=(), vmem=48, scalars=(), waits=()):
    moved = sum(a.size * a.dtype.itemsize for a in (*args, *far, *outs))
    used = len(scalars) + len(args) + len(far)

    def run(*refs):
        body(*refs[:used], *refs[used + len(waits) :])

    return pl.pallas_call(
        run,
        out_shape=tuple(outs),
        in_specs=[pl.BlockSpec(memory_space=pltpu.SMEM)] * len(scalars)
        + [pl.BlockSpec(memory_space=pltpu.VMEM)] * len(args)
        + [pl.BlockSpec(memory_space=pl.ANY)] * (len(far) + len(waits)),
        out_specs=tuple(pl.BlockSpec(memory_space=pltpu.VMEM) for unused in outs),
        scratch_shapes=list(scratch),
        compiler_params=pltpu.CompilerParams(vmem_limit_bytes=vmem * MIB),
        cost_estimate=pl.CostEstimate(
            flops=int(flops), bytes_accessed=int(moved), transcendentals=0
        ),
        name=body.func.__name__ if isinstance(body, functools.partial) else body.__name__,
    )(*scalars, *args, *far, *waits)


def swapped(value, step):
    rows = lax.axis_size("row")
    return lax.ppermute(value, "row", [(r, r ^ step) for r in range(rows)])


def norm_parts(stream):
    return lax.rsqrt(jnp.mean(stream * stream, -1, keepdims=True) + EPSILON)


def norm_back(grad, stream, gain):
    inverse = norm_parts(stream)
    unit = stream * inverse
    scaled = grad * gain
    back = inverse * (scaled - unit * jnp.mean(scaled * unit, -1, keepdims=True))
    return back, jnp.sum(grad * unit, 0, keepdims=True)


def turned(vectors, cosine, sine):
    done = []
    for at in range(0, vectors.shape[1], HEAD_DIM):
        one = vectors[:, at : at + HEAD_DIM]
        done.append(one * cosine + pltpu.roll(one, HEAD_DIM // 2, 1) * sine)
    return jnp.concatenate(done, -1) if len(done) > 1 else done[0]


def stacked_heads(value, first, count):
    return jnp.concatenate(
        [value[:, (first + j) * HEAD_DIM : (first + j + 1) * HEAD_DIM] for j in range(count)], 0
    )


def unstacked_heads(value, count):
    tokens = value.shape[0] // count
    return jnp.concatenate([value[j * tokens : (j + 1) * tokens] for j in range(count)], 1)


def cuts_of(total, most=512):
    return [(at, min(most, total - at)) for at in range(0, total, most)]


def project(
    flag, came, entering, gain, cosine, sine, dense, stream, normed, query, pair, weights, sems
):
    width = stream.shape[1]
    cuts = cuts_of(weights.shape[1])
    copies = [
        pltpu.make_async_copy(
            dense.at[:, pl.ds(at, size)], weights.at[:, pl.ds(at, size)], sems.at[k]
        )
        for k, (at, size) in enumerate(cuts)
    ]
    for copy in copies:
        copy.start()
    x = jnp.where(flag[0] > 0, came[...].astype(F32), entering[...].astype(F32))
    stream[...] = x
    low = (x * norm_parts(x) * gain[...]).astype(BF)
    normed[...] = low
    keys = pair.shape[1] // 2
    for copy, (at, size) in zip(copies, cuts):
        copy.wait()
        part = dot(low, weights[:, at : at + size])
        for begin in range(at, at + size, HEAD_DIM):
            head = part[:, begin - at : begin - at + HEAD_DIM]
            if begin < width + keys:
                head = turned(head, cosine[...], sine[...])
            if begin < width:
                query[:, begin : begin + HEAD_DIM] = head.astype(BF)
            else:
                pair[:, begin - width : begin - width + HEAD_DIM] = head.astype(BF)


def scaled_rows(dispatch, gates, low):
    slots = dispatch.shape[0]
    own = lax.broadcasted_iota(jnp.int32, (slots, LANES), 0) // ROOMS
    here = own == lax.broadcasted_iota(jnp.int32, (slots, LANES), 1)
    scale = jnp.sum(jnp.where(here, dot(dispatch, gates.astype(BF)), 0.0), -1, keepdims=True)
    return (dot(dispatch, low) * scale).astype(BF)


def attend(
    stream, query, pair0, pair1, pair2, pair3, bias, gain, chosen, dispatch, *rest,
):
    targets, rest = rest[:-10], rest[-10:]
    dense, mixed, middle, normed_ffn, gates, outgoing, probs, weights, router, sems = rest
    width = stream.shape[1]
    block = (outgoing.shape[0], -1, width)
    per = dispatch.shape[0] // outgoing.shape[0]
    at = dense.shape[1] - width - LANES
    copies = [
        pltpu.make_async_copy(dense.at[:, pl.ds(at + LANES, width)], weights, sems.at[0]),
        pltpu.make_async_copy(dense.at[:, pl.ds(at, LANES)], router, sems.at[1]),
    ]
    for copy in copies:
        copy.start()
    pairs = jnp.concatenate([pair0[...], pair1[...], pair2[...], pair3[...]], 0)
    kv_heads = pairs.shape[1] // (2 * HEAD_DIM)
    group = width // HEAD_DIM // kv_heads
    biases = jnp.concatenate([bias[...]] * group, 0)
    tokens = stream.shape[0]
    for h in range(kv_heads):
        keys = pairs[:, h * HEAD_DIM : (h + 1) * HEAD_DIM]
        values = pairs[:, (kv_heads + h) * HEAD_DIM : (kv_heads + h + 1) * HEAD_DIM]
        queries = stacked_heads(query, h * group, group)
        scores = dot(queries, keys, (1, 1)) * HEAD_DIM ** (-0.5) + biases
        expo = jnp.exp(scores - jnp.max(scores, -1, keepdims=True))
        weight = (expo * (1.0 / jnp.sum(expo, -1, keepdims=True))).astype(BF)
        probs[h] = weight
        done = dot(weight, values).astype(BF)
        for j in range(group):
            begin = (h * group + j) * HEAD_DIM
            mixed[:, begin : begin + HEAD_DIM] = done[j * tokens : (j + 1) * tokens]
    copies[0].wait()
    x = stream[...] + dot(mixed[...], weights[...])
    middle[...] = x
    low = (x * norm_parts(x) * gain[...]).astype(BF)
    normed_ffn[...] = low
    copies[1].wait()
    taken = chosen[...] > 0
    logits = jnp.where(taken, dot(low, router[...]), -1e30)
    expo = jnp.where(taken, jnp.exp(logits - jnp.max(logits, -1, keepdims=True)), 0.0)
    share = expo / jnp.sum(expo, -1, keepdims=True)
    gates[...] = share
    outgoing[:, :per, :] = dot(dispatch[...], low).astype(BF).reshape(block)
    if targets:
        outgoing[:, per:, :] = scaled_rows(dispatch[...], share, targets[0][...]).reshape(block)


def fetch(shards, weights, sems):
    copies = []
    for j in range(weights.shape[1]):
        line = []
        for k in range(weights.shape[0]):
            some = []
            for p in range(4):
                size = shards[k][p].shape[1]
                some.append(
                    pltpu.make_async_copy(
                        shards[k][p].at[j],
                        weights.at[k, j, pl.ds(p * size, size)],
                        sems.at[k, j, p],
                    )
                )
            line.append(some)
        copies.append(line)
    for line in copies:
        for some in line:
            for copy in some:
                copy.start()
    return copies


def done_with(copies):
    for copy in copies:
        copy.wait()


def rows_of(value, j, begin=0):
    columns, unused, width = value.shape
    at = begin + j * ROOMS
    return value[:, at : at + ROOMS, :].reshape(columns * ROOMS, width)


def expert_forward(both, arrived, *refs):
    shards = [refs[4 * k : 4 * k + 4] for k in range(3)]
    outs, weights, sems = refs[12:-2], refs[-2], refs[-1]
    copies = fetch(shards, weights, sems)
    per = weights.shape[1] * ROOMS
    for j in range(weights.shape[1]):
        at = j * ROOMS
        rows = rows_of(arrived, j)
        done_with(copies[j][0])
        gate = dot(rows, weights[0, j], (1, 1))
        done_with(copies[j][1])
        lifted = dot(rows, weights[1, j], (1, 1))
        square = gate * gate
        bend = jnp.tanh(0.7978845608028654 * gate * (1.0 + 0.044715 * square))
        active = 0.5 * gate * (1.0 + bend)
        hidden = (active * lifted).astype(BF)
        done_with(copies[j][2])
        made = dot(hidden, weights[2, j]).astype(BF)
        outs[0][:, at : at + ROOMS, :] = made.reshape(-1, ROOMS, made.shape[1])
        if both:
            slope = 0.5 * (1.0 + bend) + 0.5 * gate * (1.0 - bend * bend) * (
                0.7978845608028654 * (1.0 + 3 * 0.044715 * square)
            )
            bent = slope * lifted
            outs[1][j] = hidden
            outs[2][j] = active.astype(BF)
            outs[3][j] = bent.astype(BF)
            hidden_grads = dot(rows_of(arrived, j, per), weights[2, j], (1, 1))
            gate_part = (hidden_grads * bent).astype(BF)
            lifted_part = (hidden_grads * active).astype(BF)
            outs[4][j] = gate_part
            outs[5][j] = lifted_part
            back = dot(gate_part, weights[0, j]) + dot(lifted_part, weights[1, j])
            outs[0][:, per + at : per + at + ROOMS, :] = back.astype(BF).reshape(
                -1, ROOMS, back.shape[1]
            )


def first_rows(returned, places):
    columns, unused, width = returned.shape
    return returned[:, : places.shape[1] // columns, :].reshape(-1, width)


def combine(returned, middle, gates, spread, places, result, low):
    weights = dot(gates[...].astype(BF), spread[...]) * places[...].astype(F32)
    done = middle[...] + dot(weights.astype(BF), first_rows(returned, places))
    result[...] = done
    low[...] = done.astype(BF)


def send_grads(flag, came, target, gates, dispatch, grad, outgoing):
    low = jnp.where(flag[0] > 0, came[...], target[...])
    grad[...] = low
    outgoing[...] = scaled_rows(dispatch[...], gates[...], low).reshape(outgoing.shape)


def expert_backward(arrived, active, bent, *refs):
    shards = [refs[4 * k : 4 * k + 4] for k in range(3)]
    sent, gate_back, lifted_back, weights, sems = refs[12:]
    copies = fetch(shards, weights, sems)
    for j in range(weights.shape[1]):
        done_with(copies[j][0])
        hidden_grads = dot(rows_of(arrived, j), weights[0, j], (1, 1))
        gate_part = (hidden_grads * bent[j].astype(F32)).astype(BF)
        lifted_part = (hidden_grads * active[j].astype(F32)).astype(BF)
        gate_back[j] = gate_part
        lifted_back[j] = lifted_part
        done_with(copies[j][1])
        done = dot(gate_part, weights[1, j])
        done_with(copies[j][2])
        done = (done + dot(lifted_part, weights[2, j])).astype(BF)
        sent[:, j * ROOMS : (j + 1) * ROOMS, :] = done.reshape(-1, ROOMS, done.shape[1])


def attend_back(
    keep, row, token_grads, returned, gates, spread, places, middle, gain, grad, query, pair0, pair1,
    pair2, pair3, probs, cosine, sine, dense, middle_grads, query_back, part0, part1, part2, part3,
    *rest,
):
    tokens, width = middle.shape
    kept, (branch, weights, router, sems) = rest[:-4], rest[-4:]
    at = dense.shape[1] - width - LANES
    copies = [
        pltpu.make_async_copy(dense.at[:, pl.ds(at, LANES)], router, sems.at[1]),
        pltpu.make_async_copy(dense.at[:, pl.ds(at + LANES, width)], weights, sems.at[0]),
    ]
    for copy in copies:
        copy.start()
    inner = dot(grad[...], first_rows(returned, places), (1, 1)) * places[...].astype(F32)
    gate_grads = dot(inner.astype(BF), spread[...], (1, 1))
    chances = gates[...]
    logit_grads = (
        chances * (gate_grads - jnp.sum(chances * gate_grads, -1, keepdims=True))
    ).astype(BF)
    per = places.shape[1] // returned.shape[0]
    came = token_grads[:, token_grads.shape[1] - per :, :].reshape(-1, width)
    ffn_grads = dot(places[...], came)
    copies[0].wait()
    ffn_grads = ffn_grads + dot(logit_grads, router[...], (1, 1))
    part, total = norm_back(ffn_grads, middle[...], gain[...])
    above = grad[...].astype(F32) + part
    middle_grads[...] = above
    low = above.astype(BF)
    if keep:
        kept[0][...] = logit_grads
        kept[1][...] = jnp.broadcast_to(total, kept[1].shape)
        branch[...] = low
        share = width // 4
        for s, out in enumerate(kept[2:]):
            out[...] = branch[:, pl.ds(pl.multiple_of((row[0] ^ s) * share, LANES), share)]
    copies[1].wait()
    mixed_grads = dot(low, weights[...], (1, 1)).astype(BF)
    pairs = jnp.concatenate([pair0[...], pair1[...], pair2[...], pair3[...]], 0)
    kv_heads = pairs.shape[1] // (2 * HEAD_DIM)
    group = width // HEAD_DIM // kv_heads
    scale = HEAD_DIM ** (-0.5)
    parts = (part0, part1, part2, part3)
    for h in range(kv_heads):
        keys = pairs[:, h * HEAD_DIM : (h + 1) * HEAD_DIM]
        values = pairs[:, (kv_heads + h) * HEAD_DIM : (kv_heads + h + 1) * HEAD_DIM]
        queries = stacked_heads(query, h * group, group)
        top = stacked_heads(mixed_grads, h * group, group)
        weight = probs[h]
        wide = weight.astype(F32)
        weight_grads = dot(top, values, (1, 1))
        value_grads = dot(weight, top, (0, 0)).astype(BF)
        inner = wide * weight_grads
        score_grads = (inner - wide * jnp.sum(inner, -1, keepdims=True)).astype(BF)
        query_grads = dot(score_grads, keys) * scale
        key_grads = (dot(score_grads, queries, (0, 0)) * scale).astype(BF)
        for j in range(group):
            begin = (h * group + j) * HEAD_DIM
            one = query_grads[j * tokens : (j + 1) * tokens]
            query_back[:, begin : begin + HEAD_DIM] = turned(one, cosine[...], -sine[...]).astype(BF)
        for p, part in enumerate(parts):
            part[:, h * HEAD_DIM : (h + 1) * HEAD_DIM] = key_grads[p * tokens : (p + 1) * tokens]
            begin = (kv_heads + h) * HEAD_DIM
            part[:, begin : begin + HEAD_DIM] = value_grads[p * tokens : (p + 1) * tokens]


def project_back(
    keep, row, part0, part1, part2, part3, query_back, stream, gain, middle_grads, cosine, sine,
    dense, grad, low, *rest,
):
    width = stream.shape[1]
    kept, (backs, weights, sems) = rest[:-3], rest[-3:]
    cuts = cuts_of(weights.shape[1])
    copies = [
        pltpu.make_async_copy(
            dense.at[:, pl.ds(at, size)], weights.at[:, pl.ds(at, size)], sems.at[k]
        )
        for k, (at, size) in enumerate(cuts)
    ]
    for copy in copies:
        copy.start()
    total = sum(part[...].astype(F32) for part in (part0, part1, part2, part3))
    keys = total.shape[1] // 2
    backs[:, :width] = query_back[...]
    backs[:, width : width + keys] = turned(total[:, :keys], cosine[...], -sine[...]).astype(BF)
    backs[:, width + keys :] = total[:, keys:].astype(BF)
    above = jnp.zeros(stream.shape, F32)
    for copy, (at, size) in zip(copies, cuts):
        copy.wait()
        above = above + dot(backs[:, at : at + size], weights[:, at : at + size], (1, 1))
    part, sums = norm_back(above, stream[...], gain[...])
    if keep:
        kept[0][...] = jnp.broadcast_to(sums, kept[0].shape)
        share = backs.shape[1] // 4
        for s, out in enumerate(kept[1:]):
            out[...] = backs[:, pl.ds(pl.multiple_of((row[0] ^ s) * share, LANES), share)]
    done = middle_grads[...] + part
    grad[...] = done
    low[...] = done.astype(BF)


def expert_weight_grads(half, begin, left0, left1, right0, right1, first, second):
    size = first.shape[1]
    wide = 2 * size
    for j in range(first.shape[0]):
        total = dot(left0[j, :, half * wide : (half + 1) * wide], rows_of(right0, j, begin), (0, 0))
        total = total + dot(
            left1[j, :, half * wide : (half + 1) * wide], rows_of(right1, j, begin), (0, 0)
        )
        first[j] = total[:size].astype(BF)
        second[j] = total[size:].astype(BF)


def pack(*refs):
    for k, value in enumerate(refs[:-1]):
        refs[-1][k] = value[...]


def stacked(refs):
    return jnp.concatenate([r[...] for r in refs], 0)


def out_grads(*refs):
    lefts, rights, out = refs[:4], refs[4:12], refs[12]
    left = jnp.concatenate([one[k] for one in lefts for k in (2, 3)], 0)
    out[...] = dot(left, stacked(rights), (0, 0)).astype(BF)


def qkv_grads(*refs):
    lefts, rights, normed, logits, gains, out = (
        refs[:4], refs[4:12], refs[12:14], refs[14:16], refs[16:20], refs[20],
    )
    width, wide = out.shape
    left = jnp.concatenate([one[k] for one in lefts for k in (0, 1)], 0)
    out[:, : wide - LANES] = dot(left, stacked(rights), (0, 0)).astype(BF)
    first = gains[0][:1] + gains[1][:1]
    second = gains[2][:1] + gains[3][:1]
    line = lax.broadcasted_iota(jnp.int32, (LANES, width), 0)
    sums = jnp.where(
        line == LANES - 2, first, jnp.where(line == LANES - 1, second, jnp.zeros((1, 1), F32))
    )
    out[:, wide - LANES :] = (dot(stacked(normed), stacked(logits), (0, 0)) + sums.T).astype(BF)


def fold(row, first, second, out0, out1, out2, out3, total):
    share = first.shape[2]
    total[:, :share] = jnp.sum(first[...].astype(F32), 0)
    total[:, share:] = jnp.sum(second[...].astype(F32), 0)
    for s, out in enumerate((out0, out1, out2, out3)):
        size = out.shape[0]
        out[...] = total[pl.ds(pl.multiple_of((row[0] ^ s) * size, 8), size), :]


def finish(row, in0, in1, in2, in3, o_grad, q_grad, k_grad, v_grad, rest, total):
    share = o_grad.shape[1] // 4
    piece = total.shape[1] // 4
    ins = (in0, in1, in2, in3)
    for s, one in enumerate(ins):
        where = row[0] ^ s
        o_grad[:, pl.ds(pl.multiple_of(where * share, LANES), share)] = one[:, :share]
        total[:, pl.ds(pl.multiple_of(where * piece, LANES), piece)] = one[:, share : share + piece]
    rest[...] = sum(one[:, share + piece :] for one in ins)
    begin = 0
    for out in (q_grad, k_grad, v_grad):
        out[...] = total[:, begin : begin + out.shape[1]]
        begin += out.shape[1]


def over_columns(value):
    return lax.all_to_all(value, "col", split_axis=0, concat_axis=0, tiled=True)


def on_device(
    inputs, cotangent, segment_ids, routes, attn_gain, w_query, w_key, w_value, w_out, ffn_gain,
    w_router, w_gate, w_up, w_down,
):
    section = lax.axis_index("section")
    row = lax.axis_index("row")
    rows = lax.axis_size("row")
    columns = lax.axis_size("col")
    micro, tokens, width = inputs.shape[0], inputs.shape[2], inputs.shape[3]
    experts = w_router.shape[2]
    per_column = w_gate.shape[1]
    hidden_width = w_gate.shape[2] * rows
    kv_width = w_key.shape[2]
    qkv_width = width + 2 * kv_width
    slots = experts * ROOMS
    share = width // rows
    shard = width // (rows * columns)
    heads = width // HEAD_DIM
    kv_heads = kv_width // HEAD_DIM
    length = rows * tokens
    pieces = range(micro)
    steps = range(rows)
    here = row.astype(jnp.int32)[None]
    second = (section == 1).astype(jnp.int32)[None]
    block = (columns, slots // columns, width)

    dense = jnp.concatenate(
        [w_query[0], w_key[0], w_value[0], w_router[0], attn_gain[0][:, None], ffn_gain[0][:, None],
         jnp.zeros((shard, LANES - experts - 2), BF), w_out[0]], 1
    )
    dense = lax.all_gather(dense, ("row", "col"), axis=0, tiled=True)
    small = dense[:, qkv_width : qkv_width + LANES]
    gain_a = small[:, experts].astype(F32)[None, :]
    gain_f = small[:, experts + 1].astype(F32)[None, :]

    def across(value, only):
        lines = [(only * rows + r, only * rows + (r ^ 2)) for r in range(rows)]
        return lax.ppermute(value, ("section", "row"), lines)

    owns = (w_gate[0], w_up[0], w_down[0])
    ones = [swapped(own, 1) for own in owns]
    early_twos = [across(own, 0) for own in owns]
    early_shards = [
        (own, one, two, swapped(two, 1)) for own, one, two in zip(owns, ones, early_twos)
    ]
    twos = [two + across(own, 1) for own, two in zip(owns, early_twos)]
    gate_shards, up_shards, down_shards = [
        (own, one, two, swapped(two, 1)) for own, one, two in zip(owns, ones, twos)
    ]

    lane = jnp.arange(LANES, dtype=jnp.int32)
    half = HEAD_DIM // 2
    freqs = 10000.0 ** (-2.0 * jnp.arange(half).astype(F32) / HEAD_DIM)
    positions = row * tokens + jnp.arange(tokens, dtype=jnp.int32)
    angles = positions.astype(F32)[:, None] * freqs[None, :]
    cosine = jnp.concatenate([jnp.cos(angles)] * 2, 1)
    sine = jnp.concatenate([-jnp.sin(angles), jnp.sin(angles)], 1)
    key_positions = jnp.concatenate(
        [(row ^ step) * tokens + jnp.arange(tokens, dtype=jnp.int32) for step in steps]
    )
    spread = (lane[:, None] == jnp.arange(slots, dtype=jnp.int32)[None, :] // ROOMS).astype(BF)
    below = (jnp.arange(tokens)[:, None] > jnp.arange(tokens)[None, :]).astype(BF)
    biases, chosens, places, dispatches = [], [], [], []
    for m in pieces:
        segments = segment_ids[m, 0]
        own_segments = lax.dynamic_slice_in_dim(segments, row * tokens, tokens)
        key_segments = jnp.concatenate(
            [lax.dynamic_slice_in_dim(segments, (row ^ s) * tokens, tokens) for s in steps]
        )
        counted = (key_positions[None, :] <= positions[:, None]) & (
            key_segments[None, :] == own_segments[:, None]
        )
        biases.append(jnp.where(counted, 0.0, -1e30).astype(F32))
        chosen = jnp.any(routes[0, m, 0][:, :, None] == lane[None, None, :], 1)
        chosens.append(chosen.astype(F32))
        rank = dot(below, chosen.astype(BF))
        rank = jnp.where(chosen, rank, -1.0)[:, :experts]
        place = (
            rank[:, :, None] == jnp.arange(ROOMS, dtype=F32)[None, None, :]
        ).reshape(tokens, slots)
        places.append(place.astype(BF))
        dispatches.append(place.T.astype(BF))

    token_low, token_wide = like((tokens, width), BF), like((tokens, width), F32)
    pair_like = like((tokens, 2 * kv_width), BF)
    block_like = like(block, BF)
    sums_like = like((8, width), F32)
    kept_like = like((per_column, columns * ROOMS, hidden_width), BF)
    probs_like = like((kv_heads, heads // kv_heads * tokens, length), BF)
    qkv_scratch = [pltpu.VMEM((width, qkv_width), BF), pltpu.SemaphoreType.DMA((8,))]
    out_scratch = [
        pltpu.VMEM((width, width), BF), pltpu.VMEM((width, LANES), BF),
        pltpu.SemaphoreType.DMA((2,)),
    ]
    expert_scratch = [
        pltpu.VMEM((3, per_column, hidden_width, width), BF),
        pltpu.SemaphoreType.DMA((3, per_column, 4)),
    ]
    qkv_flops = 2 * tokens * width * qkv_width
    out_flops = 2 * tokens * width * width + 2 * slots * tokens * width
    score_flops = 2 * heads * tokens * length * HEAD_DIM
    expert_flops = 2 * slots * hidden_width * width

    per = slots // columns
    double_like = like((columns, 2 * per, width), BF)

    def forward(came, entering, shards, targets, waits):
        projected, pairs = [], []
        for m in pieces:
            projected.append(
                call(
                    project, (token_wide, token_low, token_low, pair_like),
                    (came[m], entering[m], gain_a, cosine, sine), qkv_flops, (dense,), qkv_scratch,
                    scalars=(second,), waits=(*waits[m], *(p[0] for p in projected)),
                )
            )
            pair = projected[m][3]
            pairs.append([pair] + [swapped(pair, s) for s in steps[1:]])
        attended = [
            call(
                attend,
                (token_low, token_wide, token_low, like((tokens, LANES), F32),
                 double_like if targets else block_like, probs_like),
                (projected[m][0], projected[m][2], *pairs[m], biases[m], gain_f, chosens[m],
                 dispatches[m], *targets[m : m + 1]),
                out_flops + 2 * score_flops, (dense,), out_scratch,
            )
            for m in pieces
        ]
        arrived = [over_columns(a[4]) for a in attended]
        applied = [
            call(
                functools.partial(expert_forward, bool(targets)),
                (double_like,) + (kept_like,) * 5 if targets else (block_like,), (arrived[m],),
                (6 if targets else 3) * expert_flops, shards, expert_scratch,
                waits=() if m else (attended[1][4],),
            )
            for m in pieces
        ]
        returned = [over_columns(a[0]) for a in applied]
        results = [
            call(
                combine, (token_wide, token_low),
                (returned[m], attended[m][1], attended[m][3], spread, places[m]),
                2 * slots * tokens * width, waits=() if m else (applied[1][0],),
            )
            for m in pieces
        ]
        return projected, pairs, attended, arrived, applied, returned, results

    def far_and_near(lefts, rights, begins, side):
        return [
            call(
                functools.partial(expert_weight_grads, side, begin),
                (like((per_column, hidden_width // 4, width), BF),) * 2, (*left, *right),
                expert_flops,
            )
            for left, right, begin in zip(lefts, rights, begins)
        ]

    def merged(halves):
        return [(h[0].astype(F32) + swapped(h[1], 1).astype(F32)).astype(BF) for h in halves]

    def attention_back(keep, m, grad, token_grads, waits):
        return call(
            functools.partial(attend_back, keep),
            (token_wide, token_low) + (pair_like,) * 4
            + ((like((tokens, LANES), BF), sums_like) + (like((tokens, share), BF),) * rows
               if keep else ()),
            (token_grads, returned[m], attended[m][3], spread, places[m], attended[m][1], gain_f,
             grad, projected[m][2], *pairs[m], attended[m][5], cosine, sine),
            out_flops + 4 * score_flops, (dense,), [pltpu.VMEM((tokens, width), BF)] + out_scratch,
            scalars=(here,), waits=waits,
        )

    def projection_back(keep, m, inner, waits):
        parts = [inner[2]] + [swapped(inner[2 + s], s) for s in steps[1:]]
        return call(
            functools.partial(project_back, keep),
            (token_wide, token_low)
            + ((sums_like,) + (like((tokens, qkv_width // rows), BF),) * rows if keep else ()),
            (*parts, inner[1], projected[m][0], gain_a, inner[0], cosine, sine),
            qkv_flops, (dense,), [pltpu.VMEM((tokens, qkv_width), BF)] + qkv_scratch,
            scalars=(here,), waits=waits,
        )

    def by_columns(value):
        cut = value.reshape(rows, columns, shard, value.shape[1]).transpose(1, 0, 2, 3)
        return over_columns(cut.reshape(columns, rows * shard, value.shape[1]))

    entering = [inputs[m, 0] for m in pieces]
    targets = [cotangent[m, 0] for m in pieces]
    shards = [one for line in early_shards for one in line]
    here_by_now = [one for line in early_shards for one in line[1:3]]
    results = forward(entering, entering, shards, (), (here_by_now, ()))[6]
    came = [lax.ppermute(r[1], "section", [(0, 1)]) for r in results]

    shards = (*gate_shards, *up_shards, *down_shards)
    here_by_now = [line[3] for line in (gate_shards, up_shards, down_shards)]
    kept = forward(came, entering, shards, targets, ((), here_by_now))
    projected, pairs, attended, arrived, applied, returned, results = kept
    left = call(
        pack, (like((2 * micro, tokens, width), BF),),
        [p[1] for p in projected] + [a[0] for a in attended], 0,
    )[0]
    two = swapped(left, 2)
    lefts = [left, swapped(left, 1), two, swapped(two, 1)]
    hidden = [a[1] for a in applied]

    far = far_and_near(
        (hidden, [a[4] for a in applied], [a[5] for a in applied]), (arrived,) * 3, (per, 0, 0), 1
    )
    between = merged(far)
    inner, outer = [], []
    for m in pieces:
        waits = (*between, *lefts[1:], outer[0][0]) if m else (applied[1][0], *(f[0] for f in far))
        inner.append(attention_back(False, m, targets[m], returned[m], waits))
        outer.append(projection_back(False, m, inner[m], ()))
    came = [lax.ppermute(o[1], "section", [(1, 0)]) for o in outer]
    early = [across(b, 1) for b in between]

    sent = [
        call(
            send_grads, (token_low, block_like),
            (came[m], targets[m], attended[m][3], dispatches[m]),
            2 * slots * tokens * width, scalars=(1 - second,),
        )
        for m in pieces
    ]
    arrived_grads = [over_columns(s[1]) for s in sent]
    moved = [
        call(
            expert_backward, (block_like, kept_like, kept_like),
            (arrived_grads[m], applied[m][2], applied[m][3]), 3 * expert_flops,
            (*down_shards, *gate_shards, *up_shards), expert_scratch,
            waits=() if m else (sent[1][1],),
        )
        for m in pieces
    ]
    back = [over_columns(a[0]) for a in moved]
    operands = (
        (hidden, [a[1] for a in moved], [a[2] for a in moved]), (arrived_grads, arrived, arrived),
        (0, 0, 0),
    )
    far = far_and_near(*operands, 1)
    between = merged(far)
    late = [across(b, 0) for b in between]
    near = far_and_near(*operands, 0)
    done = [r[0] for r in results]

    inner = [attention_back(
        True, 0, sent[0][0], back[0], (moved[1][0], *(p[0] for p in far), *early, *done)
    )]
    outer = [projection_back(True, 0, inner[0], ())]
    inner.append(attention_back(
        True, 1, sent[1][0], back[1], (*between, outer[0][0], *(p[0] for p in near))
    ))
    branches = [[a[8]] + [swapped(a[8 + s], s) for s in steps[1:]] for a in inner]
    o_grads = call(
        out_grads, (like((width, share), BF),),
        (*lefts, *[b[s] for s in steps for b in branches]), 2 * width * length * micro * share,
        waits=late,
    )[0]
    outer.append(projection_back(True, 1, inner[1], (o_grads,)))
    backs = [[o[3]] + [swapped(o[3 + s], s) for s in steps[1:]] for o in outer]
    w_grads = call(
        qkv_grads, (like((width, qkv_width // rows + LANES), BF),),
        (*lefts, *[b[s] for s in steps for b in backs], *[a[2] for a in attended],
         *[a[6] for a in inner], *[o[2] for o in outer], *[a[7] for a in inner]),
        2 * width * length * micro * qkv_width // rows,
    )[0]
    expert_grads = [
        n[0].astype(F32) + swapped(n[1], 1).astype(F32) + e.astype(F32) + l.astype(F32)
        for n, e, l in zip(near, early, late)
    ]

    pieces_out = call(
        fold, (like((shard, share + qkv_width // rows + LANES), F32),) * rows,
        (by_columns(o_grads), by_columns(w_grads)), 0,
        scratch=[pltpu.VMEM((rows * shard, share + qkv_width // rows + LANES), F32)],
        scalars=(here,),
    )
    pieces_out = [pieces_out[0]] + [swapped(pieces_out[s], s) for s in steps[1:]]
    o_grad, q_grad, k_grad, v_grad, rest = call(
        finish,
        (like((shard, width), F32), like((shard, width), F32), like((shard, kv_width), F32),
         like((shard, kv_width), F32), like((shard, LANES), F32)),
        pieces_out, 0, scratch=[pltpu.VMEM((shard, qkv_width), F32)], scalars=(here,),
    )

    return (
        jnp.stack(done)[None, :, None],
        jnp.stack([o[0] for o in outer])[None, :, None],
        rest[:, LANES - 2][None],
        q_grad[None],
        k_grad[None],
        v_grad[None],
        o_grad[None],
        rest[:, LANES - 1][None],
        rest[:, :experts][None],
        expert_grads[1][None],
        expert_grads[2][None],
        expert_grads[0][None],
    )


def solution(mesh):
    dense = P("section", ("row", "col"), None)
    gain = P("section", ("row", "col"))
    expert = P("section", "col", "row", None)
    token = P(None, "col", "row", None)
    layered = P("section", None, "col", "row", None)
    return jax.shard_map(
        on_device,
        mesh=mesh,
        in_specs=(
            token, token, P(None, "col", None), layered, gain, dense, dense, dense, dense, gain,
            dense, expert, expert, expert,
        ),
        out_specs=(
            layered, layered, gain, dense, dense, dense, dense, gain, dense, expert, expert, expert,
        ),
        check_vma=False,
    )
```

```python
import functools

import jax
import jax.numpy as jnp
from jax import lax
from jax.experimental import pallas as pl
from jax.experimental.pallas import tpu as pltpu
from jax.sharding import PartitionSpec as P

HEAD_DIM = 128
ROOMS = 16
EPSILON = 1e-06
LANES = 128
BF = jnp.bfloat16
F32 = jnp.float32
MIB = 1 << 20


def dot(left, right, contract=(1, 0)):
    return lax.dot_general(
        left, right, (((contract[0],), (contract[1],)), ((), ())), preferred_element_type=F32
    )


def like(shape, dtype):
    return jax.ShapeDtypeStruct(shape, dtype)


def call(body, outs, args, flops, far=(), scratch=(), vmem=48, scalars=(), waits=()):
    moved = sum(a.size * a.dtype.itemsize for a in (*args, *far, *outs))
    used = len(scalars) + len(args) + len(far)

    def run(*refs):
        body(*refs[:used], *refs[used + len(waits) :])

    return pl.pallas_call(
        run,
        out_shape=tuple(outs),
        in_specs=[pl.BlockSpec(memory_space=pltpu.SMEM)] * len(scalars)
        + [pl.BlockSpec(memory_space=pltpu.VMEM)] * len(args)
        + [pl.BlockSpec(memory_space=pl.ANY)] * (len(far) + len(waits)),
        out_specs=tuple(pl.BlockSpec(memory_space=pltpu.VMEM) for unused in outs),
        scratch_shapes=list(scratch),
        compiler_params=pltpu.CompilerParams(vmem_limit_bytes=vmem * MIB),
        cost_estimate=pl.CostEstimate(
            flops=int(flops), bytes_accessed=int(moved), transcendentals=0
        ),
        name=body.func.__name__ if isinstance(body, functools.partial) else body.__name__,
    )(*scalars, *args, *far, *waits)


def nothing(*refs):
    pass


def hold(value, *waits):
    return pl.pallas_call(
        nothing,
        out_shape=like(value.shape, value.dtype),
        in_specs=[pl.BlockSpec(memory_space=pl.ANY)] * (1 + len(waits)),
        out_specs=pl.BlockSpec(memory_space=pl.ANY),
        input_output_aliases={0: 0},
        name="hold",
    )(value, *waits)


def swapped(value, step):
    rows = lax.axis_size("row")
    return lax.ppermute(value, "row", [(r, r ^ step) for r in range(rows)])


def norm_parts(stream):
    return lax.rsqrt(jnp.mean(stream * stream, -1, keepdims=True) + EPSILON)


def norm_back(grad, stream, gain):
    inverse = norm_parts(stream)
    unit = stream * inverse
    scaled = grad * gain
    back = inverse * (scaled - unit * jnp.mean(scaled * unit, -1, keepdims=True))
    return back, jnp.sum(grad * unit, 0, keepdims=True)


def turned(vectors, cosine, sine):
    done = []
    for at in range(0, vectors.shape[1], HEAD_DIM):
        one = vectors[:, at : at + HEAD_DIM]
        done.append(one * cosine + pltpu.roll(one, HEAD_DIM // 2, 1) * sine)
    return jnp.concatenate(done, -1) if len(done) > 1 else done[0]


def stacked_heads(value, first, count):
    return jnp.concatenate(
        [value[:, (first + j) * HEAD_DIM : (first + j + 1) * HEAD_DIM] for j in range(count)], 0
    )


def unstacked_heads(value, count):
    tokens = value.shape[0] // count
    return jnp.concatenate([value[j * tokens : (j + 1) * tokens] for j in range(count)], 1)


def cuts_of(total, most=512):
    return [(at, min(most, total - at)) for at in range(0, total, most)]


def project(
    flag, came, entering, gain, cosine, sine, dense, stream, normed, query, pair, weights, sems
):
    width = stream.shape[1]
    cuts = cuts_of(weights.shape[1])
    copies = [
        pltpu.make_async_copy(
            dense.at[:, pl.ds(at, size)], weights.at[:, pl.ds(at, size)], sems.at[k]
        )
        for k, (at, size) in enumerate(cuts)
    ]
    for copy in copies:
        copy.start()
    x = jnp.where(flag[0] > 0, came[...].astype(F32), entering[...].astype(F32))
    stream[...] = x
    low = (x * norm_parts(x) * gain[...]).astype(BF)
    normed[...] = low
    keys = pair.shape[1] // 2
    for copy, (at, size) in zip(copies, cuts):
        copy.wait()
        part = dot(low, weights[:, at : at + size])
        for begin in range(at, at + size, HEAD_DIM):
            head = part[:, begin - at : begin - at + HEAD_DIM]
            if begin < width + keys:
                head = turned(head, cosine[...], sine[...])
            if begin < width:
                query[:, begin : begin + HEAD_DIM] = head.astype(BF)
            else:
                pair[:, begin - width : begin - width + HEAD_DIM] = head.astype(BF)


def scaled_rows(dispatch, gates, low):
    slots = dispatch.shape[0]
    own = lax.broadcasted_iota(jnp.int32, (slots, LANES), 0) // ROOMS
    here = own == lax.broadcasted_iota(jnp.int32, (slots, LANES), 1)
    scale = jnp.sum(jnp.where(here, dot(dispatch, gates.astype(BF)), 0.0), -1, keepdims=True)
    return (dot(dispatch, low) * scale).astype(BF)


def attend(
    stream, query, pair0, pair1, pair2, pair3, bias, gain, chosen, dispatch, *rest,
):
    targets, rest = rest[:-10], rest[-10:]
    dense, mixed, middle, normed_ffn, gates, outgoing, probs, weights, router, sems = rest
    width = stream.shape[1]
    block = (outgoing.shape[0], -1, width)
    per = dispatch.shape[0] // outgoing.shape[0]
    at = dense.shape[1] - width - LANES
    copies = [
        pltpu.make_async_copy(dense.at[:, pl.ds(at + LANES, width)], weights, sems.at[0]),
        pltpu.make_async_copy(dense.at[:, pl.ds(at, LANES)], router, sems.at[1]),
    ]
    for copy in copies:
        copy.start()
    pairs = jnp.concatenate([pair0[...], pair1[...], pair2[...], pair3[...]], 0)
    kv_heads = pairs.shape[1] // (2 * HEAD_DIM)
    group = width // HEAD_DIM // kv_heads
    biases = jnp.concatenate([bias[...]] * group, 0)
    tokens = stream.shape[0]
    for h in range(kv_heads):
        keys = pairs[:, h * HEAD_DIM : (h + 1) * HEAD_DIM]
        values = pairs[:, (kv_heads + h) * HEAD_DIM : (kv_heads + h + 1) * HEAD_DIM]
        queries = stacked_heads(query, h * group, group)
        scores = dot(queries, keys, (1, 1)) * HEAD_DIM ** (-0.5) + biases
        expo = jnp.exp(scores - jnp.max(scores, -1, keepdims=True))
        weight = (expo * (1.0 / jnp.sum(expo, -1, keepdims=True))).astype(BF)
        probs[h] = weight
        done = dot(weight, values).astype(BF)
        for j in range(group):
            begin = (h * group + j) * HEAD_DIM
            mixed[:, begin : begin + HEAD_DIM] = done[j * tokens : (j + 1) * tokens]
    copies[0].wait()
    x = stream[...] + dot(mixed[...], weights[...])
    middle[...] = x
    low = (x * norm_parts(x) * gain[...]).astype(BF)
    normed_ffn[...] = low
    copies[1].wait()
    taken = chosen[...] > 0
    logits = jnp.where(taken, dot(low, router[...]), -1e30)
    expo = jnp.where(taken, jnp.exp(logits - jnp.max(logits, -1, keepdims=True)), 0.0)
    share = expo / jnp.sum(expo, -1, keepdims=True)
    gates[...] = share
    outgoing[:, :per, :] = dot(dispatch[...], low).astype(BF).reshape(block)
    if targets:
        outgoing[:, per:, :] = scaled_rows(dispatch[...], share, targets[0][...]).reshape(block)


def fetch(shards, weights, sems):
    copies = []
    for j in range(weights.shape[1]):
        line = []
        for k in range(weights.shape[0]):
            some = []
            for p in range(4):
                size = shards[k][p].shape[1]
                some.append(
                    pltpu.make_async_copy(
                        shards[k][p].at[j],
                        weights.at[k, j, pl.ds(p * size, size)],
                        sems.at[k, j, p],
                    )
                )
            line.append(some)
        copies.append(line)
    for line in copies:
        for some in line:
            for copy in some:
                copy.start()
    return copies


def done_with(copies):
    for copy in copies:
        copy.wait()


def rows_of(value, j, begin=0):
    columns, unused, width = value.shape
    at = begin + j * ROOMS
    return value[:, at : at + ROOMS, :].reshape(columns * ROOMS, width)


def expert_forward(both, arrived, *refs):
    shards = [refs[4 * k : 4 * k + 4] for k in range(3)]
    outs, weights, sems = refs[12:-2], refs[-2], refs[-1]
    copies = fetch(shards, weights, sems)
    per = weights.shape[1] * ROOMS
    for j in range(weights.shape[1]):
        at = j * ROOMS
        rows = rows_of(arrived, j)
        done_with(copies[j][0])
        gate = dot(rows, weights[0, j], (1, 1))
        done_with(copies[j][1])
        lifted = dot(rows, weights[1, j], (1, 1))
        square = gate * gate
        bend = jnp.tanh(0.7978845608028654 * gate * (1.0 + 0.044715 * square))
        active = 0.5 * gate * (1.0 + bend)
        hidden = (active * lifted).astype(BF)
        done_with(copies[j][2])
        made = dot(hidden, weights[2, j]).astype(BF)
        outs[0][:, at : at + ROOMS, :] = made.reshape(-1, ROOMS, made.shape[1])
        if both:
            slope = 0.5 * (1.0 + bend) + 0.5 * gate * (1.0 - bend * bend) * (
                0.7978845608028654 * (1.0 + 3 * 0.044715 * square)
            )
            bent = slope * lifted
            outs[1][j] = hidden
            outs[2][j] = active.astype(BF)
            outs[3][j] = bent.astype(BF)
            hidden_grads = dot(rows_of(arrived, j, per), weights[2, j], (1, 1))
            gate_part = (hidden_grads * bent).astype(BF)
            lifted_part = (hidden_grads * active).astype(BF)
            outs[4][j] = gate_part
            outs[5][j] = lifted_part
            back = dot(gate_part, weights[0, j]) + dot(lifted_part, weights[1, j])
            outs[0][:, per + at : per + at + ROOMS, :] = back.astype(BF).reshape(
                -1, ROOMS, back.shape[1]
            )


def first_rows(returned, places):
    columns, unused, width = returned.shape
    return returned[:, : places.shape[1] // columns, :].reshape(-1, width)


def combine(returned, middle, gates, spread, places, result, low):
    weights = dot(gates[...].astype(BF), spread[...]) * places[...].astype(F32)
    done = middle[...] + dot(weights.astype(BF), first_rows(returned, places))
    result[...] = done
    low[...] = done.astype(BF)


def send_grads(flag, came, target, gates, dispatch, grad, outgoing):
    low = jnp.where(flag[0] > 0, came[...], target[...])
    grad[...] = low
    outgoing[...] = scaled_rows(dispatch[...], gates[...], low).reshape(outgoing.shape)


def expert_backward(arrived, active, bent, *refs):
    shards = [refs[4 * k : 4 * k + 4] for k in range(3)]
    sent, gate_back, lifted_back, weights, sems = refs[12:]
    copies = fetch(shards, weights, sems)
    for j in range(weights.shape[1]):
        done_with(copies[j][0])
        hidden_grads = dot(rows_of(arrived, j), weights[0, j], (1, 1))
        gate_part = (hidden_grads * bent[j].astype(F32)).astype(BF)
        lifted_part = (hidden_grads * active[j].astype(F32)).astype(BF)
        gate_back[j] = gate_part
        lifted_back[j] = lifted_part
        done_with(copies[j][1])
        done = dot(gate_part, weights[1, j])
        done_with(copies[j][2])
        done = (done + dot(lifted_part, weights[2, j])).astype(BF)
        sent[:, j * ROOMS : (j + 1) * ROOMS, :] = done.reshape(-1, ROOMS, done.shape[1])


def attend_back(
    keep, row, token_grads, returned, gates, spread, places, middle, gain, grad, query, pair0, pair1,
    pair2, pair3, probs, cosine, sine, dense, middle_grads, query_back, part0, part1, part2, part3,
    *rest,
):
    tokens, width = middle.shape
    kept, (branch, weights, router, sems) = rest[:-4], rest[-4:]
    at = dense.shape[1] - width - LANES
    copies = [
        pltpu.make_async_copy(dense.at[:, pl.ds(at, LANES)], router, sems.at[1]),
        pltpu.make_async_copy(dense.at[:, pl.ds(at + LANES, width)], weights, sems.at[0]),
    ]
    for copy in copies:
        copy.start()
    inner = dot(grad[...], first_rows(returned, places), (1, 1)) * places[...].astype(F32)
    gate_grads = dot(inner.astype(BF), spread[...], (1, 1))
    chances = gates[...]
    logit_grads = (
        chances * (gate_grads - jnp.sum(chances * gate_grads, -1, keepdims=True))
    ).astype(BF)
    per = places.shape[1] // returned.shape[0]
    came = token_grads[:, token_grads.shape[1] - per :, :].reshape(-1, width)
    ffn_grads = dot(places[...], came)
    copies[0].wait()
    ffn_grads = ffn_grads + dot(logit_grads, router[...], (1, 1))
    part, total = norm_back(ffn_grads, middle[...], gain[...])
    above = grad[...].astype(F32) + part
    middle_grads[...] = above
    low = above.astype(BF)
    if keep:
        kept[0][...] = logit_grads
        kept[1][...] = jnp.broadcast_to(total, kept[1].shape)
        branch[...] = low
        share = width // 4
        for s, part in enumerate((part0, part1, part2, part3)):
            begin = pl.multiple_of((row[0] ^ s) * share, LANES)
            part[:, part.shape[1] - share :] = branch[:, pl.ds(begin, share)]
    copies[1].wait()
    mixed_grads = dot(low, weights[...], (1, 1)).astype(BF)
    pairs = jnp.concatenate([pair0[...], pair1[...], pair2[...], pair3[...]], 0)
    kv_heads = pairs.shape[1] // (2 * HEAD_DIM)
    group = width // HEAD_DIM // kv_heads
    scale = HEAD_DIM ** (-0.5)
    parts = (part0, part1, part2, part3)
    for h in range(kv_heads):
        keys = pairs[:, h * HEAD_DIM : (h + 1) * HEAD_DIM]
        values = pairs[:, (kv_heads + h) * HEAD_DIM : (kv_heads + h + 1) * HEAD_DIM]
        queries = stacked_heads(query, h * group, group)
        top = stacked_heads(mixed_grads, h * group, group)
        weight = probs[h]
        wide = weight.astype(F32)
        weight_grads = dot(top, values, (1, 1))
        value_grads = dot(weight, top, (0, 0)).astype(BF)
        inner = wide * weight_grads
        score_grads = (inner - wide * jnp.sum(inner, -1, keepdims=True)).astype(BF)
        query_grads = dot(score_grads, keys) * scale
        key_grads = (dot(score_grads, queries, (0, 0)) * scale).astype(BF)
        for j in range(group):
            begin = (h * group + j) * HEAD_DIM
            one = query_grads[j * tokens : (j + 1) * tokens]
            query_back[:, begin : begin + HEAD_DIM] = turned(one, cosine[...], -sine[...]).astype(BF)
        for p, part in enumerate(parts):
            part[:, h * HEAD_DIM : (h + 1) * HEAD_DIM] = key_grads[p * tokens : (p + 1) * tokens]
            begin = (kv_heads + h) * HEAD_DIM
            part[:, begin : begin + HEAD_DIM] = value_grads[p * tokens : (p + 1) * tokens]


def project_back(
    keep, row, part0, part1, part2, part3, query_back, stream, gain, middle_grads, cosine, sine,
    dense, grad, low, *rest,
):
    width = stream.shape[1]
    kept, (backs, weights, sems) = rest[:-3], rest[-3:]
    cuts = cuts_of(weights.shape[1])
    copies = [
        pltpu.make_async_copy(
            dense.at[:, pl.ds(at, size)], weights.at[:, pl.ds(at, size)], sems.at[k]
        )
        for k, (at, size) in enumerate(cuts)
    ]
    for copy in copies:
        copy.start()
    pairs = weights.shape[1] - width
    total = sum(part[:, :pairs].astype(F32) for part in (part0, part1, part2, part3))
    keys = pairs // 2
    backs[:, :width] = query_back[...]
    backs[:, width : width + keys] = turned(total[:, :keys], cosine[...], -sine[...]).astype(BF)
    backs[:, width + keys :] = total[:, keys:].astype(BF)
    above = jnp.zeros(stream.shape, F32)
    for copy, (at, size) in zip(copies, cuts):
        copy.wait()
        above = above + dot(backs[:, at : at + size], weights[:, at : at + size], (1, 1))
    part, sums = norm_back(above, stream[...], gain[...])
    if keep:
        kept[0][...] = jnp.broadcast_to(sums, kept[0].shape)
        share = backs.shape[1] // 4
        for s, out in enumerate(kept[1:]):
            out[...] = backs[:, pl.ds(pl.multiple_of((row[0] ^ s) * share, LANES), share)]
    done = middle_grads[...] + part
    grad[...] = done
    low[...] = done.astype(BF)


def expert_weight_grads(half, begin, left0, left1, right0, right1, first, second):
    size = first.shape[1]
    wide = 2 * size
    for j in range(first.shape[0]):
        total = dot(left0[j, :, half * wide : (half + 1) * wide], rows_of(right0, j, begin), (0, 0))
        total = total + dot(
            left1[j, :, half * wide : (half + 1) * wide], rows_of(right1, j, begin), (0, 0)
        )
        first[j] = total[:size].astype(BF)
        second[j] = total[size:].astype(BF)


def add(one, other, total):
    total[...] = (one[...].astype(F32) + other[...].astype(F32)).astype(BF)


def pack(*refs):
    for k, value in enumerate(refs[:-1]):
        refs[-1][k] = value[...]


def stacked(refs):
    return jnp.concatenate([r[...] for r in refs], 0)


def out_grads(*refs):
    lefts, rights, out = refs[:4], refs[4:12], refs[12]
    share = out.shape[1]
    left = jnp.concatenate([one[k] for one in lefts for k in (2, 3)], 0)
    right = jnp.concatenate([r[:, r.shape[1] - share :] for r in rights], 0)
    out[...] = dot(left, right, (0, 0)).astype(BF)


def qkv_grads(*refs):
    lefts, rights, normed, logits, gains, out = (
        refs[:4], refs[4:12], refs[12:14], refs[14:16], refs[16:20], refs[20],
    )
    width, wide = out.shape
    left = jnp.concatenate([one[k] for one in lefts for k in (0, 1)], 0)
    out[:, : wide - LANES] = dot(left, stacked(rights), (0, 0)).astype(BF)
    first = gains[0][:1] + gains[1][:1]
    second = gains[2][:1] + gains[3][:1]
    line = lax.broadcasted_iota(jnp.int32, (LANES, width), 0)
    sums = jnp.where(
        line == LANES - 2, first, jnp.where(line == LANES - 1, second, jnp.zeros((1, 1), F32))
    )
    out[:, wide - LANES :] = (dot(stacked(normed), stacked(logits), (0, 0)) + sums.T).astype(BF)


def fold(row, first, second, out0, out1, out2, out3, total):
    share = first.shape[2]
    total[:, :share] = jnp.sum(first[...].astype(F32), 0)
    total[:, share:] = jnp.sum(second[...].astype(F32), 0)
    for s, out in enumerate((out0, out1, out2, out3)):
        size = out.shape[0]
        out[...] = total[pl.ds(pl.multiple_of((row[0] ^ s) * size, 8), size), :]


def finish(row, in0, in1, in2, in3, o_grad, q_grad, k_grad, v_grad, rest, total):
    share = o_grad.shape[1] // 4
    piece = total.shape[1] // 4
    ins = (in0, in1, in2, in3)
    for s, one in enumerate(ins):
        where = row[0] ^ s
        o_grad[:, pl.ds(pl.multiple_of(where * share, LANES), share)] = one[:, :share]
        total[:, pl.ds(pl.multiple_of(where * piece, LANES), piece)] = one[:, share : share + piece]
    rest[...] = sum(one[:, share + piece :] for one in ins)
    begin = 0
    for out in (q_grad, k_grad, v_grad):
        out[...] = total[:, begin : begin + out.shape[1]]
        begin += out.shape[1]


def over_columns(value):
    return lax.all_to_all(value, "col", split_axis=0, concat_axis=0, tiled=True)


def on_device(
    inputs, cotangent, segment_ids, routes, attn_gain, w_query, w_key, w_value, w_out, ffn_gain,
    w_router, w_gate, w_up, w_down,
):
    section = lax.axis_index("section")
    row = lax.axis_index("row")
    rows = lax.axis_size("row")
    columns = lax.axis_size("col")
    micro, tokens, width = inputs.shape[0], inputs.shape[2], inputs.shape[3]
    experts = w_router.shape[2]
    per_column = w_gate.shape[1]
    hidden_width = w_gate.shape[2] * rows
    kv_width = w_key.shape[2]
    qkv_width = width + 2 * kv_width
    slots = experts * ROOMS
    share = width // rows
    shard = width // (rows * columns)
    heads = width // HEAD_DIM
    kv_heads = kv_width // HEAD_DIM
    length = rows * tokens
    pieces = range(micro)
    steps = range(rows)
    here = row.astype(jnp.int32)[None]
    second = (section == 1).astype(jnp.int32)[None]
    block = (columns, slots // columns, width)

    dense = jnp.concatenate(
        [w_query[0], w_key[0], w_value[0], w_router[0], attn_gain[0][:, None], ffn_gain[0][:, None],
         jnp.zeros((shard, LANES - experts - 2), BF), w_out[0]], 1
    )
    dense = lax.all_gather(dense, ("row", "col"), axis=0, tiled=True)
    small = dense[:, qkv_width : qkv_width + LANES]
    gain_a = small[:, experts].astype(F32)[None, :]
    gain_f = small[:, experts + 1].astype(F32)[None, :]

    def shards_of(own):
        two = swapped(own, 2)
        return own, swapped(own, 1), two, swapped(two, 1)

    gate_shards, up_shards = shards_of(w_gate[0]), shards_of(w_up[0])
    down_shards = (w_down[0], swapped(w_down[0], 1), swapped(w_down[0], 2))

    lane = jnp.arange(LANES, dtype=jnp.int32)
    half = HEAD_DIM // 2
    freqs = 10000.0 ** (-2.0 * jnp.arange(half).astype(F32) / HEAD_DIM)
    positions = row * tokens + jnp.arange(tokens, dtype=jnp.int32)
    angles = positions.astype(F32)[:, None] * freqs[None, :]
    cosine = jnp.concatenate([jnp.cos(angles)] * 2, 1)
    sine = jnp.concatenate([-jnp.sin(angles), jnp.sin(angles)], 1)
    key_positions = jnp.concatenate(
        [(row ^ step) * tokens + jnp.arange(tokens, dtype=jnp.int32) for step in steps]
    )
    spread = (lane[:, None] == jnp.arange(slots, dtype=jnp.int32)[None, :] // ROOMS).astype(BF)
    below = (jnp.arange(tokens)[:, None] > jnp.arange(tokens)[None, :]).astype(BF)
    biases, chosens, places, dispatches = [], [], [], []
    for m in pieces:
        segments = segment_ids[m, 0]
        own_segments = lax.dynamic_slice_in_dim(segments, row * tokens, tokens)
        key_segments = jnp.concatenate(
            [lax.dynamic_slice_in_dim(segments, (row ^ s) * tokens, tokens) for s in steps]
        )
        counted = (key_positions[None, :] <= positions[:, None]) & (
            key_segments[None, :] == own_segments[:, None]
        )
        biases.append(jnp.where(counted, 0.0, -1e30).astype(F32))
        chosen = jnp.any(routes[0, m, 0][:, :, None] == lane[None, None, :], 1)
        chosens.append(chosen.astype(F32))
        rank = dot(below, chosen.astype(BF))
        rank = jnp.where(chosen, rank, -1.0)[:, :experts]
        place = (
            rank[:, :, None] == jnp.arange(ROOMS, dtype=F32)[None, None, :]
        ).reshape(tokens, slots)
        places.append(place.astype(BF))
        dispatches.append(place.T.astype(BF))

    token_low, token_wide = like((tokens, width), BF), like((tokens, width), F32)
    pair_like = like((tokens, 2 * kv_width), BF)
    block_like = like(block, BF)
    sums_like = like((8, width), F32)
    kept_like = like((per_column, columns * ROOMS, hidden_width), BF)
    probs_like = like((kv_heads, heads // kv_heads * tokens, length), BF)
    qkv_scratch = [pltpu.VMEM((width, qkv_width), BF), pltpu.SemaphoreType.DMA((8,))]
    out_scratch = [
        pltpu.VMEM((width, width), BF), pltpu.VMEM((width, LANES), BF),
        pltpu.SemaphoreType.DMA((2,)),
    ]
    expert_scratch = [
        pltpu.VMEM((3, per_column, hidden_width, width), BF),
        pltpu.SemaphoreType.DMA((3, per_column, 4)),
    ]
    qkv_flops = 2 * tokens * width * qkv_width
    out_flops = 2 * tokens * width * width + 2 * slots * tokens * width
    score_flops = 2 * heads * tokens * length * HEAD_DIM
    expert_flops = 2 * slots * hidden_width * width

    per = slots // columns
    double_like = like((columns, 2 * per, width), BF)

    def forward(came, entering, targets, waits):
        projected, pairs = [], []
        for m in pieces:
            projected.append(
                call(
                    project, (token_wide, token_low, token_low, pair_like),
                    (came[m], entering[m], gain_a, cosine, sine), qkv_flops, (dense,), qkv_scratch,
                    scalars=(second,), waits=(*waits[m], *(p[0] for p in projected)),
                )
            )
            pair = projected[m][3]
            pairs.append([pair] + [swapped(pair, s) for s in steps[1:]])
        attended = [
            call(
                attend,
                (token_low, token_wide, token_low, like((tokens, LANES), F32),
                 double_like if targets else block_like, probs_like),
                (projected[m][0], projected[m][2], *pairs[m], biases[m], gain_f, chosens[m],
                 dispatches[m], *targets[m : m + 1]),
                out_flops + 2 * score_flops, (dense,), out_scratch,
            )
            for m in pieces
        ]
        arrived = [over_columns(a[4]) for a in attended]
        lefts, rows_there, down_there = [], (), down_shards
        if targets:
            left = call(
                pack, (like((2 * micro, tokens, width), BF),),
                [p[1] for p in projected] + [a[0] for a in attended], 0,
            )[0]
            two = swapped(left, 2)
            lefts = [left, swapped(left, 1), two, swapped(two, 1)]
            rows_there = (two,)
        else:
            two = hold(down_shards[2], attended[1][4])
            down_there = (*down_shards[:2], two, swapped(two, 1))
        applied = [
            call(
                functools.partial(expert_forward, bool(targets)),
                (double_like,) + (kept_like,) * 5 if targets else (block_like,), (arrived[m],),
                (6 if targets else 3) * expert_flops, (*gate_shards, *up_shards, *down_there),
                expert_scratch, waits=rows_there if m else (attended[1][4],),
            )
            for m in pieces
        ]
        returned = [over_columns(a[0]) for a in applied]
        results = [
            call(
                combine, (token_wide, token_low),
                (returned[m], attended[m][1], attended[m][3], spread, places[m]),
                2 * slots * tokens * width, waits=() if m else (applied[1][0],),
            )
            for m in pieces
        ]
        return projected, pairs, attended, arrived, applied, returned, results, lefts, down_there

    def far_and_near(lefts, rights, begins, side):
        return [
            call(
                functools.partial(expert_weight_grads, side, begin),
                (like((per_column, hidden_width // 4, width), BF),) * 2, (*left, *right),
                expert_flops,
            )
            for left, right, begin in zip(lefts, rights, begins)
        ]

    def merged(half, waits):
        return call(add, (like(half[0].shape, BF),), (half[0], swapped(half[1], 1)), 0, waits=waits)[0]

    def attention_back(keep, m, grad, token_grads, waits):
        return call(
            functools.partial(attend_back, keep),
            (token_wide, token_low)
            + (like((tokens, 2 * kv_width + (share if keep else 0)), BF),) * rows
            + ((like((tokens, LANES), BF), sums_like) if keep else ()),
            (token_grads, returned[m], attended[m][3], spread, places[m], attended[m][1], gain_f,
             grad, projected[m][2], *pairs[m], attended[m][5], cosine, sine),
            out_flops + 4 * score_flops, (dense,), [pltpu.VMEM((tokens, width), BF)] + out_scratch,
            scalars=(here,), waits=waits,
        )

    def parts_of(inner):
        return [inner[2]] + [swapped(inner[2 + s], s) for s in steps[1:]]

    def projection_back(keep, m, inner, parts, waits):
        return call(
            functools.partial(project_back, keep),
            (token_wide, token_low)
            + ((sums_like,) + (like((tokens, qkv_width // rows), BF),) * rows if keep else ()),
            (*parts, inner[1], projected[m][0], gain_a, inner[0], cosine, sine),
            qkv_flops, (dense,), [pltpu.VMEM((tokens, qkv_width), BF)] + qkv_scratch,
            scalars=(here,), waits=waits,
        )

    def by_columns(value):
        cut = value.reshape(rows, columns, shard, value.shape[1]).transpose(1, 0, 2, 3)
        return over_columns(cut.reshape(columns, rows * shard, value.shape[1]))

    entering = [inputs[m, 0] for m in pieces]
    targets = [cotangent[m, 0] for m in pieces]
    here_by_now = (gate_shards[2], up_shards[2])
    results, unused, down_shards = forward(entering, entering, (), (here_by_now, ()))[6:]
    came = [lax.ppermute(r[1], "section", [(0, 1)]) for r in results]

    kept = forward(came, entering, targets, ((), ()))
    projected, pairs, attended, arrived, applied, returned, results, lefts, unused = kept
    hidden = [a[1] for a in applied]
    done = [r[0] for r in results]

    inner, outer = [], []
    for m in pieces:
        waits = (*done, *lefts[1:], outer[0][0]) if m else (applied[1][0],)
        inner.append(attention_back(False, m, targets[m], returned[m], waits))
        outer.append(projection_back(False, m, inner[m], parts_of(inner[m]), ()))
    came = [lax.ppermute(o[1], "section", [(1, 0)]) for o in outer]

    sent = [
        call(
            send_grads, (token_low, block_like),
            (came[m], targets[m], attended[m][3], dispatches[m]),
            2 * slots * tokens * width, scalars=(1 - second,),
        )
        for m in pieces
    ]
    arrived_grads = [over_columns(s[1]) for s in sent]
    moved = [
        call(
            expert_backward, (block_like, kept_like, kept_like),
            (arrived_grads[m], applied[m][2], applied[m][3]), 3 * expert_flops,
            (*down_shards, *gate_shards, *up_shards), expert_scratch,
            waits=() if m else (sent[1][1],),
        )
        for m in pieces
    ]
    back = [over_columns(a[0]) for a in moved]
    operands = (
        (hidden, [a[1] for a in moved], [a[2] for a in moved]), (arrived_grads, arrived, arrived),
        (0, 0, 0),
    )
    far, near = far_and_near(*operands, 1), far_and_near(*operands, 0)
    crossed = [swapped(merged(far[0], ()), 2)]

    inner = [attention_back(
        True, 0, sent[0][0], back[0], (moved[1][0], *(p[0] for p in far), near[0][0]),
    )]
    parts = [parts_of(inner[0])]
    outer = [projection_back(True, 0, inner[0], parts[0], ())]
    inner.append(attention_back(True, 1, sent[1][0], back[1], (inner[0][0], crossed[0])))
    parts.append(parts_of(inner[1]))
    crossed.append(swapped(merged(far[1], parts[1][1:]), 2))
    o_grads = call(
        out_grads, (like((width, share), BF),),
        (*lefts, *[p[s] for s in steps for p in parts]), 2 * width * length * micro * share,
        waits=(outer[0][0],),
    )[0]
    outer.append(projection_back(True, 1, inner[1], parts[1], (o_grads,)))
    backs = [[o[3]] + [swapped(o[3 + s], s) for s in steps[1:]] for o in outer]
    w_grads = call(
        qkv_grads, (like((width, qkv_width // rows + LANES), BF),),
        (*lefts, *[b[s] for s in steps for b in backs], *[a[2] for a in attended],
         *[a[6] for a in inner], *[o[2] for o in outer], *[a[7] for a in inner]),
        2 * width * length * micro * qkv_width // rows, waits=(near[1][0], crossed[1]),
    )[0]
    crossed.append(swapped(merged(far[2], backs[1][1:]), 2))
    expert_grads = [
        n[0].astype(F32) + swapped(n[1], 1).astype(F32) + c.astype(F32)
        for n, c in zip(near, crossed)
    ]

    pieces_out = call(
        fold, (like((shard, share + qkv_width // rows + LANES), F32),) * rows,
        (by_columns(o_grads), by_columns(w_grads)), 0,
        scratch=[pltpu.VMEM((rows * shard, share + qkv_width // rows + LANES), F32)],
        scalars=(here,),
    )
    pieces_out = [pieces_out[0]] + [swapped(pieces_out[s], s) for s in steps[1:]]
    o_grad, q_grad, k_grad, v_grad, rest = call(
        finish,
        (like((shard, width), F32), like((shard, width), F32), like((shard, kv_width), F32),
         like((shard, kv_width), F32), like((shard, LANES), F32)),
        pieces_out, 0, scratch=[pltpu.VMEM((shard, qkv_width), F32)], scalars=(here,),
    )

    return (
        jnp.stack(done)[None, :, None],
        jnp.stack([o[0] for o in outer])[None, :, None],
        rest[:, LANES - 2][None],
        q_grad[None],
        k_grad[None],
        v_grad[None],
        o_grad[None],
        rest[:, LANES - 1][None],
        rest[:, :experts][None],
        expert_grads[1][None],
        expert_grads[2][None],
        expert_grads[0][None],
    )


def solution(mesh):
    dense = P("section", ("row", "col"), None)
    gain = P("section", ("row", "col"))
    expert = P("section", "col", "row", None)
    token = P(None, "col", "row", None)
    layered = P("section", None, "col", "row", None)
    return jax.shard_map(
        on_device,
        mesh=mesh,
        in_specs=(
            token, token, P(None, "col", None), layered, gain, dense, dense, dense, dense, gain,
            dense, expert, expert, expert,
        ),
        out_specs=(
            layered, layered, gain, dense, dense, dense, dense, gain, dense, expert, expert, expert,
        ),
        check_vma=False,
    )
```

```python
import functools

import jax
import jax.numpy as jnp
from jax import lax
from jax.experimental import pallas as pl
from jax.experimental.pallas import tpu as pltpu
from jax.sharding import PartitionSpec as P

HEAD_DIM = 128
ROOMS = 16
EPSILON = 1e-06
LANES = 128
BF = jnp.bfloat16
F32 = jnp.float32
MIB = 1 << 20


def dot(left, right, contract=(1, 0)):
    return lax.dot_general(
        left, right, (((contract[0],), (contract[1],)), ((), ())), preferred_element_type=F32
    )


def like(shape, dtype):
    return jax.ShapeDtypeStruct(shape, dtype)


class Late:
    def __init__(self, source, target=None, sem=None):
        self.source, self.target, self.copy = source, target, None
        if target is not None:
            self.copy = pltpu.make_async_copy(source, target, sem)
            self.copy.start()
            self.waiting = True

    def ready(self):
        if self.waiting:
            self.copy.wait()
            self.waiting = False
        return self.target

    def __getitem__(self, index):
        return self.ready()[index]

    @property
    def shape(self):
        return self.source.shape


class Sent:
    def __init__(self, source, target=None, sem=None):
        self.source, self.target, self.sem, self.copy = source, target, sem, None

    def __getitem__(self, index):
        return self.source[index]

    def __setitem__(self, index, value):
        self.source[index] = value

    def send(self):
        self.copy = pltpu.make_async_copy(self.source, self.target, self.sem)
        self.copy.start()

    @property
    def shape(self):
        return self.source.shape


def sent(out):
    if isinstance(out, Sent):
        out.send()


def call(body, outs, args, flops, far=(), scratch=(), scalars=(), waits=()):
    arrays = [a.source if isinstance(a, Late) else a for a in args]
    shapes = [o.source if isinstance(o, Sent) else o for o in outs]
    moved = sum(a.size * a.dtype.itemsize for a in (*arrays, *far, *shapes))
    count = len(scalars) + len(args) + len(far)
    kinds = [isinstance(a, Late) for a in args]
    out_kinds = [isinstance(o, Sent) for o in outs]
    buffers = [pltpu.VMEM(a.shape, a.dtype) for a, k in zip(arrays, kinds) if k]
    buffers += [pltpu.VMEM(o.shape, o.dtype) for o, k in zip(shapes, out_kinds) if k]

    def run(*refs):
        given, refs = list(refs[:count]), refs[count + len(waits) :]
        results, refs = list(refs[: len(outs)]), refs[len(outs) :]
        own, rest = list(refs[: len(buffers)]), refs[len(buffers) :]
        sems, rest = (rest[0], rest[1:]) if buffers else (None, rest)
        used = 0
        for k, late in enumerate(kinds):
            if late:
                at = len(scalars) + k
                given[at] = Late(given[at], own[used], sems.at[used])
                used += 1
        for k, kind in enumerate(out_kinds):
            if kind:
                results[k] = Sent(own[used], results[k], sems.at[used])
                used += 1
        body(*given, *results, *rest)
        for one in given:
            if isinstance(one, Late):
                one.ready()
        for one in results:
            if isinstance(one, Sent) and one.copy is None:
                one.send()
        for one in results:
            if isinstance(one, Sent):
                one.copy.wait()

    anywhere, local = pl.BlockSpec(memory_space=pl.ANY), pl.BlockSpec(memory_space=pltpu.VMEM)
    return pl.pallas_call(
        run,
        out_shape=tuple(shapes),
        in_specs=[pl.BlockSpec(memory_space=pltpu.SMEM)] * len(scalars)
        + [anywhere if k else local for k in kinds]
        + [anywhere] * (len(far) + len(waits)),
        out_specs=tuple(anywhere if k else local for k in out_kinds),
        scratch_shapes=buffers
        + ([pltpu.SemaphoreType.DMA((len(buffers),))] if buffers else [])
        + list(scratch),
        compiler_params=pltpu.CompilerParams(vmem_limit_bytes=60 * MIB),
        cost_estimate=pl.CostEstimate(
            flops=int(flops), bytes_accessed=int(moved), transcendentals=0
        ),
        name=body.func.__name__ if isinstance(body, functools.partial) else body.__name__,
    )(*scalars, *arrays, *far, *waits)


def late(values):
    return [Late(v) for v in values]


def nothing(*refs):
    pass


def hold(value, *waits):
    return pl.pallas_call(
        nothing,
        out_shape=like(value.shape, value.dtype),
        in_specs=[pl.BlockSpec(memory_space=pl.ANY)] * (1 + len(waits)),
        out_specs=pl.BlockSpec(memory_space=pl.ANY),
        input_output_aliases={0: 0},
        name="hold",
    )(value, *waits)


def swapped(value, step):
    rows = lax.axis_size("row")
    return lax.ppermute(value, "row", [(r, r ^ step) for r in range(rows)])


def norm_parts(stream):
    return lax.rsqrt(jnp.mean(stream * stream, -1, keepdims=True) + EPSILON)


def norm_back(grad, stream, gain):
    inverse = norm_parts(stream)
    unit = stream * inverse
    scaled = grad * gain
    back = inverse * (scaled - unit * jnp.mean(scaled * unit, -1, keepdims=True))
    return back, jnp.sum(grad * unit, 0, keepdims=True)


def turned(vectors, cosine, sine):
    done = []
    for at in range(0, vectors.shape[1], HEAD_DIM):
        one = vectors[:, at : at + HEAD_DIM]
        done.append(one * cosine + pltpu.roll(one, HEAD_DIM // 2, 1) * sine)
    return jnp.concatenate(done, -1) if len(done) > 1 else done[0]


def stacked_heads(value, first, count):
    return jnp.concatenate(
        [value[:, (first + j) * HEAD_DIM : (first + j + 1) * HEAD_DIM] for j in range(count)], 0
    )


def unstacked_heads(value, count):
    tokens = value.shape[0] // count
    return jnp.concatenate([value[j * tokens : (j + 1) * tokens] for j in range(count)], 1)


def cuts_of(total, most=512):
    return [(at, min(most, total - at)) for at in range(0, total, most)]


def project(
    keep, flag, came, entering, gain, cosine, sine, dense, stream, query, pair, *rest
):
    kept, (weights, sems) = rest[:-2], rest[-2:]
    width = stream.shape[1]
    cuts = cuts_of(weights.shape[1])
    copies = [
        pltpu.make_async_copy(
            dense.at[:, pl.ds(at, size)], weights.at[:, pl.ds(at, size)], sems.at[k]
        )
        for k, (at, size) in enumerate(cuts)
    ]
    for copy in copies:
        copy.start()
    x = jnp.where(flag[0] > 0, came[...].astype(F32), entering[...].astype(F32))
    stream[...] = x
    low = (x * norm_parts(x) * gain[...]).astype(BF)
    if keep:
        kept[0][...] = low
        kept[1][...] = x
        sent(kept[0])
        sent(kept[1])
    keys = pair.shape[1] // 2
    for copy, (at, size) in zip(copies, cuts):
        copy.wait()
        part = dot(low, weights[:, at : at + size])
        for begin in range(at, at + size, HEAD_DIM):
            head = part[:, begin - at : begin - at + HEAD_DIM]
            if begin < width + keys:
                head = turned(head, cosine[...], sine[...])
            head = head.astype(BF)
            if begin < width:
                query[:, begin : begin + HEAD_DIM] = head
            else:
                pair[:, begin - width : begin - width + HEAD_DIM] = head
    if keep:
        kept[2][...] = query[...]
        kept[3][...] = pair[...]


def slot_experts(slots):
    own = lax.broadcasted_iota(jnp.int32, (slots, LANES), 0) // ROOMS
    return own == lax.broadcasted_iota(jnp.int32, (slots, LANES), 1)


def scaled_rows(dispatch, gates, low):
    here = slot_experts(dispatch.shape[0])
    scale = jnp.sum(jnp.where(here, dot(dispatch, gates.astype(BF)), 0.0), -1, keepdims=True)
    return (dot(dispatch, low) * scale).astype(BF)


def attend(
    keep, stream, query, pair0, pair1, pair2, pair3, bias, gain, chosen, dispatch, *rest,
):
    targets, rest = (rest[:1], rest[1:]) if keep else ((), rest)
    dense, middle, gates, outgoing = rest[:4]
    kept, (mixed, weights, router, sems) = rest[4:-4], rest[-4:]
    width = stream.shape[1]
    block = (outgoing.shape[0], -1, width)
    per = dispatch.shape[0] // outgoing.shape[0]
    at = dense.shape[1] - width - LANES
    copies = [
        pltpu.make_async_copy(dense.at[:, pl.ds(at + LANES, width)], weights, sems.at[0]),
        pltpu.make_async_copy(dense.at[:, pl.ds(at, LANES)], router, sems.at[1]),
    ]
    for copy in copies:
        copy.start()
    pairs = jnp.concatenate([pair0[...], pair1[...], pair2[...], pair3[...]], 0)
    kv_heads = pairs.shape[1] // (2 * HEAD_DIM)
    group = width // HEAD_DIM // kv_heads
    biases = jnp.concatenate([bias[...]] * group, 0)
    tokens = stream.shape[0]
    for h in range(kv_heads):
        keys = pairs[:, h * HEAD_DIM : (h + 1) * HEAD_DIM]
        values = pairs[:, (kv_heads + h) * HEAD_DIM : (kv_heads + h + 1) * HEAD_DIM]
        queries = stacked_heads(query, h * group, group)
        scores = dot(queries, keys, (1, 1)) * HEAD_DIM ** (-0.5) + biases
        expo = jnp.exp(scores - jnp.max(scores, -1, keepdims=True))
        weight = (expo * (1.0 / jnp.sum(expo, -1, keepdims=True))).astype(BF)
        if keep:
            kept[0][h] = weight
        done = dot(weight, values).astype(BF)
        for j in range(group):
            begin = (h * group + j) * HEAD_DIM
            mixed[:, begin : begin + HEAD_DIM] = done[j * tokens : (j + 1) * tokens]
    if keep:
        kept[1][...] = mixed[...]
        sent(kept[0])
        sent(kept[1])
    copies[0].wait()
    x = stream[...] + dot(mixed[...], weights[...])
    middle[...] = x
    sent(middle)
    low = (x * norm_parts(x) * gain[...]).astype(BF)
    if keep:
        kept[2][...] = low
        sent(kept[2])
    copies[1].wait()
    taken = chosen[...] > 0
    logits = jnp.where(taken, dot(low, router[...]), -1e30)
    expo = jnp.where(taken, jnp.exp(logits - jnp.max(logits, -1, keepdims=True)), 0.0)
    share = expo / jnp.sum(expo, -1, keepdims=True)
    gates[...] = share
    sent(gates)
    slots = dispatch[...]
    outgoing[:, :per, :] = dot(slots, low).astype(BF).reshape(block)
    if targets:
        outgoing[:, per:, :] = scaled_rows(slots, share, targets[0][...]).reshape(block)


def fetch(shards, weights, sems):
    copies = []
    for j in range(weights.shape[1]):
        line = []
        for k in range(weights.shape[0]):
            some = []
            for p in range(4):
                size = shards[k][p].shape[1]
                some.append(
                    pltpu.make_async_copy(
                        shards[k][p].at[j],
                        weights.at[k, j, pl.ds(p * size, size)],
                        sems.at[k, j, p],
                    )
                )
            line.append(some)
        copies.append(line)
    for line in copies:
        for some in line:
            for copy in some:
                copy.start()
    return copies


def done_with(copies):
    for copy in copies:
        copy.wait()


def rows_of(value, j, begin=0):
    columns, unused, width = value.shape
    at = begin + j * ROOMS
    return value[:, at : at + ROOMS, :].reshape(columns * ROOMS, width)


def put_rows(out, j, rows, inner):
    at, width = j * ROOMS, rows.shape[1]
    out[:, at : at + ROOMS, :width] = rows.reshape(-1, ROOMS, width)
    high = inner.astype(BF).astype(F32)
    lane = lax.broadcasted_iota(jnp.int32, (rows.shape[0], LANES), 1)
    both = jnp.where(lane == 0, high, jnp.where(lane == 1, inner - high, 0.0))
    out[:, at : at + ROOMS, width:] = both.astype(BF).reshape(-1, ROOMS, LANES)


def expert_forward(both, arrived, *refs):
    shards = [refs[4 * k : 4 * k + 4] for k in range(3)]
    outs, weights, sems = refs[12:-2], refs[-2], refs[-1]
    copies = fetch(shards, weights, sems)
    per = weights.shape[1] * ROOMS
    for j in range(weights.shape[1]):
        at = j * ROOMS
        rows = rows_of(arrived, j)
        done_with(copies[j][0])
        gate = dot(rows, weights[0, j], (1, 1))
        done_with(copies[j][1])
        lifted = dot(rows, weights[1, j], (1, 1))
        square = gate * gate
        bend = jnp.tanh(0.7978845608028654 * gate * (1.0 + 0.044715 * square))
        active = 0.5 * gate * (1.0 + bend)
        hidden = (active * lifted).astype(BF)
        done_with(copies[j][2])
        made = dot(hidden, weights[2, j]).astype(BF)
        outs[0][:, at : at + ROOMS, :] = made.reshape(-1, ROOMS, made.shape[1])
        if both:
            slope = 0.5 * (1.0 + bend) + 0.5 * gate * (1.0 - bend * bend) * (
                0.7978845608028654 * (1.0 + 3 * 0.044715 * square)
            )
            bent = slope * lifted
            outs[1][j] = hidden
            outs[2][j] = active.astype(BF)
            outs[3][j] = bent.astype(BF)
            hidden_grads = dot(rows_of(arrived, j, per), weights[2, j], (1, 1))
            gate_part = (hidden_grads * bent).astype(BF)
            lifted_part = (hidden_grads * active).astype(BF)
            inner = jnp.sum(hidden_grads * hidden.astype(F32), -1, keepdims=True)
            back = dot(gate_part, weights[0, j]) + dot(lifted_part, weights[1, j])
            put_rows(outs[4], j, back.astype(BF), inner)
    if both:
        for out in outs[:4]:
            sent(out)


def combine(returned, middle, gates, spread, places, result, low):
    weights = (dot(gates[...].astype(BF), spread[...]) * places[...].astype(F32)).astype(BF)
    done = middle[...] + dot(weights, returned[...].reshape(-1, returned.shape[2]))
    result[...] = done
    sent(result)
    low[...] = done.astype(BF)


def last_outputs(flag, spread, *refs):
    out = refs[-1]
    width = out.shape[2]
    for m in range(out.shape[0]):
        returned, middle, gates, places, before = refs[5 * m : 5 * m + 5]
        weights = (dot(gates[...].astype(BF), spread[...]) * places[...].astype(F32)).astype(BF)
        rows = returned[:, :, :width].reshape(-1, width)
        out[m] = jnp.where(flag[0] > 0, middle[...] + dot(weights, rows), before[...])


def send_grads(flag, came, target, gates, dispatch, grad, outgoing):
    low = jnp.where(flag[0] > 0, came[...], target[...])
    grad[...] = low
    sent(grad)
    outgoing[...] = scaled_rows(dispatch[...], gates[...], low).reshape(outgoing.shape)


def expert_backward(flag, arrived, hidden, active, bent, produced, *refs):
    shards = [refs[4 * k : 4 * k + 4] for k in range(3)]
    out, gate_back, lifted_back, weights, sems = refs[12:]
    copies = fetch(shards, weights, sems)
    for j in range(weights.shape[1]):
        done_with(copies[j][0])
        hidden_grads = dot(rows_of(arrived, j), weights[0, j], (1, 1))
        gate_part = (hidden_grads * bent[j].astype(F32)).astype(BF)
        lifted_part = (hidden_grads * active[j].astype(F32)).astype(BF)
        gate_back[j] = gate_part
        lifted_back[j] = lifted_part
        inner = jnp.sum(hidden_grads * hidden[j].astype(F32), -1, keepdims=True)
        done_with(copies[j][1])
        done = dot(gate_part, weights[1, j])
        done_with(copies[j][2])
        done = (done + dot(lifted_part, weights[2, j])).astype(BF)
        put_rows(out, j, jnp.where(flag[0] > 0, rows_of(produced, j), done), inner)
    sent(gate_back)
    sent(lifted_back)


def attend_back(
    keep, row, flag, token_grads, before, gates, places, middle, gain, grad, query, pair0, pair1,
    pair2, pair3, probs, cosine, sine, dense, middle_grads, query_back, part0, part1, part2, part3,
    *rest,
):
    tokens, width = middle.shape
    kept, (branch, weights, router, sems) = rest[:-4], rest[-4:]
    at = dense.shape[1] - width - LANES
    copies = [
        pltpu.make_async_copy(dense.at[:, pl.ds(at, LANES)], router, sems.at[1]),
        pltpu.make_async_copy(dense.at[:, pl.ds(at + LANES, width)], weights, sems.at[0]),
    ]
    for copy in copies:
        copy.start()
    came = token_grads[...]
    if keep:
        came = jnp.where(flag[0] > 0, before[...], came)
    came = came.reshape(-1, came.shape[2])
    place = places[...]
    here = slot_experts(came.shape[0])
    notes = came[:, width:].astype(F32)
    high = jnp.where(here, notes[:, :1], 0.0).astype(BF)
    rest_of = jnp.where(here, notes[:, 1:2], 0.0).astype(BF)
    inner = dot(place, high) + dot(place, rest_of)
    logit_grads = (inner - gates[...] * jnp.sum(inner, -1, keepdims=True)).astype(BF)
    ffn_grads = dot(place, came[:, :width])
    copies[0].wait()
    ffn_grads = ffn_grads + dot(logit_grads, router[...], (1, 1))
    part, total = norm_back(ffn_grads, middle[...], gain[...])
    above = grad[...].astype(F32) + part
    middle_grads[...] = above
    low = above.astype(BF)
    if keep:
        kept[0][...] = logit_grads
        kept[1][...] = jnp.broadcast_to(total, kept[1].shape)
        sent(kept[0])
        sent(kept[1])
        branch[...] = low
        share = width // 4
        for s, part in enumerate((part0, part1, part2, part3)):
            begin = pl.multiple_of((row[0] ^ s) * share, LANES)
            part[:, part.shape[1] - share :] = branch[:, pl.ds(begin, share)]
    copies[1].wait()
    mixed_grads = dot(low, weights[...], (1, 1)).astype(BF)
    pairs = jnp.concatenate([pair0[...], pair1[...], pair2[...], pair3[...]], 0)
    kv_heads = pairs.shape[1] // (2 * HEAD_DIM)
    group = width // HEAD_DIM // kv_heads
    scale = HEAD_DIM ** (-0.5)
    parts = (part0, part1, part2, part3)
    for h in range(kv_heads):
        keys = pairs[:, h * HEAD_DIM : (h + 1) * HEAD_DIM]
        values = pairs[:, (kv_heads + h) * HEAD_DIM : (kv_heads + h + 1) * HEAD_DIM]
        queries = stacked_heads(query, h * group, group)
        top = stacked_heads(mixed_grads, h * group, group)
        weight = probs[h]
        wide = weight.astype(F32)
        weight_grads = dot(top, values, (1, 1))
        value_grads = dot(weight, top, (0, 0)).astype(BF)
        inner = wide * weight_grads
        score_grads = (inner - wide * jnp.sum(inner, -1, keepdims=True)).astype(BF)
        query_grads = dot(score_grads, keys) * scale
        key_grads = (dot(score_grads, queries, (0, 0)) * scale).astype(BF)
        for j in range(group):
            begin = (h * group + j) * HEAD_DIM
            one = query_grads[j * tokens : (j + 1) * tokens]
            query_back[:, begin : begin + HEAD_DIM] = turned(one, cosine[...], -sine[...]).astype(BF)
        for p, part in enumerate(parts):
            part[:, h * HEAD_DIM : (h + 1) * HEAD_DIM] = key_grads[p * tokens : (p + 1) * tokens]
            begin = (kv_heads + h) * HEAD_DIM
            part[:, begin : begin + HEAD_DIM] = value_grads[p * tokens : (p + 1) * tokens]


def project_back(
    keep, row, part0, part1, part2, part3, query_back, stream, gain, middle_grads, cosine, sine,
    dense, low, *rest,
):
    width = stream.shape[1]
    kept, (backs, weights, sems) = rest[:-3], rest[-3:]
    cuts = cuts_of(weights.shape[1])
    copies = [
        pltpu.make_async_copy(
            dense.at[:, pl.ds(at, size)], weights.at[:, pl.ds(at, size)], sems.at[k]
        )
        for k, (at, size) in enumerate(cuts)
    ]
    for copy in copies:
        copy.start()
    pairs = weights.shape[1] - width
    total = sum(part[:, :pairs].astype(F32) for part in (part0, part1, part2, part3))
    keys = pairs // 2
    backs[:, :width] = query_back[...]
    backs[:, width : width + keys] = turned(total[:, :keys], cosine[...], -sine[...]).astype(BF)
    backs[:, width + keys :] = total[:, keys:].astype(BF)
    if keep:
        share = backs.shape[1] // 4
        for s, out in enumerate(kept[2:]):
            out[...] = backs[:, pl.ds(pl.multiple_of((row[0] ^ s) * share, LANES), share)]
    above = jnp.zeros(stream.shape, F32)
    for copy, (at, size) in zip(copies, cuts):
        copy.wait()
        above = above + dot(backs[:, at : at + size], weights[:, at : at + size], (1, 1))
    part, sums = norm_back(above, stream[...], gain[...])
    done = middle_grads[...] + part
    if keep:
        kept[0][...] = done
        kept[1][...] = jnp.broadcast_to(sums, kept[1].shape)
    low[...] = done.astype(BF)


def expert_weight_grads(half, begin, left0, left1, right0, right1, first, second):
    size = first.shape[1]
    wide = 2 * size
    for j in range(first.shape[0]):
        total = dot(left0[j, :, half * wide : (half + 1) * wide], rows_of(right0, j, begin), (0, 0))
        total = total + dot(
            left1[j, :, half * wide : (half + 1) * wide], rows_of(right1, j, begin), (0, 0)
        )
        first[j] = total[:size].astype(BF)
        second[j] = total[size:].astype(BF)


def add(one, other, total):
    total[...] = (one[...].astype(F32) + other[...].astype(F32)).astype(BF)


def pack(*refs):
    for k, value in enumerate(refs[:-1]):
        refs[-1][k] = value[...]


def stacked(refs):
    return jnp.concatenate([r[...] for r in refs], 0)


def by_owner(out, grads, begin):
    columns, lines, unused = out.shape
    size = lines // 4
    for c in range(columns):
        some = [grads[(r * columns + c) * size : (r * columns + c + 1) * size] for r in range(4)]
        out[c, :, begin : begin + grads.shape[1]] = jnp.concatenate(some, 0).astype(BF)


def out_grads(*refs):
    lefts, rights, out = refs[:4], refs[4:12], refs[12]
    share = out.shape[2]
    left = jnp.concatenate([one[k] for one in lefts for k in (2, 3)], 0)
    right = jnp.concatenate([r[:, r.shape[1] - share :] for r in rights], 0)
    by_owner(out, dot(left, right, (0, 0)), 0)


def qkv_grads(*refs):
    lefts, rights, normed, logits, gains, out = (
        refs[:4], refs[4:12], refs[12:14], refs[14:16], refs[16:20], refs[20],
    )
    wide = out.shape[2]
    left = jnp.concatenate([one[k] for one in lefts for k in (0, 1)], 0)
    by_owner(out, dot(left, stacked(rights), (0, 0)), 0)
    width = left.shape[1]
    first = gains[0][:1, :] + gains[1][:1, :]
    second = gains[2][:1, :] + gains[3][:1, :]
    line = lax.broadcasted_iota(jnp.int32, (LANES, width), 0)
    sums = jnp.where(
        line == LANES - 2, first, jnp.where(line == LANES - 1, second, jnp.zeros((1, 1), F32))
    )
    by_owner(out, dot(stacked(normed), stacked(logits), (0, 0)) + sums.T, wide - LANES)


def fold(row, first, second, out0, out1, out2, out3, total):
    share = first.shape[2]
    total[:, :share] = jnp.sum(first[...].astype(F32), 0)
    total[:, share:] = jnp.sum(second[...].astype(F32), 0)
    for s, out in enumerate((out0, out1, out2, out3)):
        size = out.shape[0]
        out[...] = total[pl.ds(pl.multiple_of((row[0] ^ s) * size, 8), size), :]


def finish(row, in0, in1, in2, in3, o_grad, q_grad, k_grad, v_grad, rest, total):
    share = o_grad.shape[1] // 4
    piece = total.shape[1] // 4
    ins = (in0, in1, in2, in3)
    for s, one in enumerate(ins):
        where = row[0] ^ s
        o_grad[:, pl.ds(pl.multiple_of(where * share, LANES), share)] = one[:, :share]
        total[:, pl.ds(pl.multiple_of(where * piece, LANES), piece)] = one[:, share : share + piece]
    rest[...] = sum(one[:, share + piece :] for one in ins)
    begin = 0
    for out in (q_grad, k_grad, v_grad):
        out[...] = total[:, begin : begin + out.shape[1]]
        begin += out.shape[1]


def over_columns(value):
    return lax.all_to_all(value, "col", split_axis=0, concat_axis=0, tiled=True)


def on_device(
    inputs, cotangent, segment_ids, routes, attn_gain, w_query, w_key, w_value, w_out, ffn_gain,
    w_router, w_gate, w_up, w_down,
):
    section = lax.axis_index("section")
    row = lax.axis_index("row")
    rows = lax.axis_size("row")
    columns = lax.axis_size("col")
    micro, tokens, width = inputs.shape[0], inputs.shape[2], inputs.shape[3]
    experts = w_router.shape[2]
    per_column = w_gate.shape[1]
    hidden_width = w_gate.shape[2] * rows
    kv_width = w_key.shape[2]
    qkv_width = width + 2 * kv_width
    slots = experts * ROOMS
    share = width // rows
    shard = width // (rows * columns)
    heads = width // HEAD_DIM
    kv_heads = kv_width // HEAD_DIM
    length = rows * tokens
    pieces = range(micro)
    steps = range(rows)
    here = row.astype(jnp.int32)[None]
    second = (section == 1).astype(jnp.int32)[None]
    block = (columns, slots // columns, width)

    dense = jnp.concatenate(
        [w_query[0], w_key[0], w_value[0], w_router[0], attn_gain[0][:, None], ffn_gain[0][:, None],
         jnp.zeros((shard, LANES - experts - 2), BF), w_out[0]], 1
    )
    dense = lax.all_gather(dense, ("row", "col"), axis=0, tiled=True)
    small = dense[:, qkv_width : qkv_width + LANES]
    gain_a = small[:, experts].astype(F32)[None, :]
    gain_f = small[:, experts + 1].astype(F32)[None, :]

    def shards_of(own):
        two = swapped(own, 2)
        return own, swapped(own, 1), two, swapped(two, 1)

    gate_shards, up_shards = shards_of(w_gate[0]), shards_of(w_up[0])
    down_shards = (w_down[0], swapped(w_down[0], 1), swapped(w_down[0], 2))

    lane = jnp.arange(LANES, dtype=jnp.int32)
    half = HEAD_DIM // 2
    freqs = 10000.0 ** (-2.0 * jnp.arange(half).astype(F32) / HEAD_DIM)
    positions = row * tokens + jnp.arange(tokens, dtype=jnp.int32)
    angles = positions.astype(F32)[:, None] * freqs[None, :]
    cosine = jnp.concatenate([jnp.cos(angles)] * 2, 1)
    sine = jnp.concatenate([-jnp.sin(angles), jnp.sin(angles)], 1)
    key_positions = jnp.concatenate(
        [(row ^ step) * tokens + jnp.arange(tokens, dtype=jnp.int32) for step in steps]
    )
    spread = (lane[:, None] == jnp.arange(slots, dtype=jnp.int32)[None, :] // ROOMS).astype(BF)
    below = (jnp.arange(tokens)[:, None] > jnp.arange(tokens)[None, :]).astype(BF)
    biases, chosens, places, dispatches = [], [], [], []
    for m in pieces:
        segments = segment_ids[m, 0]
        own_segments = lax.dynamic_slice_in_dim(segments, row * tokens, tokens)
        key_segments = jnp.concatenate(
            [lax.dynamic_slice_in_dim(segments, (row ^ s) * tokens, tokens) for s in steps]
        )
        counted = (key_positions[None, :] <= positions[:, None]) & (
            key_segments[None, :] == own_segments[:, None]
        )
        biases.append(jnp.where(counted, 0.0, -1e30).astype(F32))
        chosen = jnp.any(routes[0, m, 0][:, :, None] == lane[None, None, :], 1)
        chosens.append(chosen.astype(F32))
        rank = dot(below, chosen.astype(BF))
        rank = jnp.where(chosen, rank, -1.0)[:, :experts]
        place = (
            rank[:, :, None] == jnp.arange(ROOMS, dtype=F32)[None, None, :]
        ).reshape(tokens, slots)
        places.append(place.astype(BF))
        dispatches.append(place.T.astype(BF))

    token_low, token_wide = like((tokens, width), BF), like((tokens, width), F32)
    pair_like = like((tokens, 2 * kv_width), BF)
    block_like = like(block, BF)
    sums_like = like((8, width), F32)
    kept_like = like((per_column, columns * ROOMS, hidden_width), BF)
    probs_like = like((kv_heads, heads // kv_heads * tokens, length), BF)
    qkv_scratch = [pltpu.VMEM((width, qkv_width), BF), pltpu.SemaphoreType.DMA((8,))]
    out_scratch = [
        pltpu.VMEM((width, width), BF), pltpu.VMEM((width, LANES), BF),
        pltpu.SemaphoreType.DMA((2,)),
    ]
    expert_scratch = [
        pltpu.VMEM((3, per_column, hidden_width, width), BF),
        pltpu.SemaphoreType.DMA((3, per_column, 4)),
    ]
    qkv_flops = 2 * tokens * width * qkv_width
    out_flops = 2 * tokens * width * width + 2 * slots * tokens * width
    score_flops = 2 * heads * tokens * length * HEAD_DIM
    expert_flops = 2 * slots * hidden_width * width

    per = slots // columns
    back_like = like((columns, per, width + LANES), BF)
    double_like = like((columns, 2 * per, width), BF)
    lanes_like = like((tokens, LANES), F32)
    tables = late([cosine, sine])
    first_flag = (1 - second)

    def forward(came, entering, targets, waits, down):
        keep = bool(targets)
        projected, pairs = [], []
        for m in pieces:
            projected.append(
                call(
                    functools.partial(project, keep),
                    (token_wide, token_low, pair_like)
                    + ((Sent(token_low), Sent(token_wide), Sent(token_low), Sent(pair_like))
                       if keep else ()),
                    (came[m], Late(entering[m]), Late(gain_a), *tables), qkv_flops, (dense,),
                    qkv_scratch, (second,), waits=(*waits, *(p[0] for p in projected)),
                )
            )
            pair = projected[m][2]
            pairs.append([swapped(pair, s) for s in steps[1:]])
        attended = [
            call(
                functools.partial(attend, keep),
                (Sent(token_wide), Sent(lanes_like), Sent(double_like if keep else block_like))
                + ((Sent(probs_like), Sent(token_low), Sent(token_low)) if keep else ()),
                (*projected[m][:3], *late([*pairs[m], biases[m], gain_f, chosens[m], dispatches[m],
                                           *targets[m : m + 1]])),
                out_flops + 2 * score_flops, (dense,), [pltpu.VMEM((tokens, width), BF)] + out_scratch,
                waits=() if keep or m else (projected[1][2],),
            )
            for m in pieces
        ]
        arrived = [over_columns(a[2]) for a in attended]
        lefts, ready = [], ()
        if keep:
            left = call(
                pack, (Sent(like((2 * micro, tokens, width), BF)),),
                late([p[3] for p in projected] + [a[4] for a in attended]), 0,
            )[0]
            two = swapped(left, 2)
            lefts = [left, swapped(left, 1), two, swapped(two, 1)]
            ready = (two,)
        else:
            two = hold(down[2], attended[1][2])
            down = (*down[:2], two, swapped(two, 1))
        applied = [
            call(
                functools.partial(expert_forward, keep),
                (Sent(block_like),)
                + ((Sent(kept_like),) * 3 + (Sent(back_like),) if keep else ()),
                late([arrived[m]]), (6 if keep else 3) * expert_flops,
                (*gate_shards, *up_shards, *down), expert_scratch,
                waits=ready if m else (attended[1][2],),
            )
            for m in pieces
        ]
        return projected, pairs, attended, arrived, applied, lefts, down

    def far_and_near(side):
        return [
            call(
                functools.partial(expert_weight_grads, side, begin),
                (Sent(like((per_column, hidden_width // 4, width), BF)),) * 2,
                late([*left, *right]), expert_flops,
            )
            for left, right, begin in (
                (hidden, arrived_grads, 0), ([a[1] for a in moved], arrived, 0),
                ([a[2] for a in moved], arrived, 0),
            )
        ]

    def merged(half, waits):
        return call(
            add, (Sent(half[0]),), late([half[0], swapped(half[1], 1)]), 0, waits=waits
        )[0]

    def attention_back(keep, m, grad, token_grads, waits):
        return call(
            functools.partial(attend_back, keep),
            (token_wide, token_low)
            + (like((tokens, 2 * kv_width + (share if keep else 0)), BF),) * rows
            + ((Sent(like((tokens, LANES), BF)), Sent(sums_like)) if keep else ()),
            late([token_grads, shared[m] if keep else spread, attended[m][1], places[m],
                  attended[m][0], gain_f, grad, projected[m][5], projected[m][6], *pairs[m],
                  attended[m][3], cosine, sine]),
            out_flops + 4 * score_flops, (dense,), [pltpu.VMEM((tokens, width), BF)] + out_scratch,
            (here, second), waits,
        )

    def parts_of(inner):
        return [inner[2]] + [swapped(inner[2 + s], s) for s in steps[1:]]

    def projection_back(keep, m, inner, parts, waits):
        return call(
            functools.partial(project_back, keep),
            (token_low,)
            + ((Sent(token_wide), Sent(sums_like))
               + (like((tokens, qkv_width // rows), BF),) * rows if keep else ()),
            (parts[0], *late(parts[1:]), inner[1], Late(projected[m][4]), Late(gain_a), inner[0],
             *tables),
            qkv_flops, (dense,), [pltpu.VMEM((tokens, qkv_width), BF)] + qkv_scratch,
            (here,), waits,
        )

    entering = [inputs[m, 0] for m in pieces]
    targets = [cotangent[m, 0] for m in pieces]
    kept = forward(entering, entering, (), (gate_shards[2], up_shards[2]), down_shards)
    attended, applied, down_shards = kept[2], kept[4], kept[6]
    returned = [over_columns(a[0]) for a in applied]
    results = [
        call(
            combine, (Sent(token_wide), token_low),
            late([returned[m], attended[m][0], attended[m][1], spread, places[m]]),
            2 * slots * tokens * width, waits=() if m else (applied[1][0],),
        )
        for m in pieces
    ]
    came = [lax.ppermute(r[1], "section", [(0, 1)]) for r in results]

    kept = forward(came, entering, targets, (), down_shards)
    projected, pairs, attended, arrived, applied, lefts, down_shards = kept
    hidden = [a[1] for a in applied]
    shared = [over_columns(a[4]) for a in applied]
    inner, outer = [], []
    for m in pieces:
        waits = (*lefts[1:], outer[0][0]) if m else (applied[1][4],)
        inner.append(attention_back(False, m, targets[m], shared[m], waits))
        outer.append(projection_back(False, m, inner[m], parts_of(inner[m]), ()))
    came = [lax.ppermute(o[0], "section", [(1, 0)]) for o in outer]

    given = [
        call(
            send_grads, (Sent(token_low), Sent(block_like)),
            (came[m], *late([targets[m], attended[m][1], dispatches[m]])),
            2 * slots * tokens * width, scalars=(first_flag,),
        )
        for m in pieces
    ]
    arrived_grads = [over_columns(g[1]) for g in given]
    moved = [
        call(
            expert_backward, (Sent(back_like), Sent(kept_like), Sent(kept_like)),
            late([arrived_grads[m], hidden[m], applied[m][2], applied[m][3], applied[m][0]]),
            3 * expert_flops, (*down_shards, *gate_shards, *up_shards), expert_scratch,
            (second,), () if m else (given[1][1],),
        )
        for m in pieces
    ]
    back = [over_columns(a[0]) for a in moved]
    far, near = far_and_near(1), far_and_near(0)
    crossed = [swapped(merged(far[0], ()), 2)]

    inner = [attention_back(True, 0, given[0][0], back[0], (moved[1][0],))]
    parts = [parts_of(inner[0])]
    outer = [projection_back(True, 0, inner[0], parts[0], ())]
    inner.append(attention_back(
        True, 1, given[1][0], back[1], (inner[0][0], *(f[0] for f in far), near[0][0])
    ))
    parts.append(parts_of(inner[1]))
    crossed.append(swapped(merged(far[1], parts[1][1:]), 2))
    o_grads = call(
        out_grads, (Sent(like((columns, rows * shard, share), BF)),),
        late([*lefts, *[p[s] for s in steps for p in parts]]),
        2 * width * length * micro * share, waits=(crossed[0],),
    )[0]
    outer.append(projection_back(True, 1, inner[1], parts[1], (o_grads,)))
    backs = [[o[3]] + [swapped(o[3 + s], s) for s in steps[1:]] for o in outer]
    last = merged(far[2], backs[1][1:])
    crossed.append(swapped(last, 2))
    w_grads = call(
        qkv_grads, (Sent(like((columns, rows * shard, qkv_width // rows + LANES), BF)),),
        late([*lefts, *[b[s] for s in steps for b in backs], *[a[5] for a in attended],
              *[a[6] for a in inner], *[o[2] for o in outer], *[a[7] for a in inner]]),
        2 * width * length * micro * qkv_width // rows,
        waits=(near[1][0], crossed[1], last),
    )[0]
    expert_grads = [
        n[0].astype(F32) + swapped(n[1], 1).astype(F32) + c.astype(F32)
        for n, c in zip(near, crossed)
    ]
    layer_outputs = call(
        last_outputs, (Sent(like((micro, tokens, width), F32)),),
        late([spread] + [v for m in pieces for v in (
            back[m], attended[m][0], attended[m][1], places[m], results[m][0])]),
        4 * slots * tokens * width, scalars=(second,), waits=(w_grads,),
    )[0]

    wide = share + qkv_width // rows + LANES
    pieces_out = call(
        fold, (like((shard, wide), F32),) * rows,
        late([over_columns(o_grads), over_columns(w_grads)]), 0,
        scratch=[pltpu.VMEM((rows * shard, wide), F32)], scalars=(here,),
    )
    pieces_out = [pieces_out[0]] + [swapped(pieces_out[s], s) for s in steps[1:]]
    o_grad, q_grad, k_grad, v_grad, rest = call(
        finish,
        (like((shard, width), F32), like((shard, width), F32), like((shard, kv_width), F32),
         like((shard, kv_width), F32), like((shard, LANES), F32)),
        pieces_out, 0, scratch=[pltpu.VMEM((shard, qkv_width), F32)], scalars=(here,),
    )

    return (
        layer_outputs[None, :, None],
        jnp.stack([o[1] for o in outer])[None, :, None],
        rest[:, LANES - 2][None],
        q_grad[None],
        k_grad[None],
        v_grad[None],
        o_grad[None],
        rest[:, LANES - 1][None],
        rest[:, :experts][None],
        expert_grads[1][None],
        expert_grads[2][None],
        expert_grads[0][None],
    )


def solution(mesh):
    dense = P("section", ("row", "col"), None)
    gain = P("section", ("row", "col"))
    expert = P("section", "col", "row", None)
    token = P(None, "col", "row", None)
    layered = P("section", None, "col", "row", None)
    return jax.shard_map(
        on_device,
        mesh=mesh,
        in_specs=(
            token, token, P(None, "col", None), layered, gain, dense, dense, dense, dense, gain,
            dense, expert, expert, expert,
        ),
        out_specs=(
            layered, layered, gain, dense, dense, dense, dense, gain, dense, expert, expert, expert,
        ),
        check_vma=False,
    )
```

```python
import functools

import jax
import jax.numpy as jnp
from jax import lax
from jax.experimental import pallas as pl
from jax.experimental.pallas import tpu as pltpu
from jax.sharding import PartitionSpec as P

HEAD_DIM = 128
ROOMS = 16
EPSILON = 1e-06
LANES = 128
BF = jnp.bfloat16
F32 = jnp.float32
MIB = 1 << 20


def dot(left, right, contract=(1, 0)):
    return lax.dot_general(
        left, right, (((contract[0],), (contract[1],)), ((), ())), preferred_element_type=F32
    )


def like(shape, dtype):
    return jax.ShapeDtypeStruct(shape, dtype)


class Late:
    def __init__(self, source, target=None, sem=None):
        self.source, self.target, self.copy = source, target, None
        if target is not None:
            self.copy = pltpu.make_async_copy(source, target, sem)
            self.copy.start()
            self.waiting = True

    def ready(self):
        if self.waiting:
            self.copy.wait()
            self.waiting = False
        return self.target

    def __getitem__(self, index):
        return self.ready()[index]

    @property
    def shape(self):
        return self.source.shape


class Sent:
    def __init__(self, source, target=None, sems=None):
        self.source, self.target, self.sems, self.copies = source, target, sems, []

    def __getitem__(self, index):
        return self.source[index]

    def __setitem__(self, index, value):
        self.source[index] = value

    def send(self, *parts):
        for part in parts or (...,):
            at = len(self.copies)
            whole = part is ...
            copy = pltpu.make_async_copy(
                self.source if whole else self.source.at[part],
                self.target if whole else self.target.at[part],
                self.sems.at[at],
            )
            copy.start()
            self.copies.append(copy)

    @property
    def shape(self):
        return self.source.shape


class Raw:
    def __init__(self, source):
        self.source = source


PARTS = 4


def sent(out, *parts):
    if isinstance(out, Sent):
        out.send(*parts)


def call(body, outs, args, flops, far=(), scratch=(), scalars=(), waits=()):
    arrays = [a.source if isinstance(a, Late) else a for a in args]
    shapes = [o.source if isinstance(o, (Sent, Raw)) else o for o in outs]
    moved = sum(a.size * a.dtype.itemsize for a in (*arrays, *far, *shapes))
    count = len(scalars) + len(args) + len(far)
    kinds = [isinstance(a, Late) for a in args]
    out_kinds = [isinstance(o, Sent) for o in outs]
    raw_kinds = [isinstance(o, Raw) for o in outs]
    buffers = [pltpu.VMEM(a.shape, a.dtype) for a, k in zip(arrays, kinds) if k]
    buffers += [pltpu.VMEM(o.shape, o.dtype) for o, k in zip(shapes, out_kinds) if k]

    def run(*refs):
        given, refs = list(refs[:count]), refs[count + len(waits) :]
        results, refs = list(refs[: len(outs)]), refs[len(outs) :]
        own, rest = list(refs[: len(buffers)]), refs[len(buffers) :]
        sems, rest = (rest[0], rest[1:]) if buffers else (None, rest)
        used = 0
        for k, kind in enumerate(kinds):
            if kind:
                at = len(scalars) + k
                given[at] = Late(given[at], own[used], sems.at[used, 0])
                used += 1
        for k, kind in enumerate(out_kinds):
            if kind:
                results[k] = Sent(own[used], results[k], sems.at[used])
                used += 1
        body(*given, *results, *rest)
        for one in given:
            if isinstance(one, Late):
                one.ready()
        for one in results:
            if isinstance(one, Sent) and not one.copies:
                one.send()
        for one in results:
            if isinstance(one, Sent):
                done_with(one.copies)

    anywhere, local = pl.BlockSpec(memory_space=pl.ANY), pl.BlockSpec(memory_space=pltpu.VMEM)
    return pl.pallas_call(
        run,
        out_shape=tuple(shapes),
        in_specs=[pl.BlockSpec(memory_space=pltpu.SMEM)] * len(scalars)
        + [anywhere if k else local for k in kinds]
        + [anywhere] * (len(far) + len(waits)),
        out_specs=tuple(
            anywhere if k or raw else local for k, raw in zip(out_kinds, raw_kinds)
        ),
        scratch_shapes=buffers
        + ([pltpu.SemaphoreType.DMA((len(buffers), PARTS))] if buffers else [])
        + list(scratch),
        compiler_params=pltpu.CompilerParams(vmem_limit_bytes=60 * MIB),
        cost_estimate=pl.CostEstimate(
            flops=int(flops), bytes_accessed=int(moved), transcendentals=0
        ),
        name=body.func.__name__ if isinstance(body, functools.partial) else body.__name__,
    )(*scalars, *arrays, *far, *waits)


def late(values):
    return [Late(v) for v in values]


def nothing(*refs):
    pass


def hold(value, *waits):
    return pl.pallas_call(
        nothing,
        out_shape=like(value.shape, value.dtype),
        in_specs=[pl.BlockSpec(memory_space=pl.ANY)] * (1 + len(waits)),
        out_specs=pl.BlockSpec(memory_space=pl.ANY),
        input_output_aliases={0: 0},
        name="hold",
    )(value, *waits)


def swapped(value, step):
    rows = lax.axis_size("row")
    return lax.ppermute(value, "row", [(r, r ^ step) for r in range(rows)])


def norm_parts(stream):
    return lax.rsqrt(jnp.mean(stream * stream, -1, keepdims=True) + EPSILON)


def norm_back(grad, stream, gain):
    inverse = norm_parts(stream)
    unit = stream * inverse
    scaled = grad * gain
    back = inverse * (scaled - unit * jnp.mean(scaled * unit, -1, keepdims=True))
    return back, jnp.sum(grad * unit, 0, keepdims=True)


def turned(vectors, cosine, sine):
    done = []
    for at in range(0, vectors.shape[1], HEAD_DIM):
        one = vectors[:, at : at + HEAD_DIM]
        done.append(one * cosine + pltpu.roll(one, HEAD_DIM // 2, 1) * sine)
    return jnp.concatenate(done, -1) if len(done) > 1 else done[0]


def stacked_heads(value, first, count):
    return jnp.concatenate(
        [value[:, (first + j) * HEAD_DIM : (first + j + 1) * HEAD_DIM] for j in range(count)], 0
    )


def unstacked_heads(value, count):
    tokens = value.shape[0] // count
    return jnp.concatenate([value[j * tokens : (j + 1) * tokens] for j in range(count)], 1)


def cuts_of(total, most=512):
    return [(at, min(most, total - at)) for at in range(0, total, most)]


def project(
    flag, came, entering, gain, cosine, sine, dense, stream, normed, query, pair, weights, sems
):
    width = stream.shape[1]
    cuts = cuts_of(weights.shape[1])
    copies = [
        pltpu.make_async_copy(
            dense.at[:, pl.ds(at, size)], weights.at[:, pl.ds(at, size)], sems.at[k]
        )
        for k, (at, size) in enumerate(cuts)
    ]
    for copy in copies:
        copy.start()
    x = jnp.where(flag[0] > 0, came[...].astype(F32), entering[...].astype(F32))
    stream[...] = x
    low = (x * norm_parts(x) * gain[...]).astype(BF)
    normed[...] = low
    keys = pair.shape[1] // 2
    for copy, (at, size) in zip(copies, cuts):
        copy.wait()
        part = dot(low, weights[:, at : at + size])
        for begin in range(at, at + size, HEAD_DIM):
            head = part[:, begin - at : begin - at + HEAD_DIM]
            if begin < width + keys:
                head = turned(head, cosine[...], sine[...])
            head = head.astype(BF)
            if begin < width:
                query[:, begin : begin + HEAD_DIM] = head
            else:
                pair[:, begin - width : begin - width + HEAD_DIM] = head


def slot_experts(slots):
    own = lax.broadcasted_iota(jnp.int32, (slots, LANES), 0) // ROOMS
    return own == lax.broadcasted_iota(jnp.int32, (slots, LANES), 1)


def scaled_rows(dispatch, gates, low):
    here = slot_experts(dispatch.shape[0])
    scale = jnp.sum(jnp.where(here, dot(dispatch, gates.astype(BF)), 0.0), -1, keepdims=True)
    return (dot(dispatch, low) * scale).astype(BF)


def attend(
    keep, stream, query, pair0, pair1, pair2, pair3, bias, gain, chosen, dispatch, *rest,
):
    (normed, target), rest = (rest[:2], rest[2:]) if keep else ((None, None), rest)
    dense, middle, gates, outgoing = rest[:4]
    kept, (mixed, weights, router, sems) = rest[4:-4], rest[-4:]
    width = stream.shape[1]
    block = (outgoing.shape[0], -1, width)
    per = dispatch.shape[0] // outgoing.shape[0]
    at = dense.shape[1] - width - LANES
    copies = [
        pltpu.make_async_copy(dense.at[:, pl.ds(at + LANES, width)], weights, sems.at[0]),
        pltpu.make_async_copy(dense.at[:, pl.ds(at, LANES)], router, sems.at[1]),
    ]
    if keep:
        own = [(stream, kept[3]), (query, kept[4]), (normed, kept[5])]
        own += [(p, kept[6].at[k]) for k, p in enumerate((pair0, pair1, pair2, pair3))]
        copies += [pltpu.make_async_copy(a, b, sems.at[2 + k]) for k, (a, b) in enumerate(own)]
    for copy in copies:
        copy.start()
    pairs = jnp.concatenate([pair0[...], pair1[...], pair2[...], pair3[...]], 0)
    kv_heads = pairs.shape[1] // (2 * HEAD_DIM)
    group = width // HEAD_DIM // kv_heads
    biases = jnp.concatenate([bias[...]] * group, 0)
    tokens = stream.shape[0]
    for h in range(kv_heads):
        keys = pairs[:, h * HEAD_DIM : (h + 1) * HEAD_DIM]
        values = pairs[:, (kv_heads + h) * HEAD_DIM : (kv_heads + h + 1) * HEAD_DIM]
        queries = stacked_heads(query, h * group, group)
        scores = dot(queries, keys, (1, 1)) * HEAD_DIM ** (-0.5) + biases
        expo = jnp.exp(scores - jnp.max(scores, -1, keepdims=True))
        weight = (expo * (1.0 / jnp.sum(expo, -1, keepdims=True))).astype(BF)
        if keep:
            kept[0][h] = weight
        done = dot(weight, values).astype(BF)
        for j in range(group):
            begin = (h * group + j) * HEAD_DIM
            mixed[:, begin : begin + HEAD_DIM] = done[j * tokens : (j + 1) * tokens]
    if keep:
        kept[1][...] = mixed[...]
        sent(kept[0])
        sent(kept[1])
    copies[0].wait()
    x = stream[...] + dot(mixed[...], weights[...])
    middle[...] = x
    sent(middle)
    low = (x * norm_parts(x) * gain[...]).astype(BF)
    if keep:
        kept[2][...] = low
        sent(kept[2])
    copies[1].wait()
    taken = chosen[...] > 0
    logits = jnp.where(taken, dot(low, router[...]), -1e30)
    expo = jnp.where(taken, jnp.exp(logits - jnp.max(logits, -1, keepdims=True)), 0.0)
    share = expo / jnp.sum(expo, -1, keepdims=True)
    gates[...] = share
    sent(gates)
    slots = dispatch[...]
    outgoing[:, :per, :] = dot(slots, low).astype(BF).reshape(block)
    if keep:
        sent(outgoing, (slice(None), pl.ds(0, per)))
        outgoing[:, per:, :] = scaled_rows(slots, share, target[...]).reshape(block)
        sent(outgoing, (slice(None), pl.ds(per, per)))
    done_with(copies[2:])


class Fetched:
    def __init__(self, shards, weights, sems):
        self.weights = weights
        self.copies = {}
        for j in range(weights.shape[1]):
            for k in range(weights.shape[0]):
                self.copies[k, j] = [
                    pltpu.make_async_copy(
                        shards[k][p].at[j],
                        weights.at[k, j, pl.ds(p * shards[k][p].shape[1], shards[k][p].shape[1])],
                        sems.at[k, j, p],
                    )
                    for p in range(4)
                ]
        for k in range(weights.shape[0]):
            self.start(k, 0)

    def start(self, k, j):
        for copy in self.copies.get((k, j), ()):
            copy.start()

    def ready(self, k, j):
        done_with(self.copies[k, j])
        self.start(k, j + 1)


def done_with(copies):
    for copy in copies:
        copy.wait()


def rows_of(value, j, begin=0):
    columns, unused, width = value.shape
    at = begin + j * ROOMS
    return value[:, at : at + ROOMS, :].reshape(columns * ROOMS, width)


def put_rows(out, j, rows, inner):
    at, width = j * ROOMS, rows.shape[1]
    out[:, at : at + ROOMS, :width] = rows.reshape(-1, ROOMS, width)
    high = inner.astype(BF).astype(F32)
    lane = lax.broadcasted_iota(jnp.int32, (rows.shape[0], LANES), 1)
    both = jnp.where(lane == 0, high, jnp.where(lane == 1, inner - high, 0.0))
    out[:, at : at + ROOMS, width:] = both.astype(BF).reshape(-1, ROOMS, LANES)


def expert_forward(both, arrived, *refs):
    shards = [refs[4 * k : 4 * k + 4] for k in range(3)]
    outs, weights, sems = refs[12:-2], refs[-2], refs[-1]
    fetched = Fetched(shards, weights, sems)
    per = weights.shape[1] * ROOMS
    for j in range(weights.shape[1]):
        at = j * ROOMS
        rows = rows_of(arrived, j)
        fetched.ready(0, j)
        gate = dot(rows, weights[0, j], (1, 1))
        fetched.ready(1, j)
        lifted = dot(rows, weights[1, j], (1, 1))
        square = gate * gate
        bend = jnp.tanh(0.7978845608028654 * gate * (1.0 + 0.044715 * square))
        active = 0.5 * gate * (1.0 + bend)
        hidden = (active * lifted).astype(BF)
        fetched.ready(2, j)
        made = dot(hidden, weights[2, j]).astype(BF)
        outs[0][:, at : at + ROOMS, :] = made.reshape(-1, ROOMS, made.shape[1])
        sent(outs[0], (slice(None), pl.ds(at, ROOMS)))
        if both:
            slope = 0.5 * (1.0 + bend) + 0.5 * gate * (1.0 - bend * bend) * (
                0.7978845608028654 * (1.0 + 3 * 0.044715 * square)
            )
            bent = slope * lifted
            outs[1][j] = hidden
            outs[2][j] = active.astype(BF)
            outs[3][j] = bent.astype(BF)
            hidden_grads = dot(rows_of(arrived, j, per), weights[2, j], (1, 1))
            gate_part = (hidden_grads * bent).astype(BF)
            lifted_part = (hidden_grads * active).astype(BF)
            inner = jnp.sum(hidden_grads * hidden.astype(F32), -1, keepdims=True)
            back = dot(gate_part, weights[0, j]) + dot(lifted_part, weights[1, j])
            put_rows(outs[4], j, back.astype(BF), inner)
            sent(outs[4], (slice(None), pl.ds(at, ROOMS)))
            for out in outs[1:4]:
                sent(out, j)


def combine(returned, middle, gates, spread, places, result, low):
    weights = (dot(gates[...].astype(BF), spread[...]) * places[...].astype(F32)).astype(BF)
    done = middle[...] + dot(weights, returned[...].reshape(-1, returned.shape[2]))
    result[...] = done
    sent(result)
    low[...] = done.astype(BF)


def last_outputs(flag, spread, *refs):
    out = refs[-1]
    width = out.shape[2]
    for m in range(out.shape[0]):
        returned, middle, gates, places, before = refs[5 * m : 5 * m + 5]
        weights = (dot(gates[...].astype(BF), spread[...]) * places[...].astype(F32)).astype(BF)
        rows = returned[:, :, :width].reshape(-1, width)
        out[m] = jnp.where(flag[0] > 0, middle[...] + dot(weights, rows), before[...])


def send_grads(flag, came, target, gates, dispatch, grad, outgoing):
    low = jnp.where(flag[0] > 0, came[...], target[...])
    grad[...] = low
    sent(grad)
    outgoing[...] = scaled_rows(dispatch[...], gates[...], low).reshape(outgoing.shape)


def expert_backward(flag, arrived, hidden, active, bent, produced, *refs):
    shards = [refs[4 * k : 4 * k + 4] for k in range(3)]
    out, gate_back, lifted_back, weights, sems = refs[12:]
    fetched = Fetched(shards, weights, sems)
    for j in range(weights.shape[1]):
        fetched.ready(0, j)
        hidden_grads = dot(rows_of(arrived, j), weights[0, j], (1, 1))
        gate_part = (hidden_grads * bent[j].astype(F32)).astype(BF)
        lifted_part = (hidden_grads * active[j].astype(F32)).astype(BF)
        gate_back[j] = gate_part
        lifted_back[j] = lifted_part
        inner = jnp.sum(hidden_grads * hidden[j].astype(F32), -1, keepdims=True)
        fetched.ready(1, j)
        done = dot(gate_part, weights[1, j])
        fetched.ready(2, j)
        done = (done + dot(lifted_part, weights[2, j])).astype(BF)
        put_rows(out, j, jnp.where(flag[0] > 0, rows_of(produced, j), done), inner)
        sent(out, (slice(None), pl.ds(j * ROOMS, ROOMS)))
        sent(gate_back, j)
        sent(lifted_back, j)


def attend_back(
    keep, row, flag, token_grads, before, gates, places, middle, gain, grad, query, pairs, probs,
    cosine, sine, dense, middle_grads, query_back, part0, part1, part2, part3, *rest,
):
    tokens, width = middle.shape
    kept, (branch, weights, router, sems) = rest[:-4], rest[-4:]
    at = dense.shape[1] - width - LANES
    copies = [
        pltpu.make_async_copy(dense.at[:, pl.ds(at, LANES)], router, sems.at[1]),
        pltpu.make_async_copy(dense.at[:, pl.ds(at + LANES, width)], weights, sems.at[0]),
    ]
    for copy in copies:
        copy.start()
    came = token_grads[...]
    if keep:
        came = jnp.where(flag[0] > 0, before[...], came)
    came = came.reshape(-1, came.shape[2])
    place = places[...]
    here = slot_experts(came.shape[0])
    notes = came[:, width:].astype(F32)
    high = jnp.where(here, notes[:, :1], 0.0).astype(BF)
    rest_of = jnp.where(here, notes[:, 1:2], 0.0).astype(BF)
    inner = dot(place, high) + dot(place, rest_of)
    logit_grads = (inner - gates[...] * jnp.sum(inner, -1, keepdims=True)).astype(BF)
    ffn_grads = dot(place, came[:, :width])
    copies[0].wait()
    ffn_grads = ffn_grads + dot(logit_grads, router[...], (1, 1))
    part, total = norm_back(ffn_grads, middle[...], gain[...])
    above = grad[...].astype(F32) + part
    middle_grads[...] = above
    low = above.astype(BF)
    if keep:
        kept[0][...] = logit_grads
        kept[1][...] = jnp.broadcast_to(total, kept[1].shape)
        sent(kept[0])
        sent(kept[1])
        branch[...] = low
        share = width // 4
        for s, part in enumerate((part0, part1, part2, part3)):
            begin = pl.multiple_of((row[0] ^ s) * share, LANES)
            part[:, part.shape[1] - share :] = branch[:, pl.ds(begin, share)]
    copies[1].wait()
    mixed_grads = dot(low, weights[...], (1, 1)).astype(BF)
    pairs = pairs[...].reshape(-1, pairs.shape[2])
    kv_heads = pairs.shape[1] // (2 * HEAD_DIM)
    group = width // HEAD_DIM // kv_heads
    scale = HEAD_DIM ** (-0.5)
    parts = (part0, part1, part2, part3)
    for h in range(kv_heads):
        keys = pairs[:, h * HEAD_DIM : (h + 1) * HEAD_DIM]
        values = pairs[:, (kv_heads + h) * HEAD_DIM : (kv_heads + h + 1) * HEAD_DIM]
        queries = stacked_heads(query, h * group, group)
        top = stacked_heads(mixed_grads, h * group, group)
        weight = probs[h]
        wide = weight.astype(F32)
        weight_grads = dot(top, values, (1, 1))
        value_grads = dot(weight, top, (0, 0)).astype(BF)
        inner = wide * weight_grads
        score_grads = (inner - wide * jnp.sum(inner, -1, keepdims=True)).astype(BF)
        query_grads = dot(score_grads, keys) * scale
        key_grads = (dot(score_grads, queries, (0, 0)) * scale).astype(BF)
        for j in range(group):
            begin = (h * group + j) * HEAD_DIM
            one = query_grads[j * tokens : (j + 1) * tokens]
            query_back[:, begin : begin + HEAD_DIM] = turned(one, cosine[...], -sine[...]).astype(BF)
        for p, part in enumerate(parts):
            part[:, h * HEAD_DIM : (h + 1) * HEAD_DIM] = key_grads[p * tokens : (p + 1) * tokens]
            begin = (kv_heads + h) * HEAD_DIM
            part[:, begin : begin + HEAD_DIM] = value_grads[p * tokens : (p + 1) * tokens]


def project_back(
    keep, row, part0, part1, part2, part3, query_back, stream, gain, middle_grads, cosine, sine,
    dense, low, *rest,
):
    width = stream.shape[1]
    kept, (backs, weights, sems) = rest[:-3], rest[-3:]
    cuts = cuts_of(weights.shape[1])
    copies = [
        pltpu.make_async_copy(
            dense.at[:, pl.ds(at, size)], weights.at[:, pl.ds(at, size)], sems.at[k]
        )
        for k, (at, size) in enumerate(cuts)
    ]
    for copy in copies:
        copy.start()
    pairs = weights.shape[1] - width
    total = sum(part[:, :pairs].astype(F32) for part in (part0, part1, part2, part3))
    keys = pairs // 2
    backs[:, :width] = query_back[...]
    backs[:, width : width + keys] = turned(total[:, :keys], cosine[...], -sine[...]).astype(BF)
    backs[:, width + keys :] = total[:, keys:].astype(BF)
    if keep:
        share = backs.shape[1] // 4
        for s, out in enumerate(kept[2:]):
            out[...] = backs[:, pl.ds(pl.multiple_of((row[0] ^ s) * share, LANES), share)]
    above = jnp.zeros(stream.shape, F32)
    for copy, (at, size) in zip(copies, cuts):
        copy.wait()
        above = above + dot(backs[:, at : at + size], weights[:, at : at + size], (1, 1))
    part, sums = norm_back(above, stream[...], gain[...])
    done = middle_grads[...] + part
    if keep:
        kept[0][...] = done
        kept[1][...] = jnp.broadcast_to(sums, kept[1].shape)
    low[...] = done.astype(BF)


def expert_weight_grads(half, begin, left0, left1, right0, right1, first, second):
    size = first.shape[1]
    wide = 2 * size
    for j in range(first.shape[0]):
        total = dot(left0[j, :, half * wide : (half + 1) * wide], rows_of(right0, j, begin), (0, 0))
        total = total + dot(
            left1[j, :, half * wide : (half + 1) * wide], rows_of(right1, j, begin), (0, 0)
        )
        first[j] = total[:size].astype(BF)
        second[j] = total[size:].astype(BF)


def add(one, other, total):
    total[...] = (one[...].astype(F32) + other[...].astype(F32)).astype(BF)


def pack(*refs):
    for k, value in enumerate(refs[:-1]):
        refs[-1][k] = value[...]


def stacked(refs):
    return jnp.concatenate([r[...] for r in refs], 0)


def by_owner(out, grads, begin):
    columns, lines, unused = out.shape
    size = lines // 4
    for c in range(columns):
        some = [grads[(r * columns + c) * size : (r * columns + c + 1) * size] for r in range(4)]
        out[c, :, begin : begin + grads.shape[1]] = jnp.concatenate(some, 0).astype(BF)


def out_grads(*refs):
    lefts, rights, out = refs[:4], refs[4:12], refs[12]
    share = out.shape[2]
    left = jnp.concatenate([one[k] for one in lefts for k in (2, 3)], 0)
    right = jnp.concatenate([r[:, r.shape[1] - share :] for r in rights], 0)
    by_owner(out, dot(left, right, (0, 0)), 0)


def qkv_grads(*refs):
    lefts, rights, normed, logits, gains, out = (
        refs[:4], refs[4:12], refs[12:14], refs[14:16], refs[16:20], refs[20],
    )
    wide = out.shape[2]
    left = jnp.concatenate([one[k] for one in lefts for k in (0, 1)], 0)
    by_owner(out, dot(left, stacked(rights), (0, 0)), 0)
    width = left.shape[1]
    first = gains[0][:1, :] + gains[1][:1, :]
    second = gains[2][:1, :] + gains[3][:1, :]
    line = lax.broadcasted_iota(jnp.int32, (LANES, width), 0)
    sums = jnp.where(
        line == LANES - 2, first, jnp.where(line == LANES - 1, second, jnp.zeros((1, 1), F32))
    )
    by_owner(out, dot(stacked(normed), stacked(logits), (0, 0)) + sums.T, wide - LANES)


def fold(row, first, second, out0, out1, out2, out3, total):
    share = first.shape[2]
    total[:, :share] = jnp.sum(first[...].astype(F32), 0)
    total[:, share:] = jnp.sum(second[...].astype(F32), 0)
    for s, out in enumerate((out0, out1, out2, out3)):
        size = out.shape[0]
        out[...] = total[pl.ds(pl.multiple_of((row[0] ^ s) * size, 8), size), :]


def finish(
    row, in0, in1, in2, in3, o_grad, q_grad, k_grad, v_grad, r_grad, first, second, total
):
    share = o_grad.shape[1] // 4
    piece = total.shape[1] // 4
    ins = (in0, in1, in2, in3)
    for s, one in enumerate(ins):
        where = row[0] ^ s
        o_grad[:, pl.ds(pl.multiple_of(where * share, LANES), share)] = one[:, :share]
        total[:, pl.ds(pl.multiple_of(where * piece, LANES), piece)] = one[:, share : share + piece]
    rest = sum(one[:, share + piece :] for one in ins)
    r_grad[...] = rest[:, : r_grad.shape[1]]
    turned_rest = rest.T
    first[...] = turned_rest[LANES - 2 : LANES - 1, :]
    second[...] = turned_rest[LANES - 1 :, :]
    begin = 0
    for out in (q_grad, k_grad, v_grad):
        out[...] = total[:, begin : begin + out.shape[1]]
        begin += out.shape[1]


def over_columns(value):
    return lax.all_to_all(value, "col", split_axis=0, concat_axis=0, tiled=True)


def on_device(
    inputs, cotangent, segment_ids, routes, attn_gain, w_query, w_key, w_value, w_out, ffn_gain,
    w_router, w_gate, w_up, w_down,
):
    section = lax.axis_index("section")
    row = lax.axis_index("row")
    rows = lax.axis_size("row")
    columns = lax.axis_size("col")
    micro, tokens, width = inputs.shape[0], inputs.shape[2], inputs.shape[3]
    experts = w_router.shape[2]
    per_column = w_gate.shape[1]
    hidden_width = w_gate.shape[2] * rows
    kv_width = w_key.shape[2]
    qkv_width = width + 2 * kv_width
    slots = experts * ROOMS
    share = width // rows
    shard = width // (rows * columns)
    heads = width // HEAD_DIM
    kv_heads = kv_width // HEAD_DIM
    length = rows * tokens
    pieces = range(micro)
    steps = range(rows)
    here = row.astype(jnp.int32)[None]
    second = (section == 1).astype(jnp.int32)[None]
    block = (columns, slots // columns, width)

    dense = jnp.concatenate(
        [w_query[0], w_key[0], w_value[0], w_router[0], attn_gain[0][:, None], ffn_gain[0][:, None],
         jnp.zeros((shard, LANES - experts - 2), BF), w_out[0]], 1
    )
    dense = lax.all_gather(dense, ("row", "col"), axis=0, tiled=True)
    small = dense[:, qkv_width : qkv_width + LANES]
    gain_a = small[:, experts].astype(F32)[None, :]
    gain_f = small[:, experts + 1].astype(F32)[None, :]

    def shards_of(own):
        two = swapped(own, 2)
        return own, swapped(own, 1), two, swapped(two, 1)

    gate_shards, up_shards = shards_of(w_gate[0]), shards_of(w_up[0])
    down_shards = (w_down[0], swapped(w_down[0], 1), swapped(w_down[0], 2))

    lane = jnp.arange(LANES, dtype=jnp.int32)
    half = HEAD_DIM // 2
    freqs = 10000.0 ** (-2.0 * jnp.arange(half).astype(F32) / HEAD_DIM)
    positions = row * tokens + jnp.arange(tokens, dtype=jnp.int32)
    angles = positions.astype(F32)[:, None] * freqs[None, :]
    cosine = jnp.concatenate([jnp.cos(angles)] * 2, 1)
    sine = jnp.concatenate([-jnp.sin(angles), jnp.sin(angles)], 1)
    key_positions = jnp.concatenate(
        [(row ^ step) * tokens + jnp.arange(tokens, dtype=jnp.int32) for step in steps]
    )
    spread = (lane[:, None] == jnp.arange(slots, dtype=jnp.int32)[None, :] // ROOMS).astype(BF)
    below = (jnp.arange(tokens)[:, None] > jnp.arange(tokens)[None, :]).astype(BF)
    biases, chosens, places, dispatches = [], [], [], []
    for m in pieces:
        segments = segment_ids[m, 0]
        own_segments = lax.dynamic_slice_in_dim(segments, row * tokens, tokens)
        key_segments = jnp.concatenate(
            [lax.dynamic_slice_in_dim(segments, (row ^ s) * tokens, tokens) for s in steps]
        )
        counted = (key_positions[None, :] <= positions[:, None]) & (
            key_segments[None, :] == own_segments[:, None]
        )
        biases.append(jnp.where(counted, 0.0, -1e30).astype(F32))
        chosen = jnp.any(routes[0, m, 0][:, :, None] == lane[None, None, :], 1)
        chosens.append(chosen.astype(F32))
        rank = dot(below, chosen.astype(BF))
        rank = jnp.where(chosen, rank, -1.0)[:, :experts]
        place = (
            rank[:, :, None] == jnp.arange(ROOMS, dtype=F32)[None, None, :]
        ).reshape(tokens, slots)
        places.append(place.astype(BF))
        dispatches.append(place.T.astype(BF))

    token_low, token_wide = like((tokens, width), BF), like((tokens, width), F32)
    pair_like = like((tokens, 2 * kv_width), BF)
    block_like = like(block, BF)
    sums_like = like((8, width), F32)
    kept_like = like((per_column, columns * ROOMS, hidden_width), BF)
    probs_like = like((kv_heads, heads // kv_heads * tokens, length), BF)
    qkv_scratch = [pltpu.VMEM((width, qkv_width), BF), pltpu.SemaphoreType.DMA((8,))]
    out_scratch = [
        pltpu.VMEM((width, width), BF), pltpu.VMEM((width, LANES), BF),
        pltpu.SemaphoreType.DMA((16,)),
    ]
    expert_scratch = [
        pltpu.VMEM((3, per_column, hidden_width, width), BF),
        pltpu.SemaphoreType.DMA((3, per_column, 4)),
    ]
    qkv_flops = 2 * tokens * width * qkv_width
    out_flops = 2 * tokens * width * width + 2 * slots * tokens * width
    score_flops = 2 * heads * tokens * length * HEAD_DIM
    expert_flops = 2 * slots * hidden_width * width

    per = slots // columns
    back_like = like((columns, per, width + LANES), BF)
    double_like = like((columns, 2 * per, width), BF)
    lanes_like = like((tokens, LANES), F32)
    tables = late([cosine, sine])
    first_flag = (1 - second)

    def forward(came, entering, targets, waits, down):
        keep = bool(targets)
        projected, pairs = [], []
        for m in pieces:
            projected.append(
                call(
                    project, (token_wide, token_low, token_low, pair_like),
                    (came[m], Late(entering[m]), Late(gain_a), *tables), qkv_flops, (dense,),
                    qkv_scratch, (second,), waits=(*waits, *(p[0] for p in projected)),
                )
            )
            pair = projected[m][3]
            pairs.append([swapped(pair, s) for s in steps[1:]])
        attended = [
            call(
                functools.partial(attend, keep),
                (Sent(token_wide), Sent(lanes_like), Sent(double_like if keep else block_like))
                + ((Sent(probs_like), Sent(token_low), Sent(token_low), Raw(token_wide),
                    Raw(token_low), Raw(token_low), Raw(like((rows, tokens, 2 * kv_width), BF)))
                   if keep else ()),
                (projected[m][0], projected[m][2], projected[m][3], *pairs[m],
                 *late([biases[m], gain_f, chosens[m], dispatches[m]]),
                 *((projected[m][1], Late(targets[m])) if keep else ())),
                out_flops + 2 * score_flops, (dense,), [pltpu.VMEM((tokens, width), BF)] + out_scratch,
                waits=() if keep or m else pairs[1],
            )
            for m in pieces
        ]
        arrived = [over_columns(a[2]) for a in attended]
        lefts, ready = [], ()
        if keep:
            left = call(
                pack, (Sent(like((2 * micro, tokens, width), BF)),),
                late([a[8] for a in attended] + [a[4] for a in attended]), 0,
            )[0]
            two = swapped(left, 2)
            lefts = [left, swapped(left, 1), two, swapped(two, 1)]
            ready = (two,)
        else:
            two = hold(down[2], attended[1][2])
            down = (*down[:2], two, swapped(two, 1))
        applied = [
            call(
                functools.partial(expert_forward, keep),
                (Sent(block_like),)
                + ((Sent(kept_like),) * 3 + (Sent(back_like),) if keep else ()),
                late([arrived[m]]), (6 if keep else 3) * expert_flops,
                (*gate_shards, *up_shards, *down), expert_scratch,
                waits=ready if m else (attended[1][2],),
            )
            for m in pieces
        ]
        return attended, arrived, applied, lefts, down

    def far_and_near(side, waits):
        return [
            call(
                functools.partial(expert_weight_grads, side, begin),
                (Sent(like((per_column, hidden_width // 4, width), BF)),) * 2,
                late([*left, *right]), expert_flops, waits=() if left is hidden else waits,
            )
            for left, right, begin in (
                (hidden, arrived_grads, 0), ([a[1] for a in moved], arrived, 0),
                ([a[2] for a in moved], arrived, 0),
            )
        ]

    def merged(half, waits):
        return call(
            add, (Sent(half[0]),), late([half[0], swapped(half[1], 1)]), 0, waits=waits
        )[0]

    def attention_back(keep, m, grad, token_grads, waits):
        return call(
            functools.partial(attend_back, keep),
            (token_wide, token_low)
            + (like((tokens, 2 * kv_width + (share if keep else 0)), BF),) * rows
            + ((Sent(like((tokens, LANES), BF)), Sent(sums_like)) if keep else ()),
            late([token_grads, shared[m] if keep else spread, attended[m][1], places[m],
                  attended[m][0], gain_f, grad, attended[m][7], attended[m][9], attended[m][3],
                  cosine, sine]),
            out_flops + 4 * score_flops, (dense,), [pltpu.VMEM((tokens, width), BF)] + out_scratch,
            (here, second), waits,
        )

    def parts_of(inner):
        return [inner[2]] + [swapped(inner[2 + s], s) for s in steps[1:]]

    def projection_back(keep, m, inner, parts, waits):
        return call(
            functools.partial(project_back, keep),
            (token_low,)
            + ((Sent(token_wide), Sent(sums_like))
               + (like((tokens, qkv_width // rows), BF),) * rows if keep else ()),
            (*parts, inner[1], Late(attended[m][6]), Late(gain_a), inner[0],
             *tables),
            qkv_flops, (dense,), [pltpu.VMEM((tokens, qkv_width), BF)] + qkv_scratch,
            (here,), waits,
        )

    entering = [inputs[m, 0] for m in pieces]
    targets = [cotangent[m, 0] for m in pieces]
    kept = forward(entering, entering, (), (gate_shards[2], up_shards[2]), down_shards)
    attended, applied, down_shards = kept[0], kept[2], kept[4]
    returned = [over_columns(a[0]) for a in applied]
    results = [
        call(
            combine, (Sent(token_wide), token_low),
            late([returned[m], attended[m][0], attended[m][1], spread, places[m]]),
            2 * slots * tokens * width, waits=() if m else (applied[1][0],),
        )
        for m in pieces
    ]
    came = [lax.ppermute(r[1], "section", [(0, 1)]) for r in results]

    kept = forward(came, entering, targets, (), down_shards)
    attended, arrived, applied, lefts, down_shards = kept
    hidden = [a[1] for a in applied]
    shared = [over_columns(a[4]) for a in applied]
    inner, outer = [], []
    for m in pieces:
        waits = (*lefts[1:], outer[0][0]) if m else (applied[1][4],)
        inner.append(attention_back(False, m, targets[m], shared[m], waits))
        outer.append(projection_back(False, m, inner[m], parts_of(inner[m]), ()))
    came = [lax.ppermute(o[0], "section", [(1, 0)]) for o in outer]

    given = [
        call(
            send_grads, (Sent(token_low), Sent(block_like)),
            (came[m], *late([targets[m], attended[m][1], dispatches[m]])),
            2 * slots * tokens * width, scalars=(first_flag,), waits=() if m else (inner[1][0],),
        )
        for m in pieces
    ]
    arrived_grads = [over_columns(g[1]) for g in given]
    moved = [
        call(
            expert_backward, (Sent(back_like), Sent(kept_like), Sent(kept_like)),
            late([arrived_grads[m], hidden[m], applied[m][2], applied[m][3], applied[m][0]]),
            3 * expert_flops, (*down_shards, *gate_shards, *up_shards), expert_scratch,
            (second,), () if m else (given[1][1],),
        )
        for m in pieces
    ]
    back = [over_columns(a[0]) for a in moved]
    inner = [attention_back(True, 0, given[0][0], back[0], (moved[1][0],))]
    parts = [parts_of(inner[0])]
    outer = [projection_back(True, 0, inner[0], parts[0], ())]
    far = far_and_near(1, (inner[0][0],))
    crossed = [swapped(merged(far[0], parts[0][1:]), 2)]
    inner.append(attention_back(
        True, 1, given[1][0], back[1], (outer[0][0], *(f[0] for f in far))
    ))
    parts.append(parts_of(inner[1]))
    crossed.append(swapped(merged(far[1], parts[1][1:]), 2))
    near = far_and_near(0, (inner[1][0],))
    o_grads = call(
        out_grads, (Sent(like((columns, rows * shard, share), BF)),),
        late([*lefts, *[p[s] for s in steps for p in parts]]),
        2 * width * length * micro * share, waits=(crossed[0],),
    )[0]
    outer.append(projection_back(True, 1, inner[1], parts[1], (o_grads,)))
    backs = [[o[3]] + [swapped(o[3 + s], s) for s in steps[1:]] for o in outer]
    last = merged(far[2], backs[1][1:])
    crossed.append(swapped(last, 2))
    w_grads = call(
        qkv_grads, (Sent(like((columns, rows * shard, qkv_width // rows + LANES), BF)),),
        late([*lefts, *[b[s] for s in steps for b in backs], *[a[5] for a in attended],
              *[a[6] for a in inner], *[o[2] for o in outer], *[a[7] for a in inner]]),
        2 * width * length * micro * qkv_width // rows,
        waits=(near[0][0], crossed[1], last),
    )[0]
    expert_grads = [
        n[0].astype(F32) + swapped(n[1], 1).astype(F32) + c.astype(F32)
        for n, c in zip(near, crossed)
    ]
    layer_outputs = call(
        last_outputs, (Sent(like((micro, tokens, width), F32)),),
        late([spread] + [v for m in pieces for v in (
            back[m], attended[m][0], attended[m][1], places[m], results[m][0])]),
        4 * slots * tokens * width, scalars=(second,), waits=(w_grads,),
    )[0]

    wide = share + qkv_width // rows + LANES
    pieces_out = call(
        fold, (like((shard, wide), F32),) * rows,
        late([over_columns(o_grads), over_columns(w_grads)]), 0,
        scratch=[pltpu.VMEM((rows * shard, wide), F32)], scalars=(here,),
    )
    pieces_out = [pieces_out[0]] + [swapped(pieces_out[s], s) for s in steps[1:]]
    o_grad, q_grad, k_grad, v_grad, r_grad, first, second_sum = call(
        finish,
        (like((shard, width), F32), like((shard, width), F32), like((shard, kv_width), F32),
         like((shard, kv_width), F32), like((shard, experts), F32), like((1, shard), F32),
         like((1, shard), F32)),
        pieces_out, 0, scratch=[pltpu.VMEM((shard, qkv_width), F32)], scalars=(here,),
    )

    return (
        layer_outputs[None, :, None],
        jnp.stack([o[1] for o in outer])[None, :, None],
        first,
        q_grad[None],
        k_grad[None],
        v_grad[None],
        o_grad[None],
        second_sum,
        r_grad[None],
        expert_grads[1][None],
        expert_grads[2][None],
        expert_grads[0][None],
    )


def solution(mesh):
    dense = P("section", ("row", "col"), None)
    gain = P("section", ("row", "col"))
    expert = P("section", "col", "row", None)
    token = P(None, "col", "row", None)
    layered = P("section", None, "col", "row", None)
    return jax.shard_map(
        on_device,
        mesh=mesh,
        in_specs=(
            token, token, P(None, "col", None), layered, gain, dense, dense, dense, dense, gain,
            dense, expert, expert, expert,
        ),
        out_specs=(
            layered, layered, gain, dense, dense, dense, dense, gain, dense, expert, expert, expert,
        ),
        check_vma=False,
    )
```

```python
import functools

import jax
import jax.numpy as jnp
from jax import lax
from jax.experimental import pallas as pl
from jax.experimental.pallas import tpu as pltpu
from jax.sharding import PartitionSpec as P

HEAD_DIM = 128
ROOMS = 16
EPSILON = 1e-06
LANES = 128
BF = jnp.bfloat16
F32 = jnp.float32
MIB = 1 << 20


def dot(left, right, contract=(1, 0)):
    return lax.dot_general(
        left, right, (((contract[0],), (contract[1],)), ((), ())), preferred_element_type=F32
    )


def like(shape, dtype):
    return jax.ShapeDtypeStruct(shape, dtype)


class Late:
    def __init__(self, source, target=None, sem=None):
        self.source, self.target, self.copy = source, target, None
        if target is not None:
            self.copy = pltpu.make_async_copy(source, target, sem)
            self.copy.start()
            self.waiting = True

    def ready(self):
        if self.waiting:
            self.copy.wait()
            self.waiting = False
        return self.target

    def __getitem__(self, index):
        return self.ready()[index]

    @property
    def shape(self):
        return self.source.shape


class Sent:
    def __init__(self, source, target=None, sems=None):
        self.source, self.target, self.sems, self.copies = source, target, sems, []

    def __getitem__(self, index):
        return self.source[index]

    def __setitem__(self, index, value):
        self.source[index] = value

    def send(self, *parts):
        for part in parts or (...,):
            at = len(self.copies)
            whole = part is ...
            copy = pltpu.make_async_copy(
                self.source if whole else self.source.at[part],
                self.target if whole else self.target.at[part],
                self.sems.at[at],
            )
            copy.start()
            self.copies.append(copy)

    @property
    def shape(self):
        return self.source.shape


class Raw:
    def __init__(self, source):
        self.source = source


PARTS = 4


def sent(out, *parts):
    if isinstance(out, Sent):
        out.send(*parts)


def call(body, outs, args, flops, far=(), scratch=(), scalars=(), waits=()):
    arrays = [a.source if isinstance(a, Late) else a for a in args]
    shapes = [o.source if isinstance(o, (Sent, Raw)) else o for o in outs]
    moved = sum(a.size * a.dtype.itemsize for a in (*arrays, *far, *shapes))
    count = len(scalars) + len(args) + len(far)
    kinds = [isinstance(a, Late) for a in args]
    out_kinds = [isinstance(o, Sent) for o in outs]
    raw_kinds = [isinstance(o, Raw) for o in outs]
    buffers = [pltpu.VMEM(a.shape, a.dtype) for a, k in zip(arrays, kinds) if k]
    buffers += [pltpu.VMEM(o.shape, o.dtype) for o, k in zip(shapes, out_kinds) if k]

    def run(*refs):
        given, refs = list(refs[:count]), refs[count + len(waits) :]
        results, refs = list(refs[: len(outs)]), refs[len(outs) :]
        own, rest = list(refs[: len(buffers)]), refs[len(buffers) :]
        sems, rest = (rest[0], rest[1:]) if buffers else (None, rest)
        used = 0
        for k, kind in enumerate(kinds):
            if kind:
                at = len(scalars) + k
                given[at] = Late(given[at], own[used], sems.at[used, 0])
                used += 1
        for k, kind in enumerate(out_kinds):
            if kind:
                results[k] = Sent(own[used], results[k], sems.at[used])
                used += 1
        body(*given, *results, *rest)
        for one in given:
            if isinstance(one, Late):
                one.ready()
        for one in results:
            if isinstance(one, Sent) and not one.copies:
                one.send()
        for one in results:
            if isinstance(one, Sent):
                done_with(one.copies)

    anywhere, local = pl.BlockSpec(memory_space=pltpu.HBM), pl.BlockSpec(memory_space=pltpu.VMEM)
    return pl.pallas_call(
        run,
        out_shape=tuple(shapes),
        in_specs=[pl.BlockSpec(memory_space=pltpu.SMEM)] * len(scalars)
        + [anywhere if k else local for k in kinds]
        + [anywhere] * (len(far) + len(waits)),
        out_specs=tuple(
            anywhere if k or raw else local for k, raw in zip(out_kinds, raw_kinds)
        ),
        scratch_shapes=buffers
        + ([pltpu.SemaphoreType.DMA((len(buffers), PARTS))] if buffers else [])
        + list(scratch),
        compiler_params=pltpu.CompilerParams(vmem_limit_bytes=60 * MIB),
        cost_estimate=pl.CostEstimate(
            flops=int(flops), bytes_accessed=int(moved), transcendentals=0
        ),
        name=body.func.__name__ if isinstance(body, functools.partial) else body.__name__,
    )(*scalars, *arrays, *far, *waits)


def late(values):
    return [Late(v) for v in values]


def nothing(*refs):
    pass


def hold(value, *waits):
    return pl.pallas_call(
        nothing,
        out_shape=like(value.shape, value.dtype),
        in_specs=[pl.BlockSpec(memory_space=pl.ANY)] * (1 + len(waits)),
        out_specs=pl.BlockSpec(memory_space=pl.ANY),
        input_output_aliases={0: 0},
        name="hold",
    )(value, *waits)


def swapped(value, step):
    rows = lax.axis_size("row")
    return lax.ppermute(value, "row", [(r, r ^ step) for r in range(rows)])


def norm_parts(stream):
    return lax.rsqrt(jnp.mean(stream * stream, -1, keepdims=True) + EPSILON)


def norm_back(grad, stream, gain):
    inverse = norm_parts(stream)
    unit = stream * inverse
    scaled = grad * gain
    back = inverse * (scaled - unit * jnp.mean(scaled * unit, -1, keepdims=True))
    return back, jnp.sum(grad * unit, 0, keepdims=True)


def turned(vectors, cosine, sine):
    done = []
    for at in range(0, vectors.shape[1], HEAD_DIM):
        one = vectors[:, at : at + HEAD_DIM]
        done.append(one * cosine + pltpu.roll(one, HEAD_DIM // 2, 1) * sine)
    return jnp.concatenate(done, -1) if len(done) > 1 else done[0]


def stacked_heads(value, first, count):
    return jnp.concatenate(
        [value[:, (first + j) * HEAD_DIM : (first + j + 1) * HEAD_DIM] for j in range(count)], 0
    )


def unstacked_heads(value, count):
    tokens = value.shape[0] // count
    return jnp.concatenate([value[j * tokens : (j + 1) * tokens] for j in range(count)], 1)


def cuts_of(total, most=512):
    return [(at, min(most, total - at)) for at in range(0, total, most)]


def project(
    flag, came, entering, gain, cosine, sine, dense, stream, normed, query, pair, weights, sems
):
    width = stream.shape[1]
    cuts = cuts_of(weights.shape[1])
    copies = [
        pltpu.make_async_copy(
            dense.at[:, pl.ds(at, size)], weights.at[:, pl.ds(at, size)], sems.at[k]
        )
        for k, (at, size) in enumerate(cuts)
    ]
    for copy in copies:
        copy.start()
    x = jnp.where(flag[0] > 0, came[...].astype(F32), entering[...].astype(F32))
    stream[...] = x
    low = (x * norm_parts(x) * gain[...]).astype(BF)
    normed[...] = low
    keys = pair.shape[1] // 2
    for copy, (at, size) in zip(copies, cuts):
        copy.wait()
        part = dot(low, weights[:, at : at + size])
        for begin in range(at, at + size, HEAD_DIM):
            head = part[:, begin - at : begin - at + HEAD_DIM]
            if begin < width + keys:
                head = turned(head, cosine[...], sine[...])
            head = head.astype(BF)
            if begin < width:
                query[:, begin : begin + HEAD_DIM] = head
            else:
                pair[:, begin - width : begin - width + HEAD_DIM] = head


def project_all(entering, gain, cosine, sine, dense, pair, *rest):
    outs, (weights, sems) = rest[:-2], rest[-2:]
    micro, tokens, width = entering.shape
    cuts = cuts_of(weights.shape[1])
    copies = [
        pltpu.make_async_copy(
            dense.at[:, pl.ds(at, size)], weights.at[:, pl.ds(at, size)], sems.at[k]
        )
        for k, (at, size) in enumerate(cuts)
    ]
    for copy in copies:
        copy.start()
    lows = []
    for m in range(micro):
        x = entering[m].astype(F32)
        outs[2 * m][...] = x
        lows.append((x * norm_parts(x) * gain[...]).astype(BF))
    low = jnp.concatenate(lows, 0)
    cosines = jnp.concatenate([cosine[...]] * micro, 0)
    sines = jnp.concatenate([sine[...]] * micro, 0)
    keys = pair.shape[1] // 2
    for copy, (at, size) in zip(copies, cuts):
        copy.wait()
        part = dot(low, weights[:, at : at + size])
        for begin in range(at, at + size, HEAD_DIM):
            head = part[:, begin - at : begin - at + HEAD_DIM]
            if begin < width + keys:
                head = turned(head, cosines, sines)
            head = head.astype(BF)
            if begin < width:
                for m in range(micro):
                    outs[2 * m + 1][:, begin : begin + HEAD_DIM] = head[
                        m * tokens : (m + 1) * tokens
                    ]
            else:
                pair[:, begin - width : begin - width + HEAD_DIM] = head


def slot_experts(slots):
    own = lax.broadcasted_iota(jnp.int32, (slots, LANES), 0) // ROOMS
    return own == lax.broadcasted_iota(jnp.int32, (slots, LANES), 1)


def scaled_rows(dispatch, gates, low):
    here = slot_experts(dispatch.shape[0])
    scale = jnp.sum(jnp.where(here, dot(dispatch, gates.astype(BF)), 0.0), -1, keepdims=True)
    return (dot(dispatch, low) * scale).astype(BF)


def attend(
    keep, m, stream, query, pair0, pair1, pair2, pair3, bias, gain, chosen, dispatch, *rest,
):
    (normed, target), rest = (rest[:2], rest[2:]) if keep else ((None, None), rest)
    dense, middle, gates, outgoing = rest[:4]
    kept, (mixed, weights, router, sems) = rest[4:-4], rest[-4:]
    width = stream.shape[1]
    block = (outgoing.shape[0], -1, width)
    per = dispatch.shape[0] // outgoing.shape[0]
    at = dense.shape[1] - width - LANES
    copies = [
        pltpu.make_async_copy(dense.at[:, pl.ds(at + LANES, width)], weights, sems.at[0]),
        pltpu.make_async_copy(dense.at[:, pl.ds(at, LANES)], router, sems.at[1]),
    ]
    if keep:
        own = [(stream, kept[3]), (query, kept[4]), (normed, kept[5])]
        own += [(p, kept[6].at[k]) for k, p in enumerate((pair0, pair1, pair2, pair3))]
        copies += [pltpu.make_async_copy(a, b, sems.at[2 + k]) for k, (a, b) in enumerate(own)]
    for copy in copies:
        copy.start()
    tokens = stream.shape[0]
    pairs = jnp.concatenate(
        [p[m * tokens : (m + 1) * tokens, :] for p in (pair0, pair1, pair2, pair3)], 0
    )
    kv_heads = pairs.shape[1] // (2 * HEAD_DIM)
    group = width // HEAD_DIM // kv_heads
    biases = jnp.concatenate([bias[...]] * group, 0)
    for h in range(kv_heads):
        keys = pairs[:, h * HEAD_DIM : (h + 1) * HEAD_DIM]
        values = pairs[:, (kv_heads + h) * HEAD_DIM : (kv_heads + h + 1) * HEAD_DIM]
        queries = stacked_heads(query, h * group, group)
        scores = dot(queries, keys, (1, 1)) * HEAD_DIM ** (-0.5) + biases
        expo = jnp.exp(scores - jnp.max(scores, -1, keepdims=True))
        weight = (expo * (1.0 / jnp.sum(expo, -1, keepdims=True))).astype(BF)
        if keep:
            kept[0][h] = weight
        done = dot(weight, values).astype(BF)
        for j in range(group):
            begin = (h * group + j) * HEAD_DIM
            mixed[:, begin : begin + HEAD_DIM] = done[j * tokens : (j + 1) * tokens]
    if keep:
        kept[1][...] = mixed[...]
        sent(kept[0])
        sent(kept[1])
    copies[0].wait()
    x = stream[...] + dot(mixed[...], weights[...])
    middle[...] = x
    sent(middle)
    low = (x * norm_parts(x) * gain[...]).astype(BF)
    if keep:
        kept[2][...] = low
        sent(kept[2])
    copies[1].wait()
    taken = chosen[...] > 0
    logits = jnp.where(taken, dot(low, router[...]), -1e30)
    expo = jnp.where(taken, jnp.exp(logits - jnp.max(logits, -1, keepdims=True)), 0.0)
    share = expo / jnp.sum(expo, -1, keepdims=True)
    gates[...] = share
    sent(gates)
    slots = dispatch[...]
    outgoing[:, :per, :] = dot(slots, low).astype(BF).reshape(block)
    if keep:
        sent(outgoing, (slice(None), pl.ds(0, per)))
        outgoing[:, per:, :] = scaled_rows(slots, share, target[...]).reshape(block)
        sent(outgoing, (slice(None), pl.ds(per, per)))
    done_with(copies[2:])


class Fetched:
    def __init__(self, shards, weights, sems):
        self.weights = weights
        self.copies = {}
        for j in range(weights.shape[1]):
            for k in range(weights.shape[0]):
                self.copies[k, j] = [
                    pltpu.make_async_copy(
                        shards[k][p].at[j],
                        weights.at[k, j, pl.ds(p * shards[k][p].shape[1], shards[k][p].shape[1])],
                        sems.at[k, j, p],
                    )
                    for p in range(4)
                ]
        for k in range(weights.shape[0]):
            self.start(k, 0)

    def start(self, k, j):
        for copy in self.copies.get((k, j), ()):
            copy.start()

    def ready(self, k, j):
        done_with(self.copies[k, j])
        self.start(k, j + 1)


def done_with(copies):
    for copy in copies:
        copy.wait()


def rows_of(value, j, begin=0):
    columns, unused, width = value.shape
    at = begin + j * ROOMS
    return value[:, at : at + ROOMS, :].reshape(columns * ROOMS, width)


def put_rows(out, j, rows, inner):
    at, width = j * ROOMS, rows.shape[1]
    out[:, at : at + ROOMS, :width] = rows.reshape(-1, ROOMS, width)
    high = inner.astype(BF).astype(F32)
    lane = lax.broadcasted_iota(jnp.int32, (rows.shape[0], LANES), 1)
    both = jnp.where(lane == 0, high, jnp.where(lane == 1, inner - high, 0.0))
    out[:, at : at + ROOMS, width:] = both.astype(BF).reshape(-1, ROOMS, LANES)


def expert_forward(both, arrived, *refs):
    shards = [refs[4 * k : 4 * k + 4] for k in range(3)]
    outs, weights, sems = refs[12:-2], refs[-2], refs[-1]
    fetched = Fetched(shards, weights, sems)
    per = weights.shape[1] * ROOMS
    for j in range(weights.shape[1]):
        at = j * ROOMS
        rows = rows_of(arrived, j)
        fetched.ready(0, j)
        gate = dot(rows, weights[0, j], (1, 1))
        fetched.ready(1, j)
        lifted = dot(rows, weights[1, j], (1, 1))
        square = gate * gate
        bend = jnp.tanh(0.7978845608028654 * gate * (1.0 + 0.044715 * square))
        active = 0.5 * gate * (1.0 + bend)
        hidden = (active * lifted).astype(BF)
        fetched.ready(2, j)
        made = dot(hidden, weights[2, j]).astype(BF)
        outs[0][:, at : at + ROOMS, :] = made.reshape(-1, ROOMS, made.shape[1])
        sent(outs[0], (slice(None), pl.ds(at, ROOMS)))
        if both:
            slope = 0.5 * (1.0 + bend) + 0.5 * gate * (1.0 - bend * bend) * (
                0.7978845608028654 * (1.0 + 3 * 0.044715 * square)
            )
            bent = slope * lifted
            outs[1][j] = hidden
            outs[2][j] = active.astype(BF)
            outs[3][j] = bent.astype(BF)
            hidden_grads = dot(rows_of(arrived, j, per), weights[2, j], (1, 1))
            gate_part = (hidden_grads * bent).astype(BF)
            lifted_part = (hidden_grads * active).astype(BF)
            inner = jnp.sum(hidden_grads * hidden.astype(F32), -1, keepdims=True)
            back = dot(gate_part, weights[0, j]) + dot(lifted_part, weights[1, j])
            put_rows(outs[4], j, back.astype(BF), inner)
            sent(outs[4], (slice(None), pl.ds(at, ROOMS)))
            for out in outs[1:4]:
                sent(out, j)


def combine(returned, middle, gates, spread, places, result, low):
    weights = (dot(gates[...].astype(BF), spread[...]) * places[...].astype(F32)).astype(BF)
    done = middle[...] + dot(weights, returned[...].reshape(-1, returned.shape[2]))
    result[...] = done
    sent(result)
    low[...] = done.astype(BF)


def last_outputs(flag, spread, *refs):
    out = refs[-1]
    width = out.shape[2]
    for m in range(out.shape[0]):
        returned, middle, gates, places, before = refs[5 * m : 5 * m + 5]
        weights = (dot(gates[...].astype(BF), spread[...]) * places[...].astype(F32)).astype(BF)
        rows = returned[:, :, :width].reshape(-1, width)
        out[m] = jnp.where(flag[0] > 0, middle[...] + dot(weights, rows), before[...])


def send_grads(flag, came, target, gates, dispatch, grad, outgoing):
    low = jnp.where(flag[0] > 0, came[...], target[...])
    grad[...] = low
    sent(grad)
    outgoing[...] = scaled_rows(dispatch[...], gates[...], low).reshape(outgoing.shape)


def expert_backward(flag, arrived, hidden, active, bent, produced, *refs):
    shards = [refs[4 * k : 4 * k + 4] for k in range(3)]
    out, gate_back, lifted_back, weights, sems = refs[12:]
    fetched = Fetched(shards, weights, sems)
    for j in range(weights.shape[1]):
        fetched.ready(0, j)
        hidden_grads = dot(rows_of(arrived, j), weights[0, j], (1, 1))
        gate_part = (hidden_grads * bent[j].astype(F32)).astype(BF)
        lifted_part = (hidden_grads * active[j].astype(F32)).astype(BF)
        gate_back[j] = gate_part
        lifted_back[j] = lifted_part
        inner = jnp.sum(hidden_grads * hidden[j].astype(F32), -1, keepdims=True)
        fetched.ready(1, j)
        done = dot(gate_part, weights[1, j])
        fetched.ready(2, j)
        done = (done + dot(lifted_part, weights[2, j])).astype(BF)
        put_rows(out, j, jnp.where(flag[0] > 0, rows_of(produced, j), done), inner)
        sent(out, (slice(None), pl.ds(j * ROOMS, ROOMS)))
        sent(gate_back, j)
        sent(lifted_back, j)


def attend_back(
    keep, row, flag, token_grads, before, gates, places, middle, gain, grad, query, pairs, probs,
    cosine, sine, dense, middle_grads, query_back, part0, part1, part2, part3, *rest,
):
    tokens, width = middle.shape
    kept, (branch, weights, router, sems) = rest[:-4], rest[-4:]
    at = dense.shape[1] - width - LANES
    copies = [
        pltpu.make_async_copy(dense.at[:, pl.ds(at, LANES)], router, sems.at[1]),
        pltpu.make_async_copy(dense.at[:, pl.ds(at + LANES, width)], weights, sems.at[0]),
    ]
    for copy in copies:
        copy.start()
    came = token_grads[...]
    if keep:
        came = jnp.where(flag[0] > 0, before[...], came)
    came = came.reshape(-1, came.shape[2])
    place = places[...]
    here = slot_experts(came.shape[0])
    notes = came[:, width:].astype(F32)
    high = jnp.where(here, notes[:, :1], 0.0).astype(BF)
    rest_of = jnp.where(here, notes[:, 1:2], 0.0).astype(BF)
    inner = dot(place, high) + dot(place, rest_of)
    logit_grads = (inner - gates[...] * jnp.sum(inner, -1, keepdims=True)).astype(BF)
    ffn_grads = dot(place, came[:, :width])
    copies[0].wait()
    ffn_grads = ffn_grads + dot(logit_grads, router[...], (1, 1))
    part, total = norm_back(ffn_grads, middle[...], gain[...])
    above = grad[...].astype(F32) + part
    middle_grads[...] = above
    low = above.astype(BF)
    if keep:
        kept[0][...] = logit_grads
        kept[1][...] = jnp.broadcast_to(total, kept[1].shape)
        sent(kept[0])
        sent(kept[1])
        branch[...] = low
        share = width // 4
        for s, part in enumerate((part0, part1, part2, part3)):
            begin = pl.multiple_of((row[0] ^ s) * share, LANES)
            part[:, part.shape[1] - share :] = branch[:, pl.ds(begin, share)]
    copies[1].wait()
    mixed_grads = dot(low, weights[...], (1, 1)).astype(BF)
    pairs = pairs[...].reshape(-1, pairs.shape[2])
    kv_heads = pairs.shape[1] // (2 * HEAD_DIM)
    group = width // HEAD_DIM // kv_heads
    scale = HEAD_DIM ** (-0.5)
    parts = (part0, part1, part2, part3)
    for h in range(kv_heads):
        keys = pairs[:, h * HEAD_DIM : (h + 1) * HEAD_DIM]
        values = pairs[:, (kv_heads + h) * HEAD_DIM : (kv_heads + h + 1) * HEAD_DIM]
        queries = stacked_heads(query, h * group, group)
        top = stacked_heads(mixed_grads, h * group, group)
        weight = probs[h]
        wide = weight.astype(F32)
        weight_grads = dot(top, values, (1, 1))
        value_grads = dot(weight, top, (0, 0)).astype(BF)
        inner = wide * weight_grads
        score_grads = (inner - wide * jnp.sum(inner, -1, keepdims=True)).astype(BF)
        query_grads = dot(score_grads, keys) * scale
        key_grads = (dot(score_grads, queries, (0, 0)) * scale).astype(BF)
        for j in range(group):
            begin = (h * group + j) * HEAD_DIM
            one = query_grads[j * tokens : (j + 1) * tokens]
            query_back[:, begin : begin + HEAD_DIM] = turned(one, cosine[...], -sine[...]).astype(BF)
        for p, part in enumerate(parts):
            part[:, h * HEAD_DIM : (h + 1) * HEAD_DIM] = key_grads[p * tokens : (p + 1) * tokens]
            begin = (kv_heads + h) * HEAD_DIM
            part[:, begin : begin + HEAD_DIM] = value_grads[p * tokens : (p + 1) * tokens]


def project_back(
    keep, row, part0, part1, part2, part3, query_back, stream, gain, middle_grads, cosine, sine,
    dense, low, *rest,
):
    width = stream.shape[1]
    kept, (backs, weights, sems) = rest[:-3], rest[-3:]
    cuts = cuts_of(weights.shape[1])
    copies = [
        pltpu.make_async_copy(
            dense.at[:, pl.ds(at, size)], weights.at[:, pl.ds(at, size)], sems.at[k]
        )
        for k, (at, size) in enumerate(cuts)
    ]
    for copy in copies:
        copy.start()
    pairs = weights.shape[1] - width
    total = sum(part[:, :pairs].astype(F32) for part in (part0, part1, part2, part3))
    keys = pairs // 2
    backs[:, :width] = query_back[...]
    backs[:, width : width + keys] = turned(total[:, :keys], cosine[...], -sine[...]).astype(BF)
    backs[:, width + keys :] = total[:, keys:].astype(BF)
    if keep:
        share = backs.shape[1] // 4
        for s, out in enumerate(kept[1:]):
            out[...] = backs[:, pl.ds(pl.multiple_of((row[0] ^ s) * share, LANES), share)]
    above = jnp.zeros(stream.shape, F32)
    for copy, (at, size) in zip(copies, cuts):
        copy.wait()
        above = above + dot(backs[:, at : at + size], weights[:, at : at + size], (1, 1))
    part, unused = norm_back(above, stream[...], gain[...])
    done = middle_grads[...] + part
    if keep:
        kept[0][...] = done
    low[...] = done.astype(BF)


def expert_weight_grads(half, begin, left0, left1, right0, right1, first, second):
    size = first.shape[1]
    wide = 2 * size
    for j in range(first.shape[0]):
        total = dot(left0[j, :, half * wide : (half + 1) * wide], rows_of(right0, j, begin), (0, 0))
        total = total + dot(
            left1[j, :, half * wide : (half + 1) * wide], rows_of(right1, j, begin), (0, 0)
        )
        first[j] = total[:size].astype(BF)
        second[j] = total[size:].astype(BF)


def add(one, other, total):
    total[...] = (one[...].astype(F32) + other[...].astype(F32)).astype(BF)


def pack(*refs):
    for k, value in enumerate(refs[:-1]):
        refs[-1][k] = value[...]


def stacked(refs):
    return jnp.concatenate([r[...] for r in refs], 0)


def by_owner(out, grads, begin):
    columns, lines, unused = out.shape
    size = lines // 4
    for c in range(columns):
        some = [grads[(r * columns + c) * size : (r * columns + c + 1) * size] for r in range(4)]
        out[c, :, begin : begin + grads.shape[1]] = jnp.concatenate(some, 0).astype(BF)


def out_grads(*refs):
    lefts, rights, normed, logits, gains, out = (
        refs[:4], refs[4:12], refs[12:14], refs[14:16], refs[16:18], refs[18],
    )
    share = out.shape[2] - LANES
    left = jnp.concatenate([one[k] for one in lefts for k in (2, 3)], 0)
    right = jnp.concatenate([r[:, r.shape[1] - share :] for r in rights], 0)
    by_owner(out, dot(left, right, (0, 0)), 0)
    width = left.shape[1]
    line = lax.broadcasted_iota(jnp.int32, (LANES, width), 0)
    sums = jnp.where(line == LANES - 1, gains[0][:1, :] + gains[1][:1, :], 0.0)
    by_owner(out, dot(stacked(normed), stacked(logits), (0, 0)) + sums.T, share)


def qkv_grads(*refs):
    lefts, rights, out = refs[:4], refs[4:12], refs[12]
    left = jnp.concatenate([one[k] for one in lefts for k in (0, 1)], 0)
    by_owner(out, dot(left, stacked(rights), (0, 0)), 0)


def fold(row, first, second, out0, out1, out2, out3, total):
    share = first.shape[2]
    total[:, :share] = jnp.sum(first[...].astype(F32), 0)
    total[:, share:] = jnp.sum(second[...].astype(F32), 0)
    for s, out in enumerate((out0, out1, out2, out3)):
        size = out.shape[0]
        out[...] = total[pl.ds(pl.multiple_of((row[0] ^ s) * size, 8), size), :]


def finish(
    row, in0, in1, in2, in3, w_query, w_key, w_value, gain, o_grad, q_grad, k_grad, v_grad, r_grad,
    first, second, total,
):
    share = o_grad.shape[1] // 4
    piece = total.shape[1] // 4
    ins = (in0, in1, in2, in3)
    for s, one in enumerate(ins):
        where = row[0] ^ s
        o_grad[:, pl.ds(pl.multiple_of(where * share, LANES), share)] = one[:, :share]
        total[:, pl.ds(pl.multiple_of(where * piece, LANES), piece)] = one[:, share + LANES :]
    rest = sum(one[:, share : share + LANES] for one in ins)
    r_grad[...] = rest[:, : r_grad.shape[1]]
    second[...] = rest.T[LANES - 1 :, :]
    begin, inner = 0, jnp.zeros((total.shape[0], 1), F32)
    for out, weight in ((q_grad, w_query), (k_grad, w_key), (v_grad, w_value)):
        part = total[:, begin : begin + out.shape[1]]
        out[...] = part
        inner = inner + jnp.sum(part * weight[...].astype(F32), -1, keepdims=True)
        begin += out.shape[1]
    line = jnp.broadcast_to(inner, (total.shape[0], LANES)).T[:1, :]
    first[...] = line / gain[...].astype(F32)


def over_columns(value):
    return lax.all_to_all(value, "col", split_axis=0, concat_axis=0, tiled=True)


def on_device(
    inputs, cotangent, segment_ids, routes, attn_gain, w_query, w_key, w_value, w_out, ffn_gain,
    w_router, w_gate, w_up, w_down,
):
    section = lax.axis_index("section")
    row = lax.axis_index("row")
    rows = lax.axis_size("row")
    columns = lax.axis_size("col")
    micro, tokens, width = inputs.shape[0], inputs.shape[2], inputs.shape[3]
    experts = w_router.shape[2]
    per_column = w_gate.shape[1]
    hidden_width = w_gate.shape[2] * rows
    kv_width = w_key.shape[2]
    qkv_width = width + 2 * kv_width
    slots = experts * ROOMS
    share = width // rows
    shard = width // (rows * columns)
    heads = width // HEAD_DIM
    kv_heads = kv_width // HEAD_DIM
    length = rows * tokens
    pieces = range(micro)
    steps = range(rows)
    here = row.astype(jnp.int32)[None]
    second = (section == 1).astype(jnp.int32)[None]
    block = (columns, slots // columns, width)

    dense = jnp.concatenate(
        [w_query[0], w_key[0], w_value[0], w_router[0], attn_gain[0][:, None], ffn_gain[0][:, None],
         jnp.zeros((shard, LANES - experts - 2), BF), w_out[0]], 1
    )
    dense = lax.all_gather(dense, ("row", "col"), axis=0, tiled=True)
    small = dense[:, qkv_width : qkv_width + LANES]
    gain_a = small[:, experts].astype(F32)[None, :]
    gain_f = small[:, experts + 1].astype(F32)[None, :]

    def shards_of(own):
        two = swapped(own, 2)
        return own, swapped(own, 1), two, swapped(two, 1)

    gate_shards, up_shards = shards_of(w_gate[0]), shards_of(w_up[0])
    down_shards = (w_down[0], swapped(w_down[0], 1), swapped(w_down[0], 2))

    lane = jnp.arange(LANES, dtype=jnp.int32)
    half = HEAD_DIM // 2
    freqs = 10000.0 ** (-2.0 * jnp.arange(half).astype(F32) / HEAD_DIM)
    positions = row * tokens + jnp.arange(tokens, dtype=jnp.int32)
    angles = positions.astype(F32)[:, None] * freqs[None, :]
    cosine = jnp.concatenate([jnp.cos(angles)] * 2, 1)
    sine = jnp.concatenate([-jnp.sin(angles), jnp.sin(angles)], 1)
    key_positions = jnp.concatenate(
        [(row ^ step) * tokens + jnp.arange(tokens, dtype=jnp.int32) for step in steps]
    )
    spread = (lane[:, None] == jnp.arange(slots, dtype=jnp.int32)[None, :] // ROOMS).astype(BF)
    below = (jnp.arange(tokens)[:, None] > jnp.arange(tokens)[None, :]).astype(BF)
    biases, chosens, places, dispatches = [], [], [], []
    for m in pieces:
        segments = segment_ids[m, 0]
        own_segments = lax.dynamic_slice_in_dim(segments, row * tokens, tokens)
        key_segments = jnp.concatenate(
            [lax.dynamic_slice_in_dim(segments, (row ^ s) * tokens, tokens) for s in steps]
        )
        counted = (key_positions[None, :] <= positions[:, None]) & (
            key_segments[None, :] == own_segments[:, None]
        )
        biases.append(jnp.where(counted, 0.0, -1e30).astype(F32))
        chosen = jnp.any(routes[0, m, 0][:, :, None] == lane[None, None, :], 1)
        chosens.append(chosen.astype(F32))
        rank = dot(below, chosen.astype(BF))
        rank = jnp.where(chosen, rank, -1.0)[:, :experts]
        place = (
            rank[:, :, None] == jnp.arange(ROOMS, dtype=F32)[None, None, :]
        ).reshape(tokens, slots)
        places.append(place.astype(BF))
        dispatches.append(place.T.astype(BF))

    token_low, token_wide = like((tokens, width), BF), like((tokens, width), F32)
    pair_like = like((tokens, 2 * kv_width), BF)
    block_like = like(block, BF)
    sums_like = like((8, width), F32)
    kept_like = like((per_column, columns * ROOMS, hidden_width), BF)
    probs_like = like((kv_heads, heads // kv_heads * tokens, length), BF)
    qkv_scratch = [pltpu.VMEM((width, qkv_width), BF), pltpu.SemaphoreType.DMA((8,))]
    out_scratch = [
        pltpu.VMEM((width, width), BF), pltpu.VMEM((width, LANES), BF),
        pltpu.SemaphoreType.DMA((16,)),
    ]
    expert_scratch = [
        pltpu.VMEM((3, per_column, hidden_width, width), BF),
        pltpu.SemaphoreType.DMA((3, per_column, 4)),
    ]
    qkv_flops = 2 * tokens * width * qkv_width
    out_flops = 2 * tokens * width * width + 2 * slots * tokens * width
    score_flops = 2 * heads * tokens * length * HEAD_DIM
    expert_flops = 2 * slots * hidden_width * width

    per = slots // columns
    back_like = like((columns, per, width + LANES), BF)
    double_like = like((columns, 2 * per, width), BF)
    lanes_like = like((tokens, LANES), F32)
    tables = late([cosine, sine])
    first_flag = (1 - second)

    def forward(came, entering, targets, waits, down):
        keep = bool(targets)
        projected, pairs = [], []
        if keep:
            for m in pieces:
                projected.append(
                    call(
                        project, (token_wide, token_low, token_low, pair_like),
                        (came[m], Late(entering[m]), Late(gain_a), *tables), qkv_flops, (dense,),
                        qkv_scratch, (second,), waits=[p[0] for p in projected],
                    )
                )
                pairs.append([projected[m][3]] + [swapped(projected[m][3], s) for s in steps[1:]])
        else:
            pair, *streams = call(
                project_all,
                (like((micro * tokens, 2 * kv_width), BF),) + (token_wide, token_low) * micro,
                (Late(inputs[:, 0]), Late(gain_a), *tables), micro * qkv_flops, (dense,),
                qkv_scratch, waits=waits,
            )
            projected = [(streams[2 * m], None, streams[2 * m + 1]) for m in pieces]
            pairs = [[pair] + [swapped(pair, s) for s in steps[1:]]] * micro
        attended = [
            call(
                functools.partial(attend, keep, 0 if keep else m),
                (Sent(token_wide), Sent(lanes_like), Sent(double_like if keep else block_like))
                + ((Sent(probs_like), Sent(token_low), Sent(token_low), Raw(token_wide),
                    Raw(token_low), Raw(token_low), Raw(like((rows, tokens, 2 * kv_width), BF)))
                   if keep else ()),
                (projected[m][0], projected[m][2], *pairs[m],
                 *late([biases[m], gain_f, chosens[m], dispatches[m]]),
                 *((projected[m][1], Late(targets[m])) if keep else ())),
                out_flops + 2 * score_flops, (dense,), [pltpu.VMEM((tokens, width), BF)] + out_scratch,
            )
            for m in pieces
        ]
        arrived = [over_columns(a[2]) for a in attended]
        lefts, ready = [], ()
        if keep:
            left = call(
                pack, (Sent(like((2 * micro, tokens, width), BF)),),
                late([a[8] for a in attended] + [a[4] for a in attended]), 0,
            )[0]
            two = swapped(left, 2)
            lefts = [left, swapped(left, 1), two, swapped(two, 1)]
            ready = (two,)
        else:
            two = hold(down[2], arrived[0], attended[1][2])
            down = (*down[:2], two, swapped(two, 1))
        applied = [
            call(
                functools.partial(expert_forward, keep),
                (Sent(block_like),)
                + ((Sent(kept_like),) * 3 + (Sent(back_like),) if keep else ()),
                late([arrived[m]]), (6 if keep else 3) * expert_flops,
                (*gate_shards, *up_shards, *down), expert_scratch,
                waits=ready if m else (attended[1][2],),
            )
            for m in pieces
        ]
        return attended, arrived, applied, lefts, down

    def far_and_near(side, waits):
        return [
            call(
                functools.partial(expert_weight_grads, side, begin),
                (Sent(like((per_column, hidden_width // 4, width), BF)),) * 2,
                late([*left, *right]), expert_flops, waits=waits,
            )
            for left, right, begin in (
                (hidden, arrived_grads, 0), ([a[1] for a in moved], arrived, 0),
                ([a[2] for a in moved], arrived, 0),
            )
        ]

    def merged(half, waits):
        return call(
            add, (Sent(half[0]),), late([half[0], swapped(half[1], 1)]), 0, waits=waits
        )[0]

    def attention_back(keep, m, grad, token_grads, waits):
        return call(
            functools.partial(attend_back, keep),
            (token_wide, token_low)
            + (like((tokens, 2 * kv_width + (share if keep else 0)), BF),) * rows
            + ((Sent(like((tokens, LANES), BF)), Sent(sums_like)) if keep else ()),
            late([token_grads, shared[m] if keep else spread, attended[m][1], places[m],
                  attended[m][0], gain_f, grad, attended[m][7], attended[m][9], attended[m][3],
                  cosine, sine]),
            out_flops + 4 * score_flops, (dense,), [pltpu.VMEM((tokens, width), BF)] + out_scratch,
            (here, second), waits,
        )

    def parts_of(inner):
        return [inner[2]] + [swapped(inner[2 + s], s) for s in steps[1:]]

    def projection_back(keep, m, inner, parts, waits):
        return call(
            functools.partial(project_back, keep),
            (token_low,)
            + ((Sent(token_wide),) + (like((tokens, qkv_width // rows), BF),) * rows if keep else ()),
            (*parts, inner[1], Late(attended[m][6]), Late(gain_a), inner[0],
             *tables),
            qkv_flops, (dense,), [pltpu.VMEM((tokens, qkv_width), BF)] + qkv_scratch,
            (here,), waits,
        )

    entering = [inputs[m, 0] for m in pieces]
    targets = [cotangent[m, 0] for m in pieces]
    kept = forward(entering, entering, (), (gate_shards[2], up_shards[2]), down_shards)
    attended, applied, down_shards = kept[0], kept[2], kept[4]
    returned = [over_columns(a[0]) for a in applied]
    results = [
        call(
            combine, (Sent(token_wide), token_low),
            late([returned[m], attended[m][0], attended[m][1], spread, places[m]]),
            2 * slots * tokens * width, waits=() if m else (applied[1][0],),
        )
        for m in pieces
    ]
    came = [lax.ppermute(r[1], "section", [(0, 1)]) for r in results]

    kept = forward(came, entering, targets, (), down_shards)
    attended, arrived, applied, lefts, down_shards = kept
    hidden = [a[1] for a in applied]
    shared = [over_columns(a[4]) for a in applied]
    inner, outer = [], []
    for m in pieces:
        waits = (*lefts[1:], outer[0][0]) if m else (applied[1][4],)
        inner.append(attention_back(False, m, targets[m], shared[m], waits))
        outer.append(projection_back(False, m, inner[m], parts_of(inner[m]), ()))
    came = [lax.ppermute(o[0], "section", [(1, 0)]) for o in outer]

    given = [
        call(
            send_grads, (Sent(token_low), Sent(block_like)),
            (came[m], *late([targets[m], attended[m][1], dispatches[m]])),
            2 * slots * tokens * width, scalars=(first_flag,), waits=() if m else (inner[1][0],),
        )
        for m in pieces
    ]
    arrived_grads = [over_columns(g[1]) for g in given]
    moved = [
        call(
            expert_backward, (Sent(back_like), Sent(kept_like), Sent(kept_like)),
            late([arrived_grads[m], hidden[m], applied[m][2], applied[m][3], applied[m][0]]),
            3 * expert_flops, (*down_shards, *gate_shards, *up_shards), expert_scratch,
            (second,), () if m else (given[1][1],),
        )
        for m in pieces
    ]
    back = [over_columns(a[0]) for a in moved]
    far = far_and_near(1, ())
    down_far = merged(far[0], ())
    crossed = [swapped(down_far, 2)]
    inner = [attention_back(True, 0, given[0][0], back[0], (moved[1][0], down_far))]
    parts = [parts_of(inner[0])]
    inner.append(attention_back(True, 1, given[1][0], back[1], (inner[0][0], far[1][0])))
    parts.append(parts_of(inner[1]))
    outer = [projection_back(True, 0, inner[0], parts[0], (inner[1][0],))]
    o_grads = call(
        out_grads, (Sent(like((columns, rows * shard, share + LANES), BF)),),
        late([*lefts, *[p[s] for s in steps for p in parts], *[a[5] for a in attended],
              *[a[6] for a in inner], *[a[7] for a in inner]]),
        2 * width * length * micro * share, waits=(crossed[0], outer[0][0]),
    )[0]
    outer.append(projection_back(True, 1, inner[1], parts[1], (o_grads,)))
    far[2] = far_and_near(1, (outer[1][0],))[2]
    backs = [[o[2]] + [swapped(o[2 + s], s) for s in steps[1:]] for o in outer]
    last = [merged(f, backs[1][1:]) for f in far[1:]]
    crossed += [swapped(one, 2) for one in last]
    w_grads = call(
        qkv_grads, (Sent(like((columns, rows * shard, qkv_width // rows), BF)),),
        late([*lefts, *[b[s] for s in steps for b in backs]]),
        2 * width * length * micro * qkv_width // rows, waits=(last[0],),
    )[0]
    near = far_and_near(0, (w_grads, last[1]))
    expert_grads = [
        n[0].astype(F32) + swapped(n[1], 1).astype(F32) + c.astype(F32)
        for n, c in zip(near, crossed)
    ]
    layer_outputs = call(
        last_outputs, (Sent(like((micro, tokens, width), F32)),),
        late([spread] + [v for m in pieces for v in (
            back[m], attended[m][0], attended[m][1], places[m], results[m][0])]),
        4 * slots * tokens * width, scalars=(second,), waits=(w_grads,),
    )[0]

    wide = share + qkv_width // rows + LANES
    pieces_out = call(
        fold, (like((shard, wide), F32),) * rows,
        late([over_columns(o_grads), over_columns(w_grads)]), 0,
        scratch=[pltpu.VMEM((rows * shard, wide), F32)], scalars=(here,),
    )
    pieces_out = [pieces_out[0]] + [swapped(pieces_out[s], s) for s in steps[1:]]
    o_grad, q_grad, k_grad, v_grad, r_grad, first, second_sum = call(
        finish,
        (like((shard, width), F32), like((shard, width), F32), like((shard, kv_width), F32),
         like((shard, kv_width), F32), like((shard, experts), F32), like((1, shard), F32),
         like((1, shard), F32)),
        (*pieces_out, *late([w_query[0], w_key[0], w_value[0], attn_gain])), 0,
        scratch=[pltpu.VMEM((shard, qkv_width), F32)], scalars=(here,),
    )

    return (
        layer_outputs[None, :, None],
        jnp.stack([o[1] for o in outer])[None, :, None],
        first,
        q_grad[None],
        k_grad[None],
        v_grad[None],
        o_grad[None],
        second_sum,
        r_grad[None],
        expert_grads[1][None],
        expert_grads[2][None],
        expert_grads[0][None],
    )


def solution(mesh):
    dense = P("section", ("row", "col"), None)
    gain = P("section", ("row", "col"))
    expert = P("section", "col", "row", None)
    token = P(None, "col", "row", None)
    layered = P("section", None, "col", "row", None)
    return jax.shard_map(
        on_device,
        mesh=mesh,
        in_specs=(
            token, token, P(None, "col", None), layered, gain, dense, dense, dense, dense, gain,
            dense, expert, expert, expert,
        ),
        out_specs=(
            layered, layered, gain, dense, dense, dense, dense, gain, dense, expert, expert, expert,
        ),
        check_vma=False,
    )
```

```python
import functools

import jax
import jax.numpy as jnp
from jax import lax
from jax.experimental import pallas as pl
from jax.experimental.pallas import tpu as pltpu
from jax.sharding import PartitionSpec as P

HEAD_DIM = 128
ROOMS = 16
EPSILON = 1e-06
LANES = 128
BF = jnp.bfloat16
F32 = jnp.float32
MIB = 1 << 20


def dot(left, right, contract=(1, 0)):
    return lax.dot_general(
        left, right, (((contract[0],), (contract[1],)), ((), ())), preferred_element_type=F32
    )


def like(shape, dtype):
    return jax.ShapeDtypeStruct(shape, dtype)


class Late:
    def __init__(self, source, index=None, target=None, sem=None):
        self.source, self.index, self.target, self.copy = source, index, target, None
        if target is not None:
            source = source if index is None else source.at[index]
            self.copy = pltpu.make_async_copy(source, target, sem)
            self.copy.start()
            self.waiting = True

    def ready(self):
        if self.waiting:
            self.copy.wait()
            self.waiting = False
        return self.target

    def __getitem__(self, index):
        return self.ready()[index]

    @property
    def shape(self):
        return self.source.shape[len(self.index or ()) :]


class Sent:
    def __init__(self, source, target=None, sems=None):
        self.source, self.target, self.sems, self.copies = source, target, sems, []

    def __getitem__(self, index):
        return self.source[index]

    def __setitem__(self, index, value):
        self.source[index] = value

    def send(self, *parts):
        for part in parts or (...,):
            at = len(self.copies)
            whole = part is ...
            copy = pltpu.make_async_copy(
                self.source if whole else self.source.at[part],
                self.target if whole else self.target.at[part],
                self.sems.at[at],
            )
            copy.start()
            self.copies.append(copy)

    @property
    def shape(self):
        return self.source.shape


PARTS = 4


def sent(out, *parts):
    if isinstance(out, Sent):
        out.send(*parts)


def call(body, outs, args, flops, far=(), scratch=(), scalars=(), waits=()):
    arrays = [a.source if isinstance(a, Late) else a for a in args]
    shapes = [o.source if isinstance(o, Sent) else o for o in outs]
    moved = sum(a.size * a.dtype.itemsize for a in (*arrays, *far, *shapes))
    count = len(scalars) + len(args) + len(far)
    kinds = [isinstance(a, Late) for a in args]
    out_kinds = [isinstance(o, Sent) for o in outs]
    buffers = [pltpu.VMEM(a.shape, a.source.dtype) for a in args if isinstance(a, Late)]
    buffers += [pltpu.VMEM(o.shape, o.dtype) for o, k in zip(shapes, out_kinds) if k]

    def run(*refs):
        given, refs = list(refs[:count]), refs[count + len(waits) :]
        results, refs = list(refs[: len(outs)]), refs[len(outs) :]
        own, rest = list(refs[: len(buffers)]), refs[len(buffers) :]
        sems, rest = (rest[0], rest[1:]) if buffers else (None, rest)
        used = 0
        for k, kind in enumerate(kinds):
            if kind:
                at = len(scalars) + k
                given[at] = Late(given[at], args[k].index, own[used], sems.at[used, 0])
                used += 1
        for k, kind in enumerate(out_kinds):
            if kind:
                results[k] = Sent(own[used], results[k], sems.at[used])
                used += 1
        body(*given, *results, *rest)
        for one in given:
            if isinstance(one, Late):
                one.ready()
        for one in results:
            if isinstance(one, Sent) and not one.copies:
                one.send()
        for one in results:
            if isinstance(one, Sent):
                done_with(one.copies)

    anywhere, local = pl.BlockSpec(memory_space=pltpu.HBM), pl.BlockSpec(memory_space=pltpu.VMEM)
    return pl.pallas_call(
        run,
        out_shape=tuple(shapes),
        in_specs=[pl.BlockSpec(memory_space=pltpu.SMEM)] * len(scalars)
        + [anywhere if k else local for k in kinds]
        + [anywhere] * (len(far) + len(waits)),
        out_specs=tuple(anywhere if k else local for k in out_kinds),
        scratch_shapes=buffers
        + ([pltpu.SemaphoreType.DMA((len(buffers), PARTS))] if buffers else [])
        + list(scratch),
        compiler_params=pltpu.CompilerParams(vmem_limit_bytes=64 * MIB),
        cost_estimate=pl.CostEstimate(
            flops=int(flops), bytes_accessed=int(moved), transcendentals=0
        ),
        name=body.func.__name__ if isinstance(body, functools.partial) else body.__name__,
    )(*scalars, *arrays, *far, *waits)


def late(values):
    return [Late(v) for v in values]


def nothing(*refs):
    pass


def hold(value, *waits):
    return pl.pallas_call(
        nothing,
        out_shape=like(value.shape, value.dtype),
        in_specs=[pl.BlockSpec(memory_space=pl.ANY)] * (1 + len(waits)),
        out_specs=pl.BlockSpec(memory_space=pl.ANY),
        input_output_aliases={0: 0},
        name="hold",
    )(value, *waits)


def swapped(value, step):
    rows = lax.axis_size("row")
    return lax.ppermute(value, "row", [(r, r ^ step) for r in range(rows)])


def norm_parts(stream):
    return lax.rsqrt(jnp.mean(stream * stream, -1, keepdims=True) + EPSILON)


def norm_back(grad, stream, gain):
    inverse = norm_parts(stream)
    unit = stream * inverse
    scaled = grad * gain
    back = inverse * (scaled - unit * jnp.mean(scaled * unit, -1, keepdims=True))
    return back, jnp.sum(grad * unit, 0, keepdims=True)


def turned(vectors, cosine, sine):
    done = []
    for at in range(0, vectors.shape[1], HEAD_DIM):
        one = vectors[:, at : at + HEAD_DIM]
        done.append(one * cosine + pltpu.roll(one, HEAD_DIM // 2, 1) * sine)
    return jnp.concatenate(done, -1) if len(done) > 1 else done[0]


def stacked_heads(value, first, count):
    return jnp.concatenate(
        [value[:, (first + j) * HEAD_DIM : (first + j + 1) * HEAD_DIM] for j in range(count)], 0
    )


def unstacked_heads(value, count):
    tokens = value.shape[0] // count
    return jnp.concatenate([value[j * tokens : (j + 1) * tokens] for j in range(count)], 1)


def cuts_of(total, most=512):
    return [(at, min(most, total - at)) for at in range(0, total, most)]


def project(
    flag, came, entering, gain, cosine, sine, dense, stream, normed, query, pair, weights, sems
):
    width = stream.shape[1]
    cuts = cuts_of(weights.shape[1])
    copies = [
        pltpu.make_async_copy(
            dense.at[:, pl.ds(at, size)], weights.at[:, pl.ds(at, size)], sems.at[k]
        )
        for k, (at, size) in enumerate(cuts)
    ]
    for copy in copies:
        copy.start()
    x = jnp.where(flag[0] > 0, came[...].astype(F32), entering[...].astype(F32))
    stream[...] = x
    sent(stream)
    low = (x * norm_parts(x) * gain[...]).astype(BF)
    normed[...] = low
    sent(normed)
    keys = pair.shape[1] // 2
    for copy, (at, size) in zip(copies, cuts):
        copy.wait()
        part = dot(low, weights[:, at : at + size])
        for begin in range(at, at + size, HEAD_DIM):
            head = part[:, begin - at : begin - at + HEAD_DIM]
            if begin < width + keys:
                head = turned(head, cosine[...], sine[...])
            head = head.astype(BF)
            if begin < width:
                query[:, begin : begin + HEAD_DIM] = head
            else:
                pair[:, begin - width : begin - width + HEAD_DIM] = head
            if begin + HEAD_DIM == width:
                sent(query)


def project_all(entering, gain, cosine, sine, dense, pair, *rest):
    outs, (weights, sems) = rest[:-2], rest[-2:]
    micro, unused, tokens, width = entering.shape
    cuts = cuts_of(weights.shape[1])
    copies = [
        pltpu.make_async_copy(
            dense.at[:, pl.ds(at, size)], weights.at[:, pl.ds(at, size)], sems.at[k]
        )
        for k, (at, size) in enumerate(cuts)
    ]
    for copy in copies:
        copy.start()
    lows = []
    for m in range(micro):
        x = entering[m, 0].astype(F32)
        outs[2 * m][...] = x
        sent(outs[2 * m])
        lows.append((x * norm_parts(x) * gain[...]).astype(BF))
    low = jnp.concatenate(lows, 0)
    cosines = jnp.concatenate([cosine[...]] * micro, 0)
    sines = jnp.concatenate([sine[...]] * micro, 0)
    keys = pair.shape[1] // 2
    for copy, (at, size) in zip(copies, cuts):
        copy.wait()
        part = dot(low, weights[:, at : at + size])
        for begin in range(at, at + size, HEAD_DIM):
            head = part[:, begin - at : begin - at + HEAD_DIM]
            if begin < width + keys:
                head = turned(head, cosines, sines)
            head = head.astype(BF)
            if begin < width:
                for m in range(micro):
                    outs[2 * m + 1][:, begin : begin + HEAD_DIM] = head[
                        m * tokens : (m + 1) * tokens
                    ]
            else:
                pair[:, begin - width : begin - width + HEAD_DIM] = head
            if begin + HEAD_DIM == width:
                for m in range(micro):
                    sent(outs[2 * m + 1])


def slot_experts(slots):
    own = lax.broadcasted_iota(jnp.int32, (slots, LANES), 0) // ROOMS
    return own == lax.broadcasted_iota(jnp.int32, (slots, LANES), 1)


def scaled_rows(dispatch, gates, low):
    here = slot_experts(dispatch.shape[0])
    scale = jnp.sum(jnp.where(here, dot(dispatch, gates.astype(BF)), 0.0), -1, keepdims=True)
    return (dot(dispatch, low) * scale).astype(BF)


def attend(
    keep, m, stream, query, pair0, pair1, pair2, pair3, bias, gain, chosen, dispatch, *rest,
):
    (target,), rest = (rest[:1], rest[1:]) if keep else ((None,), rest)
    dense, middle, gates, outgoing = rest[:4]
    kept, (mixed, weights, router, sems) = rest[4:-4], rest[-4:]
    width = stream.shape[1]
    block = (outgoing.shape[0], -1, width)
    per = dispatch.shape[0] // outgoing.shape[0]
    at = dense.shape[1] - width - LANES
    copies = [
        pltpu.make_async_copy(dense.at[:, pl.ds(at + LANES, width)], weights, sems.at[0]),
        pltpu.make_async_copy(dense.at[:, pl.ds(at, LANES)], router, sems.at[1]),
    ]
    for copy in copies:
        copy.start()
    tokens = stream.shape[0]
    pairs = jnp.concatenate(
        [p[m * tokens : (m + 1) * tokens, :] for p in (pair0, pair1, pair2, pair3)], 0
    )
    kv_heads = pairs.shape[1] // (2 * HEAD_DIM)
    group = width // HEAD_DIM // kv_heads
    biases = jnp.concatenate([bias[...]] * group, 0)
    for h in range(kv_heads):
        keys = pairs[:, h * HEAD_DIM : (h + 1) * HEAD_DIM]
        values = pairs[:, (kv_heads + h) * HEAD_DIM : (kv_heads + h + 1) * HEAD_DIM]
        queries = stacked_heads(query, h * group, group)
        scores = dot(queries, keys, (1, 1)) * HEAD_DIM ** (-0.5) + biases
        expo = jnp.exp(scores - jnp.max(scores, -1, keepdims=True))
        weight = (expo * (1.0 / jnp.sum(expo, -1, keepdims=True))).astype(BF)
        if keep:
            kept[0][h] = weight
        done = dot(weight, values).astype(BF)
        for j in range(group):
            begin = (h * group + j) * HEAD_DIM
            mixed[:, begin : begin + HEAD_DIM] = done[j * tokens : (j + 1) * tokens]
    if keep:
        kept[1][...] = mixed[...]
        sent(kept[0])
        sent(kept[1])
    copies[0].wait()
    x = stream[...] + dot(mixed[...], weights[...])
    middle[...] = x
    sent(middle)
    low = (x * norm_parts(x) * gain[...]).astype(BF)
    if keep:
        kept[2][...] = low
        sent(kept[2])
    copies[1].wait()
    taken = chosen[...] > 0
    logits = jnp.where(taken, dot(low, router[...]), -1e30)
    expo = jnp.where(taken, jnp.exp(logits - jnp.max(logits, -1, keepdims=True)), 0.0)
    share = expo / jnp.sum(expo, -1, keepdims=True)
    gates[...] = share
    sent(gates)
    slots = dispatch[...]
    outgoing[:, :per, :] = dot(slots, low).astype(BF).reshape(block)
    if keep:
        sent(outgoing, (slice(None), pl.ds(0, per)))
        outgoing[:, per:, :] = scaled_rows(slots, share, target[...]).reshape(block)
        sent(outgoing, (slice(None), pl.ds(per, per)))


class Fetched:
    def __init__(self, shards, weights, sems):
        self.weights = weights
        self.copies = {}
        for j in range(weights.shape[1]):
            for k in range(weights.shape[0]):
                self.copies[k, j] = [
                    pltpu.make_async_copy(
                        shards[k][p].at[j],
                        weights.at[k, j, pl.ds(p * shards[k][p].shape[1], shards[k][p].shape[1])],
                        sems.at[k, j, p],
                    )
                    for p in range(4)
                ]
        for k in range(weights.shape[0]):
            self.start(k, 0)

    def start(self, k, j):
        for copy in self.copies.get((k, j), ()):
            copy.start()

    def ready(self, k, j):
        done_with(self.copies[k, j])
        self.start(k, j + 1)


def done_with(copies):
    for copy in copies:
        copy.wait()


def rows_of(value, j, begin=0):
    columns, unused, width = value.shape
    at = begin + j * ROOMS
    return value[:, at : at + ROOMS, :].reshape(columns * ROOMS, width)


def put_rows(out, j, rows, inner):
    at, width = j * ROOMS, rows.shape[1]
    out[:, at : at + ROOMS, :width] = rows.reshape(-1, ROOMS, width)
    high = inner.astype(BF).astype(F32)
    lane = lax.broadcasted_iota(jnp.int32, (rows.shape[0], LANES), 1)
    both = jnp.where(lane == 0, high, jnp.where(lane == 1, inner - high, 0.0))
    out[:, at : at + ROOMS, width:] = both.astype(BF).reshape(-1, ROOMS, LANES)


def expert_forward(both, arrived, *refs):
    shards = [refs[4 * k : 4 * k + 4] for k in range(3)]
    outs, weights, sems = refs[12:-2], refs[-2], refs[-1]
    fetched = Fetched(shards, weights, sems)
    per = weights.shape[1] * ROOMS
    for j in range(weights.shape[1]):
        at = j * ROOMS
        rows = rows_of(arrived, j)
        fetched.ready(0, j)
        gate = dot(rows, weights[0, j], (1, 1))
        fetched.ready(1, j)
        lifted = dot(rows, weights[1, j], (1, 1))
        square = gate * gate
        bend = jnp.tanh(0.7978845608028654 * gate * (1.0 + 0.044715 * square))
        active = 0.5 * gate * (1.0 + bend)
        hidden = (active * lifted).astype(BF)
        fetched.ready(2, j)
        made = dot(hidden, weights[2, j]).astype(BF)
        outs[0][:, at : at + ROOMS, :] = made.reshape(-1, ROOMS, made.shape[1])
        sent(outs[0], (slice(None), pl.ds(at, ROOMS)))
        if both:
            slope = 0.5 * (1.0 + bend) + 0.5 * gate * (1.0 - bend * bend) * (
                0.7978845608028654 * (1.0 + 3 * 0.044715 * square)
            )
            bent = slope * lifted
            outs[1][j] = hidden
            outs[2][j] = active.astype(BF)
            outs[3][j] = bent.astype(BF)
            hidden_grads = dot(rows_of(arrived, j, per), weights[2, j], (1, 1))
            gate_part = (hidden_grads * bent).astype(BF)
            lifted_part = (hidden_grads * active).astype(BF)
            inner = jnp.sum(hidden_grads * hidden.astype(F32), -1, keepdims=True)
            back = dot(gate_part, weights[0, j]) + dot(lifted_part, weights[1, j])
            put_rows(outs[4], j, back.astype(BF), inner)
            sent(outs[4], (slice(None), pl.ds(at, ROOMS)))
            for out in outs[1:4]:
                sent(out, j)


def combine(returned, middle, gates, spread, places, low):
    weights = (dot(gates[...].astype(BF), spread[...]) * places[...].astype(F32)).astype(BF)
    done = middle[...] + dot(weights, returned[...].reshape(-1, returned.shape[2]))
    low[...] = done.astype(BF)


def last_outputs(flag, spread, *refs):
    out = refs[-1]
    width = out.shape[2]
    for m in range(out.shape[0]):
        returned, middle, gates, places, before = refs[5 * m : 5 * m + 5]
        weights = (dot(gates[...].astype(BF), spread[...]) * places[...].astype(F32)).astype(BF)
        rows = returned[:, :, :width].reshape(-1, width)
        out[m] = jnp.where(flag[0] > 0, middle[...] + dot(weights, rows), before[...].astype(F32))


def send_grads(flag, came, target, gates, dispatch, grad, outgoing):
    low = jnp.where(flag[0] > 0, came[...], target[...])
    grad[...] = low
    sent(grad)
    outgoing[...] = scaled_rows(dispatch[...], gates[...], low).reshape(outgoing.shape)


def expert_backward(flag, arrived, hidden, active, bent, produced, *refs):
    shards = [refs[4 * k : 4 * k + 4] for k in range(3)]
    out, gate_back, lifted_back, weights, sems = refs[12:]
    fetched = Fetched(shards, weights, sems)
    for j in range(weights.shape[1]):
        fetched.ready(0, j)
        hidden_grads = dot(rows_of(arrived, j), weights[0, j], (1, 1))
        gate_part = (hidden_grads * bent[j].astype(F32)).astype(BF)
        lifted_part = (hidden_grads * active[j].astype(F32)).astype(BF)
        gate_back[j] = gate_part
        lifted_back[j] = lifted_part
        inner = jnp.sum(hidden_grads * hidden[j].astype(F32), -1, keepdims=True)
        fetched.ready(1, j)
        done = dot(gate_part, weights[1, j])
        fetched.ready(2, j)
        done = (done + dot(lifted_part, weights[2, j])).astype(BF)
        put_rows(out, j, jnp.where(flag[0] > 0, rows_of(produced, j), done), inner)
        sent(out, (slice(None), pl.ds(j * ROOMS, ROOMS)))
        sent(gate_back, j)
        sent(lifted_back, j)


def attend_back(
    keep, row, flag, token_grads, before, gates, places, middle, gain, grad, query, pair0, pair1,
    pair2, pair3, probs, cosine, sine, dense, middle_grads, query_back, part0, part1, part2, part3,
    *rest,
):
    tokens, width = middle.shape
    kept, (branch, weights, router, sems) = rest[:-4], rest[-4:]
    at = dense.shape[1] - width - LANES
    copies = [
        pltpu.make_async_copy(dense.at[:, pl.ds(at, LANES)], router, sems.at[1]),
        pltpu.make_async_copy(dense.at[:, pl.ds(at + LANES, width)], weights, sems.at[0]),
    ]
    for copy in copies:
        copy.start()
    came = token_grads[...]
    if keep:
        came = jnp.where(flag[0] > 0, before[...], came)
    came = came.reshape(-1, came.shape[2])
    place = places[...]
    here = slot_experts(came.shape[0])
    notes = came[:, width:].astype(F32)
    high = jnp.where(here, notes[:, :1], 0.0).astype(BF)
    rest_of = jnp.where(here, notes[:, 1:2], 0.0).astype(BF)
    inner = dot(place, high) + dot(place, rest_of)
    logit_grads = (inner - gates[...] * jnp.sum(inner, -1, keepdims=True)).astype(BF)
    ffn_grads = dot(place, came[:, :width])
    copies[0].wait()
    ffn_grads = ffn_grads + dot(logit_grads, router[...], (1, 1))
    part, total = norm_back(ffn_grads, middle[...], gain[...])
    above = grad[...].astype(F32) + part
    middle_grads[...] = above
    sent(middle_grads)
    low = above.astype(BF)
    if keep:
        kept[0][...] = logit_grads
        kept[1][...] = jnp.broadcast_to(total, kept[1].shape)
        sent(kept[0])
        sent(kept[1])
        branch[...] = low
        share = width // 4
        for s, part in enumerate((part0, part1, part2, part3)):
            begin = pl.multiple_of((row[0] ^ s) * share, LANES)
            part[:, part.shape[1] - share :] = branch[:, pl.ds(begin, share)]
    copies[1].wait()
    mixed_grads = dot(low, weights[...], (1, 1)).astype(BF)
    pairs = stacked((pair0, pair1, pair2, pair3))
    kv_heads = pairs.shape[1] // (2 * HEAD_DIM)
    group = width // HEAD_DIM // kv_heads
    scale = HEAD_DIM ** (-0.5)
    parts = (part0, part1, part2, part3)
    for h in range(kv_heads):
        keys = pairs[:, h * HEAD_DIM : (h + 1) * HEAD_DIM]
        values = pairs[:, (kv_heads + h) * HEAD_DIM : (kv_heads + h + 1) * HEAD_DIM]
        queries = stacked_heads(query, h * group, group)
        top = stacked_heads(mixed_grads, h * group, group)
        weight = probs[h]
        wide = weight.astype(F32)
        weight_grads = dot(top, values, (1, 1))
        value_grads = dot(weight, top, (0, 0)).astype(BF)
        inner = wide * weight_grads
        score_grads = (inner - wide * jnp.sum(inner, -1, keepdims=True)).astype(BF)
        query_grads = dot(score_grads, keys) * scale
        key_grads = (dot(score_grads, queries, (0, 0)) * scale).astype(BF)
        for j in range(group):
            begin = (h * group + j) * HEAD_DIM
            one = query_grads[j * tokens : (j + 1) * tokens]
            query_back[:, begin : begin + HEAD_DIM] = turned(one, cosine[...], -sine[...]).astype(BF)
        for p, part in enumerate(parts):
            part[:, h * HEAD_DIM : (h + 1) * HEAD_DIM] = key_grads[p * tokens : (p + 1) * tokens]
            begin = (kv_heads + h) * HEAD_DIM
            part[:, begin : begin + HEAD_DIM] = value_grads[p * tokens : (p + 1) * tokens]


def project_back(
    keep, row, part0, part1, part2, part3, query_back, stream, gain, middle_grads, cosine, sine,
    dense, low, *rest,
):
    width = stream.shape[1]
    kept, (backs, weights, sems) = rest[:-3], rest[-3:]
    cuts = cuts_of(weights.shape[1])
    copies = [
        pltpu.make_async_copy(
            dense.at[:, pl.ds(at, size)], weights.at[:, pl.ds(at, size)], sems.at[k]
        )
        for k, (at, size) in enumerate(cuts)
    ]
    for copy in copies:
        copy.start()
    pairs = weights.shape[1] - width
    total = sum(part[:, :pairs].astype(F32) for part in (part0, part1, part2, part3))
    keys = pairs // 2
    backs[:, :width] = query_back[...]
    backs[:, width : width + keys] = turned(total[:, :keys], cosine[...], -sine[...]).astype(BF)
    backs[:, width + keys :] = total[:, keys:].astype(BF)
    if keep:
        share = backs.shape[1] // 4
        for s, out in enumerate(kept[1:]):
            out[...] = backs[:, pl.ds(pl.multiple_of((row[0] ^ s) * share, LANES), share)]
            sent(out)
    above = jnp.zeros(stream.shape, F32)
    for copy, (at, size) in zip(copies, cuts):
        copy.wait()
        above = above + dot(backs[:, at : at + size], weights[:, at : at + size], (1, 1))
    part, unused = norm_back(above, stream[...], gain[...])
    done = middle_grads[...] + part
    if keep:
        kept[0][...] = done
    low[...] = done.astype(BF)


def expert_weight_grads(begin_left, which, *refs):
    count = len(which)
    rights = sorted({w for w in which})
    sources, outs = refs[: 2 * count + 2 * len(rights)], refs[2 * count + 2 * len(rights) : -3]
    left, right, sems = refs[-3:]
    experts, deep, wide = left.shape[1:]
    columns, width = right.shape[2] // 2, right.shape[4]
    copies = {}
    for j in range(experts):
        for m in range(2):
            for r, (unused, begin) in enumerate(rights):
                copies["right", r, j, m] = pltpu.make_async_copy(
                    sources[2 * count + 2 * r + m].at[:, pl.ds(begin + j * ROOMS, ROOMS), :],
                    right.at[r, j, pl.ds(m * columns, columns)],
                    sems.at[1, r, j, m],
                )
            for k in range(count):
                copies["left", k, j, m] = pltpu.make_async_copy(
                    sources[2 * k + m].at[j, :, pl.ds(begin_left, wide)],
                    left.at[k, j, pl.ds(m * (deep // 2), deep // 2)],
                    sems.at[0, k, j, m],
                )
    for copy in copies.values():
        copy.start()
    waiting = dict(copies)

    def there(*name):
        for m in range(2):
            copy = waiting.pop((*name, m), None)
            if copy is not None:
                copy.wait()

    for j in range(experts):
        for k, name in enumerate(which):
            r = rights.index(name)
            there("right", r, j)
            there("left", k, j)
            total = dot(left[k, j], right[r, j].reshape(deep, width), (0, 0))
            some = len(outs) // count
            size = wide // some
            for q, out in enumerate(outs[some * k : some * (k + 1)]):
                out[j] = total[q * size : (q + 1) * size].astype(BF)
                sent(out, j)


def add(*refs):
    count = len(refs) // 3
    for k in range(count):
        one, other, total = refs[2 * k], refs[2 * k + 1], refs[2 * count + k]
        total[...] = (one[...].astype(F32) + other[...].astype(F32)).astype(BF)


def pack(*refs):
    for k, value in enumerate(refs[:-1]):
        refs[-1][k] = value[...]


def stacked(refs):
    return jnp.concatenate([r[...] for r in refs], 0)


def by_owner(out, grads, begin):
    columns, lines, unused = out.shape
    size = lines // 4
    for c in range(columns):
        some = [grads[(r * columns + c) * size : (r * columns + c + 1) * size] for r in range(4)]
        out[c, :, begin : begin + grads.shape[1]] = jnp.concatenate(some, 0).astype(BF)


def out_grads(*refs):
    lefts, rights, normed, logits, gains, out = (
        refs[:4], refs[4:12], refs[12:14], refs[14:16], refs[16:18], refs[18],
    )
    share = out.shape[2] - LANES
    left = jnp.concatenate([one[k] for one in lefts for k in (2, 3)], 0)
    right = jnp.concatenate([r[:, r.shape[1] - share :] for r in rights], 0)
    by_owner(out, dot(left, right, (0, 0)), 0)
    width = left.shape[1]
    line = lax.broadcasted_iota(jnp.int32, (LANES, width), 0)
    sums = jnp.where(line == LANES - 1, gains[0][:1, :] + gains[1][:1, :], 0.0)
    by_owner(out, dot(stacked(normed), stacked(logits), (0, 0)) + sums.T, share)


def qkv_grads(*refs):
    lefts, rights, out = refs[:4], refs[4:12], refs[12]
    left = jnp.concatenate([one[k] for one in lefts for k in (0, 1)], 0)
    by_owner(out, dot(left, stacked(rights), (0, 0)), 0)


def fold(row, first, second, out0, out1, out2, out3, total):
    share = first.shape[2]
    total[:, :share] = jnp.sum(first[...].astype(F32), 0)
    total[:, share:] = jnp.sum(second[...].astype(F32), 0)
    for s, out in enumerate((out0, out1, out2, out3)):
        size = out.shape[0]
        out[...] = total[pl.ds(pl.multiple_of((row[0] ^ s) * size, 8), size), :]
        sent(out)


def finish(
    row, in0, in1, in2, in3, w_query, w_key, w_value, gain, o_grad, q_grad, k_grad, v_grad, r_grad,
    first, second, total,
):
    share = o_grad.shape[1] // 4
    piece = total.shape[1] // 4
    ins = (in0, in1, in2, in3)
    for s, one in enumerate(ins):
        where = row[0] ^ s
        o_grad[:, pl.ds(pl.multiple_of(where * share, LANES), share)] = one[:, :share]
        total[:, pl.ds(pl.multiple_of(where * piece, LANES), piece)] = one[:, share + LANES :]
    rest = sum(one[:, share : share + LANES] for one in ins)
    r_grad[...] = rest[:, : r_grad.shape[1]]
    second[...] = rest.T[LANES - 1 :, :]
    begin, inner = 0, jnp.zeros((total.shape[0], 1), F32)
    for out, weight in ((q_grad, w_query), (k_grad, w_key), (v_grad, w_value)):
        part = total[:, begin : begin + out.shape[1]]
        out[...] = part
        inner = inner + jnp.sum(part * weight[...].astype(F32), -1, keepdims=True)
        begin += out.shape[1]
    line = jnp.broadcast_to(inner, (total.shape[0], LANES)).T[:1, :]
    first[...] = line / gain[...].astype(F32)


def over_columns(value):
    return lax.all_to_all(value, "col", split_axis=0, concat_axis=0, tiled=True)


def on_device(
    inputs, cotangent, segment_ids, routes, attn_gain, w_query, w_key, w_value, w_out, ffn_gain,
    w_router, w_gate, w_up, w_down,
):
    section = lax.axis_index("section")
    row = lax.axis_index("row")
    rows = lax.axis_size("row")
    columns = lax.axis_size("col")
    micro, tokens, width = inputs.shape[0], inputs.shape[2], inputs.shape[3]
    experts = w_router.shape[2]
    per_column = w_gate.shape[1]
    hidden_width = w_gate.shape[2] * rows
    kv_width = w_key.shape[2]
    qkv_width = width + 2 * kv_width
    slots = experts * ROOMS
    share = width // rows
    shard = width // (rows * columns)
    heads = width // HEAD_DIM
    kv_heads = kv_width // HEAD_DIM
    length = rows * tokens
    pieces = range(micro)
    steps = range(rows)
    here = row.astype(jnp.int32)[None]
    second = (section == 1).astype(jnp.int32)[None]
    block = (columns, slots // columns, width)

    dense = jnp.concatenate(
        [w_query[0], w_key[0], w_value[0], w_router[0], attn_gain[0][:, None], ffn_gain[0][:, None],
         jnp.zeros((shard, LANES - experts - 2), BF), w_out[0]], 1
    )
    dense = lax.all_gather(dense, ("row", "col"), axis=0, tiled=True)
    small = dense[:, qkv_width : qkv_width + LANES]
    gain_a = small[:, experts].astype(F32)[None, :]
    gain_f = small[:, experts + 1].astype(F32)[None, :]

    def shards_of(own):
        two = swapped(own, 2)
        return own, swapped(own, 1), two, swapped(two, 1)

    gate_shards, up_shards, down_shards = [shards_of(w[0]) for w in (w_gate, w_up, w_down)]

    lane = jnp.arange(LANES, dtype=jnp.int32)
    half = HEAD_DIM // 2
    freqs = 10000.0 ** (-2.0 * jnp.arange(half).astype(F32) / HEAD_DIM)
    positions = row * tokens + jnp.arange(tokens, dtype=jnp.int32)
    angles = positions.astype(F32)[:, None] * freqs[None, :]
    cosine = jnp.concatenate([jnp.cos(angles)] * 2, 1)
    sine = jnp.concatenate([-jnp.sin(angles), jnp.sin(angles)], 1)
    key_positions = jnp.concatenate(
        [(row ^ step) * tokens + jnp.arange(tokens, dtype=jnp.int32) for step in steps]
    )
    spread = (lane[:, None] == jnp.arange(slots, dtype=jnp.int32)[None, :] // ROOMS).astype(BF)
    below = (jnp.arange(tokens)[:, None] > jnp.arange(tokens)[None, :]).astype(BF)
    biases, chosens, places, dispatches = [], [], [], []
    for m in pieces:
        segments = segment_ids[m, 0]
        own_segments = lax.dynamic_slice_in_dim(segments, row * tokens, tokens)
        key_segments = jnp.concatenate(
            [lax.dynamic_slice_in_dim(segments, (row ^ s) * tokens, tokens) for s in steps]
        )
        counted = (key_positions[None, :] <= positions[:, None]) & (
            key_segments[None, :] == own_segments[:, None]
        )
        biases.append(jnp.where(counted, 0.0, -1e30).astype(F32))
        chosen = jnp.any(routes[0, m, 0][:, :, None] == lane[None, None, :], 1)
        chosens.append(chosen.astype(F32))
        rank = dot(below, chosen.astype(BF))
        rank = jnp.where(chosen, rank, -1.0)[:, :experts]
        place = (
            rank[:, :, None] == jnp.arange(ROOMS, dtype=F32)[None, None, :]
        ).reshape(tokens, slots)
        places.append(place.astype(BF))
        dispatches.append(place.T.astype(BF))

    token_low, token_wide = like((tokens, width), BF), like((tokens, width), F32)
    pair_like = like((tokens, 2 * kv_width), BF)
    block_like = like(block, BF)
    sums_like = like((8, width), F32)
    kept_like = like((per_column, columns * ROOMS, hidden_width), BF)
    probs_like = like((kv_heads, heads // kv_heads * tokens, length), BF)
    qkv_scratch = [pltpu.VMEM((width, qkv_width), BF), pltpu.SemaphoreType.DMA((8,))]
    out_scratch = [
        pltpu.VMEM((width, width), BF), pltpu.VMEM((width, LANES), BF),
        pltpu.SemaphoreType.DMA((2,)),
    ]
    expert_scratch = [
        pltpu.VMEM((3, per_column, hidden_width, width), BF),
        pltpu.SemaphoreType.DMA((3, per_column, 4)),
    ]
    qkv_flops = 2 * tokens * width * qkv_width
    out_flops = 2 * tokens * width * width + 2 * slots * tokens * width
    score_flops = 2 * heads * tokens * length * HEAD_DIM
    expert_flops = 2 * slots * hidden_width * width

    per = slots // columns
    back_like = like((columns, per, width + LANES), BF)
    double_like = like((columns, 2 * per, width), BF)
    lanes_like = like((tokens, LANES), F32)
    tables = late([cosine, sine])
    first_flag = (1 - second)

    def forward(keep, came, waits, down):
        projected, pairs = [], []
        if keep:
            for m in pieces:
                projected.append(
                    call(
                        project,
                        (Sent(token_wide), Sent(token_low), Sent(token_low), Sent(pair_like)),
                        (Late(came[m]), Late(inputs, (m, 0)), Late(gain_a), *tables), qkv_flops, (dense,),
                        qkv_scratch, (second,), waits=[p[0] for p in projected],
                    )
                )
                pairs.append([projected[m][3]] + [swapped(projected[m][3], s) for s in steps[1:]])
        else:
            pair, *streams = call(
                project_all,
                (Sent(like((micro * tokens, 2 * kv_width), BF)),)
                + (Sent(token_wide), Sent(token_low)) * micro,
                (Late(inputs), Late(gain_a), *tables), micro * qkv_flops, (dense,),
                qkv_scratch, waits=waits,
            )
            projected = [(streams[2 * m], None, streams[2 * m + 1]) for m in pieces]
            pairs = [[pair] + [swapped(pair, s) for s in steps[1:]]] * micro
        attended = [
            call(
                functools.partial(attend, keep, 0 if keep else m),
                (Sent(token_wide), Sent(lanes_like), Sent(double_like if keep else block_like))
                + ((Sent(probs_like), Sent(token_low), Sent(token_low)) if keep else ()),
                (*late([projected[m][0], projected[m][2], *pairs[m], biases[m], gain_f, chosens[m],
                        dispatches[m]]),
                 *((Late(cotangent, (m, 0)),) if keep else ())),
                out_flops + 2 * score_flops, (dense,), [pltpu.VMEM((tokens, width), BF)] + out_scratch,
            )
            for m in pieces
        ]
        arrived = [over_columns(a[2]) for a in attended]
        lefts, ready = [], ()
        if keep:
            left = call(
                pack, (Sent(like((2 * micro, tokens, width), BF)),),
                late([p[1] for p in projected] + [a[4] for a in attended]), 0,
            )[0]
            two = swapped(left, 2)
            lefts = [left, swapped(left, 1), two, swapped(two, 1)]
            ready = (two,)
        applied = [
            call(
                functools.partial(expert_forward, keep),
                (Sent(block_like),)
                + ((Sent(kept_like),) * 3 + (Sent(back_like),) if keep else ()),
                late([arrived[m]]), (6 if keep else 3) * expert_flops,
                (*gate_shards, *up_shards, *down), expert_scratch,
                waits=ready if m else (attended[1][2],),
            )
            for m in pieces
        ]
        return projected, pairs, attended, arrived, applied, lefts, down

    def weight_call(quarters, which, lefts, rights, waits):
        quarter, some = hidden_width // 4, len(quarters)
        return call(
            functools.partial(expert_weight_grads, quarters[0] * quarter, which),
            (Sent(like((per_column, quarter, width), BF)),) * (some * len(which)), (),
            len(which) * expert_flops, [*lefts, *rights],
            [pltpu.VMEM((len(which), per_column, 2 * columns * ROOMS, some * quarter), BF),
             pltpu.VMEM((len(rights) // 2, per_column, 2 * columns, ROOMS, width), BF),
             pltpu.SemaphoreType.DMA((2, len(which), per_column, 2))],
            waits=waits,
        )

    def merged(halves, waits):
        pairs = [v for a, b in halves for v in (a, swapped(b, 1))]
        return call(add, [Sent(a) for a, unused in halves], late(pairs), 0, waits=waits)

    def attention_back(keep, m, grad, token_grads, waits):
        return call(
            functools.partial(attend_back, keep),
            (Sent(token_wide), Sent(token_low))
            + (Sent(like((tokens, 2 * kv_width + (share if keep else 0)), BF)),) * rows
            + ((Sent(like((tokens, LANES), BF)), Sent(sums_like)) if keep else ()),
            (*late([token_grads, shared[m] if keep else spread, attended[m][1], places[m],
                                 attended[m][0], gain_f]), Late(*grad),
             *late([projected[m][2], *pairs[m], attended[m][3], cosine, sine])),
            out_flops + 4 * score_flops, (dense,), [pltpu.VMEM((tokens, width), BF)] + out_scratch,
            (here, second), waits,
        )

    def parts_of(inner):
        return [inner[2]] + [swapped(inner[2 + s], s) for s in steps[1:]]

    def projection_back(keep, m, inner, parts, waits):
        return call(
            functools.partial(project_back, keep),
            (Sent(token_low),)
            + ((Sent(token_wide),) + (Sent(like((tokens, qkv_width // rows), BF)),) * rows
               if keep else ()),
            (*late([*parts, inner[1], projected[m][0], gain_a, inner[0]]),
             *tables),
            qkv_flops, (dense,), [pltpu.VMEM((tokens, qkv_width), BF)] + qkv_scratch,
            (here,), waits,
        )

    kept = forward(False, None, (gate_shards[2], up_shards[2], down_shards[2]), down_shards)
    attended, applied, down_shards = kept[2], kept[4], kept[6]
    returned = [over_columns(a[0]) for a in applied]
    results = [
        call(
            combine, (Sent(token_low),),
            late([returned[m], attended[m][0], attended[m][1], spread, places[m]]),
            2 * slots * tokens * width, waits=() if m else (applied[1][0],),
        )
        for m in pieces
    ]
    came = [lax.ppermute(r[0], "section", [(0, 1)]) for r in results]

    kept = forward(True, came, (), down_shards)
    projected, pairs, attended, arrived, applied, lefts, down_shards = kept
    hidden = [a[1] for a in applied]
    shared = [over_columns(a[4]) for a in applied]
    inner, outer = [], []
    for m in pieces:
        waits = (*lefts[1:], outer[0][0]) if m else (applied[1][4],)
        inner.append(attention_back(False, m, (cotangent, (m, 0)), shared[m], waits))
        outer.append(projection_back(False, m, inner[m], parts_of(inner[m]), ()))
    came = [lax.ppermute(o[0], "section", [(1, 0)]) for o in outer]

    given = [
        call(
            send_grads, (Sent(token_low), Sent(block_like)),
            (Late(came[m]), Late(cotangent, (m, 0)), *late([attended[m][1], dispatches[m]])),
            2 * slots * tokens * width, scalars=(first_flag,), waits=() if m else (inner[1][0],),
        )
        for m in pieces
    ]
    arrived_grads = [over_columns(g[1]) for g in given]
    moved = [
        call(
            expert_backward, (Sent(back_like), Sent(kept_like), Sent(kept_like)),
            late([arrived_grads[m], hidden[m], applied[m][2], applied[m][3], applied[m][0]]),
            3 * expert_flops, (*down_shards, *gate_shards, *up_shards), expert_scratch,
            (second,), () if m else (given[1][1],),
        )
        for m in pieces
    ]
    back = [over_columns(a[0]) for a in moved]
    gate_up = [a[1] for a in moved] + [a[2] for a in moved]
    down_far = merged([weight_call((2, 3), ((0, 0),), hidden, arrived_grads, ())], ())[0]
    crossed = [swapped(down_far, 2)]
    inner = [attention_back(True, 0, given[0][:1], back[0], (moved[1][0], down_far))]
    parts = [parts_of(inner[0])]
    both = weight_call((0, 1, 2, 3), ((0, 0), (0, 0)), gate_up, arrived, (inner[0][0],))
    inner.append(attention_back(True, 1, given[1][:1], back[1], (both[0], crossed[0])))
    parts.append(parts_of(inner[1]))
    sums = merged([both[2:4], both[6:]], (inner[1][0],))
    crossed.append(swapped(hold(sums[0], *parts[1][1:]), 2))
    outer = [projection_back(True, 0, inner[0], parts[0], (inner[1][0],))]
    o_grads = call(
        out_grads, (Sent(like((columns, rows * shard, share + LANES), BF)),),
        late([*lefts, *[p[s] for s in steps for p in parts], *[a[5] for a in attended],
              *[a[6] for a in inner], *[a[7] for a in inner]]),
        2 * width * length * micro * share, waits=(crossed[0], outer[0][0], sums[0]),
    )[0]
    outer.append(projection_back(True, 1, inner[1], parts[1], (o_grads,)))
    backs = [[o[2]] + [swapped(o[2 + s], s) for s in steps[1:]] for o in outer]
    crossed.append(swapped(hold(sums[1], *backs[1][1:]), 2))
    near = weight_call((0, 1), ((0, 0),), hidden, arrived_grads, (outer[1][0],))
    w_grads = call(
        qkv_grads, (Sent(like((columns, rows * shard, qkv_width // rows), BF)),),
        late([*lefts, *[b[s] for s in steps for b in backs]]),
        2 * width * length * micro * qkv_width // rows, waits=(crossed[1], near[0]),
    )[0]
    expert_grads = [
        one.astype(F32) + swapped(other, 1).astype(F32) + c.astype(F32)
        for one, other, c in zip((near[0], both[0], both[4]), (near[1], both[1], both[5]), crossed)
    ]
    layer_outputs = call(
        last_outputs, (Sent(like((micro, tokens, width), F32)),),
        late([spread] + [v for m in pieces for v in (
            back[m], attended[m][0], attended[m][1], places[m], results[m][0])]),
        4 * slots * tokens * width, scalars=(second,), waits=(w_grads,),
    )[0]

    wide = share + qkv_width // rows + LANES
    pieces_out = call(
        fold, (Sent(like((shard, wide), F32)),) * rows,
        late([over_columns(o_grads), over_columns(w_grads)]), 0,
        scratch=[pltpu.VMEM((rows * shard, wide), F32)], scalars=(here,),
    )
    pieces_out = [pieces_out[0]] + [swapped(pieces_out[s], s) for s in steps[1:]]
    o_grad, q_grad, k_grad, v_grad, r_grad, first, second_sum = call(
        finish,
        (like((shard, width), F32), like((shard, width), F32), like((shard, kv_width), F32),
         like((shard, kv_width), F32), like((shard, experts), F32), like((1, shard), F32),
         like((1, shard), F32)),
        late([*pieces_out, w_query[0], w_key[0], w_value[0], attn_gain]), 0,
        scratch=[pltpu.VMEM((shard, qkv_width), F32)], scalars=(here,),
    )

    return (
        layer_outputs[None, :, None],
        jnp.stack([o[1] for o in outer])[None, :, None],
        first,
        q_grad[None],
        k_grad[None],
        v_grad[None],
        o_grad[None],
        second_sum,
        r_grad[None],
        expert_grads[1][None],
        expert_grads[2][None],
        expert_grads[0][None],
    )


def solution(mesh):
    dense = P("section", ("row", "col"), None)
    gain = P("section", ("row", "col"))
    expert = P("section", "col", "row", None)
    token = P(None, "col", "row", None)
    layered = P("section", None, "col", "row", None)
    return jax.shard_map(
        on_device,
        mesh=mesh,
        in_specs=(
            token, token, P(None, "col", None), layered, gain, dense, dense, dense, dense, gain,
            dense, expert, expert, expert,
        ),
        out_specs=(
            layered, layered, gain, dense, dense, dense, dense, gain, dense, expert, expert, expert,
        ),
        check_vma=False,
    )
```

```python
import functools

import jax
import jax.numpy as jnp
from jax import lax
from jax.experimental import pallas as pl
from jax.experimental.pallas import tpu as pltpu
from jax.sharding import PartitionSpec as P

HEAD_DIM = 128
ROOMS = 16
EPSILON = 1e-06
LANES = 128
BF = jnp.bfloat16
F32 = jnp.float32
MIB = 1 << 20


def dot(left, right, contract=(1, 0)):
    return lax.dot_general(
        left, right, (((contract[0],), (contract[1],)), ((), ())), preferred_element_type=F32
    )


def like(shape, dtype):
    return jax.ShapeDtypeStruct(shape, dtype)


class Late:
    def __init__(self, source, index=None, target=None, sem=None):
        self.source, self.index, self.target, self.copy = source, index, target, None
        if target is not None:
            source = source if index is None else source.at[index]
            self.copy = pltpu.make_async_copy(source, target, sem)
            self.copy.start()
            self.waiting = True

    def ready(self):
        if self.waiting:
            self.copy.wait()
            self.waiting = False
        return self.target

    def __getitem__(self, index):
        return self.ready()[index]

    @property
    def shape(self):
        return self.source.shape[len(self.index or ()) :]


class Sent:
    def __init__(self, source, target=None, sems=None):
        self.source, self.target, self.sems, self.copies = source, target, sems, []

    def __getitem__(self, index):
        return self.source[index]

    def __setitem__(self, index, value):
        self.source[index] = value

    def send(self, *parts):
        for part in parts or (...,):
            at = len(self.copies)
            whole = part is ...
            copy = pltpu.make_async_copy(
                self.source if whole else self.source.at[part],
                self.target if whole else self.target.at[part],
                self.sems.at[at],
            )
            copy.start()
            self.copies.append(copy)

    @property
    def shape(self):
        return self.source.shape


PARTS = 4


def sent(out, *parts):
    if isinstance(out, Sent):
        out.send(*parts)


def call(body, outs, args, flops, far=(), scratch=(), scalars=(), waits=()):
    arrays = [a.source if isinstance(a, Late) else a for a in args]
    shapes = [o.source if isinstance(o, Sent) else o for o in outs]
    moved = sum(a.size * a.dtype.itemsize for a in (*arrays, *far, *shapes))
    count = len(scalars) + len(args) + len(far)
    kinds = [isinstance(a, Late) for a in args]
    out_kinds = [isinstance(o, Sent) for o in outs]
    buffers = [pltpu.VMEM(a.shape, a.source.dtype) for a in args if isinstance(a, Late)]
    buffers += [pltpu.VMEM(o.shape, o.dtype) for o, k in zip(shapes, out_kinds) if k]

    def run(*refs):
        given, refs = list(refs[:count]), refs[count + len(waits) :]
        results, refs = list(refs[: len(outs)]), refs[len(outs) :]
        own, rest = list(refs[: len(buffers)]), refs[len(buffers) :]
        sems, rest = (rest[0], rest[1:]) if buffers else (None, rest)
        used = 0
        for k, kind in enumerate(kinds):
            if kind:
                at = len(scalars) + k
                given[at] = Late(given[at], args[k].index, own[used], sems.at[used, 0])
                used += 1
        for k, kind in enumerate(out_kinds):
            if kind:
                results[k] = Sent(own[used], results[k], sems.at[used])
                used += 1
        body(*given, *results, *rest)
        for one in given:
            if isinstance(one, Late):
                one.ready()
        for one in results:
            if isinstance(one, Sent) and not one.copies:
                one.send()
        for one in results:
            if isinstance(one, Sent):
                done_with(one.copies)

    anywhere, local = pl.BlockSpec(memory_space=pltpu.HBM), pl.BlockSpec(memory_space=pltpu.VMEM)
    return pl.pallas_call(
        run,
        out_shape=tuple(shapes),
        in_specs=[pl.BlockSpec(memory_space=pltpu.SMEM)] * len(scalars)
        + [anywhere if k else local for k in kinds]
        + [anywhere] * (len(far) + len(waits)),
        out_specs=tuple(anywhere if k else local for k in out_kinds),
        scratch_shapes=buffers
        + ([pltpu.SemaphoreType.DMA((len(buffers), PARTS))] if buffers else [])
        + list(scratch),
        compiler_params=pltpu.CompilerParams(vmem_limit_bytes=64 * MIB),
        cost_estimate=pl.CostEstimate(
            flops=int(flops), bytes_accessed=int(moved), transcendentals=0
        ),
        name=body.func.__name__ if isinstance(body, functools.partial) else body.__name__,
    )(*scalars, *arrays, *far, *waits)


def late(values):
    return [Late(v) for v in values]


def nothing(*refs):
    pass


def hold(value, *waits):
    return pl.pallas_call(
        nothing,
        out_shape=like(value.shape, value.dtype),
        in_specs=[pl.BlockSpec(memory_space=pl.ANY)] * (1 + len(waits)),
        out_specs=pl.BlockSpec(memory_space=pl.ANY),
        input_output_aliases={0: 0},
        name="hold",
    )(value, *waits)


def swapped(value, step):
    rows = lax.axis_size("row")
    return lax.ppermute(value, "row", [(r, r ^ step) for r in range(rows)])


def norm_parts(stream):
    return lax.rsqrt(jnp.mean(stream * stream, -1, keepdims=True) + EPSILON)


def norm_back(grad, stream, gain):
    inverse = norm_parts(stream)
    unit = stream * inverse
    scaled = grad * gain
    back = inverse * (scaled - unit * jnp.mean(scaled * unit, -1, keepdims=True))
    return back, jnp.sum(grad * unit, 0, keepdims=True)


def turned(vectors, cosine, sine):
    done = []
    for at in range(0, vectors.shape[1], HEAD_DIM):
        one = vectors[:, at : at + HEAD_DIM]
        done.append(one * cosine + pltpu.roll(one, HEAD_DIM // 2, 1) * sine)
    return jnp.concatenate(done, -1) if len(done) > 1 else done[0]


def stacked_heads(value, first, count):
    return jnp.concatenate(
        [value[:, (first + j) * HEAD_DIM : (first + j + 1) * HEAD_DIM] for j in range(count)], 0
    )


def unstacked_heads(value, count):
    tokens = value.shape[0] // count
    return jnp.concatenate([value[j * tokens : (j + 1) * tokens] for j in range(count)], 1)


def cuts_of(total, most=512):
    return [(at, min(most, total - at)) for at in range(0, total, most)]


def project(
    flag, came, entering, gain, cosine, sine, dense, stream, normed, query, pair, weights, sems
):
    width = stream.shape[1]
    cuts = cuts_of(weights.shape[1])
    copies = [
        pltpu.make_async_copy(
            dense.at[:, pl.ds(at, size)], weights.at[:, pl.ds(at, size)], sems.at[k]
        )
        for k, (at, size) in enumerate(cuts)
    ]
    for copy in copies:
        copy.start()
    x = jnp.where(flag[0] > 0, came[...].astype(F32), entering[...].astype(F32))
    stream[...] = x
    sent(stream)
    low = (x * norm_parts(x) * gain[...]).astype(BF)
    normed[...] = low
    sent(normed)
    keys = pair.shape[1] // 2
    for copy, (at, size) in zip(copies, cuts):
        copy.wait()
        part = dot(low, weights[:, at : at + size])
        for begin in range(at, at + size, HEAD_DIM):
            head = part[:, begin - at : begin - at + HEAD_DIM]
            if begin < width + keys:
                head = turned(head, cosine[...], sine[...])
            head = head.astype(BF)
            if begin < width:
                query[:, begin : begin + HEAD_DIM] = head
            else:
                pair[:, begin - width : begin - width + HEAD_DIM] = head
            if begin + HEAD_DIM == width:
                sent(query)


def project_all(entering, gain, cosine, sine, dense, pair, *rest):
    outs, (weights, sems) = rest[:-2], rest[-2:]
    micro, unused, tokens, width = entering.shape
    cuts = cuts_of(weights.shape[1])
    copies = [
        pltpu.make_async_copy(
            dense.at[:, pl.ds(at, size)], weights.at[:, pl.ds(at, size)], sems.at[k]
        )
        for k, (at, size) in enumerate(cuts)
    ]
    for copy in copies:
        copy.start()
    lows = []
    for m in range(micro):
        x = entering[m, 0].astype(F32)
        outs[2 * m][...] = x
        sent(outs[2 * m])
        lows.append((x * norm_parts(x) * gain[...]).astype(BF))
    low = jnp.concatenate(lows, 0)
    cosines = jnp.concatenate([cosine[...]] * micro, 0)
    sines = jnp.concatenate([sine[...]] * micro, 0)
    keys = pair.shape[1] // 2
    for copy, (at, size) in zip(copies, cuts):
        copy.wait()
        part = dot(low, weights[:, at : at + size])
        for begin in range(at, at + size, HEAD_DIM):
            head = part[:, begin - at : begin - at + HEAD_DIM]
            if begin < width + keys:
                head = turned(head, cosines, sines)
            head = head.astype(BF)
            if begin < width:
                for m in range(micro):
                    outs[2 * m + 1][:, begin : begin + HEAD_DIM] = head[
                        m * tokens : (m + 1) * tokens
                    ]
            else:
                pair[:, begin - width : begin - width + HEAD_DIM] = head
            if begin + HEAD_DIM == width:
                for m in range(micro):
                    sent(outs[2 * m + 1])


def slot_experts(slots):
    own = lax.broadcasted_iota(jnp.int32, (slots, LANES), 0) // ROOMS
    return own == lax.broadcasted_iota(jnp.int32, (slots, LANES), 1)


def slot_gates(dispatch, gates):
    here = slot_experts(dispatch.shape[0])
    return jnp.sum(jnp.where(here, dot(dispatch, gates.astype(BF)), 0.0), -1, keepdims=True)


def attend(
    keep, m, flag, stream, query, pair0, pair1, pair2, pair3, bias, gain, chosen, dispatch, target,
    *rest,
):
    dense, middle, gates, outgoing = rest[:4]
    kept, (mixed, weights, router, sems) = rest[4:-4], rest[-4:]
    width = stream.shape[1]
    at = dense.shape[1] - width - LANES
    copies = [
        pltpu.make_async_copy(dense.at[:, pl.ds(at + LANES, width)], weights, sems.at[0]),
        pltpu.make_async_copy(dense.at[:, pl.ds(at, LANES)], router, sems.at[1]),
    ]
    for copy in copies:
        copy.start()
    tokens = stream.shape[0]
    pairs = jnp.concatenate(
        [p[m * tokens : (m + 1) * tokens, :] for p in (pair0, pair1, pair2, pair3)], 0
    )
    kv_heads = pairs.shape[1] // (2 * HEAD_DIM)
    group = width // HEAD_DIM // kv_heads
    biases = jnp.concatenate([bias[...]] * group, 0)
    for h in range(kv_heads):
        keys = pairs[:, h * HEAD_DIM : (h + 1) * HEAD_DIM]
        values = pairs[:, (kv_heads + h) * HEAD_DIM : (kv_heads + h + 1) * HEAD_DIM]
        queries = stacked_heads(query, h * group, group)
        scores = dot(queries, keys, (1, 1)) * HEAD_DIM ** (-0.5) + biases
        expo = jnp.exp(scores - jnp.max(scores, -1, keepdims=True))
        weight = (expo * (1.0 / jnp.sum(expo, -1, keepdims=True))).astype(BF)
        if keep:
            kept[0][h] = weight
        done = dot(weight, values).astype(BF)
        for j in range(group):
            begin = (h * group + j) * HEAD_DIM
            mixed[:, begin : begin + HEAD_DIM] = done[j * tokens : (j + 1) * tokens]
    if keep:
        kept[1][...] = mixed[...]
        sent(kept[0])
        sent(kept[1])
    copies[0].wait()
    x = stream[...] + dot(mixed[...], weights[...])
    middle[...] = x
    sent(middle)
    low = (x * norm_parts(x) * gain[...]).astype(BF)
    if keep:
        kept[2][...] = low
        sent(kept[2])
    copies[1].wait()
    taken = chosen[...] > 0
    logits = jnp.where(taken, dot(low, router[...]), -1e30)
    expo = jnp.where(taken, jnp.exp(logits - jnp.max(logits, -1, keepdims=True)), 0.0)
    share = expo / jnp.sum(expo, -1, keepdims=True)
    gates[...] = share
    sent(gates)
    slots = dispatch[...]
    per, columns = outgoing.shape[1], outgoing.shape[0]
    if keep:
        outgoing[:, :, :width] = dot(slots, low).astype(BF).reshape(columns, per, width)
        lane = lax.broadcasted_iota(jnp.int32, (slots.shape[0], LANES), 1)
        notes = jnp.where(lane == 0, slot_gates(slots, share), 0.0).astype(BF)
        outgoing[:, :, width:] = notes.reshape(columns, per, LANES)
    else:
        low = jnp.where(flag[0] > 0, target[...], low)
        outgoing[...] = dot(slots, low).astype(BF).reshape(columns, per, width)


def by_expert(refs, experts):
    whole = [[[r.at[j] for j in range(experts)] for r in refs[at : at + 4]] for at in (0, 4)]
    down = [[r.at[j] for j in range(experts)] for r in refs[8:10]]
    for at in (10, 10 + experts):
        down.append([r.at[0] for r in refs[at : at + experts]])
    return [*whole, down]


class Fetched:
    def __init__(self, shards, weights, sems):
        self.weights = weights
        self.copies = {}
        for j in range(weights.shape[1]):
            for k in range(weights.shape[0]):
                self.copies[k, j] = [
                    pltpu.make_async_copy(
                        shards[k][p][j],
                        weights.at[k, j, pl.ds(p * shards[k][p][j].shape[0], shards[k][p][j].shape[0])],
                        sems.at[k, j, p],
                    )
                    for p in range(4)
                ]
        for k in range(weights.shape[0]):
            self.start(k, 0)

    def start(self, k, j):
        for copy in self.copies.get((k, j), ()):
            copy.start()

    def ready(self, k, j):
        done_with(self.copies[k, j])
        self.start(k, j + 1)


def done_with(copies):
    for copy in copies:
        copy.wait()


def rows_of(value, j, begin=0):
    columns, unused, width = value.shape
    at = begin + j * ROOMS
    return value[:, at : at + ROOMS, :].reshape(columns * ROOMS, width)


def put_rows(out, j, rows, inner):
    at, width = j * ROOMS, rows.shape[1]
    out[:, at : at + ROOMS, :width] = rows.reshape(-1, ROOMS, width)
    high = inner.astype(BF).astype(F32)
    lane = lax.broadcasted_iota(jnp.int32, (rows.shape[0], LANES), 1)
    both = jnp.where(lane == 0, high, jnp.where(lane == 1, inner - high, 0.0))
    out[:, at : at + ROOMS, width:] = both.astype(BF).reshape(-1, ROOMS, LANES)


def expert_forward(both, arrived, *refs):
    early, refs = (refs[0], refs[1:]) if both else (None, refs)
    weights, sems = refs[-2:]
    experts = weights.shape[1]
    count = 10 + 2 * experts
    outs = refs[count:-2]
    fetched = Fetched(by_expert(refs, experts), weights, sems)
    width = weights.shape[3]
    for j in range(weights.shape[1]):
        at = j * ROOMS
        noted = rows_of(arrived, j)
        rows = noted[:, :width]
        fetched.ready(0, j)
        gate = dot(rows, weights[0, j], (1, 1))
        fetched.ready(1, j)
        lifted = dot(rows, weights[1, j], (1, 1))
        square = gate * gate
        bend = jnp.tanh(0.7978845608028654 * gate * (1.0 + 0.044715 * square))
        active = 0.5 * gate * (1.0 + bend)
        hidden = (active * lifted).astype(BF)
        fetched.ready(2, j)
        made = dot(hidden, weights[2, j]).astype(BF)
        outs[0][:, at : at + ROOMS, :] = made.reshape(-1, ROOMS, made.shape[1])
        sent(outs[0], (slice(None), pl.ds(at, ROOMS)))
        if both:
            slope = 0.5 * (1.0 + bend) + 0.5 * gate * (1.0 - bend * bend) * (
                0.7978845608028654 * (1.0 + 3 * 0.044715 * square)
            )
            bent = slope * lifted
            outs[1][j] = hidden
            outs[2][j] = active.astype(BF)
            outs[3][j] = bent.astype(BF)
            grads = (rows_of(early, j).astype(F32) * noted[:, width : width + 1].astype(F32)).astype(BF)
            hidden_grads = dot(grads, weights[2, j], (1, 1))
            gate_part = (hidden_grads * bent).astype(BF)
            lifted_part = (hidden_grads * active).astype(BF)
            inner = jnp.sum(hidden_grads * hidden.astype(F32), -1, keepdims=True)
            back = dot(gate_part, weights[0, j]) + dot(lifted_part, weights[1, j])
            put_rows(outs[4], j, back.astype(BF), inner)
            sent(outs[4], (slice(None), pl.ds(at, ROOMS)))
            for out in outs[1:4]:
                sent(out, j)


def combine(returned, middle, gates, spread, places, low):
    weights = (dot(gates[...].astype(BF), spread[...]) * places[...].astype(F32)).astype(BF)
    done = middle[...] + dot(weights, returned[...].reshape(-1, returned.shape[2]))
    low[...] = done.astype(BF)


def last_outputs(flag, spread, *refs):
    out = refs[-1]
    width = out.shape[2]
    for m in range(out.shape[0]):
        returned, middle, gates, places, before = refs[5 * m : 5 * m + 5]
        weights = (dot(gates[...].astype(BF), spread[...]) * places[...].astype(F32)).astype(BF)
        rows = returned[:, :, :width].reshape(-1, width)
        out[m] = jnp.where(flag[0] > 0, middle[...] + dot(weights, rows), before[...].astype(F32))


def send_grads(flag, came, target, gates, dispatch, grad, outgoing):
    low = jnp.where(flag[0] > 0, came[...], target[...])
    grad[...] = low
    sent(grad)
    slots = dispatch[...]
    rows = dot(slots, low) * slot_gates(slots, gates[...])
    outgoing[...] = rows.astype(BF).reshape(outgoing.shape)


def expert_backward(flag, arrived, hidden, active, bent, produced, *refs):
    out, gate_back, lifted_back, weights, sems = refs[-5:]
    gate_shards, up_shards, down_shards = by_expert(refs, weights.shape[1])
    fetched = Fetched([down_shards, gate_shards, up_shards], weights, sems)
    for j in range(weights.shape[1]):
        fetched.ready(0, j)
        hidden_grads = dot(rows_of(arrived, j), weights[0, j], (1, 1))
        gate_part = (hidden_grads * bent[j].astype(F32)).astype(BF)
        lifted_part = (hidden_grads * active[j].astype(F32)).astype(BF)
        gate_back[j] = gate_part
        lifted_back[j] = lifted_part
        inner = jnp.sum(hidden_grads * hidden[j].astype(F32), -1, keepdims=True)
        fetched.ready(1, j)
        done = dot(gate_part, weights[1, j])
        fetched.ready(2, j)
        done = (done + dot(lifted_part, weights[2, j])).astype(BF)
        put_rows(out, j, jnp.where(flag[0] > 0, rows_of(produced, j), done), inner)
        sent(out, (slice(None), pl.ds(j * ROOMS, ROOMS)))
        sent(gate_back, j)
        sent(lifted_back, j)


def attend_back(
    keep, row, flag, token_grads, before, gates, places, middle, gain, grad, query, pair0, pair1,
    pair2, pair3, probs, cosine, sine, dense, middle_grads, query_back, part0, part1, part2, part3,
    *rest,
):
    tokens, width = middle.shape
    kept, (branch, weights, router, sems) = rest[:-4], rest[-4:]
    at = dense.shape[1] - width - LANES
    copies = [
        pltpu.make_async_copy(dense.at[:, pl.ds(at, LANES)], router, sems.at[1]),
        pltpu.make_async_copy(dense.at[:, pl.ds(at + LANES, width)], weights, sems.at[0]),
    ]
    for copy in copies:
        copy.start()
    came = token_grads[...]
    if keep:
        came = jnp.where(flag[0] > 0, before[...], came)
    came = came.reshape(-1, came.shape[2])
    place = places[...]
    here = slot_experts(came.shape[0])
    notes = came[:, width:].astype(F32)
    high = jnp.where(here, notes[:, :1], 0.0).astype(BF)
    rest_of = jnp.where(here, notes[:, 1:2], 0.0).astype(BF)
    inner = dot(place, high) + dot(place, rest_of)
    logit_grads = (inner - gates[...] * jnp.sum(inner, -1, keepdims=True)).astype(BF)
    ffn_grads = dot(place, came[:, :width])
    copies[0].wait()
    ffn_grads = ffn_grads + dot(logit_grads, router[...], (1, 1))
    part, total = norm_back(ffn_grads, middle[...], gain[...])
    above = grad[...].astype(F32) + part
    middle_grads[...] = above
    sent(middle_grads)
    low = above.astype(BF)
    if keep:
        kept[0][...] = logit_grads
        kept[1][...] = jnp.broadcast_to(total, kept[1].shape)
        sent(kept[0])
        sent(kept[1])
        branch[...] = low
        share = width // 4
        for s, part in enumerate((part0, part1, part2, part3)):
            begin = pl.multiple_of((row[0] ^ s) * share, LANES)
            part[:, part.shape[1] - share :] = branch[:, pl.ds(begin, share)]
    copies[1].wait()
    mixed_grads = dot(low, weights[...], (1, 1)).astype(BF)
    pairs = stacked((pair0, pair1, pair2, pair3))
    kv_heads = pairs.shape[1] // (2 * HEAD_DIM)
    group = width // HEAD_DIM // kv_heads
    scale = HEAD_DIM ** (-0.5)
    parts = (part0, part1, part2, part3)
    for h in range(kv_heads):
        keys = pairs[:, h * HEAD_DIM : (h + 1) * HEAD_DIM]
        values = pairs[:, (kv_heads + h) * HEAD_DIM : (kv_heads + h + 1) * HEAD_DIM]
        queries = stacked_heads(query, h * group, group)
        top = stacked_heads(mixed_grads, h * group, group)
        weight = probs[h]
        wide = weight.astype(F32)
        weight_grads = dot(top, values, (1, 1))
        value_grads = dot(weight, top, (0, 0)).astype(BF)
        inner = wide * weight_grads
        score_grads = (inner - wide * jnp.sum(inner, -1, keepdims=True)).astype(BF)
        query_grads = dot(score_grads, keys) * scale
        key_grads = (dot(score_grads, queries, (0, 0)) * scale).astype(BF)
        for j in range(group):
            begin = (h * group + j) * HEAD_DIM
            one = query_grads[j * tokens : (j + 1) * tokens]
            query_back[:, begin : begin + HEAD_DIM] = turned(one, cosine[...], -sine[...]).astype(BF)
        for p, part in enumerate(parts):
            part[:, h * HEAD_DIM : (h + 1) * HEAD_DIM] = key_grads[p * tokens : (p + 1) * tokens]
            begin = (kv_heads + h) * HEAD_DIM
            part[:, begin : begin + HEAD_DIM] = value_grads[p * tokens : (p + 1) * tokens]


def project_back(
    keep, row, part0, part1, part2, part3, query_back, stream, gain, middle_grads, cosine, sine,
    dense, low, *rest,
):
    width = stream.shape[1]
    kept, (backs, weights, sems) = rest[:-3], rest[-3:]
    cuts = cuts_of(weights.shape[1])
    copies = [
        pltpu.make_async_copy(
            dense.at[:, pl.ds(at, size)], weights.at[:, pl.ds(at, size)], sems.at[k]
        )
        for k, (at, size) in enumerate(cuts)
    ]
    for copy in copies:
        copy.start()
    pairs = weights.shape[1] - width
    total = sum(part[:, :pairs].astype(F32) for part in (part0, part1, part2, part3))
    keys = pairs // 2
    backs[:, :width] = query_back[...]
    backs[:, width : width + keys] = turned(total[:, :keys], cosine[...], -sine[...]).astype(BF)
    backs[:, width + keys :] = total[:, keys:].astype(BF)
    if keep:
        share = backs.shape[1] // 4
        for s, out in enumerate(kept[1:]):
            out[...] = backs[:, pl.ds(pl.multiple_of((row[0] ^ s) * share, LANES), share)]
            sent(out)
    above = jnp.zeros(stream.shape, F32)
    for copy, (at, size) in zip(copies, cuts):
        copy.wait()
        above = above + dot(backs[:, at : at + size], weights[:, at : at + size], (1, 1))
    part, unused = norm_back(above, stream[...], gain[...])
    done = middle_grads[...] + part
    if keep:
        kept[0][...] = done
    low[...] = done.astype(BF)


def expert_weight_grads(begin_left, which, *refs):
    count = len(which)
    rights = sorted({w for w in which})
    sources, outs = refs[: 2 * count + 2 * len(rights)], refs[2 * count + 2 * len(rights) : -3]
    left, right, sems = refs[-3:]
    experts, deep, wide = left.shape[1:]
    columns, width = right.shape[2] // 2, right.shape[4]
    copies = {}
    for j in range(experts):
        for m in range(2):
            for r, (unused, begin) in enumerate(rights):
                copies["right", r, j, m] = pltpu.make_async_copy(
                    sources[2 * count + 2 * r + m].at[
                        :, pl.ds(begin + j * ROOMS, ROOMS), pl.ds(0, width)
                    ],
                    right.at[r, j, pl.ds(m * columns, columns)],
                    sems.at[1, r, j, m],
                )
            for k in range(count):
                copies["left", k, j, m] = pltpu.make_async_copy(
                    sources[2 * k + m].at[j, :, pl.ds(begin_left, wide)],
                    left.at[k, j, pl.ds(m * (deep // 2), deep // 2)],
                    sems.at[0, k, j, m],
                )
    for copy in copies.values():
        copy.start()
    waiting = dict(copies)

    def there(*name):
        for m in range(2):
            copy = waiting.pop((*name, m), None)
            if copy is not None:
                copy.wait()

    for j in range(experts):
        for k, name in enumerate(which):
            r = rights.index(name)
            there("right", r, j)
            there("left", k, j)
            total = dot(left[k, j], right[r, j].reshape(deep, width), (0, 0))
            some = len(outs) // count
            size = wide // some
            for q, out in enumerate(outs[some * k : some * (k + 1)]):
                out[j] = total[q * size : (q + 1) * size].astype(BF)
                sent(out, j)


def add(*refs):
    count = len(refs) // 3
    for k in range(count):
        one, other, total = refs[2 * k], refs[2 * k + 1], refs[2 * count + k]
        total[...] = (one[...].astype(F32) + other[...].astype(F32)).astype(BF)


def pack(*refs):
    for k, value in enumerate(refs[:-1]):
        refs[-1][k] = value[...]


def stacked(refs):
    return jnp.concatenate([r[...] for r in refs], 0)


def by_owner(out, grads, begin):
    columns, lines, unused = out.shape
    size = lines // 4
    for c in range(columns):
        some = [grads[(r * columns + c) * size : (r * columns + c + 1) * size] for r in range(4)]
        out[c, :, begin : begin + grads.shape[1]] = jnp.concatenate(some, 0).astype(BF)


def out_grads(*refs):
    lefts, rights, normed, logits, gains, out = (
        refs[:4], refs[4:12], refs[12:14], refs[14:16], refs[16:18], refs[18],
    )
    share = out.shape[2] - LANES
    left = jnp.concatenate([one[k] for one in lefts for k in (2, 3)], 0)
    right = jnp.concatenate([r[:, r.shape[1] - share :] for r in rights], 0)
    by_owner(out, dot(left, right, (0, 0)), 0)
    width = left.shape[1]
    line = lax.broadcasted_iota(jnp.int32, (LANES, width), 0)
    sums = jnp.where(line == LANES - 1, gains[0][:1, :] + gains[1][:1, :], 0.0)
    by_owner(out, dot(stacked(normed), stacked(logits), (0, 0)) + sums.T, share)


def qkv_grads(*refs):
    lefts, rights, out = refs[:4], refs[4:12], refs[12]
    left = jnp.concatenate([one[k] for one in lefts for k in (0, 1)], 0)
    by_owner(out, dot(left, stacked(rights), (0, 0)), 0)


def fold(row, first, second, out0, out1, out2, out3, total):
    share = first.shape[2]
    total[:, :share] = jnp.sum(first[...].astype(F32), 0)
    total[:, share:] = jnp.sum(second[...].astype(F32), 0)
    for s, out in enumerate((out0, out1, out2, out3)):
        size = out.shape[0]
        out[...] = total[pl.ds(pl.multiple_of((row[0] ^ s) * size, 8), size), :]
        sent(out)


def finish(
    row, in0, in1, in2, in3, w_query, w_key, w_value, gain, o_grad, q_grad, k_grad, v_grad, r_grad,
    first, second, total,
):
    share = o_grad.shape[1] // 4
    piece = total.shape[1] // 4
    ins = (in0, in1, in2, in3)
    for s, one in enumerate(ins):
        where = row[0] ^ s
        o_grad[:, pl.ds(pl.multiple_of(where * share, LANES), share)] = one[:, :share]
        total[:, pl.ds(pl.multiple_of(where * piece, LANES), piece)] = one[:, share + LANES :]
    rest = sum(one[:, share : share + LANES] for one in ins)
    r_grad[...] = rest[:, : r_grad.shape[1]]
    second[...] = rest.T[LANES - 1 :, :]
    begin, inner = 0, jnp.zeros((total.shape[0], 1), F32)
    for out, weight in ((q_grad, w_query), (k_grad, w_key), (v_grad, w_value)):
        part = total[:, begin : begin + out.shape[1]]
        out[...] = part
        inner = inner + jnp.sum(part * weight[...].astype(F32), -1, keepdims=True)
        begin += out.shape[1]
    line = jnp.broadcast_to(inner, (total.shape[0], LANES)).T[:1, :]
    first[...] = line / gain[...].astype(F32)


def over_columns(value):
    return lax.all_to_all(value, "col", split_axis=0, concat_axis=0, tiled=True)


def on_device(
    inputs, cotangent, segment_ids, routes, attn_gain, w_query, w_key, w_value, w_out, ffn_gain,
    w_router, w_gate, w_up, w_down,
):
    section = lax.axis_index("section")
    row = lax.axis_index("row")
    rows = lax.axis_size("row")
    columns = lax.axis_size("col")
    micro, tokens, width = inputs.shape[0], inputs.shape[2], inputs.shape[3]
    experts = w_router.shape[2]
    per_column = w_gate.shape[1]
    hidden_width = w_gate.shape[2] * rows
    kv_width = w_key.shape[2]
    qkv_width = width + 2 * kv_width
    slots = experts * ROOMS
    share = width // rows
    shard = width // (rows * columns)
    heads = width // HEAD_DIM
    kv_heads = kv_width // HEAD_DIM
    length = rows * tokens
    pieces = range(micro)
    steps = range(rows)
    here = row.astype(jnp.int32)[None]
    second = (section == 1).astype(jnp.int32)[None]
    block = (columns, slots // columns, width)

    dense = jnp.concatenate(
        [w_query[0], w_key[0], w_value[0], w_router[0], attn_gain[0][:, None], ffn_gain[0][:, None],
         jnp.zeros((shard, LANES - experts - 2), BF), w_out[0]], 1
    )
    dense = lax.all_gather(dense, ("row", "col"), axis=0, tiled=True)
    small = dense[:, qkv_width : qkv_width + LANES]
    gain_a = small[:, experts].astype(F32)[None, :]
    gain_f = small[:, experts + 1].astype(F32)[None, :]

    def shards_of(own):
        two = swapped(own, 2)
        return own, swapped(own, 1), two, swapped(two, 1)

    gate_shards, up_shards = shards_of(w_gate[0]), shards_of(w_up[0])
    down_twos = [swapped(w_down[0, j : j + 1], 2) for j in range(per_column)]
    shards = (
        *gate_shards, *up_shards, w_down[0], swapped(w_down[0], 1), *down_twos,
        *[swapped(two, 1) for two in down_twos],
    )

    lane = jnp.arange(LANES, dtype=jnp.int32)
    half = HEAD_DIM // 2
    freqs = 10000.0 ** (-2.0 * jnp.arange(half).astype(F32) / HEAD_DIM)
    positions = row * tokens + jnp.arange(tokens, dtype=jnp.int32)
    angles = positions.astype(F32)[:, None] * freqs[None, :]
    cosine = jnp.concatenate([jnp.cos(angles)] * 2, 1)
    sine = jnp.concatenate([-jnp.sin(angles), jnp.sin(angles)], 1)
    key_positions = jnp.concatenate(
        [(row ^ step) * tokens + jnp.arange(tokens, dtype=jnp.int32) for step in steps]
    )
    spread = (lane[:, None] == jnp.arange(slots, dtype=jnp.int32)[None, :] // ROOMS).astype(BF)
    below = (jnp.arange(tokens)[:, None] > jnp.arange(tokens)[None, :]).astype(BF)
    biases, chosens, places, dispatches = [], [], [], []
    for m in pieces:
        segments = segment_ids[m, 0]
        own_segments = lax.dynamic_slice_in_dim(segments, row * tokens, tokens)
        key_segments = jnp.concatenate(
            [lax.dynamic_slice_in_dim(segments, (row ^ s) * tokens, tokens) for s in steps]
        )
        counted = (key_positions[None, :] <= positions[:, None]) & (
            key_segments[None, :] == own_segments[:, None]
        )
        biases.append(jnp.where(counted, 0.0, -1e30).astype(F32))
        chosen = jnp.any(routes[0, m, 0][:, :, None] == lane[None, None, :], 1)
        chosens.append(chosen.astype(F32))
        rank = dot(below, chosen.astype(BF))
        rank = jnp.where(chosen, rank, -1.0)[:, :experts]
        place = (
            rank[:, :, None] == jnp.arange(ROOMS, dtype=F32)[None, None, :]
        ).reshape(tokens, slots)
        places.append(place.astype(BF))
        dispatches.append(place.T.astype(BF))

    token_low, token_wide = like((tokens, width), BF), like((tokens, width), F32)
    pair_like = like((tokens, 2 * kv_width), BF)
    block_like = like(block, BF)
    sums_like = like((8, width), F32)
    kept_like = like((per_column, columns * ROOMS, hidden_width), BF)
    probs_like = like((kv_heads, heads // kv_heads * tokens, length), BF)
    qkv_scratch = [pltpu.VMEM((width, qkv_width), BF), pltpu.SemaphoreType.DMA((8,))]
    out_scratch = [
        pltpu.VMEM((width, width), BF), pltpu.VMEM((width, LANES), BF),
        pltpu.SemaphoreType.DMA((2,)),
    ]
    expert_scratch = [
        pltpu.VMEM((3, per_column, hidden_width, width), BF),
        pltpu.SemaphoreType.DMA((3, per_column, 4)),
    ]
    qkv_flops = 2 * tokens * width * qkv_width
    out_flops = 2 * tokens * width * width + 2 * slots * tokens * width
    score_flops = 2 * heads * tokens * length * HEAD_DIM
    expert_flops = 2 * slots * hidden_width * width

    per = slots // columns
    back_like = like((columns, per, width + LANES), BF)
    lanes_like = like((tokens, LANES), F32)
    tables = late([cosine, sine])
    first_flag = (1 - second)

    def forward(keep, came, waits, early):
        projected, pairs = [], []
        if keep:
            for m in pieces:
                projected.append(
                    call(
                        project,
                        (Sent(token_wide), Sent(token_low), Sent(token_low), Sent(pair_like)),
                        (Late(came[m]), Late(inputs, (m, 0)), Late(gain_a), *tables), qkv_flops, (dense,),
                        qkv_scratch, (second,), waits=[p[0] for p in projected],
                    )
                )
                pairs.append([projected[m][3]] + [swapped(projected[m][3], s) for s in steps[1:]])
        else:
            pair, *streams = call(
                project_all,
                (Sent(like((micro * tokens, 2 * kv_width), BF)),)
                + (Sent(token_wide), Sent(token_low)) * micro,
                (Late(inputs), Late(gain_a), *tables), micro * qkv_flops, (dense,),
                qkv_scratch, waits=waits,
            )
            projected = [(streams[2 * m], None, streams[2 * m + 1]) for m in pieces]
            pairs = [[pair] + [swapped(pair, s) for s in steps[1:]]] * micro
        attended = [
            call(
                functools.partial(attend, keep, 0 if keep else m),
                (Sent(token_wide), Sent(lanes_like), Sent(back_like if keep else block_like))
                + ((Sent(probs_like), Sent(token_low), Sent(token_low)) if keep else ()),
                (*late([projected[m][0], projected[m][2], *pairs[m], biases[m], gain_f, chosens[m],
                        dispatches[m]]), Late(cotangent, (m, 0))),
                out_flops + 2 * score_flops, (dense,), [pltpu.VMEM((tokens, width), BF)] + out_scratch,
                (second,),
            )
            for m in pieces
        ]
        arrived = [over_columns(a[2]) for a in attended]
        lefts, ready = [], ()
        if keep:
            left = call(
                pack, (Sent(like((2 * micro, tokens, width), BF)),),
                late([p[1] for p in projected] + [a[4] for a in attended]), 0,
            )[0]
            two = swapped(left, 2)
            lefts = [left, swapped(left, 1), two, swapped(two, 1)]
            ready = (two,)
        applied = [
            call(
                functools.partial(expert_forward, keep),
                (Sent(block_like),)
                + ((Sent(kept_like),) * 3 + (Sent(back_like),) if keep else ()),
                late([arrived[m], early[m]] if keep else [arrived[m]]),
                (6 if keep else 3) * expert_flops, shards, expert_scratch,
                waits=ready if m else (attended[1][2],),
            )
            for m in pieces
        ]
        return projected, pairs, attended, arrived, applied, lefts

    def weight_call(quarters, which, lefts, rights, waits):
        quarter, some = hidden_width // 4, len(quarters)
        return call(
            functools.partial(expert_weight_grads, quarters[0] * quarter, which),
            (Sent(like((per_column, quarter, width), BF)),) * (some * len(which)), (),
            len(which) * expert_flops, [*lefts, *rights],
            [pltpu.VMEM((len(which), per_column, 2 * columns * ROOMS, some * quarter), BF),
             pltpu.VMEM((len(rights) // 2, per_column, 2 * columns, ROOMS, width), BF),
             pltpu.SemaphoreType.DMA((2, len(which), per_column, 2))],
            waits=waits,
        )

    def merged(halves, waits):
        pairs = [v for a, b in halves for v in (a, swapped(b, 1))]
        return call(add, [Sent(a) for a, unused in halves], late(pairs), 0, waits=waits)

    def attention_back(keep, m, grad, token_grads, waits):
        return call(
            functools.partial(attend_back, keep),
            (Sent(token_wide), Sent(token_low))
            + (Sent(like((tokens, 2 * kv_width + (share if keep else 0)), BF)),) * rows
            + ((Sent(like((tokens, LANES), BF)), Sent(sums_like)) if keep else ()),
            (*late([token_grads, shared[m] if keep else spread, attended[m][1], places[m],
                                 attended[m][0], gain_f]), Late(*grad),
             *late([projected[m][2], *pairs[m], attended[m][3], cosine, sine])),
            out_flops + 4 * score_flops, (dense,), [pltpu.VMEM((tokens, width), BF)] + out_scratch,
            (here, second), waits,
        )

    def parts_of(inner):
        return [inner[2]] + [swapped(inner[2 + s], s) for s in steps[1:]]

    def projection_back(keep, m, inner, parts, waits):
        return call(
            functools.partial(project_back, keep),
            (Sent(token_low),)
            + ((Sent(token_wide),) + (Sent(like((tokens, qkv_width // rows), BF)),) * rows
               if keep else ()),
            (*late([*parts, inner[1], projected[m][0], gain_a, inner[0]]),
             *tables),
            qkv_flops, (dense,), [pltpu.VMEM((tokens, qkv_width), BF)] + qkv_scratch,
            (here,), waits,
        )

    kept = forward(False, None, (gate_shards[2], up_shards[2], down_twos[0]), None)
    attended, early, applied = kept[2:5]
    returned = [over_columns(a[0]) for a in applied]
    results = [
        call(
            combine, (Sent(token_low),),
            late([returned[m], attended[m][0], attended[m][1], spread, places[m]]),
            2 * slots * tokens * width, waits=() if m else (applied[1][0],),
        )
        for m in pieces
    ]
    came = [lax.ppermute(r[0], "section", [(0, 1)]) for r in results]

    projected, pairs, attended, arrived, applied, lefts = forward(True, came, (), early)
    hidden = [a[1] for a in applied]
    shared = [over_columns(a[4]) for a in applied]
    inner, outer = [], []
    for m in pieces:
        waits = (*lefts[1:], outer[0][0]) if m else (applied[1][4],)
        inner.append(attention_back(False, m, (cotangent, (m, 0)), shared[m], waits))
        outer.append(projection_back(False, m, inner[m], parts_of(inner[m]), ()))
    came = [lax.ppermute(o[0], "section", [(1, 0)]) for o in outer]

    given = [
        call(
            send_grads, (Sent(token_low), Sent(block_like)),
            (Late(came[m]), Late(cotangent, (m, 0)), *late([attended[m][1], dispatches[m]])),
            2 * slots * tokens * width, scalars=(first_flag,), waits=() if m else (inner[1][0],),
        )
        for m in pieces
    ]
    arrived_grads = [over_columns(g[1]) for g in given]
    moved = [
        call(
            expert_backward, (Sent(back_like), Sent(kept_like), Sent(kept_like)),
            late([arrived_grads[m], hidden[m], applied[m][2], applied[m][3], applied[m][0]]),
            3 * expert_flops, shards, expert_scratch,
            (second,), () if m else (given[1][1],),
        )
        for m in pieces
    ]
    back = [over_columns(a[0]) for a in moved]
    gate_up = [a[1] for a in moved] + [a[2] for a in moved]
    down_far = merged([weight_call((2, 3), ((0, 0),), hidden, arrived_grads, ())], ())[0]
    crossed = [swapped(down_far, 2)]
    inner = [attention_back(True, 0, given[0][:1], back[0], (moved[1][0], down_far))]
    parts = [parts_of(inner[0])]
    both = weight_call((0, 1, 2, 3), ((0, 0), (0, 0)), gate_up, arrived, (inner[0][0],))
    inner.append(attention_back(True, 1, given[1][:1], back[1], (both[0], crossed[0])))
    parts.append(parts_of(inner[1]))
    sums = merged([both[2:4], both[6:]], (inner[1][0],))
    gate_far = hold(sums[0], *parts[1][1:])
    crossed.append(swapped(gate_far, 2))
    o_grads = call(
        out_grads, (Sent(like((columns, rows * shard, share + LANES), BF)),),
        late([*lefts, *[p[s] for s in steps for p in parts], *[a[5] for a in attended],
              *[a[6] for a in inner], *[a[7] for a in inner]]),
        2 * width * length * micro * share, waits=(crossed[0], gate_far),
    )[0]
    last = projection_back(True, 1, inner[1], parts[1], (o_grads,))
    outer = [projection_back(True, 0, inner[0], parts[0], (last[0],)), last]
    backs = [[o[2]] + [swapped(o[2 + s], s) for s in steps[1:]] for o in outer]
    crossed.append(swapped(hold(sums[1], *backs[0][1:], *backs[1][1:]), 2))
    near = weight_call((0, 1), ((0, 0),), hidden, arrived_grads, (outer[1][0],))
    w_grads = call(
        qkv_grads, (Sent(like((columns, rows * shard, qkv_width // rows), BF)),),
        late([*lefts, *[b[s] for s in steps for b in backs]]),
        2 * width * length * micro * qkv_width // rows, waits=(crossed[1], near[0]),
    )[0]
    expert_grads = [
        one.astype(F32) + swapped(other, 1).astype(F32) + c.astype(F32)
        for one, other, c in zip((near[0], both[0], both[4]), (near[1], both[1], both[5]), crossed)
    ]
    layer_outputs = call(
        last_outputs, (Sent(like((micro, tokens, width), F32)),),
        late([spread] + [v for m in pieces for v in (
            back[m], attended[m][0], attended[m][1], places[m], results[m][0])]),
        4 * slots * tokens * width, scalars=(second,), waits=(w_grads,),
    )[0]

    wide = share + qkv_width // rows + LANES
    pieces_out = call(
        fold, (Sent(like((shard, wide), F32)),) * rows,
        late([over_columns(o_grads), over_columns(w_grads)]), 0,
        scratch=[pltpu.VMEM((rows * shard, wide), F32)], scalars=(here,),
    )
    pieces_out = [pieces_out[0]] + [swapped(pieces_out[s], s) for s in steps[1:]]
    o_grad, q_grad, k_grad, v_grad, r_grad, first, second_sum = call(
        finish,
        (like((shard, width), F32), like((shard, width), F32), like((shard, kv_width), F32),
         like((shard, kv_width), F32), like((shard, experts), F32), like((1, shard), F32),
         like((1, shard), F32)),
        late([*pieces_out, w_query[0], w_key[0], w_value[0], attn_gain]), 0,
        scratch=[pltpu.VMEM((shard, qkv_width), F32)], scalars=(here,),
    )

    return (
        layer_outputs[None, :, None],
        jnp.stack([o[1] for o in outer])[None, :, None],
        first,
        q_grad[None],
        k_grad[None],
        v_grad[None],
        o_grad[None],
        second_sum,
        r_grad[None],
        expert_grads[1][None],
        expert_grads[2][None],
        expert_grads[0][None],
    )


def solution(mesh):
    dense = P("section", ("row", "col"), None)
    gain = P("section", ("row", "col"))
    expert = P("section", "col", "row", None)
    token = P(None, "col", "row", None)
    layered = P("section", None, "col", "row", None)
    return jax.shard_map(
        on_device,
        mesh=mesh,
        in_specs=(
            token, token, P(None, "col", None), layered, gain, dense, dense, dense, dense, gain,
            dense, expert, expert, expert,
        ),
        out_specs=(
            layered, layered, gain, dense, dense, dense, dense, gain, dense, expert, expert, expert,
        ),
        check_vma=False,
    )
```

```python
import functools

import jax
import jax.numpy as jnp
from jax import lax
from jax.experimental import pallas as pl
from jax.experimental.pallas import tpu as pltpu
from jax.sharding import PartitionSpec as P

HEAD_DIM = 128
ROOMS = 16
EPSILON = 1e-06
LANES = 128
BF = jnp.bfloat16
F32 = jnp.float32
MIB = 1 << 20


def dot(left, right, contract=(1, 0)):
    return lax.dot_general(
        left, right, (((contract[0],), (contract[1],)), ((), ())), preferred_element_type=F32
    )


def like(shape, dtype):
    return jax.ShapeDtypeStruct(shape, dtype)


class Late:
    def __init__(self, source, index=None, target=None, sem=None):
        self.source, self.index, self.target, self.copy = source, index, target, None
        if target is not None:
            source = source if index is None else source.at[index]
            self.copy = pltpu.make_async_copy(source, target, sem)
            self.copy.start()
            self.waiting = True

    def ready(self):
        if self.waiting:
            self.copy.wait()
            self.waiting = False
        return self.target

    def __getitem__(self, index):
        return self.ready()[index]

    @property
    def shape(self):
        return self.source.shape[len(self.index or ()) :]


class Sent:
    def __init__(self, source, target=None, sems=None):
        self.source, self.target, self.sems, self.copies = source, target, sems, []

    def __getitem__(self, index):
        return self.source[index]

    def __setitem__(self, index, value):
        self.source[index] = value

    def send(self, *parts):
        for part in parts or (...,):
            at = len(self.copies)
            whole = part is ...
            copy = pltpu.make_async_copy(
                self.source if whole else self.source.at[part],
                self.target if whole else self.target.at[part],
                self.sems.at[at],
            )
            copy.start()
            self.copies.append(copy)

    @property
    def shape(self):
        return self.source.shape


PARTS = 4


def sent(out, *parts):
    if isinstance(out, Sent):
        out.send(*parts)


def call(body, outs, args, flops, far=(), scratch=(), scalars=(), waits=()):
    arrays = [a.source if isinstance(a, Late) else a for a in args]
    shapes = [o.source if isinstance(o, Sent) else o for o in outs]
    moved = sum(a.size * a.dtype.itemsize for a in (*arrays, *far, *shapes))
    count = len(scalars) + len(args) + len(far)
    kinds = [isinstance(a, Late) for a in args]
    out_kinds = [isinstance(o, Sent) for o in outs]
    buffers = [pltpu.VMEM(a.shape, a.source.dtype) for a in args if isinstance(a, Late)]
    buffers += [pltpu.VMEM(o.shape, o.dtype) for o, k in zip(shapes, out_kinds) if k]

    def run(*refs):
        given, refs = list(refs[:count]), refs[count + len(waits) :]
        results, refs = list(refs[: len(outs)]), refs[len(outs) :]
        own, rest = list(refs[: len(buffers)]), refs[len(buffers) :]
        sems, rest = (rest[0], rest[1:]) if buffers else (None, rest)
        used = 0
        for k, kind in enumerate(kinds):
            if kind:
                at = len(scalars) + k
                given[at] = Late(given[at], args[k].index, own[used], sems.at[used, 0])
                used += 1
        for k, kind in enumerate(out_kinds):
            if kind:
                results[k] = Sent(own[used], results[k], sems.at[used])
                used += 1
        body(*given, *results, *rest)
        for one in given:
            if isinstance(one, Late):
                one.ready()
        for one in results:
            if isinstance(one, Sent) and not one.copies:
                one.send()
        for one in results:
            if isinstance(one, Sent):
                done_with(one.copies)

    anywhere, local = pl.BlockSpec(memory_space=pltpu.HBM), pl.BlockSpec(memory_space=pltpu.VMEM)
    return pl.pallas_call(
        run,
        out_shape=tuple(shapes),
        in_specs=[pl.BlockSpec(memory_space=pltpu.SMEM)] * len(scalars)
        + [anywhere if k else local for k in kinds]
        + [anywhere] * (len(far) + len(waits)),
        out_specs=tuple(anywhere if k else local for k in out_kinds),
        scratch_shapes=buffers
        + ([pltpu.SemaphoreType.DMA((len(buffers), PARTS))] if buffers else [])
        + list(scratch),
        compiler_params=pltpu.CompilerParams(vmem_limit_bytes=64 * MIB),
        cost_estimate=pl.CostEstimate(
            flops=int(flops), bytes_accessed=int(moved), transcendentals=0
        ),
        name=body.func.__name__ if isinstance(body, functools.partial) else body.__name__,
    )(*scalars, *arrays, *far, *waits)


def late(values):
    return [Late(v) for v in values]


def nothing(*refs):
    pass


def hold(value, *waits):
    return pl.pallas_call(
        nothing,
        out_shape=like(value.shape, value.dtype),
        in_specs=[pl.BlockSpec(memory_space=pl.ANY)] * (1 + len(waits)),
        out_specs=pl.BlockSpec(memory_space=pl.ANY),
        input_output_aliases={0: 0},
        name="hold",
    )(value, *waits)


def swapped(value, step):
    rows = lax.axis_size("row")
    return lax.ppermute(value, "row", [(r, r ^ step) for r in range(rows)])


def norm_parts(stream):
    return lax.rsqrt(jnp.mean(stream * stream, -1, keepdims=True) + EPSILON)


def norm_back(grad, stream, gain):
    inverse = norm_parts(stream)
    unit = stream * inverse
    scaled = grad * gain
    back = inverse * (scaled - unit * jnp.mean(scaled * unit, -1, keepdims=True))
    return back, jnp.sum(grad * unit, 0, keepdims=True)


def turned(vectors, cosine, sine):
    done = []
    for at in range(0, vectors.shape[1], HEAD_DIM):
        one = vectors[:, at : at + HEAD_DIM]
        done.append(one * cosine + pltpu.roll(one, HEAD_DIM // 2, 1) * sine)
    return jnp.concatenate(done, -1) if len(done) > 1 else done[0]


def stacked_heads(value, first, count):
    return jnp.concatenate(
        [value[:, (first + j) * HEAD_DIM : (first + j + 1) * HEAD_DIM] for j in range(count)], 0
    )


def unstacked_heads(value, count):
    tokens = value.shape[0] // count
    return jnp.concatenate([value[j * tokens : (j + 1) * tokens] for j in range(count)], 1)


def cuts_of(total, most=512):
    return [(at, min(most, total - at)) for at in range(0, total, most)]


def project(
    flag, came, entering, gain, cosine, sine, dense, stream, normed, query, pair, weights, sems
):
    width = stream.shape[1]
    cuts = cuts_of(weights.shape[1])
    copies = [
        pltpu.make_async_copy(
            dense.at[:, pl.ds(at, size)], weights.at[:, pl.ds(at, size)], sems.at[k]
        )
        for k, (at, size) in enumerate(cuts)
    ]
    for copy in copies:
        copy.start()
    x = jnp.where(flag[0] > 0, came[...].astype(F32), entering[...].astype(F32))
    stream[...] = x
    sent(stream)
    low = (x * norm_parts(x) * gain[...]).astype(BF)
    normed[...] = low
    sent(normed)
    keys = pair.shape[1] // 2
    for copy, (at, size) in zip(copies, cuts):
        copy.wait()
        part = dot(low, weights[:, at : at + size])
        for begin in range(at, at + size, HEAD_DIM):
            head = part[:, begin - at : begin - at + HEAD_DIM]
            if begin < width + keys:
                head = turned(head, cosine[...], sine[...])
            head = head.astype(BF)
            if begin < width:
                query[:, begin : begin + HEAD_DIM] = head
            else:
                pair[:, begin - width : begin - width + HEAD_DIM] = head
            if begin + HEAD_DIM == width:
                sent(query)


def project_all(at_gain, entering, cosine, sine, dense, *rest):
    outs, (weights, small, sems) = rest[:-3], rest[-3:]
    micro, unused, tokens, width = entering.shape
    cuts = cuts_of(weights.shape[1])
    block = pltpu.make_async_copy(
        dense.at[:, pl.ds(weights.shape[1], LANES)], small, sems.at[len(cuts)]
    )
    block.start()
    copies = [
        pltpu.make_async_copy(
            dense.at[:, pl.ds(at, size)], weights.at[:, pl.ds(at, size)], sems.at[k]
        )
        for k, (at, size) in enumerate(cuts)
    ]
    for copy in copies:
        copy.start()
    scaled = []
    for m in range(micro):
        x = entering[m, 0].astype(F32)
        outs[3 * m][...] = x
        sent(outs[3 * m])
        scaled.append(x * norm_parts(x))
    block.wait()
    gain = small[...].astype(F32).T[at_gain : at_gain + 1, :]
    lows = [(x * gain).astype(BF) for x in scaled]
    low = jnp.concatenate(lows, 0)
    cosines = jnp.concatenate([cosine[...]] * micro, 0)
    sines = jnp.concatenate([sine[...]] * micro, 0)
    keys = outs[2].shape[1] // 2
    for copy, (at, size) in zip(copies, cuts):
        copy.wait()
        part = dot(low, weights[:, at : at + size])
        for begin in range(at, at + size, HEAD_DIM):
            head = part[:, begin - at : begin - at + HEAD_DIM]
            if begin < width + keys:
                head = turned(head, cosines, sines)
            head = head.astype(BF)
            for m in range(micro):
                out, to = (outs[3 * m + 1], begin) if begin < width else (outs[3 * m + 2], begin - width)
                out[:, to : to + HEAD_DIM] = head[m * tokens : (m + 1) * tokens]
                if begin + HEAD_DIM == width:
                    sent(out)


def slot_experts(slots):
    own = lax.broadcasted_iota(jnp.int32, (slots, LANES), 0) // ROOMS
    return own == lax.broadcasted_iota(jnp.int32, (slots, LANES), 1)


def slot_gates(dispatch, gates):
    here = slot_experts(dispatch.shape[0])
    return jnp.sum(jnp.where(here, dot(dispatch, gates.astype(BF)), 0.0), -1, keepdims=True)


def attend(
    keep, flag, stream, query, pair0, pair1, pair2, pair3, bias, gain, chosen, dispatch, target,
    *rest,
):
    dense, middle, gates, outgoing = rest[:4]
    kept, (mixed, weights, router, sems) = rest[4:-4], rest[-4:]
    width = stream.shape[1]
    at = dense.shape[1] - width - LANES
    copies = [
        pltpu.make_async_copy(dense.at[:, pl.ds(at + LANES, width)], weights, sems.at[0]),
        pltpu.make_async_copy(dense.at[:, pl.ds(at, LANES)], router, sems.at[1]),
    ]
    for copy in copies:
        copy.start()
    tokens = stream.shape[0]
    pairs = stacked((pair0, pair1, pair2, pair3))
    kv_heads = pairs.shape[1] // (2 * HEAD_DIM)
    group = width // HEAD_DIM // kv_heads
    biases = jnp.concatenate([bias[...]] * group, 0)
    for h in range(kv_heads):
        keys = pairs[:, h * HEAD_DIM : (h + 1) * HEAD_DIM]
        values = pairs[:, (kv_heads + h) * HEAD_DIM : (kv_heads + h + 1) * HEAD_DIM]
        queries = stacked_heads(query, h * group, group)
        scores = dot(queries, keys, (1, 1)) * HEAD_DIM ** (-0.5) + biases
        expo = jnp.exp(scores - jnp.max(scores, -1, keepdims=True))
        weight = (expo * (1.0 / jnp.sum(expo, -1, keepdims=True))).astype(BF)
        if keep:
            kept[0][h] = weight
        done = dot(weight, values).astype(BF)
        for j in range(group):
            begin = (h * group + j) * HEAD_DIM
            mixed[:, begin : begin + HEAD_DIM] = done[j * tokens : (j + 1) * tokens]
    if keep:
        kept[1][...] = mixed[...]
        sent(kept[0])
        sent(kept[1])
    copies[0].wait()
    x = stream[...] + dot(mixed[...], weights[...])
    middle[...] = x
    sent(middle)
    low = (x * norm_parts(x) * gain[...]).astype(BF)
    if keep:
        kept[2][...] = low
        sent(kept[2])
    copies[1].wait()
    taken = chosen[...] > 0
    logits = jnp.where(taken, dot(low, router[...]), -1e30)
    expo = jnp.where(taken, jnp.exp(logits - jnp.max(logits, -1, keepdims=True)), 0.0)
    share = expo / jnp.sum(expo, -1, keepdims=True)
    gates[...] = share
    sent(gates)
    slots = dispatch[...]
    per, columns = outgoing.shape[1], outgoing.shape[0]
    if keep:
        outgoing[:, :, :width] = dot(slots, low).astype(BF).reshape(columns, per, width)
        lane = lax.broadcasted_iota(jnp.int32, (slots.shape[0], LANES), 1)
        notes = jnp.where(lane == 0, slot_gates(slots, share), 0.0).astype(BF)
        outgoing[:, :, width:] = notes.reshape(columns, per, LANES)
    else:
        low = jnp.where(flag[0] > 0, target[...], low)
        outgoing[...] = dot(slots, low).astype(BF).reshape(columns, per, width)


def by_expert(refs, experts):
    whole = [[[r.at[j] for j in range(experts)] for r in refs[at : at + 4]] for at in (0, 4)]
    down = [[r.at[j] for j in range(experts)] for r in refs[8:10]]
    for at in (10, 10 + experts):
        down.append([r.at[0] for r in refs[at : at + experts]])
    return [*whole, down]


class Fetched:
    def __init__(self, shards, weights, sems):
        self.weights = weights
        self.copies = {}
        for j in range(weights.shape[1]):
            for k in range(weights.shape[0]):
                self.copies[k, j] = [
                    pltpu.make_async_copy(
                        shards[k][p][j],
                        weights.at[k, j, pl.ds(p * shards[k][p][j].shape[0], shards[k][p][j].shape[0])],
                        sems.at[k, j, p],
                    )
                    for p in range(4)
                ]
        for k in range(weights.shape[0]):
            self.start(k, 0)

    def start(self, k, j):
        for copy in self.copies.get((k, j), ()):
            copy.start()

    def ready(self, k, j):
        done_with(self.copies[k, j])
        self.start(k, j + 1)


def done_with(copies):
    for copy in copies:
        copy.wait()


def rows_of(value, j, begin=0):
    columns, unused, width = value.shape
    at = begin + j * ROOMS
    return value[:, at : at + ROOMS, :].reshape(columns * ROOMS, width)


def put_rows(out, j, rows, inner):
    at, width = j * ROOMS, rows.shape[1]
    out[:, at : at + ROOMS, :width] = rows.reshape(-1, ROOMS, width)
    high = inner.astype(BF).astype(F32)
    lane = lax.broadcasted_iota(jnp.int32, (rows.shape[0], LANES), 1)
    both = jnp.where(lane == 0, high, jnp.where(lane == 1, inner - high, 0.0))
    out[:, at : at + ROOMS, width:] = both.astype(BF).reshape(-1, ROOMS, LANES)


def expert_forward(both, arrived, *refs):
    early, refs = (refs[0], refs[1:]) if both else (None, refs)
    weights, sems = refs[-2:]
    experts = weights.shape[1]
    count = 10 + 2 * experts
    outs = refs[count:-2]
    fetched = Fetched(by_expert(refs, experts), weights, sems)
    width = weights.shape[3]
    for j in range(weights.shape[1]):
        at = j * ROOMS
        noted = rows_of(arrived, j)
        rows = noted[:, :width]
        fetched.ready(0, j)
        gate = dot(rows, weights[0, j], (1, 1))
        fetched.ready(1, j)
        lifted = dot(rows, weights[1, j], (1, 1))
        square = gate * gate
        bend = jnp.tanh(0.7978845608028654 * gate * (1.0 + 0.044715 * square))
        active = 0.5 * gate * (1.0 + bend)
        hidden = (active * lifted).astype(BF)
        fetched.ready(2, j)
        made = dot(hidden, weights[2, j]).astype(BF)
        outs[0][:, at : at + ROOMS, :] = made.reshape(-1, ROOMS, made.shape[1])
        sent(outs[0], (slice(None), pl.ds(at, ROOMS)))
        if both:
            slope = 0.5 * (1.0 + bend) + 0.5 * gate * (1.0 - bend * bend) * (
                0.7978845608028654 * (1.0 + 3 * 0.044715 * square)
            )
            bent = slope * lifted
            outs[1][j] = hidden
            outs[2][j] = active.astype(BF)
            outs[3][j] = bent.astype(BF)
            grads = (rows_of(early, j).astype(F32) * noted[:, width : width + 1].astype(F32)).astype(BF)
            hidden_grads = dot(grads, weights[2, j], (1, 1))
            gate_part = (hidden_grads * bent).astype(BF)
            lifted_part = (hidden_grads * active).astype(BF)
            inner = jnp.sum(hidden_grads * hidden.astype(F32), -1, keepdims=True)
            back = dot(gate_part, weights[0, j]) + dot(lifted_part, weights[1, j])
            put_rows(outs[4], j, back.astype(BF), inner)
            sent(outs[4], (slice(None), pl.ds(at, ROOMS)))
            for out in outs[1:4]:
                sent(out, j)


def combine(returned, middle, gates, spread, places, low):
    weights = (dot(gates[...].astype(BF), spread[...]) * places[...].astype(F32)).astype(BF)
    done = middle[...] + dot(weights, returned[...].reshape(-1, returned.shape[2]))
    low[...] = done.astype(BF)


def last_outputs(flag, spread, *refs):
    out = refs[-1]
    width = out.shape[2]
    for m in range(out.shape[0]):
        returned, middle, gates, places, before = refs[5 * m : 5 * m + 5]
        weights = (dot(gates[...].astype(BF), spread[...]) * places[...].astype(F32)).astype(BF)
        rows = returned[:, :, :width].reshape(-1, width)
        out[m] = jnp.where(flag[0] > 0, middle[...] + dot(weights, rows), before[...].astype(F32))


def send_grads(flag, came, target, gates, dispatch, grad, outgoing):
    low = jnp.where(flag[0] > 0, came[...], target[...])
    grad[...] = low
    sent(grad)
    slots = dispatch[...]
    rows = dot(slots, low) * slot_gates(slots, gates[...])
    outgoing[...] = rows.astype(BF).reshape(outgoing.shape)


def expert_backward(flag, arrived, hidden, active, bent, produced, *refs):
    out, gate_back, lifted_back, weights, sems = refs[-5:]
    gate_shards, up_shards, down_shards = by_expert(refs, weights.shape[1])
    fetched = Fetched([down_shards, gate_shards, up_shards], weights, sems)
    for j in range(weights.shape[1]):
        fetched.ready(0, j)
        hidden_grads = dot(rows_of(arrived, j), weights[0, j], (1, 1))
        gate_part = (hidden_grads * bent[j].astype(F32)).astype(BF)
        lifted_part = (hidden_grads * active[j].astype(F32)).astype(BF)
        gate_back[j] = gate_part
        lifted_back[j] = lifted_part
        inner = jnp.sum(hidden_grads * hidden[j].astype(F32), -1, keepdims=True)
        fetched.ready(1, j)
        done = dot(gate_part, weights[1, j])
        fetched.ready(2, j)
        done = (done + dot(lifted_part, weights[2, j])).astype(BF)
        put_rows(out, j, jnp.where(flag[0] > 0, rows_of(produced, j), done), inner)
        sent(out, (slice(None), pl.ds(j * ROOMS, ROOMS)))
        sent(gate_back, j)
        sent(lifted_back, j)


def attend_back(
    keep, row, flag, token_grads, before, gates, places, middle, gain, grad, query, pair0, pair1,
    pair2, pair3, probs, cosine, sine, dense, middle_grads, query_back, part0, part1, part2, part3,
    *rest,
):
    tokens, width = middle.shape
    kept, (branch, weights, router, sems) = rest[:-4], rest[-4:]
    at = dense.shape[1] - width - LANES
    copies = [
        pltpu.make_async_copy(dense.at[:, pl.ds(at, LANES)], router, sems.at[1]),
        pltpu.make_async_copy(dense.at[:, pl.ds(at + LANES, width)], weights, sems.at[0]),
    ]
    for copy in copies:
        copy.start()
    came = token_grads[...]
    if keep:
        came = jnp.where(flag[0] > 0, before[...], came)
    came = came.reshape(-1, came.shape[2])
    place = places[...]
    here = slot_experts(came.shape[0])
    notes = came[:, width:].astype(F32)
    high = jnp.where(here, notes[:, :1], 0.0).astype(BF)
    rest_of = jnp.where(here, notes[:, 1:2], 0.0).astype(BF)
    inner = dot(place, high) + dot(place, rest_of)
    logit_grads = (inner - gates[...] * jnp.sum(inner, -1, keepdims=True)).astype(BF)
    ffn_grads = dot(place, came[:, :width])
    copies[0].wait()
    ffn_grads = ffn_grads + dot(logit_grads, router[...], (1, 1))
    part, total = norm_back(ffn_grads, middle[...], gain[...])
    above = grad[...].astype(F32) + part
    middle_grads[...] = above
    sent(middle_grads)
    low = above.astype(BF)
    if keep:
        kept[0][...] = logit_grads
        kept[1][...] = jnp.broadcast_to(total, kept[1].shape)
        sent(kept[0])
        sent(kept[1])
        branch[...] = low
        share = width // 4
        for s, part in enumerate((part0, part1, part2, part3)):
            begin = pl.multiple_of((row[0] ^ s) * share, LANES)
            part[:, part.shape[1] - share :] = branch[:, pl.ds(begin, share)]
    copies[1].wait()
    mixed_grads = dot(low, weights[...], (1, 1)).astype(BF)
    pairs = stacked((pair0, pair1, pair2, pair3))
    kv_heads = pairs.shape[1] // (2 * HEAD_DIM)
    group = width // HEAD_DIM // kv_heads
    scale = HEAD_DIM ** (-0.5)
    parts = (part0, part1, part2, part3)
    for h in range(kv_heads):
        keys = pairs[:, h * HEAD_DIM : (h + 1) * HEAD_DIM]
        values = pairs[:, (kv_heads + h) * HEAD_DIM : (kv_heads + h + 1) * HEAD_DIM]
        queries = stacked_heads(query, h * group, group)
        top = stacked_heads(mixed_grads, h * group, group)
        weight = probs[h]
        wide = weight.astype(F32)
        weight_grads = dot(top, values, (1, 1))
        value_grads = dot(weight, top, (0, 0)).astype(BF)
        inner = wide * weight_grads
        score_grads = (inner - wide * jnp.sum(inner, -1, keepdims=True)).astype(BF)
        query_grads = dot(score_grads, keys) * scale
        key_grads = (dot(score_grads, queries, (0, 0)) * scale).astype(BF)
        for j in range(group):
            begin = (h * group + j) * HEAD_DIM
            one = query_grads[j * tokens : (j + 1) * tokens]
            query_back[:, begin : begin + HEAD_DIM] = turned(one, cosine[...], -sine[...]).astype(BF)
        for p, part in enumerate(parts):
            part[:, h * HEAD_DIM : (h + 1) * HEAD_DIM] = key_grads[p * tokens : (p + 1) * tokens]
            begin = (kv_heads + h) * HEAD_DIM
            part[:, begin : begin + HEAD_DIM] = value_grads[p * tokens : (p + 1) * tokens]


def project_back(
    keep, row, part0, part1, part2, part3, query_back, stream, gain, middle_grads, cosine, sine,
    dense, low, *rest,
):
    width = stream.shape[1]
    kept, (backs, weights, sems) = rest[:-3], rest[-3:]
    cuts = cuts_of(weights.shape[1])
    copies = [
        pltpu.make_async_copy(
            dense.at[:, pl.ds(at, size)], weights.at[:, pl.ds(at, size)], sems.at[k]
        )
        for k, (at, size) in enumerate(cuts)
    ]
    for copy in copies:
        copy.start()
    pairs = weights.shape[1] - width
    total = sum(part[:, :pairs].astype(F32) for part in (part0, part1, part2, part3))
    keys = pairs // 2
    backs[:, :width] = query_back[...]
    backs[:, width : width + keys] = turned(total[:, :keys], cosine[...], -sine[...]).astype(BF)
    backs[:, width + keys :] = total[:, keys:].astype(BF)
    if keep:
        share = backs.shape[1] // 4
        for s, out in enumerate(kept[1:]):
            out[...] = backs[:, pl.ds(pl.multiple_of((row[0] ^ s) * share, LANES), share)]
            sent(out)
    above = jnp.zeros(stream.shape, F32)
    for copy, (at, size) in zip(copies, cuts):
        copy.wait()
        above = above + dot(backs[:, at : at + size], weights[:, at : at + size], (1, 1))
    part, unused = norm_back(above, stream[...], gain[...])
    done = middle_grads[...] + part
    if keep:
        kept[0][...] = done
    low[...] = done.astype(BF)


def expert_weight_grads(begin_left, which, *refs):
    count = len(which)
    rights = sorted({w for w in which})
    sources, outs = refs[: 2 * count + 2 * len(rights)], refs[2 * count + 2 * len(rights) : -3]
    left, right, sems = refs[-3:]
    experts, deep, wide = left.shape[1:]
    columns, width = right.shape[2] // 2, right.shape[4]
    copies = {}
    for j in range(experts):
        for m in range(2):
            for r, (unused, begin) in enumerate(rights):
                copies["right", r, j, m] = pltpu.make_async_copy(
                    sources[2 * count + 2 * r + m].at[
                        :, pl.ds(begin + j * ROOMS, ROOMS), pl.ds(0, width)
                    ],
                    right.at[r, j, pl.ds(m * columns, columns)],
                    sems.at[1, r, j, m],
                )
            for k in range(count):
                copies["left", k, j, m] = pltpu.make_async_copy(
                    sources[2 * k + m].at[j, :, pl.ds(begin_left, wide)],
                    left.at[k, j, pl.ds(m * (deep // 2), deep // 2)],
                    sems.at[0, k, j, m],
                )
    for copy in copies.values():
        copy.start()
    waiting = dict(copies)

    def there(*name):
        for m in range(2):
            copy = waiting.pop((*name, m), None)
            if copy is not None:
                copy.wait()

    for j in range(experts):
        for k, name in enumerate(which):
            r = rights.index(name)
            there("right", r, j)
            there("left", k, j)
            total = dot(left[k, j], right[r, j].reshape(deep, width), (0, 0))
            some = len(outs) // count
            size = wide // some
            for q, out in enumerate(outs[some * k : some * (k + 1)]):
                out[j] = total[q * size : (q + 1) * size].astype(BF)
                sent(out, j)


def add(*refs):
    count = len(refs) // 3
    for k in range(count):
        one, other, total = refs[2 * k], refs[2 * k + 1], refs[2 * count + k]
        total[...] = (one[...].astype(F32) + other[...].astype(F32)).astype(BF)


def pack(*refs):
    for k, value in enumerate(refs[:-1]):
        refs[-1][k] = value[...]


def stacked(refs):
    return jnp.concatenate([r[...] for r in refs], 0)


def by_owner(out, grads, begin):
    columns, lines, unused = out.shape
    size = lines // 4
    for c in range(columns):
        some = [grads[(r * columns + c) * size : (r * columns + c + 1) * size] for r in range(4)]
        out[c, :, begin : begin + grads.shape[1]] = jnp.concatenate(some, 0).astype(BF)


def out_grads(*refs):
    lefts, rights, normed, logits, gains, out = (
        refs[:4], refs[4:12], refs[12:14], refs[14:16], refs[16:18], refs[18],
    )
    share = out.shape[2] - LANES
    left = jnp.concatenate([one[k] for one in lefts for k in (2, 3)], 0)
    right = jnp.concatenate([r[:, r.shape[1] - share :] for r in rights], 0)
    by_owner(out, dot(left, right, (0, 0)), 0)
    width = left.shape[1]
    line = lax.broadcasted_iota(jnp.int32, (LANES, width), 0)
    sums = jnp.where(line == LANES - 1, gains[0][:1, :] + gains[1][:1, :], 0.0)
    by_owner(out, dot(stacked(normed), stacked(logits), (0, 0)) + sums.T, share)


def qkv_grads(*refs):
    lefts, rights, out = refs[:4], refs[4:12], refs[12]
    left = jnp.concatenate([one[k] for one in lefts for k in (0, 1)], 0)
    by_owner(out, dot(left, stacked(rights), (0, 0)), 0)


def fold(row, first, second, out0, out1, out2, out3, total):
    share = first.shape[2]
    total[:, :share] = jnp.sum(first[...].astype(F32), 0)
    total[:, share:] = jnp.sum(second[...].astype(F32), 0)
    for s, out in enumerate((out0, out1, out2, out3)):
        size = out.shape[0]
        out[...] = total[pl.ds(pl.multiple_of((row[0] ^ s) * size, 8), size), :]
        sent(out)


def finish(
    row, in0, in1, in2, in3, w_query, w_key, w_value, gain, o_grad, q_grad, k_grad, v_grad, r_grad,
    first, second, total,
):
    share = o_grad.shape[1] // 4
    piece = total.shape[1] // 4
    ins = (in0, in1, in2, in3)
    for s, one in enumerate(ins):
        where = row[0] ^ s
        o_grad[:, pl.ds(pl.multiple_of(where * share, LANES), share)] = one[:, :share]
        total[:, pl.ds(pl.multiple_of(where * piece, LANES), piece)] = one[:, share + LANES :]
    rest = sum(one[:, share : share + LANES] for one in ins)
    r_grad[...] = rest[:, : r_grad.shape[1]]
    second[...] = rest.T[LANES - 1 :, :]
    begin, inner = 0, jnp.zeros((total.shape[0], 1), F32)
    for out, weight in ((q_grad, w_query), (k_grad, w_key), (v_grad, w_value)):
        part = total[:, begin : begin + out.shape[1]]
        out[...] = part
        inner = inner + jnp.sum(part * weight[...].astype(F32), -1, keepdims=True)
        begin += out.shape[1]
    line = jnp.broadcast_to(inner, (total.shape[0], LANES)).T[:1, :]
    first[...] = line / gain[...].astype(F32)


def over_columns(value):
    return lax.all_to_all(value, "col", split_axis=0, concat_axis=0, tiled=True)


def on_device(
    inputs, cotangent, segment_ids, routes, attn_gain, w_query, w_key, w_value, w_out, ffn_gain,
    w_router, w_gate, w_up, w_down,
):
    section = lax.axis_index("section")
    row = lax.axis_index("row")
    rows = lax.axis_size("row")
    columns = lax.axis_size("col")
    micro, tokens, width = inputs.shape[0], inputs.shape[2], inputs.shape[3]
    experts = w_router.shape[2]
    per_column = w_gate.shape[1]
    hidden_width = w_gate.shape[2] * rows
    kv_width = w_key.shape[2]
    qkv_width = width + 2 * kv_width
    slots = experts * ROOMS
    share = width // rows
    shard = width // (rows * columns)
    heads = width // HEAD_DIM
    kv_heads = kv_width // HEAD_DIM
    length = rows * tokens
    pieces = range(micro)
    steps = range(rows)
    here = row.astype(jnp.int32)[None]
    second = (section == 1).astype(jnp.int32)[None]
    block = (columns, slots // columns, width)

    dense = jnp.concatenate(
        [w_query[0], w_key[0], w_value[0], w_router[0], attn_gain[0][:, None], ffn_gain[0][:, None],
         jnp.zeros((shard, LANES - experts - 2), BF), w_out[0]], 1
    )
    dense = lax.all_gather(dense, ("row", "col"), axis=0, tiled=True)
    small = dense[:, qkv_width : qkv_width + LANES]
    gain_a = small[:, experts].astype(F32)[None, :]
    gain_f = small[:, experts + 1].astype(F32)[None, :]

    def shards_of(own):
        two = swapped(own, 2)
        return own, swapped(own, 1), two, swapped(two, 1)

    gate_shards, up_shards = shards_of(w_gate[0]), shards_of(w_up[0])
    down_twos = [swapped(w_down[0, j : j + 1], 2) for j in range(per_column)]
    shards = (
        *gate_shards, *up_shards, w_down[0], swapped(w_down[0], 1), *down_twos,
        *[swapped(two, 1) for two in down_twos],
    )

    lane = jnp.arange(LANES, dtype=jnp.int32)
    half = HEAD_DIM // 2
    freqs = 10000.0 ** (-2.0 * jnp.arange(half).astype(F32) / HEAD_DIM)
    positions = row * tokens + jnp.arange(tokens, dtype=jnp.int32)
    angles = positions.astype(F32)[:, None] * freqs[None, :]
    cosine = jnp.concatenate([jnp.cos(angles)] * 2, 1)
    sine = jnp.concatenate([-jnp.sin(angles), jnp.sin(angles)], 1)
    key_positions = jnp.concatenate(
        [(row ^ step) * tokens + jnp.arange(tokens, dtype=jnp.int32) for step in steps]
    )
    spread = (lane[:, None] == jnp.arange(slots, dtype=jnp.int32)[None, :] // ROOMS).astype(BF)
    below = (jnp.arange(tokens)[:, None] > jnp.arange(tokens)[None, :]).astype(BF)
    biases, chosens, places, dispatches = [], [], [], []
    for m in pieces:
        segments = segment_ids[m, 0]
        own_segments = lax.dynamic_slice_in_dim(segments, row * tokens, tokens)
        key_segments = jnp.concatenate(
            [lax.dynamic_slice_in_dim(segments, (row ^ s) * tokens, tokens) for s in steps]
        )
        counted = (key_positions[None, :] <= positions[:, None]) & (
            key_segments[None, :] == own_segments[:, None]
        )
        biases.append(jnp.where(counted, 0.0, -1e30).astype(F32))
        chosen = jnp.any(routes[0, m, 0][:, :, None] == lane[None, None, :], 1)
        chosens.append(chosen.astype(F32))
        rank = dot(below, chosen.astype(BF))
        rank = jnp.where(chosen, rank, -1.0)[:, :experts]
        place = (
            rank[:, :, None] == jnp.arange(ROOMS, dtype=F32)[None, None, :]
        ).reshape(tokens, slots)
        places.append(place.astype(BF))
        dispatches.append(place.T.astype(BF))

    token_low, token_wide = like((tokens, width), BF), like((tokens, width), F32)
    pair_like = like((tokens, 2 * kv_width), BF)
    block_like = like(block, BF)
    sums_like = like((8, width), F32)
    kept_like = like((per_column, columns * ROOMS, hidden_width), BF)
    probs_like = like((kv_heads, heads // kv_heads * tokens, length), BF)
    qkv_scratch = [pltpu.VMEM((width, qkv_width), BF), pltpu.SemaphoreType.DMA((8,))]
    out_scratch = [
        pltpu.VMEM((width, width), BF), pltpu.VMEM((width, LANES), BF),
        pltpu.SemaphoreType.DMA((2,)),
    ]
    expert_scratch = [
        pltpu.VMEM((3, per_column, hidden_width, width), BF),
        pltpu.SemaphoreType.DMA((3, per_column, 4)),
    ]
    qkv_flops = 2 * tokens * width * qkv_width
    out_flops = 2 * tokens * width * width + 2 * slots * tokens * width
    score_flops = 2 * heads * tokens * length * HEAD_DIM
    expert_flops = 2 * slots * hidden_width * width

    per = slots // columns
    back_like = like((columns, per, width + LANES), BF)
    lanes_like = like((tokens, LANES), F32)
    tables = late([cosine, sine])
    first_flag = (1 - second)

    def forward(keep, came, waits, early, after):
        projected, pairs = [], []
        if keep:
            for m in pieces:
                projected.append(
                    call(
                        project,
                        (Sent(token_wide), Sent(token_low), Sent(token_low), Sent(pair_like)),
                        (Late(came[m]), Late(inputs, (m, 0)), Late(gain_a), *tables), qkv_flops, (dense,),
                        qkv_scratch, (second,), waits=[p[0] for p in projected],
                    )
                )
                pairs.append([projected[m][3]] + [swapped(projected[m][3], s) for s in steps[1:]])
        else:
            made = call(
                functools.partial(project_all, experts),
                (Sent(token_wide), Sent(token_low), Sent(pair_like)) * micro,
                (Late(inputs), *tables), micro * qkv_flops, (dense,),
                [qkv_scratch[0], pltpu.VMEM((width, LANES), BF), qkv_scratch[1]], waits=waits,
            )
            projected = [(made[3 * m], None, made[3 * m + 1]) for m in pieces]
            for m in pieces:
                pair = made[3 * m + 2]
                pairs.append([pair] + [swapped(pair, s) for s in steps[1:]])
        attended = [
            call(
                functools.partial(attend, keep),
                (Sent(token_wide), Sent(lanes_like), Sent(back_like if keep else block_like))
                + ((Sent(probs_like), Sent(token_low), Sent(token_low)) if keep else ()),
                (*late([projected[m][0], projected[m][2], *pairs[m], biases[m], gain_f, chosens[m],
                        dispatches[m]]), Late(cotangent, (m, 0))),
                out_flops + 2 * score_flops, (dense,), [pltpu.VMEM((tokens, width), BF)] + out_scratch,
                (second,), () if m else after,
            )
            for m in pieces
        ]
        arrived = [over_columns(a[2]) for a in attended]
        lefts, ready = [], ()
        if keep:
            left = call(
                pack, (Sent(like((2 * micro, tokens, width), BF)),),
                late([p[1] for p in projected] + [a[4] for a in attended]), 0,
            )[0]
            two = swapped(left, 2)
            lefts = [left, swapped(left, 1), two, swapped(two, 1)]
            ready = (two,)
        applied = [
            call(
                functools.partial(expert_forward, keep),
                (Sent(block_like),)
                + ((Sent(kept_like),) * 3 + (Sent(back_like),) if keep else ()),
                late([arrived[m], early[m]] if keep else [arrived[m]]),
                (6 if keep else 3) * expert_flops, shards, expert_scratch,
                waits=ready if m else (attended[1][2],),
            )
            for m in pieces
        ]
        return projected, pairs, attended, arrived, applied, lefts

    def weight_call(quarters, which, lefts, rights, waits):
        quarter, some = hidden_width // 4, len(quarters)
        return call(
            functools.partial(expert_weight_grads, quarters[0] * quarter, which),
            (Sent(like((per_column, quarter, width), BF)),) * (some * len(which)), (),
            len(which) * expert_flops, [*lefts, *rights],
            [pltpu.VMEM((len(which), per_column, 2 * columns * ROOMS, some * quarter), BF),
             pltpu.VMEM((len(rights) // 2, per_column, 2 * columns, ROOMS, width), BF),
             pltpu.SemaphoreType.DMA((2, len(which), per_column, 2))],
            waits=waits,
        )

    def merged(halves, waits):
        pairs = [v for a, b in halves for v in (a, swapped(b, 1))]
        return call(add, [Sent(a) for a, unused in halves], late(pairs), 0, waits=waits)

    def attention_back(keep, m, grad, token_grads, waits):
        return call(
            functools.partial(attend_back, keep),
            (Sent(token_wide), Sent(token_low))
            + (Sent(like((tokens, 2 * kv_width + (share if keep else 0)), BF)),) * rows
            + ((Sent(like((tokens, LANES), BF)), Sent(sums_like)) if keep else ()),
            (*late([token_grads, shared[m] if keep else spread, attended[m][1], places[m],
                                 attended[m][0], gain_f]), Late(*grad),
             *late([projected[m][2], *pairs[m], attended[m][3], cosine, sine])),
            out_flops + 4 * score_flops, (dense,), [pltpu.VMEM((tokens, width), BF)] + out_scratch,
            (here, second), waits,
        )

    def parts_of(inner):
        return [inner[2]] + [swapped(inner[2 + s], s) for s in steps[1:]]

    def projection_back(keep, m, inner, parts, waits):
        return call(
            functools.partial(project_back, keep),
            (Sent(token_low),)
            + ((Sent(token_wide),) + (Sent(like((tokens, qkv_width // rows), BF)),) * rows
               if keep else ()),
            (*late([*parts, inner[1], projected[m][0], gain_a, inner[0]]),
             *tables),
            qkv_flops, (dense,), [pltpu.VMEM((tokens, qkv_width), BF)] + qkv_scratch,
            (here,), waits,
        )

    kept = forward(False, None, (gate_shards[2], up_shards[2], down_twos[0]), None, ())
    attended, early, applied = kept[2:5]
    returned = [over_columns(a[0]) for a in applied]
    results = [
        call(
            combine, (Sent(token_low),),
            late([returned[m], attended[m][0], attended[m][1], spread, places[m]]),
            2 * slots * tokens * width, waits=() if m else (applied[1][0],),
        )
        for m in pieces
    ]
    came = [lax.ppermute(r[0], "section", [(0, 1)]) for r in results]

    projected, pairs, attended, arrived, applied, lefts = forward(True, came, (), early, results[1])
    hidden = [a[1] for a in applied]
    shared = [over_columns(a[4]) for a in applied]
    inner, outer = [], []
    for m in pieces:
        waits = (*lefts[1:], outer[0][0]) if m else (applied[1][4],)
        inner.append(attention_back(False, m, (cotangent, (m, 0)), shared[m], waits))
        outer.append(projection_back(False, m, inner[m], parts_of(inner[m]), ()))
    came = [lax.ppermute(o[0], "section", [(1, 0)]) for o in outer]

    given = [
        call(
            send_grads, (Sent(token_low), Sent(block_like)),
            (Late(came[m]), Late(cotangent, (m, 0)), *late([attended[m][1], dispatches[m]])),
            2 * slots * tokens * width, scalars=(first_flag,), waits=() if m else (inner[1][0],),
        )
        for m in pieces
    ]
    arrived_grads = [over_columns(g[1]) for g in given]
    moved = [
        call(
            expert_backward, (Sent(back_like), Sent(kept_like), Sent(kept_like)),
            late([arrived_grads[m], hidden[m], applied[m][2], applied[m][3], applied[m][0]]),
            3 * expert_flops, shards, expert_scratch,
            (second,), () if m else (given[1][1],),
        )
        for m in pieces
    ]
    gate_up = [a[1] for a in moved] + [a[2] for a in moved]
    down_far = merged([weight_call((2, 3), ((0, 0),), hidden, arrived_grads, ())], ())[0]
    crossed = [swapped(down_far, 2)]
    back = [over_columns(moved[0][0]), over_columns(hold(moved[1][0], down_far))]
    inner = [attention_back(True, 0, given[0][:1], back[0], (moved[1][0], down_far))]
    parts = [parts_of(inner[0])]
    both = weight_call((0, 1, 2, 3), ((0, 0), (0, 0)), gate_up, arrived, (inner[0][0],))
    inner.append(attention_back(True, 1, given[1][:1], back[1], (both[0], crossed[0], *parts[0][1:])))
    parts.append(parts_of(inner[1]))
    sums = merged([both[2:4], both[6:]], (inner[1][0],))
    gate_far = hold(sums[0], *parts[1][1:])
    crossed.append(swapped(gate_far, 2))
    o_grads = call(
        out_grads, (Sent(like((columns, rows * shard, share + LANES), BF)),),
        late([*lefts, *[p[s] for s in steps for p in parts], *[a[5] for a in attended],
              *[a[6] for a in inner], *[a[7] for a in inner]]),
        2 * width * length * micro * share, waits=(crossed[0], gate_far),
    )[0]
    last = projection_back(True, 1, inner[1], parts[1], (o_grads,))
    outer = [projection_back(True, 0, inner[0], parts[0], (last[0],)), last]
    backs = [[o[2]] + [swapped(o[2 + s], s) for s in steps[1:]] for o in outer]
    crossed.append(swapped(hold(sums[1], *backs[0][1:], *backs[1][1:]), 2))
    near = weight_call((0, 1), ((0, 0),), hidden, arrived_grads, (outer[1][0],))
    w_grads = call(
        qkv_grads, (Sent(like((columns, rows * shard, qkv_width // rows), BF)),),
        late([*lefts, *[b[s] for s in steps for b in backs]]),
        2 * width * length * micro * qkv_width // rows, waits=(crossed[1], near[0]),
    )[0]
    expert_grads = [
        one.astype(F32) + swapped(other, 1).astype(F32) + c.astype(F32)
        for one, other, c in zip((near[0], both[0], both[4]), (near[1], both[1], both[5]), crossed)
    ]
    layer_outputs = call(
        last_outputs, (Sent(like((micro, tokens, width), F32)),),
        late([spread] + [v for m in pieces for v in (
            back[m], attended[m][0], attended[m][1], places[m], results[m][0])]),
        4 * slots * tokens * width, scalars=(second,), waits=(w_grads,),
    )[0]

    wide = share + qkv_width // rows + LANES
    pieces_out = call(
        fold, (Sent(like((shard, wide), F32)),) * rows,
        late([over_columns(o_grads), over_columns(w_grads)]), 0,
        scratch=[pltpu.VMEM((rows * shard, wide), F32)], scalars=(here,),
    )
    pieces_out = [pieces_out[0]] + [swapped(pieces_out[s], s) for s in steps[1:]]
    o_grad, q_grad, k_grad, v_grad, r_grad, first, second_sum = call(
        finish,
        (like((shard, width), F32), like((shard, width), F32), like((shard, kv_width), F32),
         like((shard, kv_width), F32), like((shard, experts), F32), like((1, shard), F32),
         like((1, shard), F32)),
        late([*pieces_out, w_query[0], w_key[0], w_value[0], attn_gain]), 0,
        scratch=[pltpu.VMEM((shard, qkv_width), F32)], scalars=(here,),
    )

    return (
        layer_outputs[None, :, None],
        jnp.stack([o[1] for o in outer])[None, :, None],
        first,
        q_grad[None],
        k_grad[None],
        v_grad[None],
        o_grad[None],
        second_sum,
        r_grad[None],
        expert_grads[1][None],
        expert_grads[2][None],
        expert_grads[0][None],
    )


def solution(mesh):
    dense = P("section", ("row", "col"), None)
    gain = P("section", ("row", "col"))
    expert = P("section", "col", "row", None)
    token = P(None, "col", "row", None)
    layered = P("section", None, "col", "row", None)
    return jax.shard_map(
        on_device,
        mesh=mesh,
        in_specs=(
            token, token, P(None, "col", None), layered, gain, dense, dense, dense, dense, gain,
            dense, expert, expert, expert,
        ),
        out_specs=(
            layered, layered, gain, dense, dense, dense, dense, gain, dense, expert, expert, expert,
        ),
        check_vma=False,
    )
```

```python
import functools

import jax
import jax.numpy as jnp
from jax import lax
from jax.experimental import pallas as pl
from jax.experimental.pallas import tpu as pltpu
from jax.sharding import PartitionSpec as P

HEAD_DIM = 128
ROOMS = 16
EPSILON = 1e-06
LANES = 128
BF = jnp.bfloat16
F32 = jnp.float32
MIB = 1 << 20


def dot(left, right, contract=(1, 0)):
    return lax.dot_general(
        left, right, (((contract[0],), (contract[1],)), ((), ())), preferred_element_type=F32
    )


def like(shape, dtype):
    return jax.ShapeDtypeStruct(shape, dtype)


class Late:
    def __init__(self, source, index=None, target=None, sem=None):
        self.source, self.index, self.target, self.copy = source, index, target, None
        if target is not None:
            source = source if index is None else source.at[index]
            self.copy = pltpu.make_async_copy(source, target, sem)
            self.copy.start()
            self.waiting = True

    def ready(self):
        if self.waiting:
            self.copy.wait()
            self.waiting = False
        return self.target

    def __getitem__(self, index):
        return self.ready()[index]

    @property
    def shape(self):
        return self.source.shape[len(self.index or ()) :]


class Sent:
    def __init__(self, source, target=None, sems=None):
        self.source, self.target, self.sems, self.copies = source, target, sems, []

    def __getitem__(self, index):
        return self.source[index]

    def __setitem__(self, index, value):
        self.source[index] = value

    def send(self, *parts):
        for part in parts or (...,):
            at = len(self.copies)
            whole = part is ...
            copy = pltpu.make_async_copy(
                self.source if whole else self.source.at[part],
                self.target if whole else self.target.at[part],
                self.sems.at[at],
            )
            copy.start()
            self.copies.append(copy)

    @property
    def shape(self):
        return self.source.shape


PARTS = 4


def sent(out, *parts):
    if isinstance(out, Sent):
        out.send(*parts)


def call(body, outs, args, flops, far=(), scratch=(), scalars=(), waits=()):
    arrays = [a.source if isinstance(a, Late) else a for a in args]
    shapes = [o.source if isinstance(o, Sent) else o for o in outs]
    moved = sum(a.size * a.dtype.itemsize for a in (*arrays, *far, *shapes))
    count = len(scalars) + len(args) + len(far)
    kinds = [isinstance(a, Late) for a in args]
    out_kinds = [isinstance(o, Sent) for o in outs]
    buffers = [pltpu.VMEM(a.shape, a.source.dtype) for a in args if isinstance(a, Late)]
    buffers += [pltpu.VMEM(o.shape, o.dtype) for o, k in zip(shapes, out_kinds) if k]

    def run(*refs):
        given, refs = list(refs[:count]), refs[count + len(waits) :]
        results, refs = list(refs[: len(outs)]), refs[len(outs) :]
        own, rest = list(refs[: len(buffers)]), refs[len(buffers) :]
        sems, rest = (rest[0], rest[1:]) if buffers else (None, rest)
        used = 0
        for k, kind in enumerate(kinds):
            if kind:
                at = len(scalars) + k
                given[at] = Late(given[at], args[k].index, own[used], sems.at[used, 0])
                used += 1
        for k, kind in enumerate(out_kinds):
            if kind:
                results[k] = Sent(own[used], results[k], sems.at[used])
                used += 1
        body(*given, *results, *rest)
        for one in given:
            if isinstance(one, Late):
                one.ready()
        for one in results:
            if isinstance(one, Sent) and not one.copies:
                one.send()
        for one in results:
            if isinstance(one, Sent):
                done_with(one.copies)

    anywhere, local = pl.BlockSpec(memory_space=pltpu.HBM), pl.BlockSpec(memory_space=pltpu.VMEM)
    return pl.pallas_call(
        run,
        out_shape=tuple(shapes),
        in_specs=[pl.BlockSpec(memory_space=pltpu.SMEM)] * len(scalars)
        + [anywhere if k else local for k in kinds]
        + [anywhere] * (len(far) + len(waits)),
        out_specs=tuple(anywhere if k else local for k in out_kinds),
        scratch_shapes=buffers
        + ([pltpu.SemaphoreType.DMA((len(buffers), PARTS))] if buffers else [])
        + list(scratch),
        compiler_params=pltpu.CompilerParams(vmem_limit_bytes=64 * MIB),
        cost_estimate=pl.CostEstimate(
            flops=int(flops), bytes_accessed=int(moved), transcendentals=0
        ),
        name=body.func.__name__ if isinstance(body, functools.partial) else body.__name__,
    )(*scalars, *arrays, *far, *waits)


def late(values):
    return [Late(v) for v in values]


def nothing(*refs):
    pass


def hold(value, *waits):
    return pl.pallas_call(
        nothing,
        out_shape=like(value.shape, value.dtype),
        in_specs=[pl.BlockSpec(memory_space=pl.ANY)] * (1 + len(waits)),
        out_specs=pl.BlockSpec(memory_space=pl.ANY),
        input_output_aliases={0: 0},
        name="hold",
    )(value, *waits)


def swapped(value, step):
    rows = lax.axis_size("row")
    return lax.ppermute(value, "row", [(r, r ^ step) for r in range(rows)])


def norm_parts(stream):
    return lax.rsqrt(jnp.mean(stream * stream, -1, keepdims=True) + EPSILON)


def norm_back(grad, stream, gain):
    inverse = norm_parts(stream)
    unit = stream * inverse
    scaled = grad * gain
    back = inverse * (scaled - unit * jnp.mean(scaled * unit, -1, keepdims=True))
    return back, jnp.sum(grad * unit, 0, keepdims=True)


def turned(vectors, cosine, sine):
    done = []
    for at in range(0, vectors.shape[1], HEAD_DIM):
        one = vectors[:, at : at + HEAD_DIM]
        done.append(one * cosine + pltpu.roll(one, HEAD_DIM // 2, 1) * sine)
    return jnp.concatenate(done, -1) if len(done) > 1 else done[0]


def stacked_heads(value, first, count):
    return jnp.concatenate(
        [value[:, (first + j) * HEAD_DIM : (first + j + 1) * HEAD_DIM] for j in range(count)], 0
    )


def unstacked_heads(value, count):
    tokens = value.shape[0] // count
    return jnp.concatenate([value[j * tokens : (j + 1) * tokens] for j in range(count)], 1)


def cuts_of(total, most=512):
    return [(at, min(most, total - at)) for at in range(0, total, most)]


def project(
    flag, came, entering, gain, cosine, sine, dense, stream, normed, query, pair, weights, sems
):
    width = stream.shape[1]
    cuts = cuts_of(weights.shape[1])
    copies = [
        pltpu.make_async_copy(
            dense.at[:, pl.ds(at, size)], weights.at[:, pl.ds(at, size)], sems.at[k]
        )
        for k, (at, size) in enumerate(cuts)
    ]
    for copy in copies:
        copy.start()
    x = jnp.where(flag[0] > 0, came[...].astype(F32), entering[...].astype(F32))
    stream[...] = x
    sent(stream)
    low = (x * norm_parts(x) * gain[...]).astype(BF)
    normed[...] = low
    sent(normed)
    keys = pair.shape[1] // 2
    for copy, (at, size) in zip(copies, cuts):
        copy.wait()
        part = dot(low, weights[:, at : at + size])
        for begin in range(at, at + size, HEAD_DIM):
            head = part[:, begin - at : begin - at + HEAD_DIM]
            if begin < width + keys:
                head = turned(head, cosine[...], sine[...])
            head = head.astype(BF)
            if begin < width:
                query[:, begin : begin + HEAD_DIM] = head
            else:
                pair[:, begin - width : begin - width + HEAD_DIM] = head
            if begin + HEAD_DIM == width:
                sent(query)


def project_all(at_gain, entering, cosine, sine, dense, *rest):
    outs, (weights, small, sems) = rest[:-3], rest[-3:]
    micro, unused, tokens, width = entering.shape
    cuts = cuts_of(weights.shape[1])
    block = pltpu.make_async_copy(
        dense.at[:, pl.ds(weights.shape[1], LANES)], small, sems.at[len(cuts)]
    )
    block.start()
    copies = [
        pltpu.make_async_copy(
            dense.at[:, pl.ds(at, size)], weights.at[:, pl.ds(at, size)], sems.at[k]
        )
        for k, (at, size) in enumerate(cuts)
    ]
    for copy in copies:
        copy.start()
    scaled = []
    for m in range(micro):
        x = entering[m, 0].astype(F32)
        outs[3 * m][...] = x
        sent(outs[3 * m])
        scaled.append(x * norm_parts(x))
    block.wait()
    gain = small[...].astype(F32).T[at_gain : at_gain + 1, :]
    lows = [(x * gain).astype(BF) for x in scaled]
    low = jnp.concatenate(lows, 0)
    cosines = jnp.concatenate([cosine[...]] * micro, 0)
    sines = jnp.concatenate([sine[...]] * micro, 0)
    keys = outs[2].shape[1] // 2
    for copy, (at, size) in zip(copies, cuts):
        copy.wait()
        part = dot(low, weights[:, at : at + size])
        for begin in range(at, at + size, HEAD_DIM):
            head = part[:, begin - at : begin - at + HEAD_DIM]
            if begin < width + keys:
                head = turned(head, cosines, sines)
            head = head.astype(BF)
            for m in range(micro):
                out, to = (outs[3 * m + 1], begin) if begin < width else (outs[3 * m + 2], begin - width)
                out[:, to : to + HEAD_DIM] = head[m * tokens : (m + 1) * tokens]
                if begin + HEAD_DIM == width:
                    sent(out)


def slot_experts(slots):
    own = lax.broadcasted_iota(jnp.int32, (slots, LANES), 0) // ROOMS
    return own == lax.broadcasted_iota(jnp.int32, (slots, LANES), 1)


def slot_gates(dispatch, gates):
    here = slot_experts(dispatch.shape[0])
    return jnp.sum(jnp.where(here, dot(dispatch, gates.astype(BF)), 0.0), -1, keepdims=True)


def attend(
    keep, flag, stream, query, pair0, pair1, pair2, pair3, bias, gain, chosen, dispatch, target,
    *rest,
):
    dense, middle, gates, outgoing = rest[:4]
    kept, (mixed, weights, router, sems) = rest[4:-4], rest[-4:]
    width = stream.shape[1]
    at = dense.shape[1] - width - LANES
    copies = [
        pltpu.make_async_copy(dense.at[:, pl.ds(at + LANES, width)], weights, sems.at[0]),
        pltpu.make_async_copy(dense.at[:, pl.ds(at, LANES)], router, sems.at[1]),
    ]
    for copy in copies:
        copy.start()
    tokens = stream.shape[0]
    pairs = stacked((pair0, pair1, pair2, pair3))
    kv_heads = pairs.shape[1] // (2 * HEAD_DIM)
    group = width // HEAD_DIM // kv_heads
    biases = jnp.concatenate([bias[...]] * group, 0)
    for h in range(kv_heads):
        keys = pairs[:, h * HEAD_DIM : (h + 1) * HEAD_DIM]
        values = pairs[:, (kv_heads + h) * HEAD_DIM : (kv_heads + h + 1) * HEAD_DIM]
        queries = stacked_heads(query, h * group, group)
        scores = dot(queries, keys, (1, 1)) * HEAD_DIM ** (-0.5) + biases
        expo = jnp.exp(scores - jnp.max(scores, -1, keepdims=True))
        weight = (expo * (1.0 / jnp.sum(expo, -1, keepdims=True))).astype(BF)
        if keep:
            kept[0][h] = weight
        done = dot(weight, values).astype(BF)
        for j in range(group):
            begin = (h * group + j) * HEAD_DIM
            mixed[:, begin : begin + HEAD_DIM] = done[j * tokens : (j + 1) * tokens]
    if keep:
        kept[1][...] = mixed[...]
        sent(kept[0])
        sent(kept[1])
    copies[0].wait()
    x = stream[...] + dot(mixed[...], weights[...])
    middle[...] = x
    sent(middle)
    low = (x * norm_parts(x) * gain[...]).astype(BF)
    if keep:
        kept[2][...] = low
        sent(kept[2])
    copies[1].wait()
    taken = chosen[...] > 0
    logits = jnp.where(taken, dot(low, router[...]), -1e30)
    expo = jnp.where(taken, jnp.exp(logits - jnp.max(logits, -1, keepdims=True)), 0.0)
    share = expo / jnp.sum(expo, -1, keepdims=True)
    gates[...] = share
    sent(gates)
    slots = dispatch[...]
    per, columns = outgoing.shape[1], outgoing.shape[0]
    if keep:
        outgoing[:, :, :width] = dot(slots, low).astype(BF).reshape(columns, per, width)
        lane = lax.broadcasted_iota(jnp.int32, (slots.shape[0], LANES), 1)
        notes = jnp.where(lane == 0, slot_gates(slots, share), 0.0).astype(BF)
        outgoing[:, :, width:] = notes.reshape(columns, per, LANES)
    else:
        low = jnp.where(flag[0] > 0, target[...], low)
        outgoing[...] = dot(slots, low).astype(BF).reshape(columns, per, width)


def by_expert(refs, experts):
    whole = [[[r.at[j] for j in range(experts)] for r in refs[at : at + 4]] for at in (0, 4)]
    down = [[r.at[j] for j in range(experts)] for r in refs[8:10]]
    for at in (10, 10 + experts):
        down.append([r.at[0] for r in refs[at : at + experts]])
    return [*whole, down]


class Fetched:
    def __init__(self, shards, weights, sems):
        self.weights = weights
        self.copies = {}
        for j in range(weights.shape[1]):
            for k in range(weights.shape[0]):
                self.copies[k, j] = [
                    pltpu.make_async_copy(
                        shards[k][p][j],
                        weights.at[k, j, pl.ds(p * shards[k][p][j].shape[0], shards[k][p][j].shape[0])],
                        sems.at[k, j, p],
                    )
                    for p in range(4)
                ]
        for k in range(weights.shape[0]):
            self.start(k, 0)

    def start(self, k, j):
        for copy in self.copies.get((k, j), ()):
            copy.start()

    def ready(self, k, j):
        done_with(self.copies[k, j])
        self.start(k, j + 1)


def done_with(copies):
    for copy in copies:
        copy.wait()


def rows_of(value, j, begin=0):
    columns, unused, width = value.shape
    at = begin + j * ROOMS
    return value[:, at : at + ROOMS, :].reshape(columns * ROOMS, width)


def put_rows(out, j, rows, inner):
    at, width = j * ROOMS, rows.shape[1]
    out[:, at : at + ROOMS, :width] = rows.reshape(-1, ROOMS, width)
    high = inner.astype(BF).astype(F32)
    lane = lax.broadcasted_iota(jnp.int32, (rows.shape[0], LANES), 1)
    both = jnp.where(lane == 0, high, jnp.where(lane == 1, inner - high, 0.0))
    out[:, at : at + ROOMS, width:] = both.astype(BF).reshape(-1, ROOMS, LANES)


def expert_forward(both, arrived, *refs):
    early, refs = (refs[0], refs[1:]) if both else (None, refs)
    weights, sems = refs[-2:]
    experts = weights.shape[1]
    count = 10 + 2 * experts
    outs = refs[count:-2]
    fetched = Fetched(by_expert(refs, experts), weights, sems)
    width = weights.shape[3]
    for j in range(weights.shape[1]):
        at = j * ROOMS
        noted = rows_of(arrived, j)
        rows = noted[:, :width]
        fetched.ready(0, j)
        gate = dot(rows, weights[0, j], (1, 1))
        fetched.ready(1, j)
        lifted = dot(rows, weights[1, j], (1, 1))
        square = gate * gate
        bend = jnp.tanh(0.7978845608028654 * gate * (1.0 + 0.044715 * square))
        active = 0.5 * gate * (1.0 + bend)
        hidden = (active * lifted).astype(BF)
        fetched.ready(2, j)
        made = dot(hidden, weights[2, j]).astype(BF)
        outs[0][:, at : at + ROOMS, :] = made.reshape(-1, ROOMS, made.shape[1])
        sent(outs[0], (slice(None), pl.ds(at, ROOMS)))
        if both:
            slope = 0.5 * (1.0 + bend) + 0.5 * gate * (1.0 - bend * bend) * (
                0.7978845608028654 * (1.0 + 3 * 0.044715 * square)
            )
            bent = slope * lifted
            outs[1][j] = hidden
            outs[2][j] = active.astype(BF)
            outs[3][j] = bent.astype(BF)
            grads = (rows_of(early, j).astype(F32) * noted[:, width : width + 1].astype(F32)).astype(BF)
            hidden_grads = dot(grads, weights[2, j], (1, 1))
            gate_part = (hidden_grads * bent).astype(BF)
            lifted_part = (hidden_grads * active).astype(BF)
            inner = jnp.sum(hidden_grads * hidden.astype(F32), -1, keepdims=True)
            back = dot(gate_part, weights[0, j]) + dot(lifted_part, weights[1, j])
            put_rows(outs[4], j, back.astype(BF), inner)
            sent(outs[4], (slice(None), pl.ds(at, ROOMS)))
            for out in outs[1:4]:
                sent(out, j)


def combine(returned, middle, gates, spread, places, low):
    weights = (dot(gates[...].astype(BF), spread[...]) * places[...].astype(F32)).astype(BF)
    done = middle[...] + dot(weights, returned[...].reshape(-1, returned.shape[2]))
    low[...] = done.astype(BF)


def last_outputs(flag, spread, *refs):
    out = refs[-1]
    width = out.shape[2]
    for m in range(out.shape[0]):
        returned, middle, gates, places, before = refs[5 * m : 5 * m + 5]
        weights = (dot(gates[...].astype(BF), spread[...]) * places[...].astype(F32)).astype(BF)
        rows = returned[:, :, :width].reshape(-1, width)
        out[m] = jnp.where(flag[0] > 0, middle[...] + dot(weights, rows), before[...].astype(F32))


def send_grads(flag, came, target, gates, dispatch, grad, outgoing):
    low = jnp.where(flag[0] > 0, came[...], target[...])
    grad[...] = low
    sent(grad)
    slots = dispatch[...]
    rows = dot(slots, low) * slot_gates(slots, gates[...])
    outgoing[...] = rows.astype(BF).reshape(outgoing.shape)


def expert_backward(flag, arrived, hidden, active, bent, produced, *refs):
    out, gate_back, lifted_back, weights, sems = refs[-5:]
    gate_shards, up_shards, down_shards = by_expert(refs, weights.shape[1])
    fetched = Fetched([down_shards, gate_shards, up_shards], weights, sems)
    for j in range(weights.shape[1]):
        fetched.ready(0, j)
        hidden_grads = dot(rows_of(arrived, j), weights[0, j], (1, 1))
        gate_part = (hidden_grads * bent[j].astype(F32)).astype(BF)
        lifted_part = (hidden_grads * active[j].astype(F32)).astype(BF)
        gate_back[j] = gate_part
        lifted_back[j] = lifted_part
        inner = jnp.sum(hidden_grads * hidden[j].astype(F32), -1, keepdims=True)
        fetched.ready(1, j)
        done = dot(gate_part, weights[1, j])
        fetched.ready(2, j)
        done = (done + dot(lifted_part, weights[2, j])).astype(BF)
        put_rows(out, j, jnp.where(flag[0] > 0, rows_of(produced, j), done), inner)
        sent(out, (slice(None), pl.ds(j * ROOMS, ROOMS)))
        sent(gate_back, j)
        sent(lifted_back, j)


def attend_back(
    keep, row, flag, token_grads, before, gates, places, middle, gain, grad, query, pair0, pair1,
    pair2, pair3, probs, cosine, sine, dense, middle_grads, query_back, part0, part1, part2, part3,
    *rest,
):
    tokens, width = middle.shape
    kept, (branch, weights, router, sems) = rest[:-4], rest[-4:]
    at = dense.shape[1] - width - LANES
    copies = [
        pltpu.make_async_copy(dense.at[:, pl.ds(at, LANES)], router, sems.at[1]),
        pltpu.make_async_copy(dense.at[:, pl.ds(at + LANES, width)], weights, sems.at[0]),
    ]
    for copy in copies:
        copy.start()
    came = token_grads[...]
    if keep:
        came = jnp.where(flag[0] > 0, before[...], came)
    came = came.reshape(-1, came.shape[2])
    place = places[...]
    here = slot_experts(came.shape[0])
    notes = came[:, width:].astype(F32)
    high = jnp.where(here, notes[:, :1], 0.0).astype(BF)
    rest_of = jnp.where(here, notes[:, 1:2], 0.0).astype(BF)
    inner = dot(place, high) + dot(place, rest_of)
    logit_grads = (inner - gates[...] * jnp.sum(inner, -1, keepdims=True)).astype(BF)
    ffn_grads = dot(place, came[:, :width])
    copies[0].wait()
    ffn_grads = ffn_grads + dot(logit_grads, router[...], (1, 1))
    part, total = norm_back(ffn_grads, middle[...], gain[...])
    above = grad[...].astype(F32) + part
    middle_grads[...] = above
    sent(middle_grads)
    low = above.astype(BF)
    if keep:
        kept[0][...] = logit_grads
        kept[1][...] = jnp.broadcast_to(total, kept[1].shape)
        sent(kept[0])
        sent(kept[1])
        branch[...] = low
        share = width // 4
        for s, part in enumerate((part0, part1, part2, part3)):
            begin = pl.multiple_of((row[0] ^ s) * share, LANES)
            part[:, part.shape[1] - share :] = branch[:, pl.ds(begin, share)]
    copies[1].wait()
    mixed_grads = dot(low, weights[...], (1, 1)).astype(BF)
    pairs = stacked((pair0, pair1, pair2, pair3))
    kv_heads = pairs.shape[1] // (2 * HEAD_DIM)
    group = width // HEAD_DIM // kv_heads
    scale = HEAD_DIM ** (-0.5)
    parts = (part0, part1, part2, part3)
    for h in range(kv_heads):
        keys = pairs[:, h * HEAD_DIM : (h + 1) * HEAD_DIM]
        values = pairs[:, (kv_heads + h) * HEAD_DIM : (kv_heads + h + 1) * HEAD_DIM]
        queries = stacked_heads(query, h * group, group)
        top = stacked_heads(mixed_grads, h * group, group)
        weight = probs[h]
        wide = weight.astype(F32)
        weight_grads = dot(top, values, (1, 1))
        value_grads = dot(weight, top, (0, 0)).astype(BF)
        inner = wide * weight_grads
        score_grads = (inner - wide * jnp.sum(inner, -1, keepdims=True)).astype(BF)
        query_grads = dot(score_grads, keys) * scale
        key_grads = (dot(score_grads, queries, (0, 0)) * scale).astype(BF)
        for j in range(group):
            begin = (h * group + j) * HEAD_DIM
            one = query_grads[j * tokens : (j + 1) * tokens]
            query_back[:, begin : begin + HEAD_DIM] = turned(one, cosine[...], -sine[...]).astype(BF)
        for p, part in enumerate(parts):
            part[:, h * HEAD_DIM : (h + 1) * HEAD_DIM] = key_grads[p * tokens : (p + 1) * tokens]
            begin = (kv_heads + h) * HEAD_DIM
            part[:, begin : begin + HEAD_DIM] = value_grads[p * tokens : (p + 1) * tokens]


def project_back(
    keep, row, part0, part1, part2, part3, query_back, stream, gain, middle_grads, cosine, sine,
    dense, low, *rest,
):
    width = stream.shape[1]
    kept, (backs, weights, sems) = rest[:-3], rest[-3:]
    cuts = cuts_of(weights.shape[1])
    copies = [
        pltpu.make_async_copy(
            dense.at[:, pl.ds(at, size)], weights.at[:, pl.ds(at, size)], sems.at[k]
        )
        for k, (at, size) in enumerate(cuts)
    ]
    for copy in copies:
        copy.start()
    pairs = weights.shape[1] - width
    total = sum(part[:, :pairs].astype(F32) for part in (part0, part1, part2, part3))
    keys = pairs // 2
    backs[:, :width] = query_back[...]
    backs[:, width : width + keys] = turned(total[:, :keys], cosine[...], -sine[...]).astype(BF)
    backs[:, width + keys :] = total[:, keys:].astype(BF)
    if keep:
        share = backs.shape[1] // 4
        for s, out in enumerate(kept[1:]):
            out[...] = backs[:, pl.ds(pl.multiple_of((row[0] ^ s) * share, LANES), share)]
            sent(out)
    above = jnp.zeros(stream.shape, F32)
    for copy, (at, size) in zip(copies, cuts):
        copy.wait()
        above = above + dot(backs[:, at : at + size], weights[:, at : at + size], (1, 1))
    part, unused = norm_back(above, stream[...], gain[...])
    done = middle_grads[...] + part
    if keep:
        kept[0][...] = done
    low[...] = done.astype(BF)


def expert_weight_grads(begin_left, which, *refs):
    count = len(which)
    rights = sorted({w for w in which})
    sources, outs = refs[: 2 * count + 2 * len(rights)], refs[2 * count + 2 * len(rights) : -3]
    left, right, sems = refs[-3:]
    experts, deep, wide = left.shape[1:]
    columns, width = right.shape[2] // 2, right.shape[4]
    copies = {}
    for j in range(experts):
        for m in range(2):
            for r, (unused, begin) in enumerate(rights):
                copies["right", r, j, m] = pltpu.make_async_copy(
                    sources[2 * count + 2 * r + m].at[
                        :, pl.ds(begin + j * ROOMS, ROOMS), pl.ds(0, width)
                    ],
                    right.at[r, j, pl.ds(m * columns, columns)],
                    sems.at[1, r, j, m],
                )
            for k in range(count):
                copies["left", k, j, m] = pltpu.make_async_copy(
                    sources[2 * k + m].at[j, :, pl.ds(begin_left, wide)],
                    left.at[k, j, pl.ds(m * (deep // 2), deep // 2)],
                    sems.at[0, k, j, m],
                )
    for copy in copies.values():
        copy.start()
    waiting = dict(copies)

    def there(*name):
        for m in range(2):
            copy = waiting.pop((*name, m), None)
            if copy is not None:
                copy.wait()

    for j in range(experts):
        for k, name in enumerate(which):
            r = rights.index(name)
            there("right", r, j)
            there("left", k, j)
            total = dot(left[k, j], right[r, j].reshape(deep, width), (0, 0))
            some = len(outs) // count
            size = wide // some
            for q, out in enumerate(outs[some * k : some * (k + 1)]):
                out[j] = total[q * size : (q + 1) * size].astype(BF)
                sent(out, j)


def add(*refs):
    count = len(refs) // 3
    for k in range(count):
        one, other, total = refs[2 * k], refs[2 * k + 1], refs[2 * count + k]
        total[...] = (one[...].astype(F32) + other[...].astype(F32)).astype(BF)


def add_by_expert(gate, other_gate, up, other_up, up_sum, *gate_sums):
    up_sum[...] = (up[...].astype(F32) + other_up[...].astype(F32)).astype(BF)
    for j, out in enumerate(gate_sums):
        out[0] = (gate[j].astype(F32) + other_gate[j].astype(F32)).astype(BF)


def total_by_expert(one, other, *rest):
    crossed, out = rest[:-1], rest[-1]
    for j, far in enumerate(crossed):
        out[j] = one[j].astype(F32) + other[j].astype(F32) + far[0].astype(F32)
        sent(out, j)


def pack(*refs):
    for k, value in enumerate(refs[:-1]):
        refs[-1][k] = value[...]


def stacked(refs):
    return jnp.concatenate([r[...] for r in refs], 0)


def by_owner(out, grads, begin):
    columns, lines, unused = out.shape
    size = lines // 4
    for c in range(columns):
        some = [grads[(r * columns + c) * size : (r * columns + c + 1) * size] for r in range(4)]
        out[c, :, begin : begin + grads.shape[1]] = jnp.concatenate(some, 0).astype(BF)


def out_grads(*refs):
    lefts, rights, normed, logits, gains, out = (
        refs[:4], refs[4:12], refs[12:14], refs[14:16], refs[16:18], refs[18],
    )
    share = out.shape[2] - LANES
    left = jnp.concatenate([one[k] for one in lefts for k in (2, 3)], 0)
    right = jnp.concatenate([r[:, r.shape[1] - share :] for r in rights], 0)
    by_owner(out, dot(left, right, (0, 0)), 0)
    width = left.shape[1]
    line = lax.broadcasted_iota(jnp.int32, (LANES, width), 0)
    sums = jnp.where(line == LANES - 1, gains[0][:1, :] + gains[1][:1, :], 0.0)
    by_owner(out, dot(stacked(normed), stacked(logits), (0, 0)) + sums.T, share)


def qkv_grads(*refs):
    lefts, rights, out = refs[:4], refs[4:12], refs[12]
    left = jnp.concatenate([one[k] for one in lefts for k in (0, 1)], 0)
    by_owner(out, dot(left, stacked(rights), (0, 0)), 0)


def fold(row, first, second, out0, out1, out2, out3, total):
    share = first.shape[2]
    total[:, :share] = jnp.sum(first[...].astype(F32), 0)
    total[:, share:] = jnp.sum(second[...].astype(F32), 0)
    for s, out in enumerate((out0, out1, out2, out3)):
        size = out.shape[0]
        out[...] = total[pl.ds(pl.multiple_of((row[0] ^ s) * size, 8), size), :]
        sent(out)


def finish(
    row, in0, in1, in2, in3, w_query, w_key, w_value, gain, o_grad, q_grad, k_grad, v_grad, r_grad,
    first, second, total,
):
    share = o_grad.shape[1] // 4
    piece = total.shape[1] // 4
    ins = (in0, in1, in2, in3)
    for s, one in enumerate(ins):
        where = row[0] ^ s
        o_grad[:, pl.ds(pl.multiple_of(where * share, LANES), share)] = one[:, :share]
        total[:, pl.ds(pl.multiple_of(where * piece, LANES), piece)] = one[:, share + LANES :]
    rest = sum(one[:, share : share + LANES] for one in ins)
    r_grad[...] = rest[:, : r_grad.shape[1]]
    second[...] = rest.T[LANES - 1 :, :]
    begin, inner = 0, jnp.zeros((total.shape[0], 1), F32)
    for out, weight in ((q_grad, w_query), (k_grad, w_key), (v_grad, w_value)):
        part = total[:, begin : begin + out.shape[1]]
        out[...] = part
        inner = inner + jnp.sum(part * weight[...].astype(F32), -1, keepdims=True)
        begin += out.shape[1]
    line = jnp.broadcast_to(inner, (total.shape[0], LANES)).T[:1, :]
    first[...] = line / gain[...].astype(F32)


def over_columns(value):
    return lax.all_to_all(value, "col", split_axis=0, concat_axis=0, tiled=True)


def on_device(
    inputs, cotangent, segment_ids, routes, attn_gain, w_query, w_key, w_value, w_out, ffn_gain,
    w_router, w_gate, w_up, w_down,
):
    section = lax.axis_index("section")
    row = lax.axis_index("row")
    rows = lax.axis_size("row")
    columns = lax.axis_size("col")
    micro, tokens, width = inputs.shape[0], inputs.shape[2], inputs.shape[3]
    experts = w_router.shape[2]
    per_column = w_gate.shape[1]
    hidden_width = w_gate.shape[2] * rows
    kv_width = w_key.shape[2]
    qkv_width = width + 2 * kv_width
    slots = experts * ROOMS
    share = width // rows
    shard = width // (rows * columns)
    heads = width // HEAD_DIM
    kv_heads = kv_width // HEAD_DIM
    length = rows * tokens
    pieces = range(micro)
    steps = range(rows)
    here = row.astype(jnp.int32)[None]
    second = (section == 1).astype(jnp.int32)[None]
    block = (columns, slots // columns, width)

    dense = jnp.concatenate(
        [w_query[0], w_key[0], w_value[0], w_router[0], attn_gain[0][:, None], ffn_gain[0][:, None],
         jnp.zeros((shard, LANES - experts - 2), BF), w_out[0]], 1
    )
    dense = lax.all_gather(dense, ("row", "col"), axis=0, tiled=True)
    small = dense[:, qkv_width : qkv_width + LANES]
    gain_a = small[:, experts].astype(F32)[None, :]
    gain_f = small[:, experts + 1].astype(F32)[None, :]

    def shards_of(own):
        two = swapped(own, 2)
        return own, swapped(own, 1), two, swapped(two, 1)

    gate_shards, up_shards = shards_of(w_gate[0]), shards_of(w_up[0])
    down_one, down_first = swapped(w_down[0], 1), swapped(w_down[0, :1], 2)

    def all_shards(waits):
        twos = [down_first]
        twos += [swapped(hold(w_down[0, j : j + 1], *waits), 2) for j in range(1, per_column)]
        threes = [swapped(two, 1) for two in twos]
        return (*gate_shards, *up_shards, w_down[0], down_one, *twos, *threes)


    lane = jnp.arange(LANES, dtype=jnp.int32)
    half = HEAD_DIM // 2
    freqs = 10000.0 ** (-2.0 * jnp.arange(half).astype(F32) / HEAD_DIM)
    positions = row * tokens + jnp.arange(tokens, dtype=jnp.int32)
    angles = positions.astype(F32)[:, None] * freqs[None, :]
    cosine = jnp.concatenate([jnp.cos(angles)] * 2, 1)
    sine = jnp.concatenate([-jnp.sin(angles), jnp.sin(angles)], 1)
    key_positions = jnp.concatenate(
        [(row ^ step) * tokens + jnp.arange(tokens, dtype=jnp.int32) for step in steps]
    )
    spread = (lane[:, None] == jnp.arange(slots, dtype=jnp.int32)[None, :] // ROOMS).astype(BF)
    below = (jnp.arange(tokens)[:, None] > jnp.arange(tokens)[None, :]).astype(BF)
    biases, chosens, places, dispatches = [], [], [], []
    for m in pieces:
        segments = segment_ids[m, 0]
        own_segments = lax.dynamic_slice_in_dim(segments, row * tokens, tokens)
        key_segments = jnp.concatenate(
            [lax.dynamic_slice_in_dim(segments, (row ^ s) * tokens, tokens) for s in steps]
        )
        counted = (key_positions[None, :] <= positions[:, None]) & (
            key_segments[None, :] == own_segments[:, None]
        )
        biases.append(jnp.where(counted, 0.0, -1e30).astype(F32))
        chosen = jnp.any(routes[0, m, 0][:, :, None] == lane[None, None, :], 1)
        chosens.append(chosen.astype(F32))
        rank = dot(below, chosen.astype(BF))
        rank = jnp.where(chosen, rank, -1.0)[:, :experts]
        place = (
            rank[:, :, None] == jnp.arange(ROOMS, dtype=F32)[None, None, :]
        ).reshape(tokens, slots)
        places.append(place.astype(BF))
        dispatches.append(place.T.astype(BF))

    token_low, token_wide = like((tokens, width), BF), like((tokens, width), F32)
    pair_like = like((tokens, 2 * kv_width), BF)
    block_like = like(block, BF)
    sums_like = like((8, width), F32)
    kept_like = like((per_column, columns * ROOMS, hidden_width), BF)
    probs_like = like((kv_heads, heads // kv_heads * tokens, length), BF)
    qkv_scratch = [pltpu.VMEM((width, qkv_width), BF), pltpu.SemaphoreType.DMA((8,))]
    out_scratch = [
        pltpu.VMEM((width, width), BF), pltpu.VMEM((width, LANES), BF),
        pltpu.SemaphoreType.DMA((2,)),
    ]
    expert_scratch = [
        pltpu.VMEM((3, per_column, hidden_width, width), BF),
        pltpu.SemaphoreType.DMA((3, per_column, 4)),
    ]
    qkv_flops = 2 * tokens * width * qkv_width
    out_flops = 2 * tokens * width * width + 2 * slots * tokens * width
    score_flops = 2 * heads * tokens * length * HEAD_DIM
    expert_flops = 2 * slots * hidden_width * width

    per = slots // columns
    back_like = like((columns, per, width + LANES), BF)
    lanes_like = like((tokens, LANES), F32)
    tables = late([cosine, sine])
    first_flag = (1 - second)

    def forward(keep, came, waits, early, after, shards):
        projected, pairs = [], []
        if keep:
            for m in pieces:
                projected.append(
                    call(
                        project,
                        (Sent(token_wide), Sent(token_low), Sent(token_low), Sent(pair_like)),
                        (Late(came[m]), Late(inputs, (m, 0)), Late(gain_a), *tables), qkv_flops, (dense,),
                        qkv_scratch, (second,), waits=[p[0] for p in projected],
                    )
                )
                pairs.append([projected[m][3]] + [swapped(projected[m][3], s) for s in steps[1:]])
        else:
            made = call(
                functools.partial(project_all, experts),
                (Sent(token_wide), Sent(token_low), Sent(pair_like)) * micro,
                (Late(inputs), *tables), micro * qkv_flops, (dense,),
                [qkv_scratch[0], pltpu.VMEM((width, LANES), BF), qkv_scratch[1]], waits=waits,
            )
            projected = [(made[3 * m], None, made[3 * m + 1]) for m in pieces]
            for m in pieces:
                pair = made[3 * m + 2]
                pairs.append([pair] + [swapped(pair, s) for s in steps[1:]])
        shards = shards or all_shards(pairs[1][1:])
        attended = [
            call(
                functools.partial(attend, keep),
                (Sent(token_wide), Sent(lanes_like), Sent(back_like if keep else block_like))
                + ((Sent(probs_like), Sent(token_low), Sent(token_low)) if keep else ()),
                (*late([projected[m][0], projected[m][2], *pairs[m], biases[m], gain_f, chosens[m],
                        dispatches[m]]), Late(cotangent, (m, 0))),
                out_flops + 2 * score_flops, (dense,), [pltpu.VMEM((tokens, width), BF)] + out_scratch,
                (second,), () if m else after,
            )
            for m in pieces
        ]
        arrived = [over_columns(a[2]) for a in attended]
        lefts, ready = [], ()
        if keep:
            left = call(
                pack, (Sent(like((2 * micro, tokens, width), BF)),),
                late([p[1] for p in projected] + [a[4] for a in attended]), 0,
            )[0]
            two = swapped(left, 2)
            lefts = [left, swapped(left, 1), two, swapped(two, 1)]
            ready = (two,)
        applied = [
            call(
                functools.partial(expert_forward, keep),
                (Sent(block_like),)
                + ((Sent(kept_like),) * 3 + (Sent(back_like),) if keep else ()),
                late([arrived[m], early[m]] if keep else [arrived[m]]),
                (6 if keep else 3) * expert_flops, shards, expert_scratch,
                waits=ready if m else (attended[1][2],),
            )
            for m in pieces
        ]
        return projected, pairs, attended, arrived, applied, lefts, shards

    def weight_call(quarters, which, lefts, rights, waits):
        quarter, some = hidden_width // 4, len(quarters)
        return call(
            functools.partial(expert_weight_grads, quarters[0] * quarter, which),
            (Sent(like((per_column, quarter, width), BF)),) * (some * len(which)), (),
            len(which) * expert_flops, [*lefts, *rights],
            [pltpu.VMEM((len(which), per_column, 2 * columns * ROOMS, some * quarter), BF),
             pltpu.VMEM((len(rights) // 2, per_column, 2 * columns, ROOMS, width), BF),
             pltpu.SemaphoreType.DMA((2, len(which), per_column, 2))],
            waits=waits,
        )

    def merged(halves, waits):
        pairs = [v for a, b in halves for v in (a, swapped(b, 1))]
        return call(add, [Sent(a) for a, unused in halves], late(pairs), 0, waits=waits)

    def attention_back(keep, m, grad, token_grads, waits):
        return call(
            functools.partial(attend_back, keep),
            (Sent(token_wide), Sent(token_low))
            + (Sent(like((tokens, 2 * kv_width + (share if keep else 0)), BF)),) * rows
            + ((Sent(like((tokens, LANES), BF)), Sent(sums_like)) if keep else ()),
            (*late([token_grads, shared[m] if keep else spread, attended[m][1], places[m],
                                 attended[m][0], gain_f]), Late(*grad),
             *late([projected[m][2], *pairs[m], attended[m][3], cosine, sine])),
            out_flops + 4 * score_flops, (dense,), [pltpu.VMEM((tokens, width), BF)] + out_scratch,
            (here, second), waits,
        )

    def parts_of(inner):
        return [inner[2]] + [swapped(inner[2 + s], s) for s in steps[1:]]

    def projection_back(keep, m, inner, parts, waits):
        return call(
            functools.partial(project_back, keep),
            (Sent(token_low),)
            + ((Sent(token_wide),) + (Sent(like((tokens, qkv_width // rows), BF)),) * rows
               if keep else ()),
            (*late([*parts, inner[1], projected[m][0], gain_a, inner[0]]),
             *tables),
            qkv_flops, (dense,), [pltpu.VMEM((tokens, qkv_width), BF)] + qkv_scratch,
            (here,), waits,
        )

    kept = forward(False, None, (gate_shards[2], up_shards[2], down_first), None, (), ())
    attended, early, applied, unused, shards = kept[2:]
    returned = [over_columns(a[0]) for a in applied]
    results = [
        call(
            combine, (Sent(token_low),),
            late([returned[m], attended[m][0], attended[m][1], spread, places[m]]),
            2 * slots * tokens * width, waits=() if m else (applied[1][0],),
        )
        for m in pieces
    ]
    came = [lax.ppermute(r[0], "section", [(0, 1)]) for r in results]

    kept = forward(True, came, (), early, results[1], shards)
    projected, pairs, attended, arrived, applied, lefts, unused = kept
    hidden = [a[1] for a in applied]
    shared = [over_columns(a[4]) for a in applied]
    inner, outer = [], []
    for m in pieces:
        waits = (*lefts[1:], outer[0][0]) if m else (applied[1][4],)
        inner.append(attention_back(False, m, (cotangent, (m, 0)), shared[m], waits))
        outer.append(projection_back(False, m, inner[m], parts_of(inner[m]), ()))
    came = [lax.ppermute(o[0], "section", [(1, 0)]) for o in outer]

    given = [
        call(
            send_grads, (Sent(token_low), Sent(block_like)),
            (Late(came[m]), Late(cotangent, (m, 0)), *late([attended[m][1], dispatches[m]])),
            2 * slots * tokens * width, scalars=(first_flag,), waits=() if m else (inner[1][0],),
        )
        for m in pieces
    ]
    arrived_grads = [over_columns(g[1]) for g in given]
    moved = [
        call(
            expert_backward, (Sent(back_like), Sent(kept_like), Sent(kept_like)),
            late([arrived_grads[m], hidden[m], applied[m][2], applied[m][3], applied[m][0]]),
            3 * expert_flops, shards, expert_scratch,
            (second,), () if m else (given[1][1],),
        )
        for m in pieces
    ]
    gate_up = [a[1] for a in moved] + [a[2] for a in moved]
    down_far = merged([weight_call((2, 3), ((0, 0),), hidden, arrived_grads, ())], ())[0]
    crossed = [swapped(down_far, 2)]
    back = [over_columns(moved[0][0]), over_columns(moved[1][0])]
    inner = [attention_back(True, 0, given[0][:1], back[0], (moved[1][0], down_far))]
    parts = [parts_of(inner[0])]
    both = weight_call((0, 1, 2, 3), ((0, 0), (0, 0)), gate_up, arrived, (inner[0][0],))
    inner.append(attention_back(True, 1, given[1][:1], back[1], (both[0], crossed[0])))
    parts.append(parts_of(inner[1]))
    quarter_like = like((1, hidden_width // 4, width), BF)
    sums = call(
        add_by_expert, (Sent(both[6]),) + (Sent(quarter_like),) * per_column,
        late([both[2], swapped(both[3], 1), both[6], swapped(both[7], 1)]), 0,
        waits=(inner[1][0],),
    )
    gate_far = hold(sums[1], *parts[1][1:])
    gate_crossed = [swapped(gate_far, 2)]
    o_grads = call(
        out_grads, (Sent(like((columns, rows * shard, share + LANES), BF)),),
        late([*lefts, *[p[s] for s in steps for p in parts], *[a[5] for a in attended],
              *[a[6] for a in inner], *[a[7] for a in inner]]),
        2 * width * length * micro * share, waits=(crossed[0], gate_far),
    )[0]
    last = projection_back(True, 1, inner[1], parts[1], (o_grads,))
    outer = [projection_back(True, 0, inner[0], parts[0], (last[0],)), last]
    backs = [[o[2]] + [swapped(o[2 + s], s) for s in steps[1:]] for o in outer]
    backs_there = (*backs[0][1:], *backs[1][1:])
    gate_crossed += [swapped(hold(one, *backs_there), 2) for one in sums[2:]]
    up_crossed = swapped(hold(sums[0], *backs_there), 2)
    near = weight_call((0, 1), ((0, 0),), hidden, arrived_grads, (outer[1][0],))
    w_grads = call(
        qkv_grads, (Sent(like((columns, rows * shard, qkv_width // rows), BF)),),
        late([*lefts, *[b[s] for s in steps for b in backs]]),
        2 * width * length * micro * qkv_width // rows, waits=(gate_crossed[0], near[0]),
    )[0]
    expert_grads = [
        one.astype(F32) + swapped(other, 1).astype(F32) + c.astype(F32)
        for one, other, c in ((near[0], near[1], crossed[0]), (both[4], both[5], up_crossed))
    ]
    gate_grad = call(
        total_by_expert, (Sent(like(both[0].shape, F32)),),
        late([both[0], swapped(both[1], 1), *gate_crossed]), 0,
    )[0]
    layer_outputs = call(
        last_outputs, (Sent(like((micro, tokens, width), F32)),),
        late([spread] + [v for m in pieces for v in (
            back[m], attended[m][0], attended[m][1], places[m], results[m][0])]),
        4 * slots * tokens * width, scalars=(second,), waits=(w_grads,),
    )[0]

    wide = share + qkv_width // rows + LANES
    pieces_out = call(
        fold, (Sent(like((shard, wide), F32)),) * rows,
        late([over_columns(o_grads), over_columns(w_grads)]), 0,
        scratch=[pltpu.VMEM((rows * shard, wide), F32)], scalars=(here,),
    )
    pieces_out = [pieces_out[0]] + [swapped(pieces_out[s], s) for s in steps[1:]]
    o_grad, q_grad, k_grad, v_grad, r_grad, first, second_sum = call(
        finish,
        (like((shard, width), F32), like((shard, width), F32), like((shard, kv_width), F32),
         like((shard, kv_width), F32), like((shard, experts), F32), like((1, shard), F32),
         like((1, shard), F32)),
        late([*pieces_out, w_query[0], w_key[0], w_value[0], attn_gain]), 0,
        scratch=[pltpu.VMEM((shard, qkv_width), F32)], scalars=(here,),
    )

    return (
        layer_outputs[None, :, None],
        jnp.stack([o[1] for o in outer])[None, :, None],
        first,
        q_grad[None],
        k_grad[None],
        v_grad[None],
        o_grad[None],
        second_sum,
        r_grad[None],
        gate_grad[None],
        expert_grads[1][None],
        expert_grads[0][None],
    )


def solution(mesh):
    dense = P("section", ("row", "col"), None)
    gain = P("section", ("row", "col"))
    expert = P("section", "col", "row", None)
    token = P(None, "col", "row", None)
    layered = P("section", None, "col", "row", None)
    return jax.shard_map(
        on_device,
        mesh=mesh,
        in_specs=(
            token, token, P(None, "col", None), layered, gain, dense, dense, dense, dense, gain,
            dense, expert, expert, expert,
        ),
        out_specs=(
            layered, layered, gain, dense, dense, dense, dense, gain, dense, expert, expert, expert,
        ),
        check_vma=False,
    )
```

```python
import functools

import jax
import jax.numpy as jnp
from jax import lax
from jax.experimental import pallas as pl
from jax.experimental.pallas import tpu as pltpu
from jax.sharding import PartitionSpec as P

HEAD_DIM = 128
ROOMS = 16
EPSILON = 1e-06
LANES = 128
BF = jnp.bfloat16
F32 = jnp.float32
MIB = 1 << 20


def dot(left, right, contract=(1, 0)):
    return lax.dot_general(
        left, right, (((contract[0],), (contract[1],)), ((), ())), preferred_element_type=F32
    )


def like(shape, dtype):
    return jax.ShapeDtypeStruct(shape, dtype)


class Late:
    def __init__(self, source, index=None, target=None, sem=None):
        self.source, self.index, self.target, self.copy = source, index, target, None
        if target is not None:
            source = source if index is None else source.at[index]
            self.copy = pltpu.make_async_copy(source, target, sem)
            self.copy.start()
            self.waiting = True

    def ready(self):
        if self.waiting:
            self.copy.wait()
            self.waiting = False
        return self.target

    def __getitem__(self, index):
        return self.ready()[index]

    @property
    def shape(self):
        return self.source.shape[len(self.index or ()) :]


class Sent:
    def __init__(self, source, target=None, sems=None):
        self.source, self.target, self.sems, self.copies = source, target, sems, []

    def __getitem__(self, index):
        return self.source[index]

    def __setitem__(self, index, value):
        self.source[index] = value

    def send(self, *parts):
        for part in parts or (...,):
            at = len(self.copies)
            whole = part is ...
            copy = pltpu.make_async_copy(
                self.source if whole else self.source.at[part],
                self.target if whole else self.target.at[part],
                self.sems.at[at],
            )
            copy.start()
            self.copies.append(copy)

    @property
    def shape(self):
        return self.source.shape


PARTS = 4


def sent(out, *parts):
    if isinstance(out, Sent):
        out.send(*parts)


def call(body, outs, args, flops, far=(), scratch=(), scalars=(), waits=()):
    arrays = [a.source if isinstance(a, Late) else a for a in args]
    shapes = [o.source if isinstance(o, Sent) else o for o in outs]
    moved = sum(a.size * a.dtype.itemsize for a in (*arrays, *far, *shapes))
    count = len(scalars) + len(args) + len(far)
    kinds = [isinstance(a, Late) for a in args]
    out_kinds = [isinstance(o, Sent) for o in outs]
    buffers = [pltpu.VMEM(a.shape, a.source.dtype) for a in args if isinstance(a, Late)]
    buffers += [pltpu.VMEM(o.shape, o.dtype) for o, k in zip(shapes, out_kinds) if k]

    def run(*refs):
        given, refs = list(refs[:count]), refs[count + len(waits) :]
        results, refs = list(refs[: len(outs)]), refs[len(outs) :]
        own, rest = list(refs[: len(buffers)]), refs[len(buffers) :]
        sems, rest = (rest[0], rest[1:]) if buffers else (None, rest)
        used = 0
        for k, kind in enumerate(kinds):
            if kind:
                at = len(scalars) + k
                given[at] = Late(given[at], args[k].index, own[used], sems.at[used, 0])
                used += 1
        for k, kind in enumerate(out_kinds):
            if kind:
                results[k] = Sent(own[used], results[k], sems.at[used])
                used += 1
        body(*given, *results, *rest)
        for one in given:
            if isinstance(one, Late):
                one.ready()
        for one in results:
            if isinstance(one, Sent) and not one.copies:
                one.send()
        for one in results:
            if isinstance(one, Sent):
                done_with(one.copies)

    anywhere, local = pl.BlockSpec(memory_space=pltpu.HBM), pl.BlockSpec(memory_space=pltpu.VMEM)
    return pl.pallas_call(
        run,
        out_shape=tuple(shapes),
        in_specs=[pl.BlockSpec(memory_space=pltpu.SMEM)] * len(scalars)
        + [anywhere if k else local for k in kinds]
        + [anywhere] * (len(far) + len(waits)),
        out_specs=tuple(anywhere if k else local for k in out_kinds),
        scratch_shapes=buffers
        + ([pltpu.SemaphoreType.DMA((len(buffers), PARTS))] if buffers else [])
        + list(scratch),
        compiler_params=pltpu.CompilerParams(vmem_limit_bytes=64 * MIB),
        cost_estimate=pl.CostEstimate(
            flops=int(flops), bytes_accessed=int(moved), transcendentals=0
        ),
        name=body.func.__name__ if isinstance(body, functools.partial) else body.__name__,
    )(*scalars, *arrays, *far, *waits)


def late(values):
    return [Late(v) for v in values]


def nothing(*refs):
    pass


def hold(value, *waits):
    return pl.pallas_call(
        nothing,
        out_shape=like(value.shape, value.dtype),
        in_specs=[pl.BlockSpec(memory_space=pl.ANY)] * (1 + len(waits)),
        out_specs=pl.BlockSpec(memory_space=pl.ANY),
        input_output_aliases={0: 0},
        name="hold",
    )(value, *waits)


def swapped(value, step):
    rows = lax.axis_size("row")
    return lax.ppermute(value, "row", [(r, r ^ step) for r in range(rows)])


def norm_parts(stream):
    return lax.rsqrt(jnp.mean(stream * stream, -1, keepdims=True) + EPSILON)


def norm_back(grad, stream, gain):
    inverse = norm_parts(stream)
    unit = stream * inverse
    scaled = grad * gain
    back = inverse * (scaled - unit * jnp.mean(scaled * unit, -1, keepdims=True))
    return back, jnp.sum(grad * unit, 0, keepdims=True)


def turned(vectors, cosine, sine):
    done = []
    for at in range(0, vectors.shape[1], HEAD_DIM):
        one = vectors[:, at : at + HEAD_DIM]
        done.append(one * cosine + pltpu.roll(one, HEAD_DIM // 2, 1) * sine)
    return jnp.concatenate(done, -1) if len(done) > 1 else done[0]


def stacked_heads(value, first, count):
    return jnp.concatenate(
        [value[:, (first + j) * HEAD_DIM : (first + j + 1) * HEAD_DIM] for j in range(count)], 0
    )


def unstacked_heads(value, count):
    tokens = value.shape[0] // count
    return jnp.concatenate([value[j * tokens : (j + 1) * tokens] for j in range(count)], 1)


def cuts_of(total, most=512):
    return [(at, min(most, total - at)) for at in range(0, total, most)]


def project(
    flag, came, entering, gain, cosine, sine, dense, stream, normed, query, pair, weights, sems
):
    width = stream.shape[1]
    cuts = cuts_of(weights.shape[1])
    copies = [
        pltpu.make_async_copy(
            dense.at[:, pl.ds(at, size)], weights.at[:, pl.ds(at, size)], sems.at[k]
        )
        for k, (at, size) in enumerate(cuts)
    ]
    for copy in copies:
        copy.start()
    x = jnp.where(flag[0] > 0, came[...].astype(F32), entering[...].astype(F32))
    stream[...] = x
    sent(stream)
    low = (x * norm_parts(x) * gain[...]).astype(BF)
    normed[...] = low
    sent(normed)
    keys = pair.shape[1] // 2
    for copy, (at, size) in zip(copies, cuts):
        copy.wait()
        part = dot(low, weights[:, at : at + size])
        for begin in range(at, at + size, HEAD_DIM):
            head = part[:, begin - at : begin - at + HEAD_DIM]
            if begin < width + keys:
                head = turned(head, cosine[...], sine[...])
            head = head.astype(BF)
            if begin < width:
                query[:, begin : begin + HEAD_DIM] = head
            else:
                pair[:, begin - width : begin - width + HEAD_DIM] = head
            if begin + HEAD_DIM == width:
                sent(query)


def project_all(at_gain, entering, cosine, sine, dense, *rest):
    outs, (weights, small, sems) = rest[:-3], rest[-3:]
    micro, unused, tokens, width = entering.shape
    cuts = cuts_of(weights.shape[1])
    block = pltpu.make_async_copy(
        dense.at[:, pl.ds(weights.shape[1], LANES)], small, sems.at[len(cuts)]
    )
    block.start()
    copies = [
        pltpu.make_async_copy(
            dense.at[:, pl.ds(at, size)], weights.at[:, pl.ds(at, size)], sems.at[k]
        )
        for k, (at, size) in enumerate(cuts)
    ]
    for copy in copies:
        copy.start()
    scaled = []
    for m in range(micro):
        x = entering[m, 0].astype(F32)
        outs[3 * m][...] = x
        sent(outs[3 * m])
        scaled.append(x * norm_parts(x))
    block.wait()
    gain = small[...].astype(F32).T[at_gain : at_gain + 1, :]
    lows = [(x * gain).astype(BF) for x in scaled]
    low = jnp.concatenate(lows, 0)
    cosines = jnp.concatenate([cosine[...]] * micro, 0)
    sines = jnp.concatenate([sine[...]] * micro, 0)
    keys = outs[2].shape[1] // 2
    for copy, (at, size) in zip(copies, cuts):
        copy.wait()
        part = dot(low, weights[:, at : at + size])
        for begin in range(at, at + size, HEAD_DIM):
            head = part[:, begin - at : begin - at + HEAD_DIM]
            if begin < width + keys:
                head = turned(head, cosines, sines)
            head = head.astype(BF)
            for m in range(micro):
                out, to = (outs[3 * m + 1], begin) if begin < width else (outs[3 * m + 2], begin - width)
                out[:, to : to + HEAD_DIM] = head[m * tokens : (m + 1) * tokens]
                if begin + HEAD_DIM == width:
                    sent(out)


def slot_experts(slots):
    own = lax.broadcasted_iota(jnp.int32, (slots, LANES), 0) // ROOMS
    return own == lax.broadcasted_iota(jnp.int32, (slots, LANES), 1)


def slot_gates(dispatch, gates):
    here = slot_experts(dispatch.shape[0])
    return jnp.sum(jnp.where(here, dot(dispatch, gates.astype(BF)), 0.0), -1, keepdims=True)


def attend(
    keep, flag, stream, query, pair0, pair1, pair2, pair3, bias, gain, chosen, dispatch, target,
    *rest,
):
    dense, w_out, middle, gates, outgoing = rest[:5]
    kept, (mixed, weights, router, sems) = rest[5:-4], rest[-4:]
    width = stream.shape[1]
    copies = [
        pltpu.make_async_copy(w_out, weights, sems.at[0]),
        pltpu.make_async_copy(
            dense.at[:, pl.ds(dense.shape[1] - LANES, LANES)], router, sems.at[1]
        ),
    ]
    for copy in copies:
        copy.start()
    tokens = stream.shape[0]
    pairs = stacked((pair0, pair1, pair2, pair3))
    kv_heads = pairs.shape[1] // (2 * HEAD_DIM)
    group = width // HEAD_DIM // kv_heads
    biases = jnp.concatenate([bias[...]] * group, 0)
    for h in range(kv_heads):
        keys = pairs[:, h * HEAD_DIM : (h + 1) * HEAD_DIM]
        values = pairs[:, (kv_heads + h) * HEAD_DIM : (kv_heads + h + 1) * HEAD_DIM]
        queries = stacked_heads(query, h * group, group)
        scores = dot(queries, keys, (1, 1)) * HEAD_DIM ** (-0.5) + biases
        expo = jnp.exp(scores - jnp.max(scores, -1, keepdims=True))
        weight = (expo * (1.0 / jnp.sum(expo, -1, keepdims=True))).astype(BF)
        if keep:
            kept[0][h] = weight
        done = dot(weight, values).astype(BF)
        for j in range(group):
            begin = (h * group + j) * HEAD_DIM
            mixed[:, begin : begin + HEAD_DIM] = done[j * tokens : (j + 1) * tokens]
    if keep:
        kept[1][...] = mixed[...]
        sent(kept[0])
        sent(kept[1])
    copies[0].wait()
    x = stream[...] + dot(mixed[...], weights[...])
    middle[...] = x
    sent(middle)
    low = (x * norm_parts(x) * gain[...]).astype(BF)
    if keep:
        kept[2][...] = low
        sent(kept[2])
    copies[1].wait()
    taken = chosen[...] > 0
    logits = jnp.where(taken, dot(low, router[...]), -1e30)
    expo = jnp.where(taken, jnp.exp(logits - jnp.max(logits, -1, keepdims=True)), 0.0)
    share = expo / jnp.sum(expo, -1, keepdims=True)
    gates[...] = share
    sent(gates)
    slots = dispatch[...]
    per, columns = outgoing.shape[1], outgoing.shape[0]
    if keep:
        outgoing[:, :, :width] = dot(slots, low).astype(BF).reshape(columns, per, width)
        lane = lax.broadcasted_iota(jnp.int32, (slots.shape[0], LANES), 1)
        notes = jnp.where(lane == 0, slot_gates(slots, share), 0.0).astype(BF)
        outgoing[:, :, width:] = notes.reshape(columns, per, LANES)
    else:
        low = jnp.where(flag[0] > 0, target[...], low)
        outgoing[...] = dot(slots, low).astype(BF).reshape(columns, per, width)


def by_expert(refs, experts):
    whole = [[[r.at[j] for j in range(experts)] for r in refs[at : at + 4]] for at in (0, 4)]
    down = [[r.at[j] for j in range(experts)] for r in refs[8:10]]
    for at in (10, 10 + experts):
        down.append([r.at[0] for r in refs[at : at + experts]])
    return [*whole, down]


class Fetched:
    def __init__(self, shards, weights, sems):
        self.weights = weights
        self.copies = {}
        for j in range(weights.shape[1]):
            for k in range(weights.shape[0]):
                self.copies[k, j] = [
                    pltpu.make_async_copy(
                        shards[k][p][j],
                        weights.at[k, j, pl.ds(p * shards[k][p][j].shape[0], shards[k][p][j].shape[0])],
                        sems.at[k, j, p],
                    )
                    for p in range(4)
                ]
        for k in range(weights.shape[0]):
            self.start(k, 0)

    def start(self, k, j):
        for copy in self.copies.get((k, j), ()):
            copy.start()

    def ready(self, k, j):
        done_with(self.copies[k, j])
        self.start(k, j + 1)


def done_with(copies):
    for copy in copies:
        copy.wait()


def rows_of(value, j, begin=0):
    columns, unused, width = value.shape
    at = begin + j * ROOMS
    return value[:, at : at + ROOMS, :].reshape(columns * ROOMS, width)


def put_rows(out, j, rows, inner):
    at, width = j * ROOMS, rows.shape[1]
    out[:, at : at + ROOMS, :width] = rows.reshape(-1, ROOMS, width)
    high = inner.astype(BF).astype(F32)
    lane = lax.broadcasted_iota(jnp.int32, (rows.shape[0], LANES), 1)
    both = jnp.where(lane == 0, high, jnp.where(lane == 1, inner - high, 0.0))
    out[:, at : at + ROOMS, width:] = both.astype(BF).reshape(-1, ROOMS, LANES)


def expert_forward(both, arrived, *refs):
    early, refs = (refs[0], refs[1:]) if both else (None, refs)
    weights, sems = refs[-2:]
    experts = weights.shape[1]
    count = 10 + 2 * experts
    outs = refs[count:-2]
    fetched = Fetched(by_expert(refs, experts), weights, sems)
    width = weights.shape[3]
    for j in range(weights.shape[1]):
        at = j * ROOMS
        noted = rows_of(arrived, j)
        rows = noted[:, :width]
        fetched.ready(0, j)
        gate = dot(rows, weights[0, j], (1, 1))
        fetched.ready(1, j)
        lifted = dot(rows, weights[1, j], (1, 1))
        square = gate * gate
        bend = jnp.tanh(0.7978845608028654 * gate * (1.0 + 0.044715 * square))
        active = 0.5 * gate * (1.0 + bend)
        hidden = (active * lifted).astype(BF)
        fetched.ready(2, j)
        made = dot(hidden, weights[2, j]).astype(BF)
        outs[0][:, at : at + ROOMS, :] = made.reshape(-1, ROOMS, made.shape[1])
        sent(outs[0], (slice(None), pl.ds(at, ROOMS)))
        if both:
            slope = 0.5 * (1.0 + bend) + 0.5 * gate * (1.0 - bend * bend) * (
                0.7978845608028654 * (1.0 + 3 * 0.044715 * square)
            )
            bent = slope * lifted
            outs[1][j] = hidden
            outs[2][j] = active.astype(BF)
            outs[3][j] = bent.astype(BF)
            grads = (rows_of(early, j).astype(F32) * noted[:, width : width + 1].astype(F32)).astype(BF)
            hidden_grads = dot(grads, weights[2, j], (1, 1))
            gate_part = (hidden_grads * bent).astype(BF)
            lifted_part = (hidden_grads * active).astype(BF)
            inner = jnp.sum(hidden_grads * hidden.astype(F32), -1, keepdims=True)
            back = dot(gate_part, weights[0, j]) + dot(lifted_part, weights[1, j])
            put_rows(outs[4], j, back.astype(BF), inner)
            sent(outs[4], (slice(None), pl.ds(at, ROOMS)))
            for out in outs[1:4]:
                sent(out, j)


def combine(returned, middle, gates, spread, places, low):
    weights = (dot(gates[...].astype(BF), spread[...]) * places[...].astype(F32)).astype(BF)
    done = middle[...] + dot(weights, returned[...].reshape(-1, returned.shape[2]))
    low[...] = done.astype(BF)


def last_outputs(flag, spread, *refs):
    out = refs[-1]
    width = out.shape[2]
    for m in range(out.shape[0]):
        returned, middle, gates, places, before = refs[5 * m : 5 * m + 5]
        weights = (dot(gates[...].astype(BF), spread[...]) * places[...].astype(F32)).astype(BF)
        rows = returned[:, :, :width].reshape(-1, width)
        out[m] = jnp.where(flag[0] > 0, middle[...] + dot(weights, rows), before[...].astype(F32))


def send_grads(flag, came, target, gates, dispatch, grad, outgoing):
    low = jnp.where(flag[0] > 0, came[...], target[...])
    grad[...] = low
    sent(grad)
    slots = dispatch[...]
    rows = dot(slots, low) * slot_gates(slots, gates[...])
    outgoing[...] = rows.astype(BF).reshape(outgoing.shape)


def expert_backward(flag, arrived, hidden, active, bent, produced, *refs):
    out, gate_back, lifted_back, weights, sems = refs[-5:]
    gate_shards, up_shards, down_shards = by_expert(refs, weights.shape[1])
    fetched = Fetched([down_shards, gate_shards, up_shards], weights, sems)
    for j in range(weights.shape[1]):
        fetched.ready(0, j)
        hidden_grads = dot(rows_of(arrived, j), weights[0, j], (1, 1))
        gate_part = (hidden_grads * bent[j].astype(F32)).astype(BF)
        lifted_part = (hidden_grads * active[j].astype(F32)).astype(BF)
        gate_back[j] = gate_part
        lifted_back[j] = lifted_part
        inner = jnp.sum(hidden_grads * hidden[j].astype(F32), -1, keepdims=True)
        fetched.ready(1, j)
        done = dot(gate_part, weights[1, j])
        fetched.ready(2, j)
        done = (done + dot(lifted_part, weights[2, j])).astype(BF)
        put_rows(out, j, jnp.where(flag[0] > 0, rows_of(produced, j), done), inner)
        sent(out, (slice(None), pl.ds(j * ROOMS, ROOMS)))
        sent(gate_back, j)
        sent(lifted_back, j)


def attend_back(
    keep, row, flag, token_grads, before, gates, places, middle, gain, grad, query, pair0, pair1,
    pair2, pair3, probs, cosine, sine, dense, w_out, middle_grads, query_back, part0, part1, part2, part3,
    *rest,
):
    tokens, width = middle.shape
    kept, (branch, weights, router, sems) = rest[:-4], rest[-4:]
    copies = [
        pltpu.make_async_copy(
            dense.at[:, pl.ds(dense.shape[1] - LANES, LANES)], router, sems.at[1]
        ),
        pltpu.make_async_copy(w_out, weights, sems.at[0]),
    ]
    for copy in copies:
        copy.start()
    came = token_grads[...]
    if keep:
        came = jnp.where(flag[0] > 0, before[...], came)
    came = came.reshape(-1, came.shape[2])
    place = places[...]
    here = slot_experts(came.shape[0])
    notes = came[:, width:].astype(F32)
    high = jnp.where(here, notes[:, :1], 0.0).astype(BF)
    rest_of = jnp.where(here, notes[:, 1:2], 0.0).astype(BF)
    inner = dot(place, high) + dot(place, rest_of)
    logit_grads = (inner - gates[...] * jnp.sum(inner, -1, keepdims=True)).astype(BF)
    ffn_grads = dot(place, came[:, :width])
    copies[0].wait()
    ffn_grads = ffn_grads + dot(logit_grads, router[...], (1, 1))
    part, total = norm_back(ffn_grads, middle[...], gain[...])
    above = grad[...].astype(F32) + part
    middle_grads[...] = above
    sent(middle_grads)
    low = above.astype(BF)
    if keep:
        kept[0][...] = logit_grads
        kept[1][...] = jnp.broadcast_to(total, kept[1].shape)
        sent(kept[0])
        sent(kept[1])
        branch[...] = low
        share = width // 4
        for s, part in enumerate((part0, part1, part2, part3)):
            begin = pl.multiple_of((row[0] ^ s) * share, LANES)
            part[:, part.shape[1] - share :] = branch[:, pl.ds(begin, share)]
    copies[1].wait()
    mixed_grads = dot(low, weights[...], (1, 1)).astype(BF)
    pairs = stacked((pair0, pair1, pair2, pair3))
    kv_heads = pairs.shape[1] // (2 * HEAD_DIM)
    group = width // HEAD_DIM // kv_heads
    scale = HEAD_DIM ** (-0.5)
    parts = (part0, part1, part2, part3)
    for h in range(kv_heads):
        keys = pairs[:, h * HEAD_DIM : (h + 1) * HEAD_DIM]
        values = pairs[:, (kv_heads + h) * HEAD_DIM : (kv_heads + h + 1) * HEAD_DIM]
        queries = stacked_heads(query, h * group, group)
        top = stacked_heads(mixed_grads, h * group, group)
        weight = probs[h]
        wide = weight.astype(F32)
        weight_grads = dot(top, values, (1, 1))
        value_grads = dot(weight, top, (0, 0)).astype(BF)
        inner = wide * weight_grads
        score_grads = (inner - wide * jnp.sum(inner, -1, keepdims=True)).astype(BF)
        query_grads = dot(score_grads, keys) * scale
        key_grads = (dot(score_grads, queries, (0, 0)) * scale).astype(BF)
        for j in range(group):
            begin = (h * group + j) * HEAD_DIM
            one = query_grads[j * tokens : (j + 1) * tokens]
            query_back[:, begin : begin + HEAD_DIM] = turned(one, cosine[...], -sine[...]).astype(BF)
        for p, part in enumerate(parts):
            part[:, h * HEAD_DIM : (h + 1) * HEAD_DIM] = key_grads[p * tokens : (p + 1) * tokens]
            begin = (kv_heads + h) * HEAD_DIM
            part[:, begin : begin + HEAD_DIM] = value_grads[p * tokens : (p + 1) * tokens]


def project_back(
    keep, row, part0, part1, part2, part3, query_back, stream, gain, middle_grads, cosine, sine,
    dense, low, *rest,
):
    width = stream.shape[1]
    kept, (backs, weights, sems) = rest[:-3], rest[-3:]
    cuts = cuts_of(weights.shape[1])
    copies = [
        pltpu.make_async_copy(
            dense.at[:, pl.ds(at, size)], weights.at[:, pl.ds(at, size)], sems.at[k]
        )
        for k, (at, size) in enumerate(cuts)
    ]
    for copy in copies:
        copy.start()
    pairs = weights.shape[1] - width
    total = sum(part[:, :pairs].astype(F32) for part in (part0, part1, part2, part3))
    keys = pairs // 2
    backs[:, :width] = query_back[...]
    backs[:, width : width + keys] = turned(total[:, :keys], cosine[...], -sine[...]).astype(BF)
    backs[:, width + keys :] = total[:, keys:].astype(BF)
    if keep:
        share = backs.shape[1] // 4
        for s, out in enumerate(kept[1:]):
            out[...] = backs[:, pl.ds(pl.multiple_of((row[0] ^ s) * share, LANES), share)]
            sent(out)
    above = jnp.zeros(stream.shape, F32)
    for copy, (at, size) in zip(copies, cuts):
        copy.wait()
        above = above + dot(backs[:, at : at + size], weights[:, at : at + size], (1, 1))
    part, unused = norm_back(above, stream[...], gain[...])
    done = middle_grads[...] + part
    if keep:
        kept[0][...] = done
    low[...] = done.astype(BF)


def expert_weight_grads(begin_left, which, *refs):
    count = len(which)
    rights = sorted({w for w in which})
    sources, outs = refs[: 2 * count + 2 * len(rights)], refs[2 * count + 2 * len(rights) : -3]
    left, right, sems = refs[-3:]
    experts, deep, wide = left.shape[1:]
    columns, width = right.shape[2] // 2, right.shape[4]
    copies = {}
    for j in range(experts):
        for m in range(2):
            for r, (unused, begin) in enumerate(rights):
                copies["right", r, j, m] = pltpu.make_async_copy(
                    sources[2 * count + 2 * r + m].at[
                        :, pl.ds(begin + j * ROOMS, ROOMS), pl.ds(0, width)
                    ],
                    right.at[r, j, pl.ds(m * columns, columns)],
                    sems.at[1, r, j, m],
                )
            for k in range(count):
                copies["left", k, j, m] = pltpu.make_async_copy(
                    sources[2 * k + m].at[j, :, pl.ds(begin_left, wide)],
                    left.at[k, j, pl.ds(m * (deep // 2), deep // 2)],
                    sems.at[0, k, j, m],
                )
    for copy in copies.values():
        copy.start()
    waiting = dict(copies)

    def there(*name):
        for m in range(2):
            copy = waiting.pop((*name, m), None)
            if copy is not None:
                copy.wait()

    for j in range(experts):
        for k, name in enumerate(which):
            r = rights.index(name)
            there("right", r, j)
            there("left", k, j)
            total = dot(left[k, j], right[r, j].reshape(deep, width), (0, 0))
            some = len(outs) // count
            size = wide // some
            for q, out in enumerate(outs[some * k : some * (k + 1)]):
                out[j] = total[q * size : (q + 1) * size].astype(BF)
                sent(out, j)


def add(*refs):
    count = len(refs) // 3
    for k in range(count):
        one, other, total = refs[2 * k], refs[2 * k + 1], refs[2 * count + k]
        total[...] = (one[...].astype(F32) + other[...].astype(F32)).astype(BF)


def pack(*refs):
    for k, value in enumerate(refs[:-1]):
        refs[-1][k] = value[...]


def stacked(refs):
    return jnp.concatenate([r[...] for r in refs], 0)


def by_owner(out, grads, begin):
    columns, lines, unused = out.shape
    size = lines // 4
    for c in range(columns):
        some = [grads[(r * columns + c) * size : (r * columns + c + 1) * size] for r in range(4)]
        out[c, :, begin : begin + grads.shape[1]] = jnp.concatenate(some, 0).astype(BF)


def out_grads(*refs):
    lefts, rights, normed, logits, gains, out = (
        refs[:4], refs[4:12], refs[12:14], refs[14:16], refs[16:18], refs[18],
    )
    share = out.shape[2] - LANES
    left = jnp.concatenate([one[k] for one in lefts for k in (2, 3)], 0)
    right = jnp.concatenate([r[:, r.shape[1] - share :] for r in rights], 0)
    by_owner(out, dot(left, right, (0, 0)), 0)
    width = left.shape[1]
    line = lax.broadcasted_iota(jnp.int32, (LANES, width), 0)
    sums = jnp.where(line == LANES - 1, gains[0][:1, :] + gains[1][:1, :], 0.0)
    by_owner(out, dot(stacked(normed), stacked(logits), (0, 0)) + sums.T, share)


def qkv_grads(*refs):
    lefts, rights, out = refs[:4], refs[4:12], refs[12]
    left = jnp.concatenate([one[k] for one in lefts for k in (0, 1)], 0)
    by_owner(out, dot(left, stacked(rights), (0, 0)), 0)


def fold(row, first, second, out0, out1, out2, out3, total):
    share = first.shape[2]
    total[:, :share] = jnp.sum(first[...].astype(F32), 0)
    total[:, share:] = jnp.sum(second[...].astype(F32), 0)
    for s, out in enumerate((out0, out1, out2, out3)):
        size = out.shape[0]
        out[...] = total[pl.ds(pl.multiple_of((row[0] ^ s) * size, 8), size), :]
        sent(out)


def finish(
    row, in0, in1, in2, in3, w_query, w_key, w_value, gain, o_grad, q_grad, k_grad, v_grad, r_grad,
    first, second, total,
):
    share = o_grad.shape[1] // 4
    piece = total.shape[1] // 4
    ins = (in0, in1, in2, in3)
    for s, one in enumerate(ins):
        where = row[0] ^ s
        o_grad[:, pl.ds(pl.multiple_of(where * share, LANES), share)] = one[:, :share]
        total[:, pl.ds(pl.multiple_of(where * piece, LANES), piece)] = one[:, share + LANES :]
    rest = sum(one[:, share : share + LANES] for one in ins)
    r_grad[...] = rest[:, : r_grad.shape[1]]
    second[...] = rest.T[LANES - 1 :, :]
    begin, inner = 0, jnp.zeros((total.shape[0], 1), F32)
    for out, weight in ((q_grad, w_query), (k_grad, w_key), (v_grad, w_value)):
        part = total[:, begin : begin + out.shape[1]]
        out[...] = part
        inner = inner + jnp.sum(part * weight[...].astype(F32), -1, keepdims=True)
        begin += out.shape[1]
    line = jnp.broadcast_to(inner, (total.shape[0], LANES)).T[:1, :]
    first[...] = line / gain[...].astype(F32)


def over_columns(value):
    return lax.all_to_all(value, "col", split_axis=0, concat_axis=0, tiled=True)


def on_device(
    inputs, cotangent, segment_ids, routes, attn_gain, w_query, w_key, w_value, w_out, ffn_gain,
    w_router, w_gate, w_up, w_down,
):
    section = lax.axis_index("section")
    row = lax.axis_index("row")
    rows = lax.axis_size("row")
    columns = lax.axis_size("col")
    micro, tokens, width = inputs.shape[0], inputs.shape[2], inputs.shape[3]
    experts = w_router.shape[2]
    per_column = w_gate.shape[1]
    hidden_width = w_gate.shape[2] * rows
    kv_width = w_key.shape[2]
    qkv_width = width + 2 * kv_width
    slots = experts * ROOMS
    share = width // rows
    shard = width // (rows * columns)
    heads = width // HEAD_DIM
    kv_heads = kv_width // HEAD_DIM
    length = rows * tokens
    pieces = range(micro)
    steps = range(rows)
    here = row.astype(jnp.int32)[None]
    second = (section == 1).astype(jnp.int32)[None]
    block = (columns, slots // columns, width)

    dense = jnp.concatenate(
        [w_query[0], w_key[0], w_value[0], w_router[0], attn_gain[0][:, None], ffn_gain[0][:, None],
         jnp.zeros((shard, LANES - experts - 2), BF)], 1
    )
    dense = lax.all_gather(dense, ("row", "col"), axis=0, tiled=True)
    w_o = lax.all_gather(w_out[0], "row", axis=0, tiled=True)
    w_o = over_columns(jnp.broadcast_to(w_o[None], (columns, *w_o.shape)))
    w_o = w_o.reshape(columns, rows, shard, width).transpose(1, 0, 2, 3).reshape(width, width)
    small = dense[:, qkv_width:]
    gain_a = small[:, experts].astype(F32)[None, :]
    gain_f = small[:, experts + 1].astype(F32)[None, :]

    def shards_of(own):
        two = swapped(own, 2)
        return own, swapped(own, 1), two, swapped(two, 1)

    gate_shards, up_shards = shards_of(w_gate[0]), shards_of(w_up[0])
    down_one, down_first = swapped(w_down[0], 1), swapped(w_down[0, :1], 2)

    def all_shards(waits):
        twos = [down_first]
        twos += [swapped(hold(w_down[0, j : j + 1], *waits), 2) for j in range(1, per_column)]
        threes = [swapped(two, 1) for two in twos]
        return (*gate_shards, *up_shards, w_down[0], down_one, *twos, *threes)


    lane = jnp.arange(LANES, dtype=jnp.int32)
    half = HEAD_DIM // 2
    freqs = 10000.0 ** (-2.0 * jnp.arange(half).astype(F32) / HEAD_DIM)
    positions = row * tokens + jnp.arange(tokens, dtype=jnp.int32)
    angles = positions.astype(F32)[:, None] * freqs[None, :]
    cosine = jnp.concatenate([jnp.cos(angles)] * 2, 1)
    sine = jnp.concatenate([-jnp.sin(angles), jnp.sin(angles)], 1)
    key_positions = jnp.concatenate(
        [(row ^ step) * tokens + jnp.arange(tokens, dtype=jnp.int32) for step in steps]
    )
    spread = (lane[:, None] == jnp.arange(slots, dtype=jnp.int32)[None, :] // ROOMS).astype(BF)
    below = (jnp.arange(tokens)[:, None] > jnp.arange(tokens)[None, :]).astype(BF)
    biases, chosens, places, dispatches = [], [], [], []
    for m in pieces:
        segments = segment_ids[m, 0]
        own_segments = lax.dynamic_slice_in_dim(segments, row * tokens, tokens)
        key_segments = jnp.concatenate(
            [lax.dynamic_slice_in_dim(segments, (row ^ s) * tokens, tokens) for s in steps]
        )
        counted = (key_positions[None, :] <= positions[:, None]) & (
            key_segments[None, :] == own_segments[:, None]
        )
        biases.append(jnp.where(counted, 0.0, -1e30).astype(F32))
        chosen = jnp.any(routes[0, m, 0][:, :, None] == lane[None, None, :], 1)
        chosens.append(chosen.astype(F32))
        rank = dot(below, chosen.astype(BF))
        rank = jnp.where(chosen, rank, -1.0)[:, :experts]
        place = (
            rank[:, :, None] == jnp.arange(ROOMS, dtype=F32)[None, None, :]
        ).reshape(tokens, slots)
        places.append(place.astype(BF))
        dispatches.append(place.T.astype(BF))

    token_low, token_wide = like((tokens, width), BF), like((tokens, width), F32)
    pair_like = like((tokens, 2 * kv_width), BF)
    block_like = like(block, BF)
    sums_like = like((8, width), F32)
    kept_like = like((per_column, columns * ROOMS, hidden_width), BF)
    probs_like = like((kv_heads, heads // kv_heads * tokens, length), BF)
    qkv_scratch = [pltpu.VMEM((width, qkv_width), BF), pltpu.SemaphoreType.DMA((8,))]
    out_scratch = [
        pltpu.VMEM((width, width), BF), pltpu.VMEM((width, LANES), BF),
        pltpu.SemaphoreType.DMA((2,)),
    ]
    expert_scratch = [
        pltpu.VMEM((3, per_column, hidden_width, width), BF),
        pltpu.SemaphoreType.DMA((3, per_column, 4)),
    ]
    qkv_flops = 2 * tokens * width * qkv_width
    out_flops = 2 * tokens * width * width + 2 * slots * tokens * width
    score_flops = 2 * heads * tokens * length * HEAD_DIM
    expert_flops = 2 * slots * hidden_width * width

    per = slots // columns
    back_like = like((columns, per, width + LANES), BF)
    lanes_like = like((tokens, LANES), F32)
    tables = late([cosine, sine])
    first_flag = (1 - second)

    def forward(keep, came, waits, early, after, shards):
        projected, pairs = [], []
        if keep:
            for m in pieces:
                projected.append(
                    call(
                        project,
                        (Sent(token_wide), Sent(token_low), Sent(token_low), Sent(pair_like)),
                        (Late(came[m]), Late(inputs, (m, 0)), Late(gain_a), *tables), qkv_flops, (dense,),
                        qkv_scratch, (second,), waits=[p[0] for p in projected],
                    )
                )
                pairs.append([projected[m][3]] + [swapped(projected[m][3], s) for s in steps[1:]])
        else:
            made = call(
                functools.partial(project_all, experts),
                (Sent(token_wide), Sent(token_low), Sent(pair_like)) * micro,
                (Late(inputs), *tables), micro * qkv_flops, (dense,),
                [qkv_scratch[0], pltpu.VMEM((width, LANES), BF), qkv_scratch[1]], waits=waits,
            )
            projected = [(made[3 * m], None, made[3 * m + 1]) for m in pieces]
            for m in pieces:
                pair = made[3 * m + 2]
                pairs.append([pair] + [swapped(pair, s) for s in steps[1:]])
        shards = shards or all_shards(pairs[1][1:])
        attended = [
            call(
                functools.partial(attend, keep),
                (Sent(token_wide), Sent(lanes_like), Sent(back_like if keep else block_like))
                + ((Sent(probs_like), Sent(token_low), Sent(token_low)) if keep else ()),
                (*late([projected[m][0], projected[m][2], *pairs[m], biases[m], gain_f, chosens[m],
                        dispatches[m]]), Late(cotangent, (m, 0))),
                out_flops + 2 * score_flops, (dense, w_o), [pltpu.VMEM((tokens, width), BF)] + out_scratch,
                (second,), () if m else after,
            )
            for m in pieces
        ]
        arrived = [over_columns(a[2]) for a in attended]
        lefts, ready = [], ()
        if keep:
            left = call(
                pack, (Sent(like((2 * micro, tokens, width), BF)),),
                late([p[1] for p in projected] + [a[4] for a in attended]), 0,
            )[0]
            two = swapped(left, 2)
            lefts = [left, swapped(left, 1), two, swapped(two, 1)]
            ready = (two,)
        applied = [
            call(
                functools.partial(expert_forward, keep),
                (Sent(block_like),)
                + ((Sent(kept_like),) * 3 + (Sent(back_like),) if keep else ()),
                late([arrived[m], early[m]] if keep else [arrived[m]]),
                (6 if keep else 3) * expert_flops, shards, expert_scratch,
                waits=ready if m else (attended[1][2],),
            )
            for m in pieces
        ]
        return projected, pairs, attended, arrived, applied, lefts, shards

    def weight_call(quarters, which, lefts, rights, waits):
        quarter, some = hidden_width // 4, len(quarters)
        return call(
            functools.partial(expert_weight_grads, quarters[0] * quarter, which),
            (Sent(like((per_column, quarter, width), BF)),) * (some * len(which)), (),
            len(which) * expert_flops, [*lefts, *rights],
            [pltpu.VMEM((len(which), per_column, 2 * columns * ROOMS, some * quarter), BF),
             pltpu.VMEM((len(rights) // 2, per_column, 2 * columns, ROOMS, width), BF),
             pltpu.SemaphoreType.DMA((2, len(which), per_column, 2))],
            waits=waits,
        )

    def merged(halves, waits):
        pairs = [v for a, b in halves for v in (a, swapped(b, 1))]
        return call(add, [Sent(a) for a, unused in halves], late(pairs), 0, waits=waits)

    def attention_back(keep, m, grad, token_grads, waits):
        return call(
            functools.partial(attend_back, keep),
            (Sent(token_wide), Sent(token_low))
            + (Sent(like((tokens, 2 * kv_width + (share if keep else 0)), BF)),) * rows
            + ((Sent(like((tokens, LANES), BF)), Sent(sums_like)) if keep else ()),
            (*late([token_grads, shared[m] if keep else spread, attended[m][1], places[m],
                                 attended[m][0], gain_f]), Late(*grad),
             *late([projected[m][2], *pairs[m], attended[m][3], cosine, sine])),
            out_flops + 4 * score_flops, (dense, w_o), [pltpu.VMEM((tokens, width), BF)] + out_scratch,
            (here, second), waits,
        )

    def parts_of(inner):
        return [inner[2]] + [swapped(inner[2 + s], s) for s in steps[1:]]

    def projection_back(keep, m, inner, parts, waits):
        return call(
            functools.partial(project_back, keep),
            (Sent(token_low),)
            + ((Sent(token_wide),) + (Sent(like((tokens, qkv_width // rows), BF)),) * rows
               if keep else ()),
            (*late([*parts, inner[1], projected[m][0], gain_a, inner[0]]),
             *tables),
            qkv_flops, (dense,), [pltpu.VMEM((tokens, qkv_width), BF)] + qkv_scratch,
            (here,), waits,
        )

    kept = forward(False, None, (gate_shards[2], up_shards[2], down_first, w_o), None, (), ())
    attended, early, applied, unused, shards = kept[2:]
    returned = [over_columns(a[0]) for a in applied]
    results = [
        call(
            combine, (Sent(token_low),),
            late([returned[m], attended[m][0], attended[m][1], spread, places[m]]),
            2 * slots * tokens * width, waits=() if m else (applied[1][0],),
        )
        for m in pieces
    ]
    came = [lax.ppermute(r[0], "section", [(0, 1)]) for r in results]

    kept = forward(True, came, (), early, results[1], shards)
    projected, pairs, attended, arrived, applied, lefts, unused = kept
    hidden = [a[1] for a in applied]
    shared = [over_columns(a[4]) for a in applied]
    inner, outer = [], []
    for m in pieces:
        waits = (*lefts[1:], outer[0][0]) if m else (applied[1][4],)
        inner.append(attention_back(False, m, (cotangent, (m, 0)), shared[m], waits))
        outer.append(projection_back(False, m, inner[m], parts_of(inner[m]), ()))
    came = [lax.ppermute(o[0], "section", [(1, 0)]) for o in outer]

    given = [
        call(
            send_grads, (Sent(token_low), Sent(block_like)),
            (Late(came[m]), Late(cotangent, (m, 0)), *late([attended[m][1], dispatches[m]])),
            2 * slots * tokens * width, scalars=(first_flag,), waits=() if m else (inner[1][0],),
        )
        for m in pieces
    ]
    arrived_grads = [over_columns(g[1]) for g in given]
    moved = [
        call(
            expert_backward, (Sent(back_like), Sent(kept_like), Sent(kept_like)),
            late([arrived_grads[m], hidden[m], applied[m][2], applied[m][3], applied[m][0]]),
            3 * expert_flops, shards, expert_scratch,
            (second,), () if m else (given[1][1],),
        )
        for m in pieces
    ]
    gate_up = [a[1] for a in moved] + [a[2] for a in moved]
    down_far = merged([weight_call((2, 3), ((0, 0),), hidden, arrived_grads, ())], ())[0]
    crossed = [swapped(down_far, 2)]
    back = [over_columns(moved[0][0]), over_columns(moved[1][0])]
    inner = [attention_back(True, 0, given[0][:1], back[0], (moved[1][0], down_far))]
    parts = [parts_of(inner[0])]
    both = weight_call((0, 1, 2, 3), ((0, 0), (0, 0)), gate_up, arrived, (inner[0][0],))
    inner.append(attention_back(True, 1, given[1][:1], back[1], (both[0], crossed[0])))
    parts.append(parts_of(inner[1]))
    sums = merged([both[2:4], both[6:]], (inner[1][0],))
    gate_far = hold(sums[0], *parts[1][1:])
    crossed.append(swapped(gate_far, 2))
    o_grads = call(
        out_grads, (Sent(like((columns, rows * shard, share + LANES), BF)),),
        late([*lefts, *[p[s] for s in steps for p in parts], *[a[5] for a in attended],
              *[a[6] for a in inner], *[a[7] for a in inner]]),
        2 * width * length * micro * share, waits=(crossed[0], gate_far),
    )[0]
    last = projection_back(True, 1, inner[1], parts[1], (o_grads,))
    outer = [projection_back(True, 0, inner[0], parts[0], (last[0],)), last]
    backs = [[o[2]] + [swapped(o[2 + s], s) for s in steps[1:]] for o in outer]
    crossed.append(swapped(hold(sums[1], *backs[0][1:], *backs[1][1:]), 2))
    near = weight_call((0, 1), ((0, 0),), hidden, arrived_grads, (outer[1][0],))
    w_grads = call(
        qkv_grads, (Sent(like((columns, rows * shard, qkv_width // rows), BF)),),
        late([*lefts, *[b[s] for s in steps for b in backs]]),
        2 * width * length * micro * qkv_width // rows, waits=(crossed[1], near[0]),
    )[0]
    expert_grads = [
        one.astype(F32) + swapped(other, 1).astype(F32) + c.astype(F32)
        for one, other, c in zip((near[0], both[0], both[4]), (near[1], both[1], both[5]), crossed)
    ]
    layer_outputs = call(
        last_outputs, (Sent(like((micro, tokens, width), F32)),),
        late([spread] + [v for m in pieces for v in (
            back[m], attended[m][0], attended[m][1], places[m], results[m][0])]),
        4 * slots * tokens * width, scalars=(second,), waits=(w_grads,),
    )[0]

    wide = share + qkv_width // rows + LANES
    pieces_out = call(
        fold, (Sent(like((shard, wide), F32)),) * rows,
        late([over_columns(o_grads), over_columns(w_grads)]), 0,
        scratch=[pltpu.VMEM((rows * shard, wide), F32)], scalars=(here,),
    )
    pieces_out = [pieces_out[0]] + [swapped(pieces_out[s], s) for s in steps[1:]]
    o_grad, q_grad, k_grad, v_grad, r_grad, first, second_sum = call(
        finish,
        (like((shard, width), F32), like((shard, width), F32), like((shard, kv_width), F32),
         like((shard, kv_width), F32), like((shard, experts), F32), like((1, shard), F32),
         like((1, shard), F32)),
        late([*pieces_out, w_query[0], w_key[0], w_value[0], attn_gain]), 0,
        scratch=[pltpu.VMEM((shard, qkv_width), F32)], scalars=(here,),
    )

    return (
        layer_outputs[None, :, None],
        jnp.stack([o[1] for o in outer])[None, :, None],
        first,
        q_grad[None],
        k_grad[None],
        v_grad[None],
        o_grad[None],
        second_sum,
        r_grad[None],
        expert_grads[1][None],
        expert_grads[2][None],
        expert_grads[0][None],
    )


def solution(mesh):
    dense = P("section", ("row", "col"), None)
    gain = P("section", ("row", "col"))
    expert = P("section", "col", "row", None)
    token = P(None, "col", "row", None)
    layered = P("section", None, "col", "row", None)
    return jax.shard_map(
        on_device,
        mesh=mesh,
        in_specs=(
            token, token, P(None, "col", None), layered, gain, dense, dense, dense, dense, gain,
            dense, expert, expert, expert,
        ),
        out_specs=(
            layered, layered, gain, dense, dense, dense, dense, gain, dense, expert, expert, expert,
        ),
        check_vma=False,
    )
```

```python
import functools

import jax
import jax.numpy as jnp
from jax import lax
from jax.experimental import pallas as pl
from jax.experimental.pallas import tpu as pltpu
from jax.sharding import PartitionSpec as P

HEAD_DIM = 128
ROOMS = 16
EPSILON = 1e-06
LANES = 128
BF = jnp.bfloat16
F32 = jnp.float32
MIB = 1 << 20


def dot(left, right, contract=(1, 0)):
    return lax.dot_general(
        left, right, (((contract[0],), (contract[1],)), ((), ())), preferred_element_type=F32
    )


def like(shape, dtype):
    return jax.ShapeDtypeStruct(shape, dtype)


class Late:
    def __init__(self, source, index=None, target=None, sem=None):
        self.source, self.index, self.target, self.copy = source, index, target, None
        if target is not None:
            source = source if index is None else source.at[index]
            self.copy = pltpu.make_async_copy(source, target, sem)
            self.copy.start()
            self.waiting = True

    def ready(self):
        if self.waiting:
            self.copy.wait()
            self.waiting = False
        return self.target

    def __getitem__(self, index):
        return self.ready()[index]

    @property
    def shape(self):
        return self.source.shape[len(self.index or ()) :]


class Sent:
    def __init__(self, source, target=None, sems=None):
        self.source, self.target, self.sems, self.copies = source, target, sems, []

    def __getitem__(self, index):
        return self.source[index]

    def __setitem__(self, index, value):
        self.source[index] = value

    def send(self, *parts):
        for part in parts or (...,):
            at = len(self.copies)
            whole = part is ...
            copy = pltpu.make_async_copy(
                self.source if whole else self.source.at[part],
                self.target if whole else self.target.at[part],
                self.sems.at[at],
            )
            copy.start()
            self.copies.append(copy)

    @property
    def shape(self):
        return self.source.shape


PARTS = 4


def sent(out, *parts):
    if isinstance(out, Sent):
        out.send(*parts)


def call(body, outs, args, flops, far=(), scratch=(), scalars=(), waits=()):
    arrays = [a.source if isinstance(a, Late) else a for a in args]
    shapes = [o.source if isinstance(o, Sent) else o for o in outs]
    moved = sum(a.size * a.dtype.itemsize for a in (*arrays, *far, *shapes))
    count = len(scalars) + len(args) + len(far)
    kinds = [isinstance(a, Late) for a in args]
    out_kinds = [isinstance(o, Sent) for o in outs]
    buffers = [pltpu.VMEM(a.shape, a.source.dtype) for a in args if isinstance(a, Late)]
    buffers += [pltpu.VMEM(o.shape, o.dtype) for o, k in zip(shapes, out_kinds) if k]

    def run(*refs):
        given, refs = list(refs[:count]), refs[count + len(waits) :]
        results, refs = list(refs[: len(outs)]), refs[len(outs) :]
        own, rest = list(refs[: len(buffers)]), refs[len(buffers) :]
        sems, rest = (rest[0], rest[1:]) if buffers else (None, rest)
        used = 0
        for k, kind in enumerate(kinds):
            if kind:
                at = len(scalars) + k
                given[at] = Late(given[at], args[k].index, own[used], sems.at[used, 0])
                used += 1
        for k, kind in enumerate(out_kinds):
            if kind:
                results[k] = Sent(own[used], results[k], sems.at[used])
                used += 1
        body(*given, *results, *rest)
        for one in given:
            if isinstance(one, Late):
                one.ready()
        for one in results:
            if isinstance(one, Sent) and not one.copies:
                one.send()
        for one in results:
            if isinstance(one, Sent):
                done_with(one.copies)

    anywhere, local = pl.BlockSpec(memory_space=pltpu.HBM), pl.BlockSpec(memory_space=pltpu.VMEM)
    return pl.pallas_call(
        run,
        out_shape=tuple(shapes),
        in_specs=[pl.BlockSpec(memory_space=pltpu.SMEM)] * len(scalars)
        + [anywhere if k else local for k in kinds]
        + [anywhere] * (len(far) + len(waits)),
        out_specs=tuple(anywhere if k else local for k in out_kinds),
        scratch_shapes=buffers
        + ([pltpu.SemaphoreType.DMA((len(buffers), PARTS))] if buffers else [])
        + list(scratch),
        compiler_params=pltpu.CompilerParams(vmem_limit_bytes=64 * MIB),
        cost_estimate=pl.CostEstimate(
            flops=int(flops), bytes_accessed=int(moved), transcendentals=0
        ),
        name=body.func.__name__ if isinstance(body, functools.partial) else body.__name__,
    )(*scalars, *arrays, *far, *waits)


def late(values):
    return [Late(v) for v in values]


def nothing(*refs):
    pass


def hold(value, *waits):
    return pl.pallas_call(
        nothing,
        out_shape=like(value.shape, value.dtype),
        in_specs=[pl.BlockSpec(memory_space=pl.ANY)] * (1 + len(waits)),
        out_specs=pl.BlockSpec(memory_space=pl.ANY),
        input_output_aliases={0: 0},
        name="hold",
    )(value, *waits)


def swapped(value, step):
    rows = lax.axis_size("row")
    return lax.ppermute(value, "row", [(r, r ^ step) for r in range(rows)])


def norm_parts(stream):
    return lax.rsqrt(jnp.mean(stream * stream, -1, keepdims=True) + EPSILON)


def norm_back(grad, stream, gain):
    inverse = norm_parts(stream)
    unit = stream * inverse
    scaled = grad * gain
    back = inverse * (scaled - unit * jnp.mean(scaled * unit, -1, keepdims=True))
    return back, jnp.sum(grad * unit, 0, keepdims=True)


def turned(vectors, cosine, sine):
    done = []
    for at in range(0, vectors.shape[1], HEAD_DIM):
        one = vectors[:, at : at + HEAD_DIM]
        done.append(one * cosine + pltpu.roll(one, HEAD_DIM // 2, 1) * sine)
    return jnp.concatenate(done, -1) if len(done) > 1 else done[0]


def stacked_heads(value, first, count):
    return jnp.concatenate(
        [value[:, (first + j) * HEAD_DIM : (first + j + 1) * HEAD_DIM] for j in range(count)], 0
    )


def unstacked_heads(value, count):
    tokens = value.shape[0] // count
    return jnp.concatenate([value[j * tokens : (j + 1) * tokens] for j in range(count)], 1)


def cuts_of(total, most=512):
    return [(at, min(most, total - at)) for at in range(0, total, most)]


def project(
    flag, came, entering, gain, cosine, sine, dense, stream, normed, query, pair, weights, sems
):
    width = stream.shape[1]
    cuts = cuts_of(weights.shape[1])
    copies = [
        pltpu.make_async_copy(
            dense.at[:, pl.ds(at, size)], weights.at[:, pl.ds(at, size)], sems.at[k]
        )
        for k, (at, size) in enumerate(cuts)
    ]
    for copy in copies:
        copy.start()
    x = jnp.where(flag[0] > 0, came[...].astype(F32), entering[...].astype(F32))
    stream[...] = x
    sent(stream)
    low = (x * norm_parts(x) * gain[...]).astype(BF)
    normed[...] = low
    sent(normed)
    keys = pair.shape[1] // 2
    for copy, (at, size) in zip(copies, cuts):
        copy.wait()
        part = dot(low, weights[:, at : at + size])
        for begin in range(at, at + size, HEAD_DIM):
            head = part[:, begin - at : begin - at + HEAD_DIM]
            if begin < width + keys:
                head = turned(head, cosine[...], sine[...])
            head = head.astype(BF)
            if begin < width:
                query[:, begin : begin + HEAD_DIM] = head
            else:
                pair[:, begin - width : begin - width + HEAD_DIM] = head
            if begin + HEAD_DIM == width:
                sent(query)


def project_all(at_gain, entering, cosine, sine, dense, *rest):
    outs, (weights, small, sems) = rest[:-3], rest[-3:]
    micro, unused, tokens, width = entering.shape
    cuts = cuts_of(weights.shape[1])
    block = pltpu.make_async_copy(
        dense.at[:, pl.ds(weights.shape[1], LANES)], small, sems.at[len(cuts)]
    )
    block.start()
    copies = [
        pltpu.make_async_copy(
            dense.at[:, pl.ds(at, size)], weights.at[:, pl.ds(at, size)], sems.at[k]
        )
        for k, (at, size) in enumerate(cuts)
    ]
    for copy in copies:
        copy.start()
    scaled = []
    for m in range(micro):
        x = entering[m, 0].astype(F32)
        outs[3 * m][...] = x
        sent(outs[3 * m])
        scaled.append(x * norm_parts(x))
    block.wait()
    gain = small[...].astype(F32).T[at_gain : at_gain + 1, :]
    lows = [(x * gain).astype(BF) for x in scaled]
    low = jnp.concatenate(lows, 0)
    cosines = jnp.concatenate([cosine[...]] * micro, 0)
    sines = jnp.concatenate([sine[...]] * micro, 0)
    keys = outs[2].shape[1] // 2
    for copy, (at, size) in zip(copies, cuts):
        copy.wait()
        part = dot(low, weights[:, at : at + size])
        for begin in range(at, at + size, HEAD_DIM):
            head = part[:, begin - at : begin - at + HEAD_DIM]
            if begin < width + keys:
                head = turned(head, cosines, sines)
            head = head.astype(BF)
            for m in range(micro):
                out, to = (outs[3 * m + 1], begin) if begin < width else (outs[3 * m + 2], begin - width)
                out[:, to : to + HEAD_DIM] = head[m * tokens : (m + 1) * tokens]
                if begin + HEAD_DIM == width:
                    sent(out)


def slot_experts(slots):
    own = lax.broadcasted_iota(jnp.int32, (slots, LANES), 0) // ROOMS
    return own == lax.broadcasted_iota(jnp.int32, (slots, LANES), 1)


def slot_gates(dispatch, gates):
    here = slot_experts(dispatch.shape[0])
    return jnp.sum(jnp.where(here, dot(dispatch, gates.astype(BF)), 0.0), -1, keepdims=True)


def attend(
    keep, flag, stream, query, pair0, pair1, pair2, pair3, bias, gain, chosen, dispatch, target,
    *rest,
):
    dense, middle, gates, outgoing = rest[:4]
    kept, (mixed, weights, router, sems) = rest[4:-4], rest[-4:]
    width = stream.shape[1]
    at = dense.shape[1] - width - LANES
    copies = [
        pltpu.make_async_copy(dense.at[:, pl.ds(at + LANES, width)], weights, sems.at[0]),
        pltpu.make_async_copy(dense.at[:, pl.ds(at, LANES)], router, sems.at[1]),
    ]
    for copy in copies:
        copy.start()
    tokens = stream.shape[0]
    pairs = stacked((pair0, pair1, pair2, pair3))
    kv_heads = pairs.shape[1] // (2 * HEAD_DIM)
    group = width // HEAD_DIM // kv_heads
    biases = jnp.concatenate([bias[...]] * group, 0)
    for h in range(kv_heads):
        keys = pairs[:, h * HEAD_DIM : (h + 1) * HEAD_DIM]
        values = pairs[:, (kv_heads + h) * HEAD_DIM : (kv_heads + h + 1) * HEAD_DIM]
        queries = stacked_heads(query, h * group, group)
        scores = dot(queries, keys, (1, 1)) * HEAD_DIM ** (-0.5) + biases
        expo = jnp.exp(scores - jnp.max(scores, -1, keepdims=True))
        weight = (expo * (1.0 / jnp.sum(expo, -1, keepdims=True))).astype(BF)
        if keep:
            kept[0][h] = weight
        done = dot(weight, values).astype(BF)
        for j in range(group):
            begin = (h * group + j) * HEAD_DIM
            mixed[:, begin : begin + HEAD_DIM] = done[j * tokens : (j + 1) * tokens]
    if keep:
        kept[1][...] = mixed[...]
        sent(kept[0])
        sent(kept[1])
    copies[0].wait()
    x = stream[...] + dot(mixed[...], weights[...])
    middle[...] = x
    sent(middle)
    low = (x * norm_parts(x) * gain[...]).astype(BF)
    if keep:
        kept[2][...] = low
        sent(kept[2])
    copies[1].wait()
    taken = chosen[...] > 0
    logits = jnp.where(taken, dot(low, router[...]), -1e30)
    expo = jnp.where(taken, jnp.exp(logits - jnp.max(logits, -1, keepdims=True)), 0.0)
    share = expo / jnp.sum(expo, -1, keepdims=True)
    gates[...] = share
    sent(gates)
    slots = dispatch[...]
    per, columns = outgoing.shape[1], outgoing.shape[0]
    if keep:
        outgoing[:, :, :width] = dot(slots, low).astype(BF).reshape(columns, per, width)
        lane = lax.broadcasted_iota(jnp.int32, (slots.shape[0], LANES), 1)
        notes = jnp.where(lane == 0, slot_gates(slots, share), 0.0).astype(BF)
        outgoing[:, :, width:] = notes.reshape(columns, per, LANES)
    else:
        low = jnp.where(flag[0] > 0, target[...], low)
        outgoing[...] = dot(slots, low).astype(BF).reshape(columns, per, width)


def by_expert(refs, experts):
    whole = [[[r.at[j] for j in range(experts)] for r in refs[at : at + 4]] for at in (0, 4)]
    down = [[r.at[j] for j in range(experts)] for r in refs[8:10]]
    for at in (10, 10 + experts):
        down.append([r.at[0] for r in refs[at : at + experts]])
    return [*whole, down]


class Fetched:
    def __init__(self, shards, weights, sems):
        self.weights = weights
        self.copies = {}
        for j in range(weights.shape[1]):
            for k in range(weights.shape[0]):
                self.copies[k, j] = [
                    pltpu.make_async_copy(
                        shards[k][p][j],
                        weights.at[k, j, pl.ds(p * shards[k][p][j].shape[0], shards[k][p][j].shape[0])],
                        sems.at[k, j, p],
                    )
                    for p in range(4)
                ]
        for k in range(weights.shape[0]):
            self.start(k, 0)

    def start(self, k, j):
        for copy in self.copies.get((k, j), ()):
            copy.start()

    def ready(self, k, j):
        done_with(self.copies[k, j])
        self.start(k, j + 1)


def done_with(copies):
    for copy in copies:
        copy.wait()


def rows_of(value, j, begin=0):
    columns, unused, width = value.shape
    at = begin + j * ROOMS
    return value[:, at : at + ROOMS, :].reshape(columns * ROOMS, width)


def put_rows(out, j, rows, inner):
    at, width = j * ROOMS, rows.shape[1]
    out[:, at : at + ROOMS, :width] = rows.reshape(-1, ROOMS, width)
    high = inner.astype(BF).astype(F32)
    lane = lax.broadcasted_iota(jnp.int32, (rows.shape[0], LANES), 1)
    both = jnp.where(lane == 0, high, jnp.where(lane == 1, inner - high, 0.0))
    out[:, at : at + ROOMS, width:] = both.astype(BF).reshape(-1, ROOMS, LANES)


def expert_forward(both, arrived, *refs):
    early, refs = (refs[0], refs[1:]) if both else (None, refs)
    weights, sems = refs[-2:]
    experts = weights.shape[1]
    count = 10 + 2 * experts
    outs = refs[count:-2]
    fetched = Fetched(by_expert(refs, experts), weights, sems)
    width = weights.shape[3]
    for j in range(weights.shape[1]):
        at = j * ROOMS
        noted = rows_of(arrived, j)
        rows = noted[:, :width]
        fetched.ready(0, j)
        gate = dot(rows, weights[0, j], (1, 1))
        fetched.ready(1, j)
        lifted = dot(rows, weights[1, j], (1, 1))
        square = gate * gate
        bend = jnp.tanh(0.7978845608028654 * gate * (1.0 + 0.044715 * square))
        active = 0.5 * gate * (1.0 + bend)
        hidden = (active * lifted).astype(BF)
        fetched.ready(2, j)
        made = dot(hidden, weights[2, j]).astype(BF)
        outs[0][:, at : at + ROOMS, :] = made.reshape(-1, ROOMS, made.shape[1])
        sent(outs[0], (slice(None), pl.ds(at, ROOMS)))
        if both:
            slope = 0.5 * (1.0 + bend) + 0.5 * gate * (1.0 - bend * bend) * (
                0.7978845608028654 * (1.0 + 3 * 0.044715 * square)
            )
            bent = slope * lifted
            outs[1][j] = hidden
            outs[2][j] = active.astype(BF)
            outs[3][j] = bent.astype(BF)
            grads = (rows_of(early, j).astype(F32) * noted[:, width : width + 1].astype(F32)).astype(BF)
            hidden_grads = dot(grads, weights[2, j], (1, 1))
            gate_part = (hidden_grads * bent).astype(BF)
            lifted_part = (hidden_grads * active).astype(BF)
            inner = jnp.sum(hidden_grads * hidden.astype(F32), -1, keepdims=True)
            back = dot(gate_part, weights[0, j]) + dot(lifted_part, weights[1, j])
            put_rows(outs[4], j, back.astype(BF), inner)
            sent(outs[4], (slice(None), pl.ds(at, ROOMS)))
            for out in outs[1:4]:
                sent(out, j)


def combine(returned, middle, gates, spread, places, low):
    weights = (dot(gates[...].astype(BF), spread[...]) * places[...].astype(F32)).astype(BF)
    done = middle[...] + dot(weights, returned[...].reshape(-1, returned.shape[2]))
    low[...] = done.astype(BF)


def last_outputs(flag, spread, *refs):
    out = refs[-1]
    width = out.shape[2]
    for m in range(out.shape[0]):
        returned, middle, gates, places, before = refs[5 * m : 5 * m + 5]
        weights = (dot(gates[...].astype(BF), spread[...]) * places[...].astype(F32)).astype(BF)
        rows = returned[:, :, :width].reshape(-1, width)
        out[m] = jnp.where(flag[0] > 0, middle[...] + dot(weights, rows), before[...].astype(F32))


def send_grads(flag, came, target, gates, dispatch, grad, outgoing):
    low = jnp.where(flag[0] > 0, came[...], target[...])
    grad[...] = low
    sent(grad)
    slots = dispatch[...]
    rows = dot(slots, low) * slot_gates(slots, gates[...])
    outgoing[...] = rows.astype(BF).reshape(outgoing.shape)


def expert_backward(flag, arrived, hidden, active, bent, produced, *refs):
    out, gate_back, lifted_back, weights, sems = refs[-5:]
    gate_shards, up_shards, down_shards = by_expert(refs, weights.shape[1])
    fetched = Fetched([down_shards, gate_shards, up_shards], weights, sems)
    for j in range(weights.shape[1]):
        fetched.ready(0, j)
        hidden_grads = dot(rows_of(arrived, j), weights[0, j], (1, 1))
        gate_part = (hidden_grads * bent[j].astype(F32)).astype(BF)
        lifted_part = (hidden_grads * active[j].astype(F32)).astype(BF)
        gate_back[j] = gate_part
        lifted_back[j] = lifted_part
        inner = jnp.sum(hidden_grads * hidden[j].astype(F32), -1, keepdims=True)
        fetched.ready(1, j)
        done = dot(gate_part, weights[1, j])
        fetched.ready(2, j)
        done = (done + dot(lifted_part, weights[2, j])).astype(BF)
        put_rows(out, j, jnp.where(flag[0] > 0, rows_of(produced, j), done), inner)
        sent(out, (slice(None), pl.ds(j * ROOMS, ROOMS)))
        sent(gate_back, j)
        sent(lifted_back, j)


def attend_back(
    keep, row, flag, token_grads, before, gates, places, middle, gain, grad, query, pair0, pair1,
    pair2, pair3, probs, cosine, sine, dense, middle_grads, query_back, part0, part1, part2, part3,
    *rest,
):
    tokens, width = middle.shape
    kept, (branch, weights, router, sems) = rest[:-4], rest[-4:]
    at = dense.shape[1] - width - LANES
    copies = [
        pltpu.make_async_copy(dense.at[:, pl.ds(at, LANES)], router, sems.at[1]),
        pltpu.make_async_copy(dense.at[:, pl.ds(at + LANES, width)], weights, sems.at[0]),
    ]
    for copy in copies:
        copy.start()
    came = token_grads[...]
    if keep:
        came = jnp.where(flag[0] > 0, before[...], came)
    came = came.reshape(-1, came.shape[2])
    place = places[...]
    here = slot_experts(came.shape[0])
    notes = came[:, width:].astype(F32)
    high = jnp.where(here, notes[:, :1], 0.0).astype(BF)
    rest_of = jnp.where(here, notes[:, 1:2], 0.0).astype(BF)
    inner = dot(place, high) + dot(place, rest_of)
    logit_grads = (inner - gates[...] * jnp.sum(inner, -1, keepdims=True)).astype(BF)
    ffn_grads = dot(place, came[:, :width])
    copies[0].wait()
    ffn_grads = ffn_grads + dot(logit_grads, router[...], (1, 1))
    part, total = norm_back(ffn_grads, middle[...], gain[...])
    above = grad[...].astype(F32) + part
    middle_grads[...] = above
    sent(middle_grads)
    low = above.astype(BF)
    if keep:
        kept[0][...] = logit_grads
        kept[1][...] = jnp.broadcast_to(total, kept[1].shape)
        sent(kept[0])
        sent(kept[1])
        branch[...] = low
        share = width // 4
        for s, part in enumerate((part0, part1, part2, part3)):
            begin = pl.multiple_of((row[0] ^ s) * share, LANES)
            part[:, part.shape[1] - share :] = branch[:, pl.ds(begin, share)]
    copies[1].wait()
    mixed_grads = dot(low, weights[...], (1, 1)).astype(BF)
    pairs = stacked((pair0, pair1, pair2, pair3))
    kv_heads = pairs.shape[1] // (2 * HEAD_DIM)
    group = width // HEAD_DIM // kv_heads
    scale = HEAD_DIM ** (-0.5)
    parts = (part0, part1, part2, part3)
    for h in range(kv_heads):
        keys = pairs[:, h * HEAD_DIM : (h + 1) * HEAD_DIM]
        values = pairs[:, (kv_heads + h) * HEAD_DIM : (kv_heads + h + 1) * HEAD_DIM]
        queries = stacked_heads(query, h * group, group)
        top = stacked_heads(mixed_grads, h * group, group)
        weight = probs[h]
        wide = weight.astype(F32)
        weight_grads = dot(top, values, (1, 1))
        value_grads = dot(weight, top, (0, 0)).astype(BF)
        inner = wide * weight_grads
        score_grads = (inner - wide * jnp.sum(inner, -1, keepdims=True)).astype(BF)
        query_grads = dot(score_grads, keys) * scale
        key_grads = (dot(score_grads, queries, (0, 0)) * scale).astype(BF)
        for j in range(group):
            begin = (h * group + j) * HEAD_DIM
            one = query_grads[j * tokens : (j + 1) * tokens]
            query_back[:, begin : begin + HEAD_DIM] = turned(one, cosine[...], -sine[...]).astype(BF)
        for p, part in enumerate(parts):
            part[:, h * HEAD_DIM : (h + 1) * HEAD_DIM] = key_grads[p * tokens : (p + 1) * tokens]
            begin = (kv_heads + h) * HEAD_DIM
            part[:, begin : begin + HEAD_DIM] = value_grads[p * tokens : (p + 1) * tokens]


def project_back(
    keep, row, part0, part1, part2, part3, query_back, stream, gain, middle_grads, cosine, sine,
    dense, low, *rest,
):
    width = stream.shape[1]
    kept, (backs, weights, sems) = rest[:-3], rest[-3:]
    cuts = cuts_of(weights.shape[1])
    copies = [
        pltpu.make_async_copy(
            dense.at[:, pl.ds(at, size)], weights.at[:, pl.ds(at, size)], sems.at[k]
        )
        for k, (at, size) in enumerate(cuts)
    ]
    for copy in copies:
        copy.start()
    pairs = weights.shape[1] - width
    total = sum(part[:, :pairs].astype(F32) for part in (part0, part1, part2, part3))
    keys = pairs // 2
    backs[:, :width] = query_back[...]
    backs[:, width : width + keys] = turned(total[:, :keys], cosine[...], -sine[...]).astype(BF)
    backs[:, width + keys :] = total[:, keys:].astype(BF)
    if keep:
        share = backs.shape[1] // 4
        for s, out in enumerate(kept[1:]):
            out[...] = backs[:, pl.ds(pl.multiple_of((row[0] ^ s) * share, LANES), share)]
            sent(out)
    above = jnp.zeros(stream.shape, F32)
    for copy, (at, size) in zip(copies, cuts):
        copy.wait()
        above = above + dot(backs[:, at : at + size], weights[:, at : at + size], (1, 1))
    part, unused = norm_back(above, stream[...], gain[...])
    done = middle_grads[...] + part
    if keep:
        kept[0][...] = done
    low[...] = done.astype(BF)


def expert_weight_grads(begin_left, which, *refs):
    count = len(which)
    rights = sorted({w for w in which})
    sources, outs = refs[: 2 * count + 2 * len(rights)], refs[2 * count + 2 * len(rights) : -3]
    left, right, sems = refs[-3:]
    experts, deep, wide = left.shape[1:]
    columns, width = right.shape[2] // 2, right.shape[4]
    copies = {}
    for j in range(experts):
        for m in range(2):
            for r, (unused, begin) in enumerate(rights):
                copies["right", r, j, m] = pltpu.make_async_copy(
                    sources[2 * count + 2 * r + m].at[
                        :, pl.ds(begin + j * ROOMS, ROOMS), pl.ds(0, width)
                    ],
                    right.at[r, j, pl.ds(m * columns, columns)],
                    sems.at[1, r, j, m],
                )
            for k in range(count):
                copies["left", k, j, m] = pltpu.make_async_copy(
                    sources[2 * k + m].at[j, :, pl.ds(begin_left, wide)],
                    left.at[k, j, pl.ds(m * (deep // 2), deep // 2)],
                    sems.at[0, k, j, m],
                )
    for copy in copies.values():
        copy.start()
    waiting = dict(copies)

    def there(*name):
        for m in range(2):
            copy = waiting.pop((*name, m), None)
            if copy is not None:
                copy.wait()

    for j in range(experts):
        for k, name in enumerate(which):
            r = rights.index(name)
            there("right", r, j)
            there("left", k, j)
            total = dot(left[k, j], right[r, j].reshape(deep, width), (0, 0))
            some = len(outs) // count
            size = wide // some
            for q, out in enumerate(outs[some * k : some * (k + 1)]):
                out[j] = total[q * size : (q + 1) * size].astype(BF)
                sent(out, j)


def add(*refs):
    count = len(refs) // 3
    for k in range(count):
        one, other, total = refs[2 * k], refs[2 * k + 1], refs[2 * count + k]
        total[...] = (one[...].astype(F32) + other[...].astype(F32)).astype(BF)


def pack(*refs):
    for k, value in enumerate(refs[:-1]):
        refs[-1][k] = value[...]


def stacked(refs):
    return jnp.concatenate([r[...] for r in refs], 0)


def by_owner(out, grads, begin):
    columns, lines, unused = out.shape
    size = lines // 4
    for c in range(columns):
        some = [grads[(r * columns + c) * size : (r * columns + c + 1) * size] for r in range(4)]
        out[c, :, begin : begin + grads.shape[1]] = jnp.concatenate(some, 0).astype(BF)


def out_grads(*refs):
    lefts, rights, normed, logits, gains, out = (
        refs[:4], refs[4:12], refs[12:14], refs[14:16], refs[16:18], refs[18],
    )
    share = out.shape[2] - LANES
    left = jnp.concatenate([one[k] for one in lefts for k in (2, 3)], 0)
    right = jnp.concatenate([r[:, r.shape[1] - share :] for r in rights], 0)
    by_owner(out, dot(left, right, (0, 0)), 0)
    width = left.shape[1]
    line = lax.broadcasted_iota(jnp.int32, (LANES, width), 0)
    sums = jnp.where(line == LANES - 1, gains[0][:1, :] + gains[1][:1, :], 0.0)
    by_owner(out, dot(stacked(normed), stacked(logits), (0, 0)) + sums.T, share)


def qkv_grads(*refs):
    lefts, rights, out = refs[:4], refs[4:12], refs[12]
    left = jnp.concatenate([one[k] for one in lefts for k in (0, 1)], 0)
    by_owner(out, dot(left, stacked(rights), (0, 0)), 0)


def fold(row, first, second, out0, out1, out2, out3, total):
    share = first.shape[2]
    total[:, :share] = jnp.sum(first[...].astype(F32), 0)
    total[:, share:] = jnp.sum(second[...].astype(F32), 0)
    for s, out in enumerate((out0, out1, out2, out3)):
        size = out.shape[0]
        out[...] = total[pl.ds(pl.multiple_of((row[0] ^ s) * size, 8), size), :]
        sent(out)


def finish(
    row, in0, in1, in2, in3, w_query, w_key, w_value, gain, o_grad, q_grad, k_grad, v_grad, r_grad,
    first, second, total,
):
    share = o_grad.shape[1] // 4
    piece = total.shape[1] // 4
    ins = (in0, in1, in2, in3)
    for s, one in enumerate(ins):
        where = row[0] ^ s
        o_grad[:, pl.ds(pl.multiple_of(where * share, LANES), share)] = one[:, :share]
        total[:, pl.ds(pl.multiple_of(where * piece, LANES), piece)] = one[:, share + LANES :]
    rest = sum(one[:, share : share + LANES] for one in ins)
    r_grad[...] = rest[:, : r_grad.shape[1]]
    second[...] = rest.T[LANES - 1 :, :]
    begin, inner = 0, jnp.zeros((total.shape[0], 1), F32)
    for out, weight in ((q_grad, w_query), (k_grad, w_key), (v_grad, w_value)):
        part = total[:, begin : begin + out.shape[1]]
        out[...] = part
        inner = inner + jnp.sum(part * weight[...].astype(F32), -1, keepdims=True)
        begin += out.shape[1]
    line = jnp.broadcast_to(inner, (total.shape[0], LANES)).T[:1, :]
    first[...] = line / gain[...].astype(F32)


def over_columns(value):
    return lax.all_to_all(value, "col", split_axis=0, concat_axis=0, tiled=True)


def on_device(
    inputs, cotangent, segment_ids, routes, attn_gain, w_query, w_key, w_value, w_out, ffn_gain,
    w_router, w_gate, w_up, w_down,
):
    section = lax.axis_index("section")
    row = lax.axis_index("row")
    rows = lax.axis_size("row")
    columns = lax.axis_size("col")
    micro, tokens, width = inputs.shape[0], inputs.shape[2], inputs.shape[3]
    experts = w_router.shape[2]
    per_column = w_gate.shape[1]
    hidden_width = w_gate.shape[2] * rows
    kv_width = w_key.shape[2]
    qkv_width = width + 2 * kv_width
    slots = experts * ROOMS
    share = width // rows
    shard = width // (rows * columns)
    heads = width // HEAD_DIM
    kv_heads = kv_width // HEAD_DIM
    length = rows * tokens
    pieces = range(micro)
    steps = range(rows)
    here = row.astype(jnp.int32)[None]
    second = (section == 1).astype(jnp.int32)[None]
    block = (columns, slots // columns, width)

    dense = jnp.concatenate(
        [w_query[0], w_key[0], w_value[0], w_router[0], attn_gain[0][:, None], ffn_gain[0][:, None],
         jnp.zeros((shard, LANES - experts - 2), BF), w_out[0]], 1
    )
    dense = lax.all_gather(dense, ("row", "col"), axis=0, tiled=True)
    small = dense[:, qkv_width : qkv_width + LANES]
    gain_a = small[:, experts].astype(F32)[None, :]
    gain_f = small[:, experts + 1].astype(F32)[None, :]

    def shards_of(own):
        two = swapped(own, 2)
        return own, swapped(own, 1), two, swapped(two, 1)

    gate_shards, up_shards = shards_of(w_gate[0]), shards_of(w_up[0])
    down_one, down_first = swapped(w_down[0], 1), swapped(w_down[0, :1], 2)

    def all_shards(waits):
        twos = [down_first]
        twos += [swapped(hold(w_down[0, j : j + 1], *waits), 2) for j in range(1, per_column)]
        threes = [swapped(two, 1) for two in twos]
        return (*gate_shards, *up_shards, w_down[0], down_one, *twos, *threes)


    lane = jnp.arange(LANES, dtype=jnp.int32)
    half = HEAD_DIM // 2
    freqs = 10000.0 ** (-2.0 * jnp.arange(half).astype(F32) / HEAD_DIM)
    positions = row * tokens + jnp.arange(tokens, dtype=jnp.int32)
    angles = positions.astype(F32)[:, None] * freqs[None, :]
    cosine = jnp.concatenate([jnp.cos(angles)] * 2, 1)
    sine = jnp.concatenate([-jnp.sin(angles), jnp.sin(angles)], 1)
    key_positions = jnp.concatenate(
        [(row ^ step) * tokens + jnp.arange(tokens, dtype=jnp.int32) for step in steps]
    )
    spread = (lane[:, None] == jnp.arange(slots, dtype=jnp.int32)[None, :] // ROOMS).astype(BF)
    below = (jnp.arange(tokens)[:, None] > jnp.arange(tokens)[None, :]).astype(BF)
    biases, chosens, places, dispatches = [], [], [], []
    for m in pieces:
        segments = segment_ids[m, 0]
        own_segments = lax.dynamic_slice_in_dim(segments, row * tokens, tokens)
        key_segments = jnp.concatenate(
            [lax.dynamic_slice_in_dim(segments, (row ^ s) * tokens, tokens) for s in steps]
        )
        counted = (key_positions[None, :] <= positions[:, None]) & (
            key_segments[None, :] == own_segments[:, None]
        )
        biases.append(jnp.where(counted, 0.0, -1e30).astype(F32))
        chosen = jnp.any(routes[0, m, 0][:, :, None] == lane[None, None, :], 1)
        chosens.append(chosen.astype(F32))
        rank = dot(below, chosen.astype(BF))
        rank = jnp.where(chosen, rank, -1.0)[:, :experts]
        place = (
            rank[:, :, None] == jnp.arange(ROOMS, dtype=F32)[None, None, :]
        ).reshape(tokens, slots)
        places.append(place.astype(BF))
        dispatches.append(place.T.astype(BF))

    token_low, token_wide = like((tokens, width), BF), like((tokens, width), F32)
    pair_like = like((tokens, 2 * kv_width), BF)
    block_like = like(block, BF)
    sums_like = like((8, width), F32)
    kept_like = like((per_column, columns * ROOMS, hidden_width), BF)
    probs_like = like((kv_heads, heads // kv_heads * tokens, length), BF)
    qkv_scratch = [pltpu.VMEM((width, qkv_width), BF), pltpu.SemaphoreType.DMA((8,))]
    out_scratch = [
        pltpu.VMEM((width, width), BF), pltpu.VMEM((width, LANES), BF),
        pltpu.SemaphoreType.DMA((2,)),
    ]
    expert_scratch = [
        pltpu.VMEM((3, per_column, hidden_width, width), BF),
        pltpu.SemaphoreType.DMA((3, per_column, 4)),
    ]
    qkv_flops = 2 * tokens * width * qkv_width
    out_flops = 2 * tokens * width * width + 2 * slots * tokens * width
    score_flops = 2 * heads * tokens * length * HEAD_DIM
    expert_flops = 2 * slots * hidden_width * width

    per = slots // columns
    back_like = like((columns, per, width + LANES), BF)
    lanes_like = like((tokens, LANES), F32)
    tables = late([cosine, sine])
    first_flag = (1 - second)

    def forward(keep, came, waits, early, after, shards):
        projected, pairs = [], []
        if keep:
            for m in pieces:
                projected.append(
                    call(
                        project,
                        (Sent(token_wide), Sent(token_low), Sent(token_low), Sent(pair_like)),
                        (Late(came[m]), Late(inputs, (m, 0)), Late(gain_a), *tables), qkv_flops, (dense,),
                        qkv_scratch, (second,), waits=[p[0] for p in projected],
                    )
                )
                pairs.append([projected[m][3]] + [swapped(projected[m][3], s) for s in steps[1:]])
        else:
            made = call(
                functools.partial(project_all, experts),
                (Sent(token_wide), Sent(token_low), Sent(pair_like)) * micro,
                (Late(inputs), *tables), micro * qkv_flops, (dense,),
                [qkv_scratch[0], pltpu.VMEM((width, LANES), BF), qkv_scratch[1]], waits=waits,
            )
            projected = [(made[3 * m], None, made[3 * m + 1]) for m in pieces]
            for m in pieces:
                pair = made[3 * m + 2]
                pairs.append([pair] + [swapped(pair, s) for s in steps[1:]])
        shards = shards or all_shards(pairs[1][1:])
        attended = [
            call(
                functools.partial(attend, keep),
                (Sent(token_wide), Sent(lanes_like), Sent(back_like if keep else block_like))
                + ((Sent(probs_like), Sent(token_low), Sent(token_low)) if keep else ()),
                (*late([projected[m][0], projected[m][2], *pairs[m], biases[m], gain_f, chosens[m],
                        dispatches[m]]), Late(cotangent, (m, 0))),
                out_flops + 2 * score_flops, (dense,), [pltpu.VMEM((tokens, width), BF)] + out_scratch,
                (second,), () if m else after,
            )
            for m in pieces
        ]
        arrived = [over_columns(a[2]) for a in attended]
        lefts, ready = [], ()
        if keep:
            left = call(
                pack, (Sent(like((2 * micro, tokens, width), BF)),),
                late([p[1] for p in projected] + [a[4] for a in attended]), 0,
            )[0]
            two = swapped(left, 2)
            lefts = [left, swapped(left, 1), two, swapped(two, 1)]
            ready = (two,)
        applied = [
            call(
                functools.partial(expert_forward, keep),
                (Sent(block_like),)
                + ((Sent(kept_like),) * 3 + (Sent(back_like),) if keep else ()),
                late([arrived[m], early[m]] if keep else [arrived[m]]),
                (6 if keep else 3) * expert_flops, shards, expert_scratch,
                waits=ready if m else (attended[1][2],),
            )
            for m in pieces
        ]
        return projected, pairs, attended, arrived, applied, lefts, shards

    def weight_call(quarters, which, lefts, rights, waits):
        quarter, some = hidden_width // 4, len(quarters)
        return call(
            functools.partial(expert_weight_grads, quarters[0] * quarter, which),
            (Sent(like((per_column, quarter, width), BF)),) * (some * len(which)), (),
            len(which) * expert_flops, [*lefts, *rights],
            [pltpu.VMEM((len(which), per_column, 2 * columns * ROOMS, some * quarter), BF),
             pltpu.VMEM((len(rights) // 2, per_column, 2 * columns, ROOMS, width), BF),
             pltpu.SemaphoreType.DMA((2, len(which), per_column, 2))],
            waits=waits,
        )

    def merged(halves, waits):
        pairs = [v for a, b in halves for v in (a, swapped(b, 1))]
        return call(add, [Sent(a) for a, unused in halves], late(pairs), 0, waits=waits)

    def attention_back(keep, m, grad, token_grads, waits):
        return call(
            functools.partial(attend_back, keep),
            (Sent(token_wide), Sent(token_low))
            + (Sent(like((tokens, 2 * kv_width + (share if keep else 0)), BF)),) * rows
            + ((Sent(like((tokens, LANES), BF)), Sent(sums_like)) if keep else ()),
            (*late([token_grads, shared[m] if keep else spread, attended[m][1], places[m],
                                 attended[m][0], gain_f]), Late(*grad),
             *late([projected[m][2], *pairs[m], attended[m][3], cosine, sine])),
            out_flops + 4 * score_flops, (dense,), [pltpu.VMEM((tokens, width), BF)] + out_scratch,
            (here, second), waits,
        )

    def parts_of(inner):
        return [inner[2]] + [swapped(inner[2 + s], s) for s in steps[1:]]

    def projection_back(keep, m, inner, parts, waits):
        return call(
            functools.partial(project_back, keep),
            (Sent(token_low),)
            + ((Sent(token_wide),) + (Sent(like((tokens, qkv_width // rows), BF)),) * rows
               if keep else ()),
            (*late([*parts, inner[1], projected[m][0], gain_a, inner[0]]),
             *tables),
            qkv_flops, (dense,), [pltpu.VMEM((tokens, qkv_width), BF)] + qkv_scratch,
            (here,), waits,
        )

    kept = forward(False, None, (gate_shards[2], up_shards[2], down_first), None, (), ())
    attended, early, applied, unused, shards = kept[2:]
    returned = [over_columns(a[0]) for a in applied]
    results = [
        call(
            combine, (Sent(token_low),),
            late([returned[m], attended[m][0], attended[m][1], spread, places[m]]),
            2 * slots * tokens * width, waits=() if m else (applied[1][0],),
        )
        for m in pieces
    ]
    came = [lax.ppermute(r[0], "section", [(0, 1)]) for r in results]

    kept = forward(True, came, (), early, results[1], shards)
    projected, pairs, attended, arrived, applied, lefts, unused = kept
    hidden = [a[1] for a in applied]
    shared = [over_columns(a[4]) for a in applied]
    inner, outer = [], []
    for m in pieces:
        waits = (*lefts[1:], outer[0][0]) if m else (applied[1][4],)
        inner.append(attention_back(False, m, (cotangent, (m, 0)), shared[m], waits))
        outer.append(projection_back(False, m, inner[m], parts_of(inner[m]), ()))
    came = [lax.ppermute(o[0], "section", [(1, 0)]) for o in outer]

    given = [
        call(
            send_grads, (Sent(token_low), Sent(block_like)),
            (Late(came[m]), Late(cotangent, (m, 0)), *late([attended[m][1], dispatches[m]])),
            2 * slots * tokens * width, scalars=(first_flag,), waits=() if m else (inner[1][0],),
        )
        for m in pieces
    ]
    arrived_grads = [over_columns(g[1]) for g in given]
    moved = [
        call(
            expert_backward, (Sent(back_like), Sent(kept_like), Sent(kept_like)),
            late([arrived_grads[m], hidden[m], applied[m][2], applied[m][3], applied[m][0]]),
            3 * expert_flops, shards, expert_scratch,
            (second,), () if m else (given[1][1],),
        )
        for m in pieces
    ]
    gate_up = [a[1] for a in moved] + [a[2] for a in moved]
    down_far = merged([weight_call((2, 3), ((0, 0),), hidden, arrived_grads, ())], ())[0]
    crossed = [swapped(down_far, 2)]
    back = [over_columns(moved[0][0]), over_columns(moved[1][0])]
    inner = [attention_back(True, 0, given[0][:1], back[0], (moved[1][0], down_far))]
    parts = [parts_of(inner[0])]
    both = weight_call((0, 1, 2, 3), ((0, 0), (0, 0)), gate_up, arrived, (inner[0][0],))
    inner.append(attention_back(True, 1, given[1][:1], back[1], (both[0], crossed[0])))
    parts.append(parts_of(inner[1]))
    sums = merged([both[2:4], both[6:]], (inner[1][0],))
    gate_far = hold(sums[0], *parts[1][1:])
    crossed.append(swapped(gate_far, 2))
    o_grads = call(
        out_grads, (Sent(like((columns, rows * shard, share + LANES), BF)),),
        late([*lefts, *[p[s] for s in steps for p in parts], *[a[5] for a in attended],
              *[a[6] for a in inner], *[a[7] for a in inner]]),
        2 * width * length * micro * share, waits=(crossed[0], gate_far),
    )[0]
    last = projection_back(True, 1, inner[1], parts[1], (o_grads,))
    outer = [projection_back(True, 0, inner[0], parts[0], (last[0],)), last]
    backs = [[o[2]] + [swapped(o[2 + s], s) for s in steps[1:]] for o in outer]
    crossed.append(swapped(hold(sums[1], *backs[0][1:], *backs[1][1:]), 2))
    near = weight_call((0, 1), ((0, 0),), hidden, arrived_grads, (outer[1][0],))
    w_grads = call(
        qkv_grads, (Sent(like((columns, rows * shard, qkv_width // rows), BF)),),
        late([*lefts, *[b[s] for s in steps for b in backs]]),
        2 * width * length * micro * qkv_width // rows, waits=(crossed[1], near[0]),
    )[0]
    expert_grads = [
        one.astype(F32) + swapped(other, 1).astype(F32) + c.astype(F32)
        for one, other, c in zip((near[0], both[0], both[4]), (near[1], both[1], both[5]), crossed)
    ]
    layer_outputs = call(
        last_outputs, (Sent(like((micro, tokens, width), F32)),),
        late([spread] + [v for m in pieces for v in (
            back[m], attended[m][0], attended[m][1], places[m], results[m][0])]),
        4 * slots * tokens * width, scalars=(second,), waits=(w_grads,),
    )[0]

    wide = share + qkv_width // rows + LANES
    pieces_out = call(
        fold, (Sent(like((shard, wide), F32)),) * rows,
        late([over_columns(o_grads), over_columns(w_grads)]), 0,
        scratch=[pltpu.VMEM((rows * shard, wide), F32)], scalars=(here,),
    )
    pieces_out = [pieces_out[0]] + [swapped(pieces_out[s], s) for s in steps[1:]]
    o_grad, q_grad, k_grad, v_grad, r_grad, first, second_sum = call(
        finish,
        (like((shard, width), F32), like((shard, width), F32), like((shard, kv_width), F32),
         like((shard, kv_width), F32), like((shard, experts), F32), like((1, shard), F32),
         like((1, shard), F32)),
        late([*pieces_out, w_query[0], w_key[0], w_value[0], attn_gain]), 0,
        scratch=[pltpu.VMEM((shard, qkv_width), F32)], scalars=(here,),
    )

    return (
        layer_outputs[None, :, None],
        jnp.stack([o[1] for o in outer])[None, :, None],
        first,
        q_grad[None],
        k_grad[None],
        v_grad[None],
        o_grad[None],
        second_sum,
        r_grad[None],
        expert_grads[1][None],
        expert_grads[2][None],
        expert_grads[0][None],
    )


def solution(mesh):
    dense = P("section", ("row", "col"), None)
    gain = P("section", ("row", "col"))
    expert = P("section", "col", "row", None)
    token = P(None, "col", "row", None)
    layered = P("section", None, "col", "row", None)
    return jax.shard_map(
        on_device,
        mesh=mesh,
        in_specs=(
            token, token, P(None, "col", None), layered, gain, dense, dense, dense, dense, gain,
            dense, expert, expert, expert,
        ),
        out_specs=(
            layered, layered, gain, dense, dense, dense, dense, gain, dense, expert, expert, expert,
        ),
        check_vma=False,
    )
```

```python
import functools

import jax
import jax.numpy as jnp
from jax import lax
from jax.experimental import pallas as pl
from jax.experimental.pallas import tpu as pltpu
from jax.sharding import PartitionSpec as P

HEAD_DIM = 128
ROOMS = 16
EPSILON = 1e-06
LANES = 128
BF = jnp.bfloat16
F32 = jnp.float32
MIB = 1 << 20


def dot(left, right, contract=(1, 0)):
    return lax.dot_general(
        left, right, (((contract[0],), (contract[1],)), ((), ())), preferred_element_type=F32
    )


def like(shape, dtype):
    return jax.ShapeDtypeStruct(shape, dtype)


class Late:
    def __init__(self, source, index=None, target=None, sem=None):
        self.source, self.index, self.target, self.copy = source, index, target, None
        if target is not None:
            source = source if index is None else source.at[index]
            self.copy = pltpu.make_async_copy(source, target, sem)
            self.copy.start()
            self.waiting = True

    def ready(self):
        if self.waiting:
            self.copy.wait()
            self.waiting = False
        return self.target

    def __getitem__(self, index):
        return self.ready()[index]

    @property
    def shape(self):
        return self.source.shape[len(self.index or ()) :]


class Sent:
    def __init__(self, source, target=None, sems=None):
        self.source, self.target, self.sems, self.copies = source, target, sems, []

    def __getitem__(self, index):
        return self.source[index]

    def __setitem__(self, index, value):
        self.source[index] = value

    def send(self, *parts):
        for part in parts or (...,):
            at = len(self.copies)
            whole = part is ...
            copy = pltpu.make_async_copy(
                self.source if whole else self.source.at[part],
                self.target if whole else self.target.at[part],
                self.sems.at[at],
            )
            copy.start()
            self.copies.append(copy)

    @property
    def shape(self):
        return self.source.shape


PARTS = 4


def sent(out, *parts):
    if isinstance(out, Sent):
        out.send(*parts)


def call(body, outs, args, flops, far=(), scratch=(), scalars=(), waits=()):
    arrays = [a.source if isinstance(a, Late) else a for a in args]
    shapes = [o.source if isinstance(o, Sent) else o for o in outs]
    moved = sum(a.size * a.dtype.itemsize for a in (*arrays, *far, *shapes))
    count = len(scalars) + len(args) + len(far)
    kinds = [isinstance(a, Late) for a in args]
    out_kinds = [isinstance(o, Sent) for o in outs]
    buffers = [pltpu.VMEM(a.shape, a.source.dtype) for a in args if isinstance(a, Late)]
    buffers += [pltpu.VMEM(o.shape, o.dtype) for o, k in zip(shapes, out_kinds) if k]

    def run(*refs):
        given, refs = list(refs[:count]), refs[count + len(waits) :]
        results, refs = list(refs[: len(outs)]), refs[len(outs) :]
        own, rest = list(refs[: len(buffers)]), refs[len(buffers) :]
        sems, rest = (rest[0], rest[1:]) if buffers else (None, rest)
        used = 0
        for k, kind in enumerate(kinds):
            if kind:
                at = len(scalars) + k
                given[at] = Late(given[at], args[k].index, own[used], sems.at[used, 0])
                used += 1
        for k, kind in enumerate(out_kinds):
            if kind:
                results[k] = Sent(own[used], results[k], sems.at[used])
                used += 1
        body(*given, *results, *rest)
        for one in given:
            if isinstance(one, Late):
                one.ready()
        for one in results:
            if isinstance(one, Sent) and not one.copies:
                one.send()
        for one in results:
            if isinstance(one, Sent):
                done_with(one.copies)

    anywhere, local = pl.BlockSpec(memory_space=pltpu.HBM), pl.BlockSpec(memory_space=pltpu.VMEM)
    return pl.pallas_call(
        run,
        out_shape=tuple(shapes),
        in_specs=[pl.BlockSpec(memory_space=pltpu.SMEM)] * len(scalars)
        + [anywhere if k else local for k in kinds]
        + [anywhere] * (len(far) + len(waits)),
        out_specs=tuple(anywhere if k else local for k in out_kinds),
        scratch_shapes=buffers
        + ([pltpu.SemaphoreType.DMA((len(buffers), PARTS))] if buffers else [])
        + list(scratch),
        compiler_params=pltpu.CompilerParams(vmem_limit_bytes=64 * MIB),
        cost_estimate=pl.CostEstimate(
            flops=int(flops), bytes_accessed=int(moved), transcendentals=0
        ),
        name=body.func.__name__ if isinstance(body, functools.partial) else body.__name__,
    )(*scalars, *arrays, *far, *waits)


def late(values):
    return [Late(v) for v in values]


def nothing(*refs):
    pass


def hold(value, *waits):
    return pl.pallas_call(
        nothing,
        out_shape=like(value.shape, value.dtype),
        in_specs=[pl.BlockSpec(memory_space=pl.ANY)] * (1 + len(waits)),
        out_specs=pl.BlockSpec(memory_space=pl.ANY),
        input_output_aliases={0: 0},
        name="hold",
    )(value, *waits)


def swapped(value, step):
    rows = lax.axis_size("row")
    return lax.ppermute(value, "row", [(r, r ^ step) for r in range(rows)])


def norm_parts(stream):
    return lax.rsqrt(jnp.mean(stream * stream, -1, keepdims=True) + EPSILON)


def norm_back(grad, stream, gain):
    inverse = norm_parts(stream)
    unit = stream * inverse
    scaled = grad * gain
    back = inverse * (scaled - unit * jnp.mean(scaled * unit, -1, keepdims=True))
    return back, jnp.sum(grad * unit, 0, keepdims=True)


def turned(vectors, cosine, sine):
    done = []
    for at in range(0, vectors.shape[1], HEAD_DIM):
        one = vectors[:, at : at + HEAD_DIM]
        done.append(one * cosine + pltpu.roll(one, HEAD_DIM // 2, 1) * sine)
    return jnp.concatenate(done, -1) if len(done) > 1 else done[0]


def stacked_heads(value, first, count):
    return jnp.concatenate(
        [value[:, (first + j) * HEAD_DIM : (first + j + 1) * HEAD_DIM] for j in range(count)], 0
    )


def unstacked_heads(value, count):
    tokens = value.shape[0] // count
    return jnp.concatenate([value[j * tokens : (j + 1) * tokens] for j in range(count)], 1)


def cuts_of(total, most=512):
    return [(at, min(most, total - at)) for at in range(0, total, most)]


def project(
    flag, came, entering, gain, cosine, sine, dense, stream, normed, query, pair, weights, sems
):
    width = stream.shape[1]
    cuts = cuts_of(weights.shape[1])
    copies = [
        pltpu.make_async_copy(
            dense.at[:, pl.ds(at, size)], weights.at[:, pl.ds(at, size)], sems.at[k]
        )
        for k, (at, size) in enumerate(cuts)
    ]
    for copy in copies:
        copy.start()
    x = jnp.where(flag[0] > 0, came[...].astype(F32), entering[...].astype(F32))
    stream[...] = x
    sent(stream)
    low = (x * norm_parts(x) * gain[...]).astype(BF)
    normed[...] = low
    sent(normed)
    keys = pair.shape[1] // 2
    for copy, (at, size) in zip(copies, cuts):
        copy.wait()
        part = dot(low, weights[:, at : at + size])
        for begin in range(at, at + size, HEAD_DIM):
            head = part[:, begin - at : begin - at + HEAD_DIM]
            if begin < width + keys:
                head = turned(head, cosine[...], sine[...])
            head = head.astype(BF)
            if begin < width:
                query[:, begin : begin + HEAD_DIM] = head
            else:
                pair[:, begin - width : begin - width + HEAD_DIM] = head
            if begin + HEAD_DIM == width:
                sent(query)


def project_all(at_gain, entering, cosine, sine, dense, *rest):
    outs, (weights, small, sems) = rest[:-3], rest[-3:]
    micro, unused, tokens, width = entering.shape
    cuts = cuts_of(weights.shape[1])
    block = pltpu.make_async_copy(
        dense.at[:, pl.ds(weights.shape[1], LANES)], small, sems.at[len(cuts)]
    )
    block.start()
    copies = [
        pltpu.make_async_copy(
            dense.at[:, pl.ds(at, size)], weights.at[:, pl.ds(at, size)], sems.at[k]
        )
        for k, (at, size) in enumerate(cuts)
    ]
    for copy in copies:
        copy.start()
    scaled = []
    for m in range(micro):
        x = entering[m, 0].astype(F32)
        outs[3 * m][...] = x
        sent(outs[3 * m])
        scaled.append(x * norm_parts(x))
    block.wait()
    gain = small[...].astype(F32).T[at_gain : at_gain + 1, :]
    lows = [(x * gain).astype(BF) for x in scaled]
    low = jnp.concatenate(lows, 0)
    cosines = jnp.concatenate([cosine[...]] * micro, 0)
    sines = jnp.concatenate([sine[...]] * micro, 0)
    keys = outs[2].shape[1] // 2
    for copy, (at, size) in zip(copies, cuts):
        copy.wait()
        part = dot(low, weights[:, at : at + size])
        for begin in range(at, at + size, HEAD_DIM):
            head = part[:, begin - at : begin - at + HEAD_DIM]
            if begin < width + keys:
                head = turned(head, cosines, sines)
            head = head.astype(BF)
            for m in range(micro):
                out, to = (outs[3 * m + 1], begin) if begin < width else (outs[3 * m + 2], begin - width)
                out[:, to : to + HEAD_DIM] = head[m * tokens : (m + 1) * tokens]
                if begin + HEAD_DIM == width:
                    sent(out)


def slot_experts(slots):
    own = lax.broadcasted_iota(jnp.int32, (slots, LANES), 0) // ROOMS
    return own == lax.broadcasted_iota(jnp.int32, (slots, LANES), 1)


def slot_gates(dispatch, gates):
    here = slot_experts(dispatch.shape[0])
    return jnp.sum(jnp.where(here, dot(dispatch, gates.astype(BF)), 0.0), -1, keepdims=True)


def attend(
    keep, flag, stream, query, pair0, pair1, pair2, pair3, bias, gain, chosen, dispatch, target,
    *rest,
):
    dense, middle, gates, outgoing = rest[:4]
    kept, (mixed, weights, router, sems) = rest[4:-4], rest[-4:]
    width = stream.shape[1]
    at = dense.shape[1] - width - LANES
    copies = [
        pltpu.make_async_copy(dense.at[:, pl.ds(at + LANES, width)], weights, sems.at[0]),
        pltpu.make_async_copy(dense.at[:, pl.ds(at, LANES)], router, sems.at[1]),
    ]
    for copy in copies:
        copy.start()
    tokens = stream.shape[0]
    pairs = stacked((pair0, pair1, pair2, pair3))
    kv_heads = pairs.shape[1] // (2 * HEAD_DIM)
    group = width // HEAD_DIM // kv_heads
    biases = jnp.concatenate([bias[...]] * group, 0)
    for h in range(kv_heads):
        keys = pairs[:, h * HEAD_DIM : (h + 1) * HEAD_DIM]
        values = pairs[:, (kv_heads + h) * HEAD_DIM : (kv_heads + h + 1) * HEAD_DIM]
        queries = stacked_heads(query, h * group, group)
        scores = dot(queries, keys, (1, 1)) * HEAD_DIM ** (-0.5) + biases
        expo = jnp.exp(scores - jnp.max(scores, -1, keepdims=True))
        weight = (expo * (1.0 / jnp.sum(expo, -1, keepdims=True))).astype(BF)
        if keep:
            kept[0][h] = weight
        done = dot(weight, values).astype(BF)
        for j in range(group):
            begin = (h * group + j) * HEAD_DIM
            mixed[:, begin : begin + HEAD_DIM] = done[j * tokens : (j + 1) * tokens]
    if keep:
        kept[1][...] = mixed[...]
        sent(kept[0])
        sent(kept[1])
    copies[0].wait()
    x = stream[...] + dot(mixed[...], weights[...])
    middle[...] = x
    sent(middle)
    low = (x * norm_parts(x) * gain[...]).astype(BF)
    if keep:
        kept[2][...] = low
        sent(kept[2])
    copies[1].wait()
    taken = chosen[...] > 0
    logits = jnp.where(taken, dot(low, router[...]), -1e30)
    expo = jnp.where(taken, jnp.exp(logits - jnp.max(logits, -1, keepdims=True)), 0.0)
    share = expo / jnp.sum(expo, -1, keepdims=True)
    gates[...] = share
    sent(gates)
    slots = dispatch[...]
    per, columns = outgoing.shape[1], outgoing.shape[0]
    if keep:
        outgoing[:, :, :width] = dot(slots, low).astype(BF).reshape(columns, per, width)
        lane = lax.broadcasted_iota(jnp.int32, (slots.shape[0], LANES), 1)
        notes = jnp.where(lane == 0, slot_gates(slots, share), 0.0).astype(BF)
        outgoing[:, :, width:] = notes.reshape(columns, per, LANES)
    else:
        low = jnp.where(flag[0] > 0, target[...], low)
        outgoing[...] = dot(slots, low).astype(BF).reshape(columns, per, width)


def by_expert(refs, experts):
    whole = [[[r.at[j] for j in range(experts)] for r in refs[at : at + 4]] for at in (0, 4)]
    down = [[r.at[j] for j in range(experts)] for r in refs[8:10]]
    for at in (10, 10 + experts):
        down.append([r.at[0] for r in refs[at : at + experts]])
    return [*whole, down]


class Fetched:
    def __init__(self, shards, weights, sems):
        self.weights = weights
        self.copies = {}
        for j in range(weights.shape[1]):
            for k in range(weights.shape[0]):
                self.copies[k, j] = [
                    pltpu.make_async_copy(
                        shards[k][p][j],
                        weights.at[k, j, pl.ds(p * shards[k][p][j].shape[0], shards[k][p][j].shape[0])],
                        sems.at[k, j, p],
                    )
                    for p in range(4)
                ]
        for k in range(weights.shape[0]):
            self.start(k, 0)

    def start(self, k, j):
        for copy in self.copies.get((k, j), ()):
            copy.start()

    def ready(self, k, j):
        done_with(self.copies[k, j])
        self.start(k, j + 1)


def done_with(copies):
    for copy in copies:
        copy.wait()


def rows_of(value, j, begin=0):
    columns, unused, width = value.shape
    at = begin + j * ROOMS
    return value[:, at : at + ROOMS, :].reshape(columns * ROOMS, width)


def put_rows(out, j, rows, inner):
    at, width = j * ROOMS, rows.shape[1]
    out[:, at : at + ROOMS, :width] = rows.reshape(-1, ROOMS, width)
    high = inner.astype(BF).astype(F32)
    lane = lax.broadcasted_iota(jnp.int32, (rows.shape[0], LANES), 1)
    both = jnp.where(lane == 0, high, jnp.where(lane == 1, inner - high, 0.0))
    out[:, at : at + ROOMS, width:] = both.astype(BF).reshape(-1, ROOMS, LANES)


def expert_forward(both, arrived, *refs):
    early, refs = (refs[0], refs[1:]) if both else (None, refs)
    weights, sems = refs[-2:]
    experts = weights.shape[1]
    count = 10 + 2 * experts
    outs = refs[count:-2]
    fetched = Fetched(by_expert(refs, experts), weights, sems)
    width = weights.shape[3]
    for j in range(weights.shape[1]):
        at = j * ROOMS
        noted = rows_of(arrived, j)
        rows = noted[:, :width]
        fetched.ready(0, j)
        gate = dot(rows, weights[0, j], (1, 1))
        fetched.ready(1, j)
        lifted = dot(rows, weights[1, j], (1, 1))
        square = gate * gate
        bend = jnp.tanh(0.7978845608028654 * gate * (1.0 + 0.044715 * square))
        active = 0.5 * gate * (1.0 + bend)
        hidden = (active * lifted).astype(BF)
        fetched.ready(2, j)
        made = dot(hidden, weights[2, j]).astype(BF)
        outs[0][:, at : at + ROOMS, :] = made.reshape(-1, ROOMS, made.shape[1])
        sent(outs[0], (slice(None), pl.ds(at, ROOMS)))
        if both:
            slope = 0.5 * (1.0 + bend) + 0.5 * gate * (1.0 - bend * bend) * (
                0.7978845608028654 * (1.0 + 3 * 0.044715 * square)
            )
            bent = slope * lifted
            outs[1][j] = hidden
            outs[2][j] = active.astype(BF)
            outs[3][j] = bent.astype(BF)
            grads = (rows_of(early, j).astype(F32) * noted[:, width : width + 1].astype(F32)).astype(BF)
            hidden_grads = dot(grads, weights[2, j], (1, 1))
            gate_part = (hidden_grads * bent).astype(BF)
            lifted_part = (hidden_grads * active).astype(BF)
            inner = jnp.sum(hidden_grads * hidden.astype(F32), -1, keepdims=True)
            back = dot(gate_part, weights[0, j]) + dot(lifted_part, weights[1, j])
            put_rows(outs[4], j, back.astype(BF), inner)
            sent(outs[4], (slice(None), pl.ds(at, ROOMS)))
            for out in outs[1:4]:
                sent(out, j)


def combine(returned, middle, gates, spread, places, low):
    weights = (dot(gates[...].astype(BF), spread[...]) * places[...].astype(F32)).astype(BF)
    done = middle[...] + dot(weights, returned[...].reshape(-1, returned.shape[2]))
    low[...] = done.astype(BF)


def last_outputs(flag, spread, *refs):
    out = refs[-1]
    width = out.shape[2]
    for m in range(out.shape[0]):
        returned, middle, gates, places, before = refs[5 * m : 5 * m + 5]
        weights = (dot(gates[...].astype(BF), spread[...]) * places[...].astype(F32)).astype(BF)
        rows = returned[:, :, :width].reshape(-1, width)
        out[m] = jnp.where(flag[0] > 0, middle[...] + dot(weights, rows), before[...].astype(F32))


def send_grads(flag, came, target, gates, dispatch, grad, outgoing):
    low = jnp.where(flag[0] > 0, came[...], target[...])
    grad[...] = low
    sent(grad)
    slots = dispatch[...]
    rows = dot(slots, low) * slot_gates(slots, gates[...])
    outgoing[...] = rows.astype(BF).reshape(outgoing.shape)


def expert_backward(flag, arrived, hidden, active, bent, produced, *refs):
    out, gate_back, lifted_back, weights, sems = refs[-5:]
    gate_shards, up_shards, down_shards = by_expert(refs, weights.shape[1])
    fetched = Fetched([down_shards, gate_shards, up_shards], weights, sems)
    for j in range(weights.shape[1]):
        fetched.ready(0, j)
        hidden_grads = dot(rows_of(arrived, j), weights[0, j], (1, 1))
        gate_part = (hidden_grads * bent[j].astype(F32)).astype(BF)
        lifted_part = (hidden_grads * active[j].astype(F32)).astype(BF)
        gate_back[j] = gate_part
        lifted_back[j] = lifted_part
        inner = jnp.sum(hidden_grads * hidden[j].astype(F32), -1, keepdims=True)
        fetched.ready(1, j)
        done = dot(gate_part, weights[1, j])
        fetched.ready(2, j)
        done = (done + dot(lifted_part, weights[2, j])).astype(BF)
        put_rows(out, j, jnp.where(flag[0] > 0, rows_of(produced, j), done), inner)
        sent(out, (slice(None), pl.ds(j * ROOMS, ROOMS)))
        sent(gate_back, j)
        sent(lifted_back, j)


def attend_back(
    keep, row, flag, token_grads, before, gates, places, middle, gain, grad, query, pair0, pair1,
    pair2, pair3, probs, cosine, sine, dense, middle_grads, query_back, part0, part1, part2, part3,
    *rest,
):
    tokens, width = middle.shape
    kept, (branch, weights, router, sems) = rest[:-4], rest[-4:]
    at = dense.shape[1] - width - LANES
    copies = [
        pltpu.make_async_copy(dense.at[:, pl.ds(at, LANES)], router, sems.at[1]),
        pltpu.make_async_copy(dense.at[:, pl.ds(at + LANES, width)], weights, sems.at[0]),
    ]
    for copy in copies:
        copy.start()
    came = token_grads[...]
    if keep:
        came = jnp.where(flag[0] > 0, before[...], came)
    came = came.reshape(-1, came.shape[2])
    place = places[...]
    here = slot_experts(came.shape[0])
    notes = came[:, width:].astype(F32)
    high = jnp.where(here, notes[:, :1], 0.0).astype(BF)
    rest_of = jnp.where(here, notes[:, 1:2], 0.0).astype(BF)
    inner = dot(place, high) + dot(place, rest_of)
    logit_grads = (inner - gates[...] * jnp.sum(inner, -1, keepdims=True)).astype(BF)
    ffn_grads = dot(place, came[:, :width])
    copies[0].wait()
    ffn_grads = ffn_grads + dot(logit_grads, router[...], (1, 1))
    part, total = norm_back(ffn_grads, middle[...], gain[...])
    above = grad[...].astype(F32) + part
    middle_grads[...] = above
    sent(middle_grads)
    low = above.astype(BF)
    if keep:
        kept[0][...] = logit_grads
        kept[1][...] = jnp.broadcast_to(total, kept[1].shape)
        sent(kept[0])
        sent(kept[1])
        branch[...] = low
        share = width // 4
        for s, part in enumerate((part0, part1, part2, part3)):
            begin = pl.multiple_of((row[0] ^ s) * share, LANES)
            part[:, part.shape[1] - share :] = branch[:, pl.ds(begin, share)]
    copies[1].wait()
    mixed_grads = dot(low, weights[...], (1, 1)).astype(BF)
    pairs = stacked((pair0, pair1, pair2, pair3))
    kv_heads = pairs.shape[1] // (2 * HEAD_DIM)
    group = width // HEAD_DIM // kv_heads
    scale = HEAD_DIM ** (-0.5)
    parts = (part0, part1, part2, part3)
    for h in range(kv_heads):
        keys = pairs[:, h * HEAD_DIM : (h + 1) * HEAD_DIM]
        values = pairs[:, (kv_heads + h) * HEAD_DIM : (kv_heads + h + 1) * HEAD_DIM]
        queries = stacked_heads(query, h * group, group)
        top = stacked_heads(mixed_grads, h * group, group)
        weight = probs[h]
        wide = weight.astype(F32)
        weight_grads = dot(top, values, (1, 1))
        value_grads = dot(weight, top, (0, 0)).astype(BF)
        inner = wide * weight_grads
        score_grads = (inner - wide * jnp.sum(inner, -1, keepdims=True)).astype(BF)
        query_grads = dot(score_grads, keys) * scale
        key_grads = (dot(score_grads, queries, (0, 0)) * scale).astype(BF)
        for j in range(group):
            begin = (h * group + j) * HEAD_DIM
            one = query_grads[j * tokens : (j + 1) * tokens]
            query_back[:, begin : begin + HEAD_DIM] = turned(one, cosine[...], -sine[...]).astype(BF)
        for p, part in enumerate(parts):
            part[:, h * HEAD_DIM : (h + 1) * HEAD_DIM] = key_grads[p * tokens : (p + 1) * tokens]
            begin = (kv_heads + h) * HEAD_DIM
            part[:, begin : begin + HEAD_DIM] = value_grads[p * tokens : (p + 1) * tokens]


def project_back(
    keep, row, part0, part1, part2, part3, query_back, stream, gain, middle_grads, cosine, sine,
    dense, low, *rest,
):
    width = stream.shape[1]
    kept, (backs, weights, sems) = rest[:-3], rest[-3:]
    cuts = cuts_of(weights.shape[1])
    copies = [
        pltpu.make_async_copy(
            dense.at[:, pl.ds(at, size)], weights.at[:, pl.ds(at, size)], sems.at[k]
        )
        for k, (at, size) in enumerate(cuts)
    ]
    for copy in copies:
        copy.start()
    pairs = weights.shape[1] - width
    total = sum(part[:, :pairs].astype(F32) for part in (part0, part1, part2, part3))
    keys = pairs // 2
    backs[:, :width] = query_back[...]
    backs[:, width : width + keys] = turned(total[:, :keys], cosine[...], -sine[...]).astype(BF)
    backs[:, width + keys :] = total[:, keys:].astype(BF)
    if keep:
        share = backs.shape[1] // 4
        for s, out in enumerate(kept[1:]):
            out[...] = backs[:, pl.ds(pl.multiple_of((row[0] ^ s) * share, LANES), share)]
            sent(out)
    above = jnp.zeros(stream.shape, F32)
    for copy, (at, size) in zip(copies, cuts):
        copy.wait()
        above = above + dot(backs[:, at : at + size], weights[:, at : at + size], (1, 1))
    part, unused = norm_back(above, stream[...], gain[...])
    done = middle_grads[...] + part
    if keep:
        kept[0][...] = done
    low[...] = done.astype(BF)


def expert_weight_grads(begin_left, which, *refs):
    count = len(which)
    rights = sorted({w for w in which})
    sources, outs = refs[: 2 * count + 2 * len(rights)], refs[2 * count + 2 * len(rights) : -3]
    left, right, sems = refs[-3:]
    experts, deep, wide = left.shape[1:]
    columns, width = right.shape[2] // 2, right.shape[4]
    copies = {}
    for j in range(experts):
        for m in range(2):
            for r, (unused, begin) in enumerate(rights):
                copies["right", r, j, m] = pltpu.make_async_copy(
                    sources[2 * count + 2 * r + m].at[
                        :, pl.ds(begin + j * ROOMS, ROOMS), pl.ds(0, width)
                    ],
                    right.at[r, j, pl.ds(m * columns, columns)],
                    sems.at[1, r, j, m],
                )
            for k in range(count):
                copies["left", k, j, m] = pltpu.make_async_copy(
                    sources[2 * k + m].at[j, :, pl.ds(begin_left, wide)],
                    left.at[k, j, pl.ds(m * (deep // 2), deep // 2)],
                    sems.at[0, k, j, m],
                )
    for copy in copies.values():
        copy.start()
    waiting = dict(copies)

    def there(*name):
        for m in range(2):
            copy = waiting.pop((*name, m), None)
            if copy is not None:
                copy.wait()

    for j in range(experts):
        for k, name in enumerate(which):
            r = rights.index(name)
            there("right", r, j)
            there("left", k, j)
            total = dot(left[k, j], right[r, j].reshape(deep, width), (0, 0))
            some = len(outs) // count
            size = wide // some
            for q, out in enumerate(outs[some * k : some * (k + 1)]):
                out[j] = total[q * size : (q + 1) * size].astype(BF)
                sent(out, j)


def add(*refs):
    count = len(refs) // 3
    for k in range(count):
        one, other, total = refs[2 * k], refs[2 * k + 1], refs[2 * count + k]
        total[...] = (one[...].astype(F32) + other[...].astype(F32)).astype(BF)


def pack(*refs):
    for k, value in enumerate(refs[:-1]):
        refs[-1][k] = value[...]


def stacked(refs):
    return jnp.concatenate([r[...] for r in refs], 0)


def by_owner(out, grads, begin):
    columns, lines, unused = out.shape
    size = lines // 4
    for c in range(columns):
        some = [grads[(r * columns + c) * size : (r * columns + c + 1) * size] for r in range(4)]
        out[c, :, begin : begin + grads.shape[1]] = jnp.concatenate(some, 0).astype(BF)


def out_grads(*refs):
    lefts, rights, normed, logits, gains, out = (
        refs[:4], refs[4:12], refs[12:14], refs[14:16], refs[16:18], refs[18],
    )
    share = out.shape[2] - LANES
    left = jnp.concatenate([one[k] for one in lefts for k in (2, 3)], 0)
    right = jnp.concatenate([r[:, r.shape[1] - share :] for r in rights], 0)
    by_owner(out, dot(left, right, (0, 0)), 0)
    width = left.shape[1]
    line = lax.broadcasted_iota(jnp.int32, (LANES, width), 0)
    sums = jnp.where(line == LANES - 1, gains[0][:1, :] + gains[1][:1, :], 0.0)
    by_owner(out, dot(stacked(normed), stacked(logits), (0, 0)) + sums.T, share)


def qkv_grads(*refs):
    lefts, rights, out = refs[:4], refs[4:12], refs[12]
    left = jnp.concatenate([one[k] for one in lefts for k in (0, 1)], 0)
    by_owner(out, dot(left, stacked(rights), (0, 0)), 0)


def fold(row, first, second, out0, out1, out2, out3, total):
    share = first.shape[2]
    total[:, :share] = jnp.sum(first[...].astype(F32), 0)
    total[:, share:] = jnp.sum(second[...].astype(F32), 0)
    for s, out in enumerate((out0, out1, out2, out3)):
        size = out.shape[0]
        out[...] = total[pl.ds(pl.multiple_of((row[0] ^ s) * size, 8), size), :]
        sent(out)


def finish(
    row, in0, in1, in2, in3, w_query, w_key, w_value, gain, o_grad, q_grad, k_grad, v_grad, r_grad,
    first, second, total,
):
    share = o_grad.shape[1] // 4
    piece = total.shape[1] // 4
    ins = (in0, in1, in2, in3)
    for s, one in enumerate(ins):
        where = row[0] ^ s
        o_grad[:, pl.ds(pl.multiple_of(where * share, LANES), share)] = one[:, :share]
        total[:, pl.ds(pl.multiple_of(where * piece, LANES), piece)] = one[:, share + LANES :]
    rest = sum(one[:, share : share + LANES] for one in ins)
    r_grad[...] = rest[:, : r_grad.shape[1]]
    second[...] = rest.T[LANES - 1 :, :]
    begin, inner = 0, jnp.zeros((total.shape[0], 1), F32)
    for out, weight in ((q_grad, w_query), (k_grad, w_key), (v_grad, w_value)):
        part = total[:, begin : begin + out.shape[1]]
        out[...] = part
        inner = inner + jnp.sum(part * weight[...].astype(F32), -1, keepdims=True)
        begin += out.shape[1]
    line = jnp.broadcast_to(inner, (total.shape[0], LANES)).T[:1, :]
    first[...] = line / gain[...].astype(F32)


def over_columns(value):
    return lax.all_to_all(value, "col", split_axis=0, concat_axis=0, tiled=True)


def on_device(
    inputs, cotangent, segment_ids, routes, attn_gain, w_query, w_key, w_value, w_out, ffn_gain,
    w_router, w_gate, w_up, w_down,
):
    section = lax.axis_index("section")
    row = lax.axis_index("row")
    rows = lax.axis_size("row")
    columns = lax.axis_size("col")
    micro, tokens, width = inputs.shape[0], inputs.shape[2], inputs.shape[3]
    experts = w_router.shape[2]
    per_column = w_gate.shape[1]
    hidden_width = w_gate.shape[2] * rows
    kv_width = w_key.shape[2]
    qkv_width = width + 2 * kv_width
    slots = experts * ROOMS
    share = width // rows
    shard = width // (rows * columns)
    heads = width // HEAD_DIM
    kv_heads = kv_width // HEAD_DIM
    length = rows * tokens
    pieces = range(micro)
    steps = range(rows)
    here = row.astype(jnp.int32)[None]
    second = (section == 1).astype(jnp.int32)[None]
    block = (columns, slots // columns, width)

    dense = jnp.concatenate(
        [w_query[0], w_key[0], w_value[0], w_router[0], attn_gain[0][:, None], ffn_gain[0][:, None],
         jnp.zeros((shard, LANES - experts - 2), BF), w_out[0]], 1
    )
    dense = lax.all_gather(dense, ("row", "col"), axis=0, tiled=True)
    small = dense[:, qkv_width : qkv_width + LANES]
    gain_a = small[:, experts].astype(F32)[None, :]
    gain_f = small[:, experts + 1].astype(F32)[None, :]

    def shards_of(own):
        two = swapped(own, 2)
        return own, swapped(own, 1), two, swapped(two, 1)

    gate_shards, up_shards = shards_of(w_gate[0]), shards_of(w_up[0])
    down_one, down_first = swapped(w_down[0], 1), swapped(w_down[0, :1], 2)

    def all_shards(waits):
        twos = [down_first]
        twos += [swapped(hold(w_down[0, j : j + 1], *waits), 2) for j in range(1, per_column)]
        threes = [swapped(two, 1) for two in twos]
        return (*gate_shards, *up_shards, w_down[0], down_one, *twos, *threes)


    lane = jnp.arange(LANES, dtype=jnp.int32)
    half = HEAD_DIM // 2
    freqs = 10000.0 ** (-2.0 * jnp.arange(half).astype(F32) / HEAD_DIM)
    positions = row * tokens + jnp.arange(tokens, dtype=jnp.int32)
    angles = positions.astype(F32)[:, None] * freqs[None, :]
    cosine = jnp.concatenate([jnp.cos(angles)] * 2, 1)
    sine = jnp.concatenate([-jnp.sin(angles), jnp.sin(angles)], 1)
    key_positions = jnp.concatenate(
        [(row ^ step) * tokens + jnp.arange(tokens, dtype=jnp.int32) for step in steps]
    )
    spread = (lane[:, None] == jnp.arange(slots, dtype=jnp.int32)[None, :] // ROOMS).astype(BF)
    below = (jnp.arange(tokens)[:, None] > jnp.arange(tokens)[None, :]).astype(BF)
    biases, chosens, places, dispatches = [], [], [], []
    for m in pieces:
        segments = segment_ids[m, 0]
        own_segments = lax.dynamic_slice_in_dim(segments, row * tokens, tokens)
        key_segments = jnp.concatenate(
            [lax.dynamic_slice_in_dim(segments, (row ^ s) * tokens, tokens) for s in steps]
        )
        counted = (key_positions[None, :] <= positions[:, None]) & (
            key_segments[None, :] == own_segments[:, None]
        )
        biases.append(jnp.where(counted, 0.0, -1e30).astype(F32))
        chosen = jnp.any(routes[0, m, 0][:, :, None] == lane[None, None, :], 1)
        chosens.append(chosen.astype(F32))
        rank = dot(below, chosen.astype(BF))
        rank = jnp.where(chosen, rank, -1.0)[:, :experts]
        place = (
            rank[:, :, None] == jnp.arange(ROOMS, dtype=F32)[None, None, :]
        ).reshape(tokens, slots)
        places.append(place.astype(BF))
        dispatches.append(place.T.astype(BF))

    token_low, token_wide = like((tokens, width), BF), like((tokens, width), F32)
    pair_like = like((tokens, 2 * kv_width), BF)
    block_like = like(block, BF)
    sums_like = like((8, width), F32)
    kept_like = like((per_column, columns * ROOMS, hidden_width), BF)
    probs_like = like((kv_heads, heads // kv_heads * tokens, length), BF)
    qkv_scratch = [pltpu.VMEM((width, qkv_width), BF), pltpu.SemaphoreType.DMA((8,))]
    out_scratch = [
        pltpu.VMEM((width, width), BF), pltpu.VMEM((width, LANES), BF),
        pltpu.SemaphoreType.DMA((2,)),
    ]
    expert_scratch = [
        pltpu.VMEM((3, per_column, hidden_width, width), BF),
        pltpu.SemaphoreType.DMA((3, per_column, 4)),
    ]
    qkv_flops = 2 * tokens * width * qkv_width
    out_flops = 2 * tokens * width * width + 2 * slots * tokens * width
    score_flops = 2 * heads * tokens * length * HEAD_DIM
    expert_flops = 2 * slots * hidden_width * width

    per = slots // columns
    back_like = like((columns, per, width + LANES), BF)
    lanes_like = like((tokens, LANES), F32)
    tables = late([cosine, sine])
    first_flag = (1 - second)

    def forward(keep, came, waits, early, after, shards):
        projected, pairs = [], []
        if keep:
            for m in pieces:
                projected.append(
                    call(
                        project,
                        (Sent(token_wide), Sent(token_low), Sent(token_low), Sent(pair_like)),
                        (Late(came[m]), Late(inputs, (m, 0)), Late(gain_a), *tables), qkv_flops, (dense,),
                        qkv_scratch, (second,), waits=[p[0] for p in projected],
                    )
                )
                pairs.append([projected[m][3]] + [swapped(projected[m][3], s) for s in steps[1:]])
        else:
            made = call(
                functools.partial(project_all, experts),
                (Sent(token_wide), Sent(token_low), Sent(pair_like)) * micro,
                (Late(inputs), *tables), micro * qkv_flops, (dense,),
                [qkv_scratch[0], pltpu.VMEM((width, LANES), BF), qkv_scratch[1]], waits=waits,
            )
            projected = [(made[3 * m], None, made[3 * m + 1]) for m in pieces]
            for m in pieces:
                pair = made[3 * m + 2]
                pairs.append([pair] + [swapped(pair, s) for s in steps[1:]])
        shards = shards or all_shards(pairs[1][1:])
        attended = [
            call(
                functools.partial(attend, keep),
                (Sent(token_wide), Sent(lanes_like), Sent(back_like if keep else block_like))
                + ((Sent(probs_like), Sent(token_low), Sent(token_low)) if keep else ()),
                (*late([projected[m][0], projected[m][2], *pairs[m], biases[m], gain_f, chosens[m],
                        dispatches[m]]), Late(cotangent, (m, 0))),
                out_flops + 2 * score_flops, (dense,), [pltpu.VMEM((tokens, width), BF)] + out_scratch,
                (second,), () if m else after,
            )
            for m in pieces
        ]
        arrived = [over_columns(a[2]) for a in attended]
        lefts, ready = [], ()
        if keep:
            left = call(
                pack, (Sent(like((2 * micro, tokens, width), BF)),),
                late([p[1] for p in projected] + [a[4] for a in attended]), 0,
            )[0]
            two = swapped(left, 2)
            lefts = [left, swapped(left, 1), two, swapped(two, 1)]
            ready = (two,)
        applied = [
            call(
                functools.partial(expert_forward, keep),
                (Sent(block_like),)
                + ((Sent(kept_like),) * 3 + (Sent(back_like),) if keep else ()),
                late([arrived[m], early[m]] if keep else [arrived[m]]),
                (6 if keep else 3) * expert_flops, shards, expert_scratch,
                waits=ready if m else (attended[1][2],),
            )
            for m in pieces
        ]
        return projected, pairs, attended, arrived, applied, lefts, shards

    def weight_call(quarters, which, lefts, rights, waits):
        quarter, some = hidden_width // 4, len(quarters)
        return call(
            functools.partial(expert_weight_grads, quarters[0] * quarter, which),
            (Sent(like((per_column, quarter, width), BF)),) * (some * len(which)), (),
            len(which) * expert_flops, [*lefts, *rights],
            [pltpu.VMEM((len(which), per_column, 2 * columns * ROOMS, some * quarter), BF),
             pltpu.VMEM((len(rights) // 2, per_column, 2 * columns, ROOMS, width), BF),
             pltpu.SemaphoreType.DMA((2, len(which), per_column, 2))],
            waits=waits,
        )

    def merged(halves, waits):
        pairs = [v for a, b in halves for v in (a, swapped(b, 1))]
        return call(add, [Sent(a) for a, unused in halves], late(pairs), 0, waits=waits)

    def attention_back(keep, m, grad, token_grads, waits):
        return call(
            functools.partial(attend_back, keep),
            (Sent(token_wide), Sent(token_low))
            + (Sent(like((tokens, 2 * kv_width + (share if keep else 0)), BF)),) * rows
            + ((Sent(like((tokens, LANES), BF)), Sent(sums_like)) if keep else ()),
            (*late([token_grads, shared[m] if keep else spread, attended[m][1], places[m],
                                 attended[m][0], gain_f]), Late(*grad),
             *late([projected[m][2], *pairs[m], attended[m][3], cosine, sine])),
            out_flops + 4 * score_flops, (dense,), [pltpu.VMEM((tokens, width), BF)] + out_scratch,
            (here, second), waits,
        )

    def parts_of(inner):
        return [inner[2]] + [swapped(inner[2 + s], s) for s in steps[1:]]

    def projection_back(keep, m, inner, parts, waits):
        return call(
            functools.partial(project_back, keep),
            (Sent(token_low),)
            + ((Sent(token_wide),) + (Sent(like((tokens, qkv_width // rows), BF)),) * rows
               if keep else ()),
            (*late([*parts, inner[1], projected[m][0], gain_a, inner[0]]),
             *tables),
            qkv_flops, (dense,), [pltpu.VMEM((tokens, qkv_width), BF)] + qkv_scratch,
            (here,), waits,
        )

    kept = forward(False, None, (gate_shards[2], up_shards[2], down_first), None, (), ())
    attended, early, applied, unused, shards = kept[2:]
    returned = [over_columns(a[0]) for a in applied]
    results = [
        call(
            combine, (Sent(token_low),),
            late([returned[m], attended[m][0], attended[m][1], spread, places[m]]),
            2 * slots * tokens * width, waits=() if m else (applied[1][0],),
        )
        for m in pieces
    ]
    came = [lax.ppermute(r[0], "section", [(0, 1)]) for r in results]

    kept = forward(True, came, (), early, results[1], shards)
    projected, pairs, attended, arrived, applied, lefts, unused = kept
    hidden = [a[1] for a in applied]
    shared = [over_columns(a[4]) for a in applied]
    inner, outer = [], []
    for m in pieces:
        waits = (*lefts[1:], outer[0][0]) if m else (applied[1][4],)
        inner.append(attention_back(False, m, (cotangent, (m, 0)), shared[m], waits))
        outer.append(projection_back(False, m, inner[m], parts_of(inner[m]), ()))
    came = [lax.ppermute(o[0], "section", [(1, 0)]) for o in outer]

    given = [
        call(
            send_grads, (Sent(token_low), Sent(block_like)),
            (Late(came[m]), Late(cotangent, (m, 0)), *late([attended[m][1], dispatches[m]])),
            2 * slots * tokens * width, scalars=(first_flag,), waits=() if m else (inner[1][0],),
        )
        for m in pieces
    ]
    arrived_grads = [over_columns(g[1]) for g in given]
    moved = [
        call(
            expert_backward, (Sent(back_like), Sent(kept_like), Sent(kept_like)),
            late([arrived_grads[m], hidden[m], applied[m][2], applied[m][3], applied[m][0]]),
            3 * expert_flops, shards, expert_scratch,
            (second,), () if m else (given[1][1],),
        )
        for m in pieces
    ]
    gate_up = [a[1] for a in moved] + [a[2] for a in moved]
    down_far = merged([weight_call((2, 3), ((0, 0),), hidden, arrived_grads, ())], ())[0]
    crossed = [swapped(down_far, 2)]
    back = [over_columns(moved[0][0]), over_columns(moved[1][0])]
    inner = [attention_back(True, 0, given[0][:1], back[0], (moved[1][0], down_far))]
    parts = [parts_of(inner[0])]
    both = weight_call((0, 1, 2, 3), ((0, 0), (0, 0)), gate_up, arrived, (inner[0][0],))
    inner.append(attention_back(True, 1, given[1][:1], back[1], (both[0], crossed[0])))
    parts.append(parts_of(inner[1]))
    sums = merged([both[2:4], both[6:]], (inner[1][0],))
    last = projection_back(True, 1, inner[1], parts[1], ())
    outer = [projection_back(True, 0, inner[0], parts[0], (last[0],)), last]
    backs = [[o[2]] + [swapped(o[2 + s], s) for s in steps[1:]] for o in outer]
    w_grads = call(
        qkv_grads, (Sent(like((columns, rows * shard, qkv_width // rows), BF)),),
        late([*lefts, *[b[s] for s in steps for b in backs]]),
        2 * width * length * micro * qkv_width // rows, waits=(sums[0],),
    )[0]
    crossed += [swapped(hold(one, *backs[0][1:], *backs[1][1:]), 2) for one in sums]
    o_grads = call(
        out_grads, (Sent(like((columns, rows * shard, share + LANES), BF)),),
        late([*lefts, *[p[s] for s in steps for p in parts], *[a[5] for a in attended],
              *[a[6] for a in inner], *[a[7] for a in inner]]),
        2 * width * length * micro * share, waits=(w_grads,),
    )[0]
    near = weight_call((0, 1), ((0, 0),), hidden, arrived_grads, (o_grads,))
    expert_grads = [
        one.astype(F32) + swapped(other, 1).astype(F32) + c.astype(F32)
        for one, other, c in zip((near[0], both[0], both[4]), (near[1], both[1], both[5]), crossed)
    ]
    layer_outputs = call(
        last_outputs, (Sent(like((micro, tokens, width), F32)),),
        late([spread] + [v for m in pieces for v in (
            back[m], attended[m][0], attended[m][1], places[m], results[m][0])]),
        4 * slots * tokens * width, scalars=(second,), waits=(w_grads,),
    )[0]

    wide = share + qkv_width // rows + LANES
    pieces_out = call(
        fold, (Sent(like((shard, wide), F32)),) * rows,
        late([over_columns(o_grads), over_columns(w_grads)]), 0,
        scratch=[pltpu.VMEM((rows * shard, wide), F32)], scalars=(here,),
    )
    pieces_out = [pieces_out[0]] + [swapped(pieces_out[s], s) for s in steps[1:]]
    o_grad, q_grad, k_grad, v_grad, r_grad, first, second_sum = call(
        finish,
        (like((shard, width), F32), like((shard, width), F32), like((shard, kv_width), F32),
         like((shard, kv_width), F32), like((shard, experts), F32), like((1, shard), F32),
         like((1, shard), F32)),
        late([*pieces_out, w_query[0], w_key[0], w_value[0], attn_gain]), 0,
        scratch=[pltpu.VMEM((shard, qkv_width), F32)], scalars=(here,),
    )

    return (
        layer_outputs[None, :, None],
        jnp.stack([o[1] for o in outer])[None, :, None],
        first,
        q_grad[None],
        k_grad[None],
        v_grad[None],
        o_grad[None],
        second_sum,
        r_grad[None],
        expert_grads[1][None],
        expert_grads[2][None],
        expert_grads[0][None],
    )


def solution(mesh):
    dense = P("section", ("row", "col"), None)
    gain = P("section", ("row", "col"))
    expert = P("section", "col", "row", None)
    token = P(None, "col", "row", None)
    layered = P("section", None, "col", "row", None)
    return jax.shard_map(
        on_device,
        mesh=mesh,
        in_specs=(
            token, token, P(None, "col", None), layered, gain, dense, dense, dense, dense, gain,
            dense, expert, expert, expert,
        ),
        out_specs=(
            layered, layered, gain, dense, dense, dense, dense, gain, dense, expert, expert, expert,
        ),
        check_vma=False,
    )
```

```python
import functools

import jax
import jax.numpy as jnp
from jax import lax
from jax.experimental import pallas as pl
from jax.experimental.pallas import tpu as pltpu
from jax.sharding import PartitionSpec as P

HEAD_DIM = 128
ROOMS = 16
EPSILON = 1e-06
LANES = 128
BF = jnp.bfloat16
F32 = jnp.float32
MIB = 1 << 20


def dot(left, right, contract=(1, 0)):
    return lax.dot_general(
        left, right, (((contract[0],), (contract[1],)), ((), ())), preferred_element_type=F32
    )


def like(shape, dtype):
    return jax.ShapeDtypeStruct(shape, dtype)


class Late:
    def __init__(self, source, index=None, target=None, sem=None):
        self.source, self.index, self.target, self.copy = source, index, target, None
        if target is not None:
            source = source if index is None else source.at[index]
            self.copy = pltpu.make_async_copy(source, target, sem)
            self.copy.start()
            self.waiting = True

    def ready(self):
        if self.waiting:
            self.copy.wait()
            self.waiting = False
        return self.target

    def __getitem__(self, index):
        return self.ready()[index]

    @property
    def shape(self):
        return self.source.shape[len(self.index or ()) :]


class Sent:
    def __init__(self, source, target=None, sems=None):
        self.source, self.target, self.sems, self.copies = source, target, sems, []

    def __getitem__(self, index):
        return self.source[index]

    def __setitem__(self, index, value):
        self.source[index] = value

    def send(self, *parts):
        for part in parts or (...,):
            at = len(self.copies)
            whole = part is ...
            copy = pltpu.make_async_copy(
                self.source if whole else self.source.at[part],
                self.target if whole else self.target.at[part],
                self.sems.at[at],
            )
            copy.start()
            self.copies.append(copy)

    @property
    def shape(self):
        return self.source.shape


PARTS = 4


def sent(out, *parts):
    if isinstance(out, Sent):
        out.send(*parts)


def call(body, outs, args, flops, far=(), scratch=(), scalars=(), waits=()):
    arrays = [a.source if isinstance(a, Late) else a for a in args]
    shapes = [o.source if isinstance(o, Sent) else o for o in outs]
    moved = sum(a.size * a.dtype.itemsize for a in (*arrays, *far, *shapes))
    count = len(scalars) + len(args) + len(far)
    kinds = [isinstance(a, Late) for a in args]
    out_kinds = [isinstance(o, Sent) for o in outs]
    buffers = [pltpu.VMEM(a.shape, a.source.dtype) for a in args if isinstance(a, Late)]
    buffers += [pltpu.VMEM(o.shape, o.dtype) for o, k in zip(shapes, out_kinds) if k]

    def run(*refs):
        given, refs = list(refs[:count]), refs[count + len(waits) :]
        results, refs = list(refs[: len(outs)]), refs[len(outs) :]
        own, rest = list(refs[: len(buffers)]), refs[len(buffers) :]
        sems, rest = (rest[0], rest[1:]) if buffers else (None, rest)
        used = 0
        for k, kind in enumerate(kinds):
            if kind:
                at = len(scalars) + k
                given[at] = Late(given[at], args[k].index, own[used], sems.at[used, 0])
                used += 1
        for k, kind in enumerate(out_kinds):
            if kind:
                results[k] = Sent(own[used], results[k], sems.at[used])
                used += 1
        body(*given, *results, *rest)
        for one in given:
            if isinstance(one, Late):
                one.ready()
        for one in results:
            if isinstance(one, Sent) and not one.copies:
                one.send()
        for one in results:
            if isinstance(one, Sent):
                done_with(one.copies)

    anywhere, local = pl.BlockSpec(memory_space=pltpu.HBM), pl.BlockSpec(memory_space=pltpu.VMEM)
    return pl.pallas_call(
        run,
        out_shape=tuple(shapes),
        in_specs=[pl.BlockSpec(memory_space=pltpu.SMEM)] * len(scalars)
        + [anywhere if k else local for k in kinds]
        + [anywhere] * (len(far) + len(waits)),
        out_specs=tuple(anywhere if k else local for k in out_kinds),
        scratch_shapes=buffers
        + ([pltpu.SemaphoreType.DMA((len(buffers), PARTS))] if buffers else [])
        + list(scratch),
        compiler_params=pltpu.CompilerParams(vmem_limit_bytes=64 * MIB),
        cost_estimate=pl.CostEstimate(
            flops=int(flops) // 1000, bytes_accessed=int(moved) // 1000, transcendentals=0
        ),
        name=body.func.__name__ if isinstance(body, functools.partial) else body.__name__,
    )(*scalars, *arrays, *far, *waits)


def late(values):
    return [Late(v) for v in values]


def nothing(*refs):
    pass


def hold(value, *waits):
    return pl.pallas_call(
        nothing,
        out_shape=like(value.shape, value.dtype),
        in_specs=[pl.BlockSpec(memory_space=pl.ANY)] * (1 + len(waits)),
        out_specs=pl.BlockSpec(memory_space=pl.ANY),
        input_output_aliases={0: 0},
        name="hold",
    )(value, *waits)


def swapped(value, step):
    rows = lax.axis_size("row")
    return lax.ppermute(value, "row", [(r, r ^ step) for r in range(rows)])


def norm_parts(stream):
    return lax.rsqrt(jnp.mean(stream * stream, -1, keepdims=True) + EPSILON)


def norm_back(grad, stream, gain):
    inverse = norm_parts(stream)
    unit = stream * inverse
    scaled = grad * gain
    back = inverse * (scaled - unit * jnp.mean(scaled * unit, -1, keepdims=True))
    return back, jnp.sum(grad * unit, 0, keepdims=True)


def turned(vectors, cosine, sine):
    done = []
    for at in range(0, vectors.shape[1], HEAD_DIM):
        one = vectors[:, at : at + HEAD_DIM]
        done.append(one * cosine + pltpu.roll(one, HEAD_DIM // 2, 1) * sine)
    return jnp.concatenate(done, -1) if len(done) > 1 else done[0]


def stacked_heads(value, first, count):
    return jnp.concatenate(
        [value[:, (first + j) * HEAD_DIM : (first + j + 1) * HEAD_DIM] for j in range(count)], 0
    )


def unstacked_heads(value, count):
    tokens = value.shape[0] // count
    return jnp.concatenate([value[j * tokens : (j + 1) * tokens] for j in range(count)], 1)


def cuts_of(total, most=512):
    return [(at, min(most, total - at)) for at in range(0, total, most)]


def project(
    flag, came, entering, gain, cosine, sine, dense, stream, normed, query, pair, weights, sems
):
    width = stream.shape[1]
    cuts = cuts_of(weights.shape[1])
    copies = [
        pltpu.make_async_copy(
            dense.at[:, pl.ds(at, size)], weights.at[:, pl.ds(at, size)], sems.at[k]
        )
        for k, (at, size) in enumerate(cuts)
    ]
    for copy in copies:
        copy.start()
    x = jnp.where(flag[0] > 0, came[...].astype(F32), entering[...].astype(F32))
    stream[...] = x
    sent(stream)
    low = (x * norm_parts(x) * gain[...]).astype(BF)
    normed[...] = low
    sent(normed)
    keys = pair.shape[1] // 2
    for copy, (at, size) in zip(copies, cuts):
        copy.wait()
        part = dot(low, weights[:, at : at + size])
        for begin in range(at, at + size, HEAD_DIM):
            head = part[:, begin - at : begin - at + HEAD_DIM]
            if begin < width + keys:
                head = turned(head, cosine[...], sine[...])
            head = head.astype(BF)
            if begin < width:
                query[:, begin : begin + HEAD_DIM] = head
            else:
                pair[:, begin - width : begin - width + HEAD_DIM] = head
            if begin + HEAD_DIM == width:
                sent(query)


def project_all(at_gain, entering, cosine, sine, dense, *rest):
    outs, (weights, small, sems) = rest[:-3], rest[-3:]
    micro, unused, tokens, width = entering.shape
    cuts = cuts_of(weights.shape[1])
    block = pltpu.make_async_copy(
        dense.at[:, pl.ds(weights.shape[1], LANES)], small, sems.at[len(cuts)]
    )
    block.start()
    copies = [
        pltpu.make_async_copy(
            dense.at[:, pl.ds(at, size)], weights.at[:, pl.ds(at, size)], sems.at[k]
        )
        for k, (at, size) in enumerate(cuts)
    ]
    for copy in copies:
        copy.start()
    scaled = []
    for m in range(micro):
        x = entering[m, 0].astype(F32)
        outs[3 * m][...] = x
        sent(outs[3 * m])
        scaled.append(x * norm_parts(x))
    block.wait()
    gain = small[...].astype(F32).T[at_gain : at_gain + 1, :]
    lows = [(x * gain).astype(BF) for x in scaled]
    low = jnp.concatenate(lows, 0)
    cosines = jnp.concatenate([cosine[...]] * micro, 0)
    sines = jnp.concatenate([sine[...]] * micro, 0)
    keys = outs[2].shape[1] // 2
    for copy, (at, size) in zip(copies, cuts):
        copy.wait()
        part = dot(low, weights[:, at : at + size])
        for begin in range(at, at + size, HEAD_DIM):
            head = part[:, begin - at : begin - at + HEAD_DIM]
            if begin < width + keys:
                head = turned(head, cosines, sines)
            head = head.astype(BF)
            for m in range(micro):
                out, to = (outs[3 * m + 1], begin) if begin < width else (outs[3 * m + 2], begin - width)
                out[:, to : to + HEAD_DIM] = head[m * tokens : (m + 1) * tokens]
                if begin + HEAD_DIM == width:
                    sent(out)


def slot_experts(slots):
    own = lax.broadcasted_iota(jnp.int32, (slots, LANES), 0) // ROOMS
    return own == lax.broadcasted_iota(jnp.int32, (slots, LANES), 1)


def slot_gates(dispatch, gates):
    here = slot_experts(dispatch.shape[0])
    return jnp.sum(jnp.where(here, dot(dispatch, gates.astype(BF)), 0.0), -1, keepdims=True)


def attend(
    keep, flag, stream, query, pair0, pair1, pair2, pair3, bias, gain, chosen, dispatch, target,
    *rest,
):
    dense, middle, gates, outgoing = rest[:4]
    kept, (mixed, weights, router, sems) = rest[4:-4], rest[-4:]
    width = stream.shape[1]
    at = dense.shape[1] - width - LANES
    copies = [
        pltpu.make_async_copy(dense.at[:, pl.ds(at + LANES, width)], weights, sems.at[0]),
        pltpu.make_async_copy(dense.at[:, pl.ds(at, LANES)], router, sems.at[1]),
    ]
    for copy in copies:
        copy.start()
    tokens = stream.shape[0]
    pairs = stacked((pair0, pair1, pair2, pair3))
    kv_heads = pairs.shape[1] // (2 * HEAD_DIM)
    group = width // HEAD_DIM // kv_heads
    biases = jnp.concatenate([bias[...]] * group, 0)
    for h in range(kv_heads):
        keys = pairs[:, h * HEAD_DIM : (h + 1) * HEAD_DIM]
        values = pairs[:, (kv_heads + h) * HEAD_DIM : (kv_heads + h + 1) * HEAD_DIM]
        queries = stacked_heads(query, h * group, group)
        scores = dot(queries, keys, (1, 1)) * HEAD_DIM ** (-0.5) + biases
        expo = jnp.exp(scores - jnp.max(scores, -1, keepdims=True))
        weight = (expo * (1.0 / jnp.sum(expo, -1, keepdims=True))).astype(BF)
        if keep:
            kept[0][h] = weight
        done = dot(weight, values).astype(BF)
        for j in range(group):
            begin = (h * group + j) * HEAD_DIM
            mixed[:, begin : begin + HEAD_DIM] = done[j * tokens : (j + 1) * tokens]
    if keep:
        kept[1][...] = mixed[...]
        sent(kept[0])
        sent(kept[1])
    copies[0].wait()
    x = stream[...] + dot(mixed[...], weights[...])
    middle[...] = x
    sent(middle)
    low = (x * norm_parts(x) * gain[...]).astype(BF)
    if keep:
        kept[2][...] = low
        sent(kept[2])
    copies[1].wait()
    taken = chosen[...] > 0
    logits = jnp.where(taken, dot(low, router[...]), -1e30)
    expo = jnp.where(taken, jnp.exp(logits - jnp.max(logits, -1, keepdims=True)), 0.0)
    share = expo / jnp.sum(expo, -1, keepdims=True)
    gates[...] = share
    sent(gates)
    slots = dispatch[...]
    per, columns = outgoing.shape[1], outgoing.shape[0]
    if keep:
        outgoing[:, :, :width] = dot(slots, low).astype(BF).reshape(columns, per, width)
        lane = lax.broadcasted_iota(jnp.int32, (slots.shape[0], LANES), 1)
        notes = jnp.where(lane == 0, slot_gates(slots, share), 0.0).astype(BF)
        outgoing[:, :, width:] = notes.reshape(columns, per, LANES)
    else:
        low = jnp.where(flag[0] > 0, target[...], low)
        outgoing[...] = dot(slots, low).astype(BF).reshape(columns, per, width)


def by_expert(refs, experts):
    whole = [[[r.at[j] for j in range(experts)] for r in refs[at : at + 4]] for at in (0, 4)]
    down = [[r.at[j] for j in range(experts)] for r in refs[8:10]]
    for at in (10, 10 + experts):
        down.append([r.at[0] for r in refs[at : at + experts]])
    return [*whole, down]


class Fetched:
    def __init__(self, shards, weights, sems):
        self.weights = weights
        self.copies = {}
        for j in range(weights.shape[1]):
            for k in range(weights.shape[0]):
                self.copies[k, j] = [
                    pltpu.make_async_copy(
                        shards[k][p][j],
                        weights.at[k, j, pl.ds(p * shards[k][p][j].shape[0], shards[k][p][j].shape[0])],
                        sems.at[k, j, p],
                    )
                    for p in range(4)
                ]
        for k in range(weights.shape[0]):
            self.start(k, 0)

    def start(self, k, j):
        for copy in self.copies.get((k, j), ()):
            copy.start()

    def ready(self, k, j):
        done_with(self.copies[k, j])
        self.start(k, j + 1)


def done_with(copies):
    for copy in copies:
        copy.wait()


def rows_of(value, j, begin=0):
    columns, unused, width = value.shape
    at = begin + j * ROOMS
    return value[:, at : at + ROOMS, :].reshape(columns * ROOMS, width)


def put_rows(out, j, rows, inner):
    at, width = j * ROOMS, rows.shape[1]
    out[:, at : at + ROOMS, :width] = rows.reshape(-1, ROOMS, width)
    high = inner.astype(BF).astype(F32)
    lane = lax.broadcasted_iota(jnp.int32, (rows.shape[0], LANES), 1)
    both = jnp.where(lane == 0, high, jnp.where(lane == 1, inner - high, 0.0))
    out[:, at : at + ROOMS, width:] = both.astype(BF).reshape(-1, ROOMS, LANES)


def expert_forward(both, arrived, *refs):
    early, refs = (refs[0], refs[1:]) if both else (None, refs)
    weights, sems = refs[-2:]
    experts = weights.shape[1]
    count = 10 + 2 * experts
    outs = refs[count:-2]
    fetched = Fetched(by_expert(refs, experts), weights, sems)
    width = weights.shape[3]
    for j in range(weights.shape[1]):
        at = j * ROOMS
        noted = rows_of(arrived, j)
        rows = noted[:, :width]
        fetched.ready(0, j)
        gate = dot(rows, weights[0, j], (1, 1))
        fetched.ready(1, j)
        lifted = dot(rows, weights[1, j], (1, 1))
        square = gate * gate
        bend = jnp.tanh(0.7978845608028654 * gate * (1.0 + 0.044715 * square))
        active = 0.5 * gate * (1.0 + bend)
        hidden = (active * lifted).astype(BF)
        fetched.ready(2, j)
        made = dot(hidden, weights[2, j]).astype(BF)
        outs[0][:, at : at + ROOMS, :] = made.reshape(-1, ROOMS, made.shape[1])
        sent(outs[0], (slice(None), pl.ds(at, ROOMS)))
        if both:
            slope = 0.5 * (1.0 + bend) + 0.5 * gate * (1.0 - bend * bend) * (
                0.7978845608028654 * (1.0 + 3 * 0.044715 * square)
            )
            bent = slope * lifted
            outs[1][j] = hidden
            outs[2][j] = active.astype(BF)
            outs[3][j] = bent.astype(BF)
            grads = (rows_of(early, j).astype(F32) * noted[:, width : width + 1].astype(F32)).astype(BF)
            hidden_grads = dot(grads, weights[2, j], (1, 1))
            gate_part = (hidden_grads * bent).astype(BF)
            lifted_part = (hidden_grads * active).astype(BF)
            inner = jnp.sum(hidden_grads * hidden.astype(F32), -1, keepdims=True)
            back = dot(gate_part, weights[0, j]) + dot(lifted_part, weights[1, j])
            put_rows(outs[4], j, back.astype(BF), inner)
            sent(outs[4], (slice(None), pl.ds(at, ROOMS)))
            for out in outs[1:4]:
                sent(out, j)


def combine(returned, middle, gates, spread, places, low):
    weights = (dot(gates[...].astype(BF), spread[...]) * places[...].astype(F32)).astype(BF)
    done = middle[...] + dot(weights, returned[...].reshape(-1, returned.shape[2]))
    low[...] = done.astype(BF)


def last_outputs(flag, spread, *refs):
    out = refs[-1]
    width = out.shape[2]
    for m in range(out.shape[0]):
        returned, middle, gates, places, before = refs[5 * m : 5 * m + 5]
        weights = (dot(gates[...].astype(BF), spread[...]) * places[...].astype(F32)).astype(BF)
        rows = returned[:, :, :width].reshape(-1, width)
        out[m] = jnp.where(flag[0] > 0, middle[...] + dot(weights, rows), before[...].astype(F32))


def send_grads(flag, came, target, gates, dispatch, grad, outgoing):
    low = jnp.where(flag[0] > 0, came[...], target[...])
    grad[...] = low
    sent(grad)
    slots = dispatch[...]
    rows = dot(slots, low) * slot_gates(slots, gates[...])
    outgoing[...] = rows.astype(BF).reshape(outgoing.shape)


def expert_backward(flag, arrived, hidden, active, bent, produced, *refs):
    out, gate_back, lifted_back, weights, sems = refs[-5:]
    gate_shards, up_shards, down_shards = by_expert(refs, weights.shape[1])
    fetched = Fetched([down_shards, gate_shards, up_shards], weights, sems)
    for j in range(weights.shape[1]):
        fetched.ready(0, j)
        hidden_grads = dot(rows_of(arrived, j), weights[0, j], (1, 1))
        gate_part = (hidden_grads * bent[j].astype(F32)).astype(BF)
        lifted_part = (hidden_grads * active[j].astype(F32)).astype(BF)
        gate_back[j] = gate_part
        lifted_back[j] = lifted_part
        inner = jnp.sum(hidden_grads * hidden[j].astype(F32), -1, keepdims=True)
        fetched.ready(1, j)
        done = dot(gate_part, weights[1, j])
        fetched.ready(2, j)
        done = (done + dot(lifted_part, weights[2, j])).astype(BF)
        put_rows(out, j, jnp.where(flag[0] > 0, rows_of(produced, j), done), inner)
        sent(out, (slice(None), pl.ds(j * ROOMS, ROOMS)))
        sent(gate_back, j)
        sent(lifted_back, j)


def attend_back(
    keep, row, flag, token_grads, before, gates, places, middle, gain, grad, query, pair0, pair1,
    pair2, pair3, probs, cosine, sine, dense, middle_grads, query_back, part0, part1, part2, part3,
    *rest,
):
    tokens, width = middle.shape
    kept, (branch, weights, router, sems) = rest[:-4], rest[-4:]
    at = dense.shape[1] - width - LANES
    copies = [
        pltpu.make_async_copy(dense.at[:, pl.ds(at, LANES)], router, sems.at[1]),
        pltpu.make_async_copy(dense.at[:, pl.ds(at + LANES, width)], weights, sems.at[0]),
    ]
    for copy in copies:
        copy.start()
    came = token_grads[...]
    if keep:
        came = jnp.where(flag[0] > 0, before[...], came)
    came = came.reshape(-1, came.shape[2])
    place = places[...]
    here = slot_experts(came.shape[0])
    notes = came[:, width:].astype(F32)
    high = jnp.where(here, notes[:, :1], 0.0).astype(BF)
    rest_of = jnp.where(here, notes[:, 1:2], 0.0).astype(BF)
    inner = dot(place, high) + dot(place, rest_of)
    logit_grads = (inner - gates[...] * jnp.sum(inner, -1, keepdims=True)).astype(BF)
    ffn_grads = dot(place, came[:, :width])
    copies[0].wait()
    ffn_grads = ffn_grads + dot(logit_grads, router[...], (1, 1))
    part, total = norm_back(ffn_grads, middle[...], gain[...])
    above = grad[...].astype(F32) + part
    middle_grads[...] = above
    sent(middle_grads)
    low = above.astype(BF)
    if keep:
        kept[0][...] = logit_grads
        kept[1][...] = jnp.broadcast_to(total, kept[1].shape)
        sent(kept[0])
        sent(kept[1])
        branch[...] = low
        share = width // 4
        for s, part in enumerate((part0, part1, part2, part3)):
            begin = pl.multiple_of((row[0] ^ s) * share, LANES)
            part[:, part.shape[1] - share :] = branch[:, pl.ds(begin, share)]
    copies[1].wait()
    mixed_grads = dot(low, weights[...], (1, 1)).astype(BF)
    pairs = stacked((pair0, pair1, pair2, pair3))
    kv_heads = pairs.shape[1] // (2 * HEAD_DIM)
    group = width // HEAD_DIM // kv_heads
    scale = HEAD_DIM ** (-0.5)
    parts = (part0, part1, part2, part3)
    for h in range(kv_heads):
        keys = pairs[:, h * HEAD_DIM : (h + 1) * HEAD_DIM]
        values = pairs[:, (kv_heads + h) * HEAD_DIM : (kv_heads + h + 1) * HEAD_DIM]
        queries = stacked_heads(query, h * group, group)
        top = stacked_heads(mixed_grads, h * group, group)
        weight = probs[h]
        wide = weight.astype(F32)
        weight_grads = dot(top, values, (1, 1))
        value_grads = dot(weight, top, (0, 0)).astype(BF)
        inner = wide * weight_grads
        score_grads = (inner - wide * jnp.sum(inner, -1, keepdims=True)).astype(BF)
        query_grads = dot(score_grads, keys) * scale
        key_grads = (dot(score_grads, queries, (0, 0)) * scale).astype(BF)
        for j in range(group):
            begin = (h * group + j) * HEAD_DIM
            one = query_grads[j * tokens : (j + 1) * tokens]
            query_back[:, begin : begin + HEAD_DIM] = turned(one, cosine[...], -sine[...]).astype(BF)
        for p, part in enumerate(parts):
            part[:, h * HEAD_DIM : (h + 1) * HEAD_DIM] = key_grads[p * tokens : (p + 1) * tokens]
            begin = (kv_heads + h) * HEAD_DIM
            part[:, begin : begin + HEAD_DIM] = value_grads[p * tokens : (p + 1) * tokens]


def project_back(
    keep, row, part0, part1, part2, part3, query_back, stream, gain, middle_grads, cosine, sine,
    dense, low, *rest,
):
    width = stream.shape[1]
    kept, (backs, weights, sems) = rest[:-3], rest[-3:]
    cuts = cuts_of(weights.shape[1])
    copies = [
        pltpu.make_async_copy(
            dense.at[:, pl.ds(at, size)], weights.at[:, pl.ds(at, size)], sems.at[k]
        )
        for k, (at, size) in enumerate(cuts)
    ]
    for copy in copies:
        copy.start()
    pairs = weights.shape[1] - width
    total = sum(part[:, :pairs].astype(F32) for part in (part0, part1, part2, part3))
    keys = pairs // 2
    backs[:, :width] = query_back[...]
    backs[:, width : width + keys] = turned(total[:, :keys], cosine[...], -sine[...]).astype(BF)
    backs[:, width + keys :] = total[:, keys:].astype(BF)
    if keep:
        share = backs.shape[1] // 4
        for s, out in enumerate(kept[1:]):
            out[...] = backs[:, pl.ds(pl.multiple_of((row[0] ^ s) * share, LANES), share)]
            sent(out)
    above = jnp.zeros(stream.shape, F32)
    for copy, (at, size) in zip(copies, cuts):
        copy.wait()
        above = above + dot(backs[:, at : at + size], weights[:, at : at + size], (1, 1))
    part, unused = norm_back(above, stream[...], gain[...])
    done = middle_grads[...] + part
    if keep:
        kept[0][...] = done
    low[...] = done.astype(BF)


def expert_weight_grads(begin_left, which, *refs):
    count = len(which)
    rights = sorted({w for w in which})
    sources, outs = refs[: 2 * count + 2 * len(rights)], refs[2 * count + 2 * len(rights) : -3]
    left, right, sems = refs[-3:]
    experts, deep, wide = left.shape[1:]
    columns, width = right.shape[2] // 2, right.shape[4]
    copies = {}
    for j in range(experts):
        for m in range(2):
            for r, (unused, begin) in enumerate(rights):
                copies["right", r, j, m] = pltpu.make_async_copy(
                    sources[2 * count + 2 * r + m].at[
                        :, pl.ds(begin + j * ROOMS, ROOMS), pl.ds(0, width)
                    ],
                    right.at[r, j, pl.ds(m * columns, columns)],
                    sems.at[1, r, j, m],
                )
            for k in range(count):
                copies["left", k, j, m] = pltpu.make_async_copy(
                    sources[2 * k + m].at[j, :, pl.ds(begin_left, wide)],
                    left.at[k, j, pl.ds(m * (deep // 2), deep // 2)],
                    sems.at[0, k, j, m],
                )
    for copy in copies.values():
        copy.start()
    waiting = dict(copies)

    def there(*name):
        for m in range(2):
            copy = waiting.pop((*name, m), None)
            if copy is not None:
                copy.wait()

    for j in range(experts):
        for k, name in enumerate(which):
            r = rights.index(name)
            there("right", r, j)
            there("left", k, j)
            total = dot(left[k, j], right[r, j].reshape(deep, width), (0, 0))
            some = len(outs) // count
            size = wide // some
            for q, out in enumerate(outs[some * k : some * (k + 1)]):
                out[j] = total[q * size : (q + 1) * size].astype(BF)
                sent(out, j)


def add(*refs):
    count = len(refs) // 3
    for k in range(count):
        one, other, total = refs[2 * k], refs[2 * k + 1], refs[2 * count + k]
        total[...] = (one[...].astype(F32) + other[...].astype(F32)).astype(BF)


def pack(*refs):
    for k, value in enumerate(refs[:-1]):
        refs[-1][k] = value[...]


def stacked(refs):
    return jnp.concatenate([r[...] for r in refs], 0)


def by_owner(out, grads, begin):
    columns, lines, unused = out.shape
    size = lines // 4
    for c in range(columns):
        some = [grads[(r * columns + c) * size : (r * columns + c + 1) * size] for r in range(4)]
        out[c, :, begin : begin + grads.shape[1]] = jnp.concatenate(some, 0).astype(BF)


def out_grads(*refs):
    lefts, rights, normed, logits, gains, out = (
        refs[:4], refs[4:12], refs[12:14], refs[14:16], refs[16:18], refs[18],
    )
    share = out.shape[2] - LANES
    left = jnp.concatenate([one[k] for one in lefts for k in (2, 3)], 0)
    right = jnp.concatenate([r[:, r.shape[1] - share :] for r in rights], 0)
    by_owner(out, dot(left, right, (0, 0)), 0)
    width = left.shape[1]
    line = lax.broadcasted_iota(jnp.int32, (LANES, width), 0)
    sums = jnp.where(line == LANES - 1, gains[0][:1, :] + gains[1][:1, :], 0.0)
    by_owner(out, dot(stacked(normed), stacked(logits), (0, 0)) + sums.T, share)


def qkv_grads(*refs):
    lefts, rights, out = refs[:4], refs[4:12], refs[12]
    left = jnp.concatenate([one[k] for one in lefts for k in (0, 1)], 0)
    by_owner(out, dot(left, stacked(rights), (0, 0)), 0)


def fold(row, first, second, out0, out1, out2, out3, total):
    share = first.shape[2]
    total[:, :share] = jnp.sum(first[...].astype(F32), 0)
    total[:, share:] = jnp.sum(second[...].astype(F32), 0)
    for s, out in enumerate((out0, out1, out2, out3)):
        size = out.shape[0]
        out[...] = total[pl.ds(pl.multiple_of((row[0] ^ s) * size, 8), size), :]
        sent(out)


def finish(
    row, in0, in1, in2, in3, w_query, w_key, w_value, gain, o_grad, q_grad, k_grad, v_grad, r_grad,
    first, second, total,
):
    share = o_grad.shape[1] // 4
    piece = total.shape[1] // 4
    ins = (in0, in1, in2, in3)
    for s, one in enumerate(ins):
        where = row[0] ^ s
        o_grad[:, pl.ds(pl.multiple_of(where * share, LANES), share)] = one[:, :share]
        total[:, pl.ds(pl.multiple_of(where * piece, LANES), piece)] = one[:, share + LANES :]
    rest = sum(one[:, share : share + LANES] for one in ins)
    r_grad[...] = rest[:, : r_grad.shape[1]]
    second[...] = rest.T[LANES - 1 :, :]
    begin, inner = 0, jnp.zeros((total.shape[0], 1), F32)
    for out, weight in ((q_grad, w_query), (k_grad, w_key), (v_grad, w_value)):
        part = total[:, begin : begin + out.shape[1]]
        out[...] = part
        inner = inner + jnp.sum(part * weight[...].astype(F32), -1, keepdims=True)
        begin += out.shape[1]
    line = jnp.broadcast_to(inner, (total.shape[0], LANES)).T[:1, :]
    first[...] = line / gain[...].astype(F32)


def over_columns(value):
    return lax.all_to_all(value, "col", split_axis=0, concat_axis=0, tiled=True)


def on_device(
    inputs, cotangent, segment_ids, routes, attn_gain, w_query, w_key, w_value, w_out, ffn_gain,
    w_router, w_gate, w_up, w_down,
):
    section = lax.axis_index("section")
    row = lax.axis_index("row")
    rows = lax.axis_size("row")
    columns = lax.axis_size("col")
    micro, tokens, width = inputs.shape[0], inputs.shape[2], inputs.shape[3]
    experts = w_router.shape[2]
    per_column = w_gate.shape[1]
    hidden_width = w_gate.shape[2] * rows
    kv_width = w_key.shape[2]
    qkv_width = width + 2 * kv_width
    slots = experts * ROOMS
    share = width // rows
    shard = width // (rows * columns)
    heads = width // HEAD_DIM
    kv_heads = kv_width // HEAD_DIM
    length = rows * tokens
    pieces = range(micro)
    steps = range(rows)
    here = row.astype(jnp.int32)[None]
    second = (section == 1).astype(jnp.int32)[None]
    block = (columns, slots // columns, width)

    dense = jnp.concatenate(
        [w_query[0], w_key[0], w_value[0], w_router[0], attn_gain[0][:, None], ffn_gain[0][:, None],
         jnp.zeros((shard, LANES - experts - 2), BF), w_out[0]], 1
    )
    dense = lax.all_gather(dense, ("row", "col"), axis=0, tiled=True)
    small = dense[:, qkv_width : qkv_width + LANES]
    gain_a = small[:, experts].astype(F32)[None, :]
    gain_f = small[:, experts + 1].astype(F32)[None, :]

    def shards_of(own):
        two = swapped(own, 2)
        return own, swapped(own, 1), two, swapped(two, 1)

    gate_shards, up_shards = shards_of(w_gate[0]), shards_of(w_up[0])
    down_one, down_first = swapped(w_down[0], 1), swapped(w_down[0, :1], 2)

    def all_shards(waits):
        twos = [down_first]
        twos += [swapped(hold(w_down[0, j : j + 1], *waits), 2) for j in range(1, per_column)]
        threes = [swapped(two, 1) for two in twos]
        return (*gate_shards, *up_shards, w_down[0], down_one, *twos, *threes)


    lane = jnp.arange(LANES, dtype=jnp.int32)
    half = HEAD_DIM // 2
    freqs = 10000.0 ** (-2.0 * jnp.arange(half).astype(F32) / HEAD_DIM)
    positions = row * tokens + jnp.arange(tokens, dtype=jnp.int32)
    angles = positions.astype(F32)[:, None] * freqs[None, :]
    cosine = jnp.concatenate([jnp.cos(angles)] * 2, 1)
    sine = jnp.concatenate([-jnp.sin(angles), jnp.sin(angles)], 1)
    key_positions = jnp.concatenate(
        [(row ^ step) * tokens + jnp.arange(tokens, dtype=jnp.int32) for step in steps]
    )
    spread = (lane[:, None] == jnp.arange(slots, dtype=jnp.int32)[None, :] // ROOMS).astype(BF)
    below = (jnp.arange(tokens)[:, None] > jnp.arange(tokens)[None, :]).astype(BF)
    biases, chosens, places, dispatches = [], [], [], []
    for m in pieces:
        segments = segment_ids[m, 0]
        own_segments = lax.dynamic_slice_in_dim(segments, row * tokens, tokens)
        key_segments = jnp.concatenate(
            [lax.dynamic_slice_in_dim(segments, (row ^ s) * tokens, tokens) for s in steps]
        )
        counted = (key_positions[None, :] <= positions[:, None]) & (
            key_segments[None, :] == own_segments[:, None]
        )
        biases.append(jnp.where(counted, 0.0, -1e30).astype(F32))
        chosen = jnp.any(routes[0, m, 0][:, :, None] == lane[None, None, :], 1)
        chosens.append(chosen.astype(F32))
        rank = dot(below, chosen.astype(BF))
        rank = jnp.where(chosen, rank, -1.0)[:, :experts]
        place = (
            rank[:, :, None] == jnp.arange(ROOMS, dtype=F32)[None, None, :]
        ).reshape(tokens, slots)
        places.append(place.astype(BF))
        dispatches.append(place.T.astype(BF))

    token_low, token_wide = like((tokens, width), BF), like((tokens, width), F32)
    pair_like = like((tokens, 2 * kv_width), BF)
    block_like = like(block, BF)
    sums_like = like((8, width), F32)
    kept_like = like((per_column, columns * ROOMS, hidden_width), BF)
    probs_like = like((kv_heads, heads // kv_heads * tokens, length), BF)
    qkv_scratch = [pltpu.VMEM((width, qkv_width), BF), pltpu.SemaphoreType.DMA((8,))]
    out_scratch = [
        pltpu.VMEM((width, width), BF), pltpu.VMEM((width, LANES), BF),
        pltpu.SemaphoreType.DMA((2,)),
    ]
    expert_scratch = [
        pltpu.VMEM((3, per_column, hidden_width, width), BF),
        pltpu.SemaphoreType.DMA((3, per_column, 4)),
    ]
    qkv_flops = 2 * tokens * width * qkv_width
    out_flops = 2 * tokens * width * width + 2 * slots * tokens * width
    score_flops = 2 * heads * tokens * length * HEAD_DIM
    expert_flops = 2 * slots * hidden_width * width

    per = slots // columns
    back_like = like((columns, per, width + LANES), BF)
    lanes_like = like((tokens, LANES), F32)
    tables = late([cosine, sine])
    first_flag = (1 - second)

    def forward(keep, came, waits, early, after, shards):
        projected, pairs = [], []
        if keep:
            for m in pieces:
                projected.append(
                    call(
                        project,
                        (Sent(token_wide), Sent(token_low), Sent(token_low), Sent(pair_like)),
                        (Late(came[m]), Late(inputs, (m, 0)), Late(gain_a), *tables), qkv_flops, (dense,),
                        qkv_scratch, (second,), waits=[p[0] for p in projected],
                    )
                )
                pairs.append([projected[m][3]] + [swapped(projected[m][3], s) for s in steps[1:]])
        else:
            made = call(
                functools.partial(project_all, experts),
                (Sent(token_wide), Sent(token_low), Sent(pair_like)) * micro,
                (Late(inputs), *tables), micro * qkv_flops, (dense,),
                [qkv_scratch[0], pltpu.VMEM((width, LANES), BF), qkv_scratch[1]], waits=waits,
            )
            projected = [(made[3 * m], None, made[3 * m + 1]) for m in pieces]
            for m in pieces:
                pair = made[3 * m + 2]
                pairs.append([pair] + [swapped(pair, s) for s in steps[1:]])
        shards = shards or all_shards(pairs[1][1:])
        attended = [
            call(
                functools.partial(attend, keep),
                (Sent(token_wide), Sent(lanes_like), Sent(back_like if keep else block_like))
                + ((Sent(probs_like), Sent(token_low), Sent(token_low)) if keep else ()),
                (*late([projected[m][0], projected[m][2], *pairs[m], biases[m], gain_f, chosens[m],
                        dispatches[m]]), Late(cotangent, (m, 0))),
                out_flops + 2 * score_flops, (dense,), [pltpu.VMEM((tokens, width), BF)] + out_scratch,
                (second,), () if m else after,
            )
            for m in pieces
        ]
        arrived = [over_columns(a[2]) for a in attended]
        lefts, ready = [], ()
        if keep:
            left = call(
                pack, (Sent(like((2 * micro, tokens, width), BF)),),
                late([p[1] for p in projected] + [a[4] for a in attended]), 0,
            )[0]
            two = swapped(left, 2)
            lefts = [left, swapped(left, 1), two, swapped(two, 1)]
            ready = (two,)
        applied = [
            call(
                functools.partial(expert_forward, keep),
                (Sent(block_like),)
                + ((Sent(kept_like),) * 3 + (Sent(back_like),) if keep else ()),
                late([arrived[m], early[m]] if keep else [arrived[m]]),
                (6 if keep else 3) * expert_flops, shards, expert_scratch,
                waits=ready if m else (attended[1][2],),
            )
            for m in pieces
        ]
        return projected, pairs, attended, arrived, applied, lefts, shards

    def weight_call(quarters, which, lefts, rights, waits):
        quarter, some = hidden_width // 4, len(quarters)
        return call(
            functools.partial(expert_weight_grads, quarters[0] * quarter, which),
            (Sent(like((per_column, quarter, width), BF)),) * (some * len(which)), (),
            len(which) * expert_flops, [*lefts, *rights],
            [pltpu.VMEM((len(which), per_column, 2 * columns * ROOMS, some * quarter), BF),
             pltpu.VMEM((len(rights) // 2, per_column, 2 * columns, ROOMS, width), BF),
             pltpu.SemaphoreType.DMA((2, len(which), per_column, 2))],
            waits=waits,
        )

    def merged(halves, waits):
        pairs = [v for a, b in halves for v in (a, swapped(b, 1))]
        return call(add, [Sent(a) for a, unused in halves], late(pairs), 0, waits=waits)

    def attention_back(keep, m, grad, token_grads, waits):
        return call(
            functools.partial(attend_back, keep),
            (Sent(token_wide), Sent(token_low))
            + (Sent(like((tokens, 2 * kv_width + (share if keep else 0)), BF)),) * rows
            + ((Sent(like((tokens, LANES), BF)), Sent(sums_like)) if keep else ()),
            (*late([token_grads, shared[m] if keep else spread, attended[m][1], places[m],
                                 attended[m][0], gain_f]), Late(*grad),
             *late([projected[m][2], *pairs[m], attended[m][3], cosine, sine])),
            out_flops + 4 * score_flops, (dense,), [pltpu.VMEM((tokens, width), BF)] + out_scratch,
            (here, second), waits,
        )

    def parts_of(inner):
        return [inner[2]] + [swapped(inner[2 + s], s) for s in steps[1:]]

    def projection_back(keep, m, inner, parts, waits):
        return call(
            functools.partial(project_back, keep),
            (Sent(token_low),)
            + ((Sent(token_wide),) + (Sent(like((tokens, qkv_width // rows), BF)),) * rows
               if keep else ()),
            (*late([*parts, inner[1], projected[m][0], gain_a, inner[0]]),
             *tables),
            qkv_flops, (dense,), [pltpu.VMEM((tokens, qkv_width), BF)] + qkv_scratch,
            (here,), waits,
        )

    kept = forward(False, None, (gate_shards[2], up_shards[2], down_first), None, (), ())
    attended, early, applied, unused, shards = kept[2:]
    returned = [over_columns(a[0]) for a in applied]
    results = [
        call(
            combine, (Sent(token_low),),
            late([returned[m], attended[m][0], attended[m][1], spread, places[m]]),
            2 * slots * tokens * width, waits=() if m else (applied[1][0],),
        )
        for m in pieces
    ]
    came = [lax.ppermute(r[0], "section", [(0, 1)]) for r in results]

    kept = forward(True, came, (), early, results[1], shards)
    projected, pairs, attended, arrived, applied, lefts, unused = kept
    hidden = [a[1] for a in applied]
    shared = [over_columns(a[4]) for a in applied]
    inner, outer = [], []
    for m in pieces:
        waits = (*lefts[1:], outer[0][0]) if m else (applied[1][4],)
        inner.append(attention_back(False, m, (cotangent, (m, 0)), shared[m], waits))
        outer.append(projection_back(False, m, inner[m], parts_of(inner[m]), ()))
    came = [lax.ppermute(o[0], "section", [(1, 0)]) for o in outer]

    given = [
        call(
            send_grads, (Sent(token_low), Sent(block_like)),
            (Late(came[m]), Late(cotangent, (m, 0)), *late([attended[m][1], dispatches[m]])),
            2 * slots * tokens * width, scalars=(first_flag,), waits=() if m else (inner[1][0],),
        )
        for m in pieces
    ]
    arrived_grads = [over_columns(g[1]) for g in given]
    moved = [
        call(
            expert_backward, (Sent(back_like), Sent(kept_like), Sent(kept_like)),
            late([arrived_grads[m], hidden[m], applied[m][2], applied[m][3], applied[m][0]]),
            3 * expert_flops, shards, expert_scratch,
            (second,), () if m else (given[1][1],),
        )
        for m in pieces
    ]
    gate_up = [a[1] for a in moved] + [a[2] for a in moved]
    down_far = merged([weight_call((2, 3), ((0, 0),), hidden, arrived_grads, ())], ())[0]
    crossed = [swapped(down_far, 2)]
    back = [over_columns(moved[0][0]), over_columns(moved[1][0])]
    inner = [attention_back(True, 0, given[0][:1], back[0], (moved[1][0], down_far))]
    parts = [parts_of(inner[0])]
    both = weight_call((0, 1, 2, 3), ((0, 0), (0, 0)), gate_up, arrived, (inner[0][0],))
    inner.append(attention_back(True, 1, given[1][:1], back[1], (both[0], crossed[0])))
    parts.append(parts_of(inner[1]))
    sums = merged([both[2:4], both[6:]], (inner[1][0],))
    gate_far = hold(sums[0], *parts[1][1:])
    crossed.append(swapped(gate_far, 2))
    o_grads = call(
        out_grads, (Sent(like((columns, rows * shard, share + LANES), BF)),),
        late([*lefts, *[p[s] for s in steps for p in parts], *[a[5] for a in attended],
              *[a[6] for a in inner], *[a[7] for a in inner]]),
        2 * width * length * micro * share, waits=(crossed[0], gate_far),
    )[0]
    last = projection_back(True, 1, inner[1], parts[1], (o_grads,))
    outer = [projection_back(True, 0, inner[0], parts[0], (last[0],)), last]
    backs = [[o[2]] + [swapped(o[2 + s], s) for s in steps[1:]] for o in outer]
    crossed.append(swapped(hold(sums[1], *backs[0][1:], *backs[1][1:]), 2))
    near = weight_call((0, 1), ((0, 0),), hidden, arrived_grads, (outer[1][0],))
    w_grads = call(
        qkv_grads, (Sent(like((columns, rows * shard, qkv_width // rows), BF)),),
        late([*lefts, *[b[s] for s in steps for b in backs]]),
        2 * width * length * micro * qkv_width // rows, waits=(crossed[1], near[0]),
    )[0]
    expert_grads = [
        one.astype(F32) + swapped(other, 1).astype(F32) + c.astype(F32)
        for one, other, c in zip((near[0], both[0], both[4]), (near[1], both[1], both[5]), crossed)
    ]
    layer_outputs = call(
        last_outputs, (Sent(like((micro, tokens, width), F32)),),
        late([spread] + [v for m in pieces for v in (
            back[m], attended[m][0], attended[m][1], places[m], results[m][0])]),
        4 * slots * tokens * width, scalars=(second,), waits=(w_grads,),
    )[0]

    wide = share + qkv_width // rows + LANES
    pieces_out = call(
        fold, (Sent(like((shard, wide), F32)),) * rows,
        late([over_columns(o_grads), over_columns(w_grads)]), 0,
        scratch=[pltpu.VMEM((rows * shard, wide), F32)], scalars=(here,),
    )
    pieces_out = [pieces_out[0]] + [swapped(pieces_out[s], s) for s in steps[1:]]
    o_grad, q_grad, k_grad, v_grad, r_grad, first, second_sum = call(
        finish,
        (like((shard, width), F32), like((shard, width), F32), like((shard, kv_width), F32),
         like((shard, kv_width), F32), like((shard, experts), F32), like((1, shard), F32),
         like((1, shard), F32)),
        late([*pieces_out, w_query[0], w_key[0], w_value[0], attn_gain]), 0,
        scratch=[pltpu.VMEM((shard, qkv_width), F32)], scalars=(here,),
    )

    return (
        layer_outputs[None, :, None],
        jnp.stack([o[1] for o in outer])[None, :, None],
        first,
        q_grad[None],
        k_grad[None],
        v_grad[None],
        o_grad[None],
        second_sum,
        r_grad[None],
        expert_grads[1][None],
        expert_grads[2][None],
        expert_grads[0][None],
    )


def solution(mesh):
    dense = P("section", ("row", "col"), None)
    gain = P("section", ("row", "col"))
    expert = P("section", "col", "row", None)
    token = P(None, "col", "row", None)
    layered = P("section", None, "col", "row", None)
    return jax.shard_map(
        on_device,
        mesh=mesh,
        in_specs=(
            token, token, P(None, "col", None), layered, gain, dense, dense, dense, dense, gain,
            dense, expert, expert, expert,
        ),
        out_specs=(
            layered, layered, gain, dense, dense, dense, dense, gain, dense, expert, expert, expert,
        ),
        check_vma=False,
    )
```
